32 devices in a mesh: row: 4 (over y, x), col: 8 (over z, core).
Axes of the slice: x: 2, y: 2, z: 4, core: 2. Of those that a mesh axis runs over, the one named last changes fastest.
Arguments:
- alignment_embedding: bfloat16 [16, 768, 64], P('row', 'col'), may hold values from -6 to 6
- coupling_embedding: bfloat16 [768, 768, 128], P('row', 'col'), may hold values from -16 to 16
- amino_validity: int32 [768], replicated, may hold values 0 or 1
- alignment_validity: int32 [16, 768], replicated, may hold values 0 or 1
- alignment_matrix: bfloat16 [64, 576], replicated, may hold values from -0.75 to 0.75
- tensor_final_matrix: bfloat16 [1024, 128], replicated, may hold values from -0.1875 to 0.1875
- coupling_logit_matrix: bfloat16 [128, 8], replicated, may hold values from -10 to 10
- mean_final_matrix: bfloat16 [256, 64], replicated, may hold values from -3 to 3
- trimul_matrices: bfloat16 [128, 640], replicated, may hold values from -0.5 to 0.5
- trimul_final_matrix: bfloat16 [128, 128], replicated, may hold values from -0.5 to 0.5
Outputs:
- alignment_updated_embedding: bfloat16 [16, 768, 64], P('row', 'col')
- pair_output: bfloat16 [768, 768, 128], P('row', 'col')
The draws below stay inside these ranges and needn't reach their ends.
All inputs are finite; a program needn't handle non-finite values.
Results may differ from the reference program's by a relative error of at most 0.019.
The reference program's roundings to bfloat16 on the way count: a program that leaves them out, or rounds other values in their place, can miss the bound.
Values may be sent and summed in bfloat16 or wider, within the bound.
No kernel may reach another device: no remote copies, remote signals or barrier semaphores. Data moves between devices by JAX's collectives and lax.ppermute only.
A program may use at most 256 MiB of HBM per device.

```python
import jax
import jax.numpy as jnp
from jax import lax

ALIGN_FEATURES = 64
CZ = 128
TENSOR_FEATURES = 32
MEAN_GROUPS = 8
GROUP_FEATURES = 32
CTRI = 128
ALIGNED_COUNT = 16
AMINO_COUNT = 768


def bias_table(key):
    sub = jax.random.fold_in(key, 11)
    spread = jnp.clip(jax.random.normal(sub, (CZ, MEAN_GROUPS), jnp.float32), -4.0, 4.0)
    table = spread * (1.0 / CZ ** 0.5)
    return table


def draw_coupling_logit_matrix(key, part):
    return bias_table(key).astype(jnp.bfloat16)


def draw_coupling_embedding(key, part):
    keys = [jax.random.fold_in(key, 30 + number) for number in range(9)]
    base = jnp.clip(jax.random.normal(keys[0], (AMINO_COUNT, AMINO_COUNT, CZ), jnp.float32), -6.0, 6.0).astype(jnp.bfloat16)
    return base


def touch_ends(array, own_key, least, largest):
    longest = array.shape.index(max(array.shape))
    spots = []
    for shift in (0, 1):
        where = [jax.random.randint(jax.random.fold_in(own_key, axis), (), 0, length) for axis, length in enumerate(array.shape)]
        where[longest] = (where[longest] + shift) % array.shape[longest]
        spots.append(tuple(where))
    return array.at[spots[0]].set(least).at[spots[1]].set(largest)


def levels(key, extent, shards, smallest, top_value):
    gain, own = 1.0, jax.random.fold_in(key, 6)
    for axis_at, shards_of in shards:
        steps = jnp.exp(jax.random.uniform(jax.random.fold_in(own, axis_at), (shards_of,), jnp.float32, smallest / len(shards), top_value / len(shards)))
        gain = gain * jnp.repeat(steps, extent[axis_at] // shards_of).reshape([-1 if axis == axis_at else 1 for axis in range(len(extent))])
    return gain


def normal_values(own_key, dims, scale, bound, shards=(), held_as=jnp.bfloat16):
    entries = scale * jax.random.normal(own_key, dims, jnp.float32)
    if shards:
        entries = entries * levels(own_key, dims, shards, -0.22, 0.18)
    return jnp.clip(entries, -bound, bound).astype(held_as)


def setup_inputs(seed: int = 0) -> dict:
    key_list = jax.random.split(jax.random.key(seed), 11)
    return {
        "alignment_embedding": normal_values(key_list[0], (ALIGNED_COUNT, AMINO_COUNT, ALIGN_FEATURES), 1.0, 6.0, ((0, 4), (1, 8))),
        "coupling_embedding": draw_coupling_embedding(jax.random.fold_in(key_list[10], 71), 0),
        "amino_validity": touch_ends((jax.random.randint(key_list[2], (AMINO_COUNT,), 0, 8) < 7).astype(jnp.int32), jax.random.fold_in(key_list[2], 1), 0, 1),
        "alignment_validity": touch_ends((jax.random.randint(key_list[3], (ALIGNED_COUNT, AMINO_COUNT), 0, 4) < 3).astype(jnp.int32), jax.random.fold_in(key_list[3], 1), 0, 1),
        "alignment_matrix": normal_values(key_list[4], (ALIGN_FEATURES, 2 * TENSOR_FEATURES + 2 * MEAN_GROUPS * GROUP_FEATURES), ALIGN_FEATURES ** -0.5, 0.75),
        "tensor_final_matrix": normal_values(key_list[5], (TENSOR_FEATURES * TENSOR_FEATURES, CZ), (TENSOR_FEATURES * TENSOR_FEATURES) ** -0.5, 0.1875),
        "coupling_logit_matrix": draw_coupling_logit_matrix(jax.random.fold_in(key_list[10], 71), 0),
        "mean_final_matrix": normal_values(key_list[7], (MEAN_GROUPS * GROUP_FEATURES, ALIGN_FEATURES), 4 ** -0.5, 3.0),
        "trimul_matrices": normal_values(key_list[8], (CZ, 4 * CTRI + CZ), CZ ** -0.5, 0.5),
        "trimul_final_matrix": normal_values(key_list[9], (CTRI, CZ), CTRI ** -0.5, 0.5),
    }


EPS = 1e-05
MASK_PENALTY = 10000.0

def standardize_features(values_in, axis):
    centre = values_in - lax.optimization_barrier(jnp.mean(values_in, axis=axis, keepdims=True))
    spread = lax.optimization_barrier(jnp.mean(centre * centre, axis=axis, keepdims=True))
    return centre * lax.rsqrt(spread + EPS)

def reference(alignment_embedding, coupling_embedding, amino_validity, alignment_validity, alignment_matrix, tensor_final_matrix, coupling_logit_matrix, mean_final_matrix, trimul_matrices, trimul_final_matrix):
    alignment_range, amino_range, alignment_feature_count = alignment_embedding.shape
    active_entries = amino_validity.astype(jnp.float32)
    first_factor = (jnp.arange(alignment_range) == 0)[:, None]
    present_entries = jnp.where(first_factor, jnp.float32(1.0), alignment_validity.astype(jnp.float32)) * active_entries[None, :]
    alignment_standardized = standardize_features(alignment_embedding.astype(jnp.float32), 2).astype(jnp.bfloat16)
    projected_rows = jnp.dot(alignment_standardized.reshape(alignment_range * amino_range, alignment_feature_count), alignment_matrix, preferred_element_type=jnp.float32).reshape(alignment_range, amino_range, -1)
    left = (projected_rows[:, :, :TENSOR_FEATURES] * present_entries[:, :, None]).astype(jnp.bfloat16)
    right = (projected_rows[:, :, TENSOR_FEATURES:2 * TENSOR_FEATURES] * present_entries[:, :, None]).astype(jnp.bfloat16)
    values = projected_rows[:, :, 2 * TENSOR_FEATURES:2 * TENSOR_FEATURES + MEAN_GROUPS * GROUP_FEATURES].astype(jnp.bfloat16)
    sequence_gate = jax.nn.sigmoid(projected_rows[:, :, 2 * TENSOR_FEATURES + MEAN_GROUPS * GROUP_FEATURES:])
    count = jnp.dot(present_entries.T, present_entries, precision=lax.Precision.HIGHEST)
    block = min(amino_range, 64)
    nblocks = amino_range // block
    right_wide = right.astype(jnp.float32)

    def front(index):
        start = (index * block).astype(jnp.int32)
        left_block = lax.dynamic_slice_in_dim(left, start, block, 1).astype(jnp.float32)
        outer = jnp.einsum('sic,sjd->ijcd', left_block, right_wide).astype(jnp.bfloat16)
        update = jnp.dot(outer.reshape(block * amino_range, TENSOR_FEATURES * TENSOR_FEATURES), tensor_final_matrix, preferred_element_type=jnp.float32).reshape(block, amino_range, -1)
        count_block = lax.dynamic_slice_in_dim(count, start, block, 0)
        pair_block = lax.dynamic_slice_in_dim(coupling_embedding, start, block, 0).astype(jnp.float32)
        mid = (pair_block + update / jnp.maximum(count_block, 1.0)[:, :, None]).astype(jnp.bfloat16)
        normed = standardize_features(mid.astype(jnp.float32), 2).astype(jnp.bfloat16).reshape(block * amino_range, -1)
        live_block = lax.dynamic_slice_in_dim(active_entries, start, block, 0)
        logits = jnp.dot(normed, coupling_logit_matrix, preferred_element_type=jnp.float32).reshape(block, amino_range, MEAN_GROUPS)
        logits = logits + MASK_PENALTY * (live_block - 1.0)[:, None, None]
        tri = jnp.dot(normed, trimul_matrices, preferred_element_type=jnp.float32).reshape(block, amino_range, -1)
        pair_live = (live_block[:, None] * active_entries[None, :])[:, :, None]
        tri_left = (jax.nn.sigmoid(tri[:, :, :CTRI]) * tri[:, :, CTRI:2 * CTRI] * pair_live).astype(jnp.bfloat16)
        tri_right = (jax.nn.sigmoid(tri[:, :, 2 * CTRI:3 * CTRI]) * tri[:, :, 3 * CTRI:4 * CTRI] * pair_live).astype(jnp.bfloat16)
        return (mid, logits, jnp.transpose(tri_left, (2, 0, 1)), jnp.transpose(tri_right, (2, 0, 1)))
    mid, logits, tri_left, tri_right = lax.map(front, jnp.arange(nblocks, dtype=jnp.int32))
    mid = mid.reshape(amino_range, amino_range, -1)
    logits = logits.reshape(amino_range, amino_range, MEAN_GROUPS)
    tri_left = jnp.transpose(tri_left, (1, 0, 2, 3)).reshape(CTRI, amino_range, amino_range)
    tri_right = jnp.transpose(tri_right, (1, 0, 2, 3)).reshape(CTRI, amino_range, amino_range)
    weights = jax.nn.softmax(logits, axis=0).astype(jnp.bfloat16)
    value_heads = values.reshape(alignment_range, amino_range, MEAN_GROUPS, GROUP_FEATURES).astype(jnp.float32)
    head_averaged = jnp.einsum('jih,sjhd->sihd', weights.astype(jnp.float32), value_heads).reshape(alignment_range, amino_range, MEAN_GROUPS * GROUP_FEATURES)
    gated_result = (sequence_gate * head_averaged).astype(jnp.bfloat16)
    blended_update = jnp.dot(gated_result.reshape(alignment_range * amino_range, -1), mean_final_matrix, preferred_element_type=jnp.float32).reshape(alignment_range, amino_range, -1)
    alignment_updated_embedding = (alignment_embedding.astype(jnp.float32) + blended_update).astype(jnp.bfloat16)
    channel_block = 8

    def triangle(index):
        start = (index * channel_block).astype(jnp.int32)
        first_part = lax.dynamic_slice_in_dim(tri_left, start, channel_block, 0).astype(jnp.float32)
        second_part = lax.dynamic_slice_in_dim(tri_right, start, channel_block, 0).astype(jnp.float32)
        return jnp.einsum('cik,cjk->cij', first_part, second_part).astype(jnp.bfloat16)
    product = lax.map(triangle, jnp.arange(CTRI // channel_block, dtype=jnp.int32)).reshape(CTRI, amino_range, amino_range)
    w_gate_tri = trimul_matrices[:, 4 * CTRI:]
    w_out_wide = trimul_final_matrix.astype(jnp.float32)

    def finish(index):
        start = (index * block).astype(jnp.int32)
        mid_block = lax.dynamic_slice_in_dim(mid, start, block, 0)
        normed = standardize_features(mid_block.astype(jnp.float32), 2).astype(jnp.bfloat16).reshape(block * amino_range, -1)
        tri_gate = jax.nn.sigmoid(jnp.dot(normed, w_gate_tri, preferred_element_type=jnp.float32)).reshape(block, amino_range, -1)
        product_block = lax.dynamic_slice_in_dim(product, start, block, 1).astype(jnp.float32)
        product_normed = standardize_features(product_block, 0).astype(jnp.bfloat16)
        out = jnp.einsum('cij,ce->ije', product_normed.astype(jnp.float32), w_out_wide)
        return (mid_block.astype(jnp.float32) + tri_gate * out).astype(jnp.bfloat16)
    pair_output = lax.map(finish, jnp.arange(nblocks, dtype=jnp.int32)).reshape(amino_range, amino_range, -1)
    return (alignment_updated_embedding, pair_output)
```

```python
import functools

import jax
import jax.numpy as jnp
from jax import lax
from jax.experimental import pallas as pl
from jax.experimental.pallas import tpu as pltpu
from jax.sharding import Mesh, PartitionSpec as P

TENSOR_FEATURES = 32
MEAN_GROUPS = 8
GROUP_FEATURES = 32
CTRI = 128

EPS = 1e-05
MASK_PENALTY = 10000.0
QUAD = 4
LANES = 128
VMEM_LIMIT = 60 * 1024 * 1024
AXES = ("row", "half", "pos")
GROUP = ("row", "pos")
F32 = jnp.float32
BF16 = jnp.bfloat16
NT = (((1,), (1,)), ((), ()))
TN = (((0,), (0,)), ((), ()))


def standardize_features(values_in, axis):
    centre = values_in - jnp.mean(values_in, axis=axis, keepdims=True)
    spread = jnp.mean(centre * centre, axis=axis, keepdims=True)
    return centre * lax.rsqrt(spread + EPS)


def sigmoid(x):
    return 0.5 * jnp.tanh(0.5 * x) + 0.5


def params(grid_dims=1):
    return pltpu.CompilerParams(
        vmem_limit_bytes=VMEM_LIMIT, dimension_semantics=("arbitrary",) * grid_dims
    )


def whole(shape):
    zeros = (0,) * len(shape)
    return pl.BlockSpec(shape, lambda *_: zeros, pipeline_mode=pl.Buffered(1))


def pack_rows(rows):
    unit = rows[0].shape[0] // 3
    return jnp.concatenate([r[: 2 * unit] for r in rows] + [r[2 * unit :] for r in rows], axis=0)


def unpack_rows(packed):
    unit = packed.shape[0] // 12
    return [
        jnp.concatenate(
            [
                packed[2 * unit * a : 2 * unit * (a + 1)],
                packed[8 * unit + unit * a : 8 * unit + unit * (a + 1)],
            ],
            axis=0,
        )
        for a in range(QUAD)
    ]


def swap_blocks(first, second, width, lane):
    low = (lane // width) % 2 == 0
    size = first.shape[1]
    return (
        jnp.where(low, first, pltpu.roll(second, width, 1)),
        jnp.where(low, pltpu.roll(first, size - width, 1), second),
    )


def exchange_blocks(packed):
    part = packed
    unit = LANES // 4
    lane = lax.broadcasted_iota(jnp.int32, part[0][0].shape, 1)
    out = [[None] * 3 for _ in range(4)]
    for pair in range(2):
        one, two = part[2 * pair], part[2 * pair + 1]
        for t in range(2):
            out[2 * t][pair], out[2 * t + 1][pair] = swap_blocks(one[t], two[t], 2 * unit, lane)
    u0, u2 = swap_blocks(part[0][2], part[2][2], 2 * unit, lane)
    u1, u3 = swap_blocks(part[1][2], part[3][2], 2 * unit, lane)
    out[0][2], out[1][2] = swap_blocks(u0, u1, unit, lane)
    out[2][2], out[3][2] = swap_blocks(u2, u3, unit, lane)
    return out


def front_kernel(left_ref, present_ref, coup_ref, weight_ref, right_ref, pcol_ref, mid_ref, normed_ref, tmp_ref):
    block = coup_ref.shape[0]
    seqs = left_ref.shape[0] // block
    wide = coup_ref.shape[2]
    features = weight_ref.shape[1] // wide
    step = 4
    for low in range(0, features, step):
        part = jnp.dot(
            left_ref[...], weight_ref[:, low * wide : (low + step) * wide], preferred_element_type=F32
        ).astype(BF16)
        for i in range(block):
            for d in range(step):
                tmp_ref[
                    i // 2,
                    (low + d) * seqs : (low + d + 1) * seqs,
                    (i % 2) * wide : (i % 2 + 1) * wide,
                ] = part[i * seqs : (i + 1) * seqs, d * wide : (d + 1) * wide]
    for pair in range(block // 2):
        update = jnp.dot(right_ref[...], tmp_ref[pair], preferred_element_type=F32)
        count = jnp.dot(pcol_ref[...], present_ref[pair], preferred_element_type=F32)
        update = update / jnp.maximum(count, 1.0)
        for e in range(2):
            i = 2 * pair + e
            mid = (coup_ref[i].astype(F32) + update[:, e * wide : (e + 1) * wide]).astype(BF16)
            mid_ref[i] = mid
            normed_ref[i] = standardize_features(mid.astype(F32), 1).astype(BF16)


def front(left_rows, present_pairs, coupling, w_tensor, right_cols, present_cols):
    rows, cols, wide = coupling.shape
    seqs = left_rows.shape[0] // rows
    block = 8
    tile = pl.BlockSpec((block, cols, wide), lambda i: (i, 0, 0))
    return pl.pallas_call(
        front_kernel,
        grid=(rows // block,),
        in_specs=[
            pl.BlockSpec((block * seqs, left_rows.shape[1]), lambda i: (i, 0)),
            pl.BlockSpec((block // 2, seqs, 2 * wide), lambda i: (i, 0, 0)),
            tile,
            whole(w_tensor.shape),
            whole(right_cols.shape),
            whole(present_cols.shape),
        ],
        out_specs=[tile, tile],
        out_shape=[jax.ShapeDtypeStruct(coupling.shape, BF16)] * 2,
        scratch_shapes=[pltpu.VMEM((block // 2, right_cols.shape[1], 2 * wide), BF16)],
        compiler_params=params(),
        name="front",
    )(left_rows, present_pairs, coupling, w_tensor, right_cols, present_cols)


def project_kernel(normed_ref, live_ref, weight_ref, out_ref, tmp_ref):
    quads = normed_ref.shape[0] // QUAD
    dests = out_ref.shape[0]
    each = out_ref.shape[1] // quads
    count = dests * each
    for m in range(quads):
        packed = pack_rows([normed_ref[QUAD * m + a] for a in range(QUAD)])
        both = lax.dot_general(weight_ref[...], packed, NT, preferred_element_type=F32)
        gated = sigmoid(both[:count]) * both[count:] * live_ref[m]
        for dest in range(dests):
            tmp_ref[dest, m * each : (m + 1) * each] = gated[dest * each : (dest + 1) * each]
    out_ref[...] = tmp_ref[...].astype(BF16)


def project(normed, live, weight, dests):
    rows, cols, wide = normed.shape
    quads = 8
    each = weight.shape[0] // (2 * dests)
    lanes = QUAD * cols
    total = rows // QUAD
    return pl.pallas_call(
        project_kernel,
        grid=(total // quads,),
        in_specs=[
            pl.BlockSpec((quads * QUAD, cols, wide), lambda i: (i, 0, 0)),
            pl.BlockSpec((quads, 1, lanes), lambda i: (i, 0, 0)),
            whole(weight.shape),
        ],
        out_specs=pl.BlockSpec((dests, quads * each, lanes), lambda i: (0, i, 0)),
        out_shape=jax.ShapeDtypeStruct((dests, total * each, lanes), BF16),
        scratch_shapes=[pltpu.VMEM((dests, quads * each, lanes), F32)],
        compiler_params=params(),
        name="project",
    )(normed, live, weight)


def assemble_kernel(half_ref, recv_ref, left_ref, own_ref, send_ref, flat_ref, right_ref, *, row_count, pos_count):
    channel = pl.program_id(0)
    lanes = recv_ref.shape[2]
    unit = lanes // 12
    cols = 3 * unit
    each = send_ref.shape[1] // (row_count * QUAD)
    stride = recv_ref.shape[1] // each
    groups = pos_count // 4
    tiles = lanes // LANES
    per_row = each * QUAD // cols

    @pl.when(channel == 0)
    def _():
        for src in range(row_count * pos_count):
            value = recv_ref[src].astype(F32)
            for t in range(tiles):
                flat_ref[src, t] = value[:, t * LANES : (t + 1) * LANES]

    def block(row, group, index):
        packed = []
        for p in range(4):
            src = row * pos_count + group * 4 + p
            packed.append(
                [flat_ref[src, t, pl.ds(index, each, stride=stride), :] for t in range(tiles)]
            )
        return exchange_blocks(packed)

    for row in range(row_count):
        for group in range(groups):
            span = slice(group * lanes, (group + 1) * lanes)
            left = block(row, group, channel)
            for a in range(QUAD):
                start = (row * QUAD + a) * each
                left_ref[0, start : start + each, span] = jnp.concatenate(left[a], axis=1).astype(
                    BF16
                )
            right = block(row, group, channel + stride // 2)
            for a in range(QUAD):
                for piece in range(per_row):
                    place = row * per_row + piece
                    base = (place // 4) * lanes
                    low = piece * (cols // QUAD)
                    mid = low + 2 * unit // QUAD
                    high = low + cols // QUAD
                    first = base + (place % 4) * 2 * unit + a
                    second = base + 8 * unit + (place % 4) * unit + a
                    for t in range(tiles):
                        value = right[a][t]
                        at = group * tiles + t
                        right_ref[at, pl.ds(first, mid - low, stride=QUAD), :] = value[low:mid]
                        right_ref[at, pl.ds(second, high - mid, stride=QUAD), :] = value[mid:high]
    width = pos_count * cols
    own = pl.multiple_of(half_ref[0] * width, width)
    other = pl.multiple_of((1 - half_ref[0]) * width, width)
    theirs = []
    for at in range(groups * tiles):
        span = slice(at * LANES, (at + 1) * LANES)
        own_ref[0, :, span] = right_ref[at, pl.ds(own, width), :].astype(BF16)
        theirs.append(right_ref[at, pl.ds(other, width), :].astype(BF16))
    theirs = jnp.concatenate(theirs, axis=1)
    for row in range(row_count):
        span = slice(row * QUAD * each, (row + 1) * QUAD * each)
        send_ref[0, span] = lax.dot_general(
            left_ref[0, span], theirs, NT, preferred_element_type=F32
        ).astype(BF16)


def assemble(half, received, row_count, pos_count, cols):
    sources, height, lanes = received.shape
    each = (2 * pos_count * cols) // (row_count * QUAD)
    stride = height // each
    channels = stride // 2
    depth = pos_count * cols
    rows = 2 * depth
    return pl.pallas_call(
        functools.partial(assemble_kernel, row_count=row_count, pos_count=pos_count),
        grid=(channels,),
        in_specs=[pl.BlockSpec(memory_space=pltpu.SMEM), whole(received.shape)],
        out_specs=[
            pl.BlockSpec((1, rows, depth), lambda c: (c, 0, 0)),
            pl.BlockSpec((1, depth, depth), lambda c: (c, 0, 0)),
            pl.BlockSpec((1, rows, depth), lambda c: (c, 0, 0)),
        ],
        out_shape=[
            jax.ShapeDtypeStruct((channels, rows, depth), BF16),
            jax.ShapeDtypeStruct((channels, depth, depth), BF16),
            jax.ShapeDtypeStruct((channels, rows, depth), BF16),
        ],
        scratch_shapes=[
            pltpu.VMEM((sources, lanes // LANES, height, LANES), F32),
            pltpu.VMEM((depth // LANES, rows, LANES), F32),
        ],
        compiler_params=params(),
        name="assemble",
    )(half, received)


def combine_kernel(left_ref, own_ref, recv_ref, out_ref, tmp_ref, *, row_count, pos_count):
    channel = pl.program_id(0)
    channels = pl.num_programs(0)
    lanes = out_ref.shape[2]
    each = left_ref.shape[1] // (row_count * QUAD)
    stride = out_ref.shape[1] // each
    tiles = lanes // LANES
    for row in range(row_count):
        for group in range(pos_count // 4):
            cols = slice(group * lanes, (group + 1) * lanes)
            blocks = []
            for a in range(QUAD):
                span = slice((row * QUAD + a) * each, (row * QUAD + a + 1) * each)
                value = lax.dot_general(
                    left_ref[0, span], own_ref[0, cols], NT, preferred_element_type=F32
                )
                value = value + recv_ref[0, span, cols].astype(F32)
                blocks.append([value[:, t * LANES : (t + 1) * LANES] for t in range(tiles)])
            for p, value in enumerate(exchange_blocks(blocks)):
                dest = row * pos_count + group * 4 + p
                for t in range(tiles):
                    tmp_ref[dest, t, pl.ds(channel, each, stride=stride), :] = value[t]

    @pl.when(channel == channels - 1)
    def _():
        for dest in range(row_count * pos_count):
            for t in range(tiles):
                out_ref[dest, :, t * LANES : (t + 1) * LANES] = tmp_ref[dest, t].astype(BF16)


def combine(left, own, received, row_count, pos_count, cols):
    channels, rows, depth = left.shape
    each = rows // (row_count * QUAD)
    shape = (row_count * pos_count, each * channels, QUAD * cols)
    return pl.pallas_call(
        functools.partial(combine_kernel, row_count=row_count, pos_count=pos_count),
        grid=(channels,),
        in_specs=[
            pl.BlockSpec((1, rows, depth), lambda c: (c, 0, 0)),
            pl.BlockSpec((1, depth, depth), lambda c: (c, 0, 0)),
            pl.BlockSpec((1, rows, depth), lambda c: (c, 0, 0)),
        ],
        out_specs=whole(shape),
        out_shape=jax.ShapeDtypeStruct(shape, BF16),
        scratch_shapes=[pltpu.VMEM((shape[0], shape[2] // LANES, shape[1], LANES), F32)],
        compiler_params=params(),
        name="combine",
    )(left, own, received)


def finish_kernel(*refs, chunks):
    parts = refs[:chunks]
    mid_ref, normed_ref, gate_ref, weight_ref, out_ref, tmp_ref = refs[chunks:]
    quads = mid_ref.shape[0] // QUAD
    sources = parts[0].shape[0]
    each = parts[0].shape[1] // quads
    total = sources * each * chunks
    for g, part in enumerate(parts):
        for src in range(sources):
            value = part[src].astype(F32)
            for m in range(quads):
                start = m * total + (src * chunks + g) * each
                tmp_ref[start : start + each] = value[m * each : (m + 1) * each]
    for m in range(quads):
        product = tmp_ref[m * total : (m + 1) * total]
        normed = standardize_features(product, 0).astype(BF16)
        out = lax.dot_general(normed, weight_ref[...], TN, preferred_element_type=F32)
        for a, value in enumerate(unpack_rows(out)):
            i = QUAD * m + a
            gate = sigmoid(jnp.dot(normed_ref[i], gate_ref[...], preferred_element_type=F32))
            out_ref[i] = (mid_ref[i].astype(F32) + gate * value).astype(BF16)


def finish(parts, mid, normed, w_gate, w_final):
    rows, cols, wide = mid.shape
    chunks = len(parts)
    sources, height, lanes = parts[0].shape
    total = rows // QUAD
    each = height // total
    quads = 8
    tile = pl.BlockSpec((quads * QUAD, cols, wide), lambda i: (i, 0, 0))
    return pl.pallas_call(
        functools.partial(finish_kernel, chunks=chunks),
        grid=(total // quads,),
        in_specs=[pl.BlockSpec((sources, quads * each, lanes), lambda i: (0, i, 0))] * chunks
        + [tile, tile, whole(w_gate.shape), whole(w_final.shape)],
        out_specs=tile,
        out_shape=jax.ShapeDtypeStruct(mid.shape, BF16),
        scratch_shapes=[pltpu.VMEM((quads * sources * each * chunks, lanes), F32)],
        compiler_params=params(),
        name="finish",
    )(*parts, mid, normed, w_gate, w_final)


def on_device(
    alignment_embedding,
    coupling_embedding,
    amino_validity,
    alignment_validity,
    alignment_matrix,
    tensor_final_matrix,
    coupling_logit_matrix,
    mean_final_matrix,
    trimul_matrices,
    trimul_final_matrix,
):
    seq_each, module_number, feature_count = alignment_embedding.shape
    rows, _, wide = coupling_embedding.shape
    row_count = lax.axis_size("row")
    pos_count = lax.axis_size("pos")
    col_count = 2 * pos_count
    row_index = lax.axis_index("row")
    half = lax.axis_index("half")
    col_index = half * pos_count + lax.axis_index("pos")
    seqs = seq_each * row_count
    active_entries = amino_validity.astype(F32)
    sequence_index = lax.broadcasted_iota(jnp.int32, alignment_validity.shape, 0)
    present_entries = (
        jnp.where(sequence_index == 0, F32(1.0), alignment_validity.astype(F32))
        * active_entries[None, :]
    )
    row_start = row_index * rows
    col_start = col_index * module_number
    present_rows = lax.dynamic_slice_in_dim(present_entries, row_start, rows, 1)
    present_cols = lax.dynamic_slice_in_dim(present_entries, col_start, module_number, 1)
    live_rows = lax.dynamic_slice_in_dim(active_entries, row_start, rows, 0)
    live_cols = lax.dynamic_slice_in_dim(active_entries, col_start, module_number, 0)

    gathered = lax.all_gather(alignment_embedding, AXES, axis=0, tiled=False)
    gathered = gathered.reshape(row_count, col_count, seq_each, module_number, feature_count)
    per_row = rows // module_number
    row_part = lax.dynamic_slice_in_dim(gathered, row_index * per_row, per_row, 1)
    row_part = jnp.transpose(row_part, (1, 3, 0, 2, 4)).reshape(rows * seqs, feature_count)
    col_part = lax.dynamic_slice_in_dim(gathered, col_index, 1, 1)
    col_part = col_part.reshape(seqs * module_number, feature_count)

    def project_msa(part, matrix):
        normed = standardize_features(part.astype(F32), 1).astype(BF16)
        return jnp.dot(normed, matrix, preferred_element_type=F32)

    left_rows = (
        project_msa(row_part, alignment_matrix[:, :TENSOR_FEATURES])
        * present_rows.T.reshape(rows * seqs, 1)
    ).astype(BF16)
    right = project_msa(col_part, alignment_matrix[:, TENSOR_FEATURES : 2 * TENSOR_FEATURES])
    right = (right * present_cols.reshape(seqs * module_number, 1)).astype(BF16)
    right_cols = jnp.transpose(
        right.reshape(seqs, module_number, TENSOR_FEATURES), (1, 2, 0)
    ).reshape(module_number, TENSOR_FEATURES * seqs)
    present_pairs = jnp.broadcast_to(
        jnp.transpose(present_rows.reshape(seqs, rows // 2, 2), (1, 0, 2))[..., None],
        (rows // 2, seqs, 2, wide),
    ).reshape(rows // 2, seqs, 2 * wide).astype(BF16)
    w_tensor = tensor_final_matrix.reshape(TENSOR_FEATURES, TENSOR_FEATURES * wide)
    pair_mid, pair_normed = front(
        left_rows,
        present_pairs,
        coupling_embedding,
        w_tensor,
        right_cols,
        present_cols.T.astype(BF16),
    )

    unit = module_number // 3
    pair_live = live_rows[:, None] * live_cols[None, :]
    quad_live = pair_live.reshape(rows // QUAD, QUAD, module_number)
    live_packed = jnp.concatenate(
        [
            quad_live[:, :, : 2 * unit].reshape(rows // QUAD, -1),
            quad_live[:, :, 2 * unit :].reshape(rows // QUAD, -1),
        ],
        axis=1,
    )[:, None, :]

    devices = row_count * pos_count
    channels = CTRI // devices
    each = min(4, channels)
    chunks = channels // each
    w_kinds = trimul_matrices[:, : 4 * CTRI].T.reshape(2, 2, devices, chunks, each, wide)
    half_scalar = half.astype(jnp.int32).reshape(1)
    pos_half = pos_count
    swap = [(0, 1), (1, 0)]
    returned = []
    for g in range(chunks):
        weight = jnp.transpose(w_kinds[:, :, :, g], (1, 2, 0, 3, 4)).reshape(-1, wide)
        sent = project(pair_normed, live_packed, weight, devices)
        received = lax.all_to_all(sent, GROUP, split_axis=0, concat_axis=0, tiled=True)
        left, own, theirs = assemble(half_scalar, received, row_count, pos_half, module_number)
        partial = lax.ppermute(theirs, "half", swap)
        product = combine(left, own, partial, row_count, pos_half, module_number)
        returned.append(lax.all_to_all(product, GROUP, split_axis=0, concat_axis=0, tiled=True))

    own_rows = project_msa(
        alignment_embedding.reshape(seq_each * module_number, feature_count),
        alignment_matrix[:, 2 * TENSOR_FEATURES :],
    ).reshape(seq_each, module_number, -1)
    values = own_rows[:, :, : MEAN_GROUPS * GROUP_FEATURES].astype(BF16)
    sequence_gate = jax.nn.sigmoid(own_rows[:, :, MEAN_GROUPS * GROUP_FEATURES :])
    logits = (
        jnp.dot(
            pair_normed.reshape(rows * module_number, wide),
            coupling_logit_matrix,
            preferred_element_type=F32,
        ).reshape(rows, module_number, MEAN_GROUPS)
        + MASK_PENALTY * (live_rows - 1.0)[:, None, None]
    )
    logits_all = lax.all_gather(logits, "row", axis=0, tiled=True)
    values_all = lax.all_gather(values, ("half", "pos"), axis=1, tiled=True)
    top_all = jnp.max(logits_all, axis=0)
    expd = jnp.exp(logits_all - top_all[None])
    weights_all = (expd / jnp.sum(expd, axis=0)[None]).astype(BF16)
    value_all_heads = values_all.reshape(seq_each, -1, MEAN_GROUPS, GROUP_FEATURES)
    summed = jnp.einsum("jih,sjhd->sihd", weights_all, value_all_heads, preferred_element_type=F32)
    head_averaged = summed.reshape(seq_each, module_number, MEAN_GROUPS * GROUP_FEATURES)
    gated_result = (sequence_gate * head_averaged).astype(BF16)
    blended_update = jnp.dot(
        gated_result.reshape(seq_each * module_number, -1),
        mean_final_matrix,
        preferred_element_type=F32,
    ).reshape(seq_each, module_number, -1)
    alignment_updated_embedding = (alignment_embedding.astype(F32) + blended_update).astype(BF16)

    pair_output = finish(
        returned, pair_mid, pair_normed, trimul_matrices[:, 4 * CTRI :], trimul_final_matrix
    )
    return (alignment_updated_embedding, pair_output)


def solution(mesh):
    rows, cols = mesh.devices.shape
    inner = Mesh(mesh.devices.reshape(rows, 2, cols // 2), AXES)
    tile = P("row", ("half", "pos"), None)
    in_specs = (tile, tile) + (P(),) * 8
    return jax.shard_map(
        on_device, mesh=inner, in_specs=in_specs, out_specs=(tile, tile), check_vma=False
    )
```

```python
import functools

import jax
import jax.numpy as jnp
from jax import lax
from jax.experimental import pallas as pl
from jax.experimental.pallas import tpu as pltpu
from jax.sharding import Mesh, PartitionSpec as P

TENSOR_FEATURES = 32
MEAN_GROUPS = 8
GROUP_FEATURES = 32
CTRI = 128

EPS = 1e-05
MASK_PENALTY = 10000.0
QUAD = 4
LANES = 128
VMEM_LIMIT = 60 * 1024 * 1024
AXES = ("row", "half", "pos")
GROUP = ("row", "pos")
F32 = jnp.float32
BF16 = jnp.bfloat16
NT = (((1,), (1,)), ((), ()))
TN = (((0,), (0,)), ((), ()))


def standardize_features(values_in, axis):
    centre = values_in - jnp.mean(values_in, axis=axis, keepdims=True)
    spread = jnp.mean(centre * centre, axis=axis, keepdims=True)
    return centre * lax.rsqrt(spread + EPS)


def sigmoid(x):
    return 0.5 * jnp.tanh(0.5 * x) + 0.5


def params(grid_dims=1):
    return pltpu.CompilerParams(
        vmem_limit_bytes=VMEM_LIMIT, dimension_semantics=("arbitrary",) * grid_dims
    )


def whole(shape):
    zeros = (0,) * len(shape)
    return pl.BlockSpec(shape, lambda *_: zeros, pipeline_mode=pl.Buffered(1))


def anywhere(after):
    return [pl.BlockSpec(memory_space=pl.ANY)] * len(after)


def pack_rows(rows):
    unit = rows[0].shape[0] // 3
    return jnp.concatenate([r[: 2 * unit] for r in rows] + [r[2 * unit :] for r in rows], axis=0)


def unpack_rows(packed):
    unit = packed.shape[0] // 12
    return [
        jnp.concatenate(
            [
                packed[2 * unit * a : 2 * unit * (a + 1)],
                packed[8 * unit + unit * a : 8 * unit + unit * (a + 1)],
            ],
            axis=0,
        )
        for a in range(QUAD)
    ]


def swap_blocks(first, second, width, lane):
    low = (lane // width) % 2 == 0
    size = first.shape[1]
    return (
        jnp.where(low, first, pltpu.roll(second, width, 1)),
        jnp.where(low, pltpu.roll(first, size - width, 1), second),
    )


def exchange_blocks(packed):
    part = packed
    unit = LANES // 4
    lane = lax.broadcasted_iota(jnp.int32, part[0][0].shape, 1)
    out = [[None] * 3 for _ in range(4)]
    for pair in range(2):
        one, two = part[2 * pair], part[2 * pair + 1]
        for t in range(2):
            out[2 * t][pair], out[2 * t + 1][pair] = swap_blocks(one[t], two[t], 2 * unit, lane)
    u0, u2 = swap_blocks(part[0][2], part[2][2], 2 * unit, lane)
    u1, u3 = swap_blocks(part[1][2], part[3][2], 2 * unit, lane)
    out[0][2], out[1][2] = swap_blocks(u0, u1, unit, lane)
    out[2][2], out[3][2] = swap_blocks(u2, u3, unit, lane)
    return out


def front_kernel(place_ref, *refs, row_count, col_count):
    lefts, rights = refs[:col_count], refs[col_count : col_count + row_count]
    refs = refs[col_count + row_count :]
    present_ref, coup_ref, weight_ref, pcol_ref, mid_ref, normed_ref = refs[:6]
    sides_ref, right_ref, tmp_ref = refs[6:]
    block, cols, wide = coup_ref.shape
    seq_each, _, width = lefts[0].shape
    seqs = seq_each * row_count
    per_row = col_count // row_count

    @pl.when(pl.program_id(0) == 0)
    def _():
        for t, part in enumerate(lefts):
            index = lax.rem(t + place_ref[1], col_count)
            first = lax.rem(index, per_row) * (cols * seqs) + index // per_row * seq_each
            for k in range(seq_each):
                sides_ref[pl.ds(first + k, cols, stride=seqs), 0:width] = part[k].astype(F32)
        right = jnp.zeros(right_ref.shape, F32)
        feature = lax.broadcasted_iota(jnp.int32, (width, width * seqs), 0)
        target = lax.broadcasted_iota(jnp.int32, (width, width * seqs), 1)
        for t, part in enumerate(rights):
            first = lax.rem(t + place_ref[0], row_count) * seq_each
            for k in range(seq_each):
                spread = (target == feature * seqs + (first + k)).astype(F32).astype(BF16)
                right += jnp.dot(part[k], spread, preferred_element_type=F32)
        right_ref[...] = right.astype(BF16)

    span = block * seqs
    start = pl.multiple_of(pl.program_id(0) * span, span)
    left = sides_ref[pl.ds(start, span), 0:width].astype(BF16)
    features = weight_ref.shape[1] // wide
    step = 4
    for low in range(0, features, step):
        part = jnp.dot(
            left, weight_ref[:, low * wide : (low + step) * wide], preferred_element_type=F32
        ).astype(BF16)
        for i in range(block):
            for d in range(step):
                tmp_ref[
                    i // 2,
                    (low + d) * seqs : (low + d + 1) * seqs,
                    (i % 2) * wide : (i % 2 + 1) * wide,
                ] = part[i * seqs : (i + 1) * seqs, d * wide : (d + 1) * wide]
    for pair in range(block // 2):
        update = jnp.dot(right_ref[...], tmp_ref[pair], preferred_element_type=F32)
        count = jnp.dot(pcol_ref[...], present_ref[pair], preferred_element_type=F32)
        update = update / jnp.maximum(count, 1.0)
        for e in range(2):
            i = 2 * pair + e
            mid = (coup_ref[i].astype(F32) + update[:, e * wide : (e + 1) * wide]).astype(BF16)
            mid_ref[i] = mid
            normed_ref[i] = standardize_features(mid.astype(F32), 1).astype(BF16)


def front(place, lefts, rights, present_pairs, coupling, w_tensor, present_cols):
    rows, cols, wide = coupling.shape
    seqs, width = present_pairs.shape[1], lefts[0].shape[2]
    block = 8
    tile = pl.BlockSpec((block, cols, wide), lambda i: (i, 0, 0))
    return pl.pallas_call(
        functools.partial(front_kernel, row_count=len(rights), col_count=len(lefts)),
        grid=(rows // block,),
        in_specs=[pl.BlockSpec(memory_space=pltpu.SMEM)]
        + [whole(part.shape) for part in lefts + rights]
        + [
            pl.BlockSpec((block // 2, seqs, 2 * wide), lambda i: (i, 0, 0)),
            tile,
            whole(w_tensor.shape),
            whole(present_cols.shape),
        ],
        out_specs=[tile, tile],
        out_shape=[jax.ShapeDtypeStruct(coupling.shape, BF16)] * 2,
        scratch_shapes=[
            pltpu.VMEM((rows * seqs, LANES), F32),
            pltpu.VMEM((cols, width * seqs), BF16),
            pltpu.VMEM((block // 2, width * seqs, 2 * wide), BF16),
        ],
        compiler_params=params(),
        name="front",
    )(place, *lefts, *rights, present_pairs, coupling, w_tensor, present_cols)


def project_kernel(normed_ref, live_ref, weight_ref, out_ref, tmp_ref):
    quads = normed_ref.shape[0] // QUAD
    dests, height, lanes = out_ref.shape
    each = height // quads
    count = dests * each
    for m in range(quads):
        packed = pack_rows([normed_ref[QUAD * m + a] for a in range(QUAD)])
        both = lax.dot_general(weight_ref[...], packed, NT, preferred_element_type=F32)
        gated = sigmoid(both[:count]) * both[count:] * live_ref[m]
        for k in range(each):
            value = gated[k * dests : (k + 1) * dests]
            for t in range(lanes // LANES):
                tmp_ref[t, pl.ds(m * each + k, dests, stride=height), :] = value[
                    :, t * LANES : (t + 1) * LANES
                ]
    for dest in range(dests):
        for t in range(lanes // LANES):
            out_ref[dest, :, t * LANES : (t + 1) * LANES] = tmp_ref[
                t, dest * height : (dest + 1) * height
            ].astype(BF16)


def project(normed, live, weight, dests):
    rows, cols, wide = normed.shape
    each = weight.shape[0] // (2 * dests)
    quads = max(8, 16 // each)
    lanes = QUAD * cols
    total = rows // QUAD
    return pl.pallas_call(
        project_kernel,
        grid=(total // quads,),
        in_specs=[
            pl.BlockSpec((quads * QUAD, cols, wide), lambda i: (i, 0, 0)),
            pl.BlockSpec((quads, 1, lanes), lambda i: (i, 0, 0)),
            whole(weight.shape),
        ],
        out_specs=pl.BlockSpec((dests, quads * each, lanes), lambda i: (0, i, 0)),
        out_shape=jax.ShapeDtypeStruct((dests, total * each, lanes), BF16),
        scratch_shapes=[pltpu.VMEM((lanes // LANES, dests * quads * each, LANES), F32)],
        compiler_params=params(),
        name="project",
    )(normed, live, weight)


def assemble_kernel(half_ref, recv_ref, *refs, row_count, pos_count):
    left_ref, own_ref, send_ref, flat_ref, right_ref = refs[-5:]
    channel = pl.program_id(0)
    lanes = recv_ref.shape[2]
    unit = lanes // 12
    cols = 3 * unit
    each = send_ref.shape[1] // (row_count * QUAD)
    stride = recv_ref.shape[1] // each
    groups = pos_count // 4
    tiles = lanes // LANES
    per_row = each * QUAD // cols

    @pl.when(channel == 0)
    def _():
        for src in range(row_count * pos_count):
            value = recv_ref[src].astype(F32)
            for t in range(tiles):
                flat_ref[src, t] = value[:, t * LANES : (t + 1) * LANES]

    def block(row, group, index):
        packed = []
        for p in range(4):
            src = row * pos_count + group * 4 + p
            packed.append(
                [flat_ref[src, t, pl.ds(index, each, stride=stride), :] for t in range(tiles)]
            )
        return exchange_blocks(packed)

    for row in range(row_count):
        for group in range(groups):
            span = slice(group * lanes, (group + 1) * lanes)
            left = block(row, group, channel)
            for a in range(QUAD):
                start = (row * QUAD + a) * each
                left_ref[0, start : start + each, span] = jnp.concatenate(left[a], axis=1).astype(
                    BF16
                )
            right = block(row, group, channel + stride // 2)
            for a in range(QUAD):
                for piece in range(per_row):
                    place = row * per_row + piece
                    base = (place // 4) * lanes
                    low = piece * (cols // QUAD)
                    mid = low + 2 * unit // QUAD
                    high = low + cols // QUAD
                    first = base + (place % 4) * 2 * unit + a
                    second = base + 8 * unit + (place % 4) * unit + a
                    for t in range(tiles):
                        value = right[a][t]
                        at = group * tiles + t
                        right_ref[at, pl.ds(first, mid - low, stride=QUAD), :] = value[low:mid]
                        right_ref[at, pl.ds(second, high - mid, stride=QUAD), :] = value[mid:high]
    width = pos_count * cols
    own = pl.multiple_of(half_ref[0] * width, width)
    other = pl.multiple_of((1 - half_ref[0]) * width, width)
    theirs = []
    for at in range(groups * tiles):
        span = slice(at * LANES, (at + 1) * LANES)
        own_ref[0, :, span] = right_ref[at, pl.ds(own, width), :].astype(BF16)
        theirs.append(right_ref[at, pl.ds(other, width), :].astype(BF16))
    theirs = jnp.concatenate(theirs, axis=1)
    for row in range(row_count):
        span = slice(row * QUAD * each, (row + 1) * QUAD * each)
        send_ref[0, span] = lax.dot_general(
            left_ref[0, span], theirs, NT, preferred_element_type=F32
        ).astype(BF16)


def assemble(half, received, after, row_count, pos_count, cols):
    sources, height, lanes = received.shape
    each = (2 * pos_count * cols) // (row_count * QUAD)
    stride = height // each
    channels = stride // 2
    depth = pos_count * cols
    rows = 2 * depth
    return pl.pallas_call(
        functools.partial(assemble_kernel, row_count=row_count, pos_count=pos_count),
        grid=(channels,),
        in_specs=[pl.BlockSpec(memory_space=pltpu.SMEM), whole(received.shape)] + anywhere(after),
        out_specs=[
            pl.BlockSpec((1, rows, depth), lambda c: (c, 0, 0)),
            pl.BlockSpec((1, depth, depth), lambda c: (c, 0, 0)),
            pl.BlockSpec((1, rows, depth), lambda c: (c, 0, 0)),
        ],
        out_shape=[
            jax.ShapeDtypeStruct((channels, rows, depth), BF16),
            jax.ShapeDtypeStruct((channels, depth, depth), BF16),
            jax.ShapeDtypeStruct((channels, rows, depth), BF16),
        ],
        scratch_shapes=[
            pltpu.VMEM((sources, lanes // LANES, height, LANES), F32),
            pltpu.VMEM((depth // LANES, rows, LANES), F32),
        ],
        compiler_params=params(),
        name="assemble",
    )(half, received, *after)


def combine_kernel(left_ref, own_ref, recv_ref, *refs, row_count, pos_count):
    out_ref, tmp_ref = refs[-2:]
    channel = pl.program_id(0)
    channels = pl.num_programs(0)
    lanes = out_ref.shape[2]
    each = left_ref.shape[1] // (row_count * QUAD)
    stride = out_ref.shape[1] // each
    tiles = lanes // LANES
    for row in range(row_count):
        for group in range(pos_count // 4):
            cols = slice(group * lanes, (group + 1) * lanes)
            blocks = []
            for a in range(QUAD):
                span = slice((row * QUAD + a) * each, (row * QUAD + a + 1) * each)
                value = lax.dot_general(
                    left_ref[0, span], own_ref[0, cols], NT, preferred_element_type=F32
                )
                value = value + recv_ref[0, span, cols].astype(F32)
                blocks.append([value[:, t * LANES : (t + 1) * LANES] for t in range(tiles)])
            for p, value in enumerate(exchange_blocks(blocks)):
                dest = row * pos_count + group * 4 + p
                for t in range(tiles):
                    tmp_ref[dest, t, pl.ds(channel, each, stride=stride), :] = value[t]

    @pl.when(channel == channels - 1)
    def _():
        for dest in range(row_count * pos_count):
            for t in range(tiles):
                out_ref[dest, :, t * LANES : (t + 1) * LANES] = tmp_ref[dest, t].astype(BF16)


def combine(left, own, received, after, row_count, pos_count, cols):
    channels, rows, depth = left.shape
    each = rows // (row_count * QUAD)
    shape = (row_count * pos_count, each * channels, QUAD * cols)
    return pl.pallas_call(
        functools.partial(combine_kernel, row_count=row_count, pos_count=pos_count),
        grid=(channels,),
        in_specs=[
            pl.BlockSpec((1, rows, depth), lambda c: (c, 0, 0)),
            pl.BlockSpec((1, depth, depth), lambda c: (c, 0, 0)),
            pl.BlockSpec((1, rows, depth), lambda c: (c, 0, 0)),
        ]
        + anywhere(after),
        out_specs=whole(shape),
        out_shape=jax.ShapeDtypeStruct(shape, BF16),
        scratch_shapes=[pltpu.VMEM((shape[0], shape[2] // LANES, shape[1], LANES), F32)],
        compiler_params=params(),
        name="combine",
    )(left, own, received, *after)


def finish_kernel(*refs, chunks):
    parts = refs[:chunks]
    mid_ref, normed_ref, gate_ref, weight_ref, out_ref = refs[chunks : chunks + 5]
    flat = refs[chunks + 5 :]
    quads = mid_ref.shape[0] // QUAD
    sources, _, lanes = parts[0].shape
    tiles = range(lanes // LANES)
    for part, tmp in zip(parts, flat):
        height = part.shape[1]
        for src in range(sources):
            value = part[src].astype(F32)
            for t in tiles:
                tmp[t, src * height : (src + 1) * height] = value[:, t * LANES : (t + 1) * LANES]
    for m in range(quads):
        pieces = []
        for part, tmp in zip(parts, flat):
            height = part.shape[1]
            each = height // quads
            for k in range(each):
                pieces.append(
                    jnp.concatenate(
                        [tmp[t, pl.ds(m * each + k, sources, stride=height), :] for t in tiles], axis=1
                    )
                )
        normed = standardize_features(jnp.concatenate(pieces, axis=0), 0).astype(BF16)
        out = lax.dot_general(normed, weight_ref[...], TN, preferred_element_type=F32)
        for a, value in enumerate(unpack_rows(out)):
            i = QUAD * m + a
            gate = sigmoid(jnp.dot(normed_ref[i], gate_ref[...], preferred_element_type=F32))
            out_ref[i] = (mid_ref[i].astype(F32) + gate * value).astype(BF16)


def finish(parts, mid, normed, w_gate, w_final):
    rows, cols, wide = mid.shape
    sources, _, lanes = parts[0].shape
    total = rows // QUAD
    heights = [part.shape[1] // total for part in parts]
    quads = max(8, 16 // min(heights))
    tile = pl.BlockSpec((quads * QUAD, cols, wide), lambda i: (i, 0, 0))
    return pl.pallas_call(
        functools.partial(finish_kernel, chunks=len(parts)),
        grid=(total // quads,),
        in_specs=[
            pl.BlockSpec((sources, quads * each, lanes), lambda i: (0, i, 0)) for each in heights
        ]
        + [tile, tile, whole(w_gate.shape), whole(w_final.shape)],
        out_specs=tile,
        out_shape=jax.ShapeDtypeStruct(mid.shape, BF16),
        scratch_shapes=[
            pltpu.VMEM((lanes // LANES, sources * quads * each, LANES), F32) for each in heights
        ],
        compiler_params=params(),
        name="finish",
    )(*parts, mid, normed, w_gate, w_final)


def chunk_sizes(channels):
    each = min(2, channels)
    return [each] * (channels // each)


def on_device(
    alignment_embedding,
    coupling_embedding,
    amino_validity,
    alignment_validity,
    alignment_matrix,
    tensor_final_matrix,
    coupling_logit_matrix,
    mean_final_matrix,
    trimul_matrices,
    trimul_final_matrix,
):
    seq_each, module_number, feature_count = alignment_embedding.shape
    rows, _, wide = coupling_embedding.shape
    row_count = lax.axis_size("row")
    pos_count = lax.axis_size("pos")
    col_count = 2 * pos_count
    row_index = lax.axis_index("row")
    half = lax.axis_index("half")
    col_index = half * pos_count + lax.axis_index("pos")
    seqs = seq_each * row_count
    active_entries = amino_validity.astype(F32)
    sequence_index = lax.broadcasted_iota(jnp.int32, alignment_validity.shape, 0)
    present_entries = (
        jnp.where(sequence_index == 0, F32(1.0), alignment_validity.astype(F32))
        * active_entries[None, :]
    )
    row_start = row_index * rows
    col_start = col_index * module_number
    present_rows = lax.dynamic_slice_in_dim(present_entries, row_start, rows, 1)
    present_cols = lax.dynamic_slice_in_dim(present_entries, col_start, module_number, 1)
    live_rows = lax.dynamic_slice_in_dim(active_entries, row_start, rows, 0)
    live_cols = lax.dynamic_slice_in_dim(active_entries, col_start, module_number, 0)

    own_start = (row_index * seq_each, col_start)
    present_own = lax.dynamic_slice(present_entries, own_start, (seq_each, module_number))
    own_normed = standardize_features(alignment_embedding.astype(F32), 2).astype(BF16)
    own_normed = own_normed.reshape(seq_each * module_number, feature_count)

    def project_msa(matrix):
        return jnp.dot(own_normed, matrix, preferred_element_type=F32).reshape(
            seq_each, module_number, -1
        )

    own_sides = project_msa(alignment_matrix[:, : 2 * TENSOR_FEATURES])
    own_sides = (own_sides * present_own[:, :, None]).astype(BF16)
    own_left = own_sides[:, :, :TENSOR_FEATURES]
    own_right = own_sides[:, :, TENSOR_FEATURES:]
    per_row = rows // module_number
    lefts = []
    for t in range(col_count):
        pairs = []
        for r in range(row_count):
            for q in range(col_count):
                to = (r * per_row + q % per_row - t) % col_count
                pairs.append((r * col_count + q, q // per_row * col_count + to))
        lefts.append(lax.ppermute(own_left, AXES, pairs))
    rights = [own_right]
    for t in range(1, row_count):
        pairs = [(r, (r - t) % row_count) for r in range(row_count)]
        rights.append(lax.ppermute(own_right, "row", pairs))

    present_pairs = jnp.broadcast_to(
        jnp.transpose(present_rows.reshape(seqs, rows // 2, 2), (1, 0, 2))[..., None],
        (rows // 2, seqs, 2, wide),
    ).reshape(rows // 2, seqs, 2 * wide).astype(BF16)
    w_tensor = tensor_final_matrix.reshape(TENSOR_FEATURES, TENSOR_FEATURES * wide)
    pair_mid, pair_normed = front(
        jnp.stack([row_index, col_index]).astype(jnp.int32),
        lefts,
        rights,
        present_pairs,
        coupling_embedding,
        w_tensor,
        present_cols.T.astype(BF16),
    )

    unit = module_number // 3
    pair_live = live_rows[:, None] * live_cols[None, :]
    quad_live = pair_live.reshape(rows // QUAD, QUAD, module_number)
    live_packed = jnp.concatenate(
        [
            quad_live[:, :, : 2 * unit].reshape(rows // QUAD, -1),
            quad_live[:, :, 2 * unit :].reshape(rows // QUAD, -1),
        ],
        axis=1,
    )[:, None, :]

    devices = row_count * pos_count
    sizes = chunk_sizes(CTRI // devices)
    w_kinds = trimul_matrices[:, : 4 * CTRI].T.reshape(2, 2, devices, -1, wide)
    half_scalar = half.astype(jnp.int32).reshape(1)
    swap = [(0, 1), (1, 0)]
    shape_of = (row_count, pos_count, module_number)
    stages = []
    start = 0
    for g, each in enumerate(sizes):
        weight = jnp.transpose(w_kinds[:, :, :, start : start + each], (1, 0, 3, 2, 4))
        start += each
        sent = project(pair_normed, live_packed, weight.reshape(-1, wide), devices)
        received = lax.all_to_all(sent, GROUP, split_axis=0, concat_axis=0, tiled=True)
        after = (stages[g - 2][2],) if g >= 2 else ()
        left, own, theirs = assemble(half_scalar, received, after, *shape_of)
        stages.append((left, own, lax.ppermute(theirs, "half", swap), theirs))

    values = project_msa(
        alignment_matrix[:, 2 * TENSOR_FEATURES : 2 * TENSOR_FEATURES + MEAN_GROUPS * GROUP_FEATURES]
    ).astype(BF16)
    sequence_gate = jax.nn.sigmoid(
        project_msa(alignment_matrix[:, 2 * TENSOR_FEATURES + MEAN_GROUPS * GROUP_FEATURES :])
    )
    logits = (
        jnp.dot(
            pair_normed.reshape(rows * module_number, wide),
            coupling_logit_matrix,
            preferred_element_type=F32,
        ).reshape(rows, module_number, MEAN_GROUPS)
        + MASK_PENALTY * (live_rows - 1.0)[:, None, None]
    )
    logits_all = lax.all_gather(logits, "row", axis=0, tiled=True)
    values_all = lax.all_gather(values, ("half", "pos"), axis=1, tiled=True)
    top_all = jnp.max(logits_all, axis=0)
    expd = jnp.exp(logits_all - top_all[None])
    weights_all = (expd / jnp.sum(expd, axis=0)[None]).astype(BF16)
    value_all_heads = values_all.reshape(seq_each, -1, MEAN_GROUPS, GROUP_FEATURES)
    summed = jnp.einsum("jih,sjhd->sihd", weights_all, value_all_heads, preferred_element_type=F32)
    head_averaged = summed.reshape(seq_each, module_number, MEAN_GROUPS * GROUP_FEATURES)
    gated_result = (sequence_gate * head_averaged).astype(BF16)
    blended_update = jnp.dot(
        gated_result.reshape(seq_each * module_number, -1),
        mean_final_matrix,
        preferred_element_type=F32,
    ).reshape(seq_each, module_number, -1)
    alignment_updated_embedding = (alignment_embedding.astype(F32) + blended_update).astype(BF16)

    returned = []
    for g, (left, own, partial, _) in enumerate(stages):
        after = (stages[g + 1][3],) if g + 1 < len(stages) else (alignment_updated_embedding,)
        product = combine(left, own, partial, after, *shape_of)
        returned.append(lax.all_to_all(product, GROUP, split_axis=0, concat_axis=0, tiled=True))
    w_final = jnp.transpose(trimul_final_matrix.reshape(devices, -1, wide), (1, 0, 2))
    pair_output = finish(
        returned, pair_mid, pair_normed, trimul_matrices[:, 4 * CTRI :], w_final.reshape(-1, wide)
    )
    return (alignment_updated_embedding, pair_output)


def solution(mesh):
    rows, cols = mesh.devices.shape
    inner = Mesh(mesh.devices.reshape(rows, 2, cols // 2), AXES)
    tile = P("row", ("half", "pos"), None)
    in_specs = (tile, tile) + (P(),) * 8
    return jax.shard_map(
        on_device, mesh=inner, in_specs=in_specs, out_specs=(tile, tile), check_vma=False
    )
```

```python
import functools

import jax
import jax.numpy as jnp
from jax import lax
from jax.experimental import pallas as pl
from jax.experimental.pallas import tpu as pltpu
from jax.sharding import Mesh, PartitionSpec as P

TENSOR_FEATURES = 32
MEAN_GROUPS = 8
GROUP_FEATURES = 32
CTRI = 128

EPS = 1e-05
MASK_PENALTY = 10000.0
QUAD = 4
LANES = 128
MIB = 1024 * 1024
AXES = ("row", "half", "pos")
GROUP = ("row", "pos")
F32 = jnp.float32
BF16 = jnp.bfloat16
NT = (((1,), (1,)), ((), ()))
TN = (((0,), (0,)), ((), ()))


def standardize_features(values_in, axis):
    centre = values_in - jnp.mean(values_in, axis=axis, keepdims=True)
    spread = jnp.mean(centre * centre, axis=axis, keepdims=True)
    return centre * lax.rsqrt(spread + EPS)


def sigmoid(x):
    return 0.5 * jnp.tanh(0.5 * x) + 0.5


def params(need):
    limit = min(need + 12 * MIB, 60 * MIB)
    return pltpu.CompilerParams(
        vmem_limit_bytes=limit, dimension_semantics=("arbitrary",)
    )


LIGHT = pl.CostEstimate(flops=1000, bytes_accessed=1000, transcendentals=0)


def whole(shape):
    zeros = (0,) * len(shape)
    return pl.BlockSpec(shape, lambda *_: zeros, pipeline_mode=pl.Buffered(1))


def anywhere(after):
    return [pl.BlockSpec(memory_space=pl.ANY)] * len(after)


def pack_rows(rows):
    unit = rows[0].shape[0] // 3
    return jnp.concatenate([r[: 2 * unit] for r in rows] + [r[2 * unit :] for r in rows], axis=0)


def unpack_rows(packed):
    unit = packed.shape[0] // 12
    return [
        jnp.concatenate(
            [
                packed[2 * unit * a : 2 * unit * (a + 1)],
                packed[8 * unit + unit * a : 8 * unit + unit * (a + 1)],
            ],
            axis=0,
        )
        for a in range(QUAD)
    ]


def swap_blocks(first, second, width, lane):
    low = (lane // width) % 2 == 0
    size = first.shape[1]
    return (
        jnp.where(low, first, pltpu.roll(second, width, 1)),
        jnp.where(low, pltpu.roll(first, size - width, 1), second),
    )


def exchange_blocks(packed):
    part = packed
    unit = LANES // 4
    lane = lax.broadcasted_iota(jnp.int32, part[0][0].shape, 1)
    out = [[None] * 3 for _ in range(4)]
    for pair in range(2):
        one, two = part[2 * pair], part[2 * pair + 1]
        for t in range(2):
            out[2 * t][pair], out[2 * t + 1][pair] = swap_blocks(one[t], two[t], 2 * unit, lane)
    u0, u2 = swap_blocks(part[0][2], part[2][2], 2 * unit, lane)
    u1, u3 = swap_blocks(part[1][2], part[3][2], 2 * unit, lane)
    out[0][2], out[1][2] = swap_blocks(u0, u1, unit, lane)
    out[2][2], out[3][2] = swap_blocks(u2, u3, unit, lane)
    return out


def front_kernel(place_ref, *refs, row_count, col_count):
    lefts, rights = refs[:col_count], refs[col_count : col_count + row_count]
    refs = refs[col_count + row_count :]
    prow_ref, coup_ref, weight_ref, pcol_ref, mid_ref, normed_ref = refs[:6]
    sides_ref, right_ref, tmp_ref = refs[6:]
    block, cols, wide = coup_ref.shape
    seq_each, _, width = lefts[0].shape
    seqs = seq_each * row_count
    per_row = col_count // row_count

    @pl.when(pl.program_id(0) == 0)
    def _():
        for t, part in enumerate(lefts):
            index = lax.rem(t + place_ref[1], col_count)
            first = lax.rem(index, per_row) * (cols * seqs) + index // per_row * seq_each
            for k in range(seq_each):
                sides_ref[pl.ds(first + k, cols, stride=seqs), 0:width] = part[k].astype(F32)
        right = jnp.zeros(right_ref.shape, F32)
        feature = lax.broadcasted_iota(jnp.int32, (width, width * seqs), 0)
        target = lax.broadcasted_iota(jnp.int32, (width, width * seqs), 1)
        for t, part in enumerate(rights):
            first = lax.rem(t + place_ref[0], row_count) * seq_each
            for k in range(seq_each):
                spread = (target == feature * seqs + (first + k)).astype(F32).astype(BF16)
                right += jnp.dot(part[k], spread, preferred_element_type=F32)
        right_ref[...] = right.astype(BF16)

    span = block * seqs
    start = pl.multiple_of(pl.program_id(0) * span, span)
    left = sides_ref[pl.ds(start, span), 0:width].astype(BF16)
    features = weight_ref.shape[1] // wide
    step = 4
    for low in range(0, features, step):
        part = jnp.dot(
            left, weight_ref[:, low * wide : (low + step) * wide], preferred_element_type=F32
        ).astype(BF16)
        for i in range(block):
            for d in range(step):
                tmp_ref[
                    i // 2,
                    (low + d) * seqs : (low + d + 1) * seqs,
                    (i % 2) * wide : (i % 2 + 1) * wide,
                ] = part[i * seqs : (i + 1) * seqs, d * wide : (d + 1) * wide]
    row_lane = lax.broadcasted_iota(jnp.int32, prow_ref.shape, 1)
    for pair in range(block // 2):
        update = jnp.dot(right_ref[...], tmp_ref[pair], preferred_element_type=F32)
        here = pl.program_id(0) * block + 2 * pair
        wanted = [jnp.where(row_lane == here + e, prow_ref[...], 0.0) for e in range(2)]
        wanted = [
            jnp.broadcast_to(jnp.sum(w, axis=1, keepdims=True), (seqs, wide)) for w in wanted
        ]
        count = jnp.dot(
            pcol_ref[...], jnp.concatenate(wanted, axis=1).astype(BF16), preferred_element_type=F32
        )
        update = update / jnp.maximum(count, 1.0)
        for e in range(2):
            i = 2 * pair + e
            mid = (coup_ref[i].astype(F32) + update[:, e * wide : (e + 1) * wide]).astype(BF16)
            mid_ref[i] = mid
            normed_ref[i] = standardize_features(mid.astype(F32), 1).astype(BF16)


def front(place, lefts, rights, present_rows, coupling, w_tensor, present_cols):
    rows, cols, wide = coupling.shape
    seqs, width = present_rows.shape[0], lefts[0].shape[2]
    block = 8
    tile = pl.BlockSpec((block, cols, wide), lambda i: (i, 0, 0))
    return pl.pallas_call(
        functools.partial(front_kernel, row_count=len(rights), col_count=len(lefts)),
        grid=(rows // block,),
        in_specs=[pl.BlockSpec(memory_space=pltpu.SMEM)]
        + [whole(part.shape) for part in lefts + rights]
        + [
            whole(present_rows.shape),
            tile,
            whole(w_tensor.shape),
            whole(present_cols.shape),
        ],
        out_specs=[tile, tile],
        out_shape=[jax.ShapeDtypeStruct(coupling.shape, BF16)] * 2,
        scratch_shapes=[
            pltpu.VMEM((rows * seqs, LANES), F32),
            pltpu.VMEM((cols, width * seqs), BF16),
            pltpu.VMEM((block // 2, width * seqs, 2 * wide), BF16),
        ],
        compiler_params=params(4 * rows * seqs * LANES + 16 * MIB),
        cost_estimate=LIGHT,
        name="front",
    )(place, *lefts, *rights, present_rows, coupling, w_tensor, present_cols)


def exchange_rows(values):
    values = list(values)
    count = len(values)
    step = count // 2
    row = lax.broadcasted_iota(jnp.int32, values[0].shape, 0)
    size = values[0].shape[0]
    while step:
        width = 8 // count * step
        low = (row // width) % 2 == 0
        for m in range(count):
            if m & step == 0:
                one, two = values[m], values[m + step]
                values[m] = jnp.where(low, one, pltpu.roll(two, width, 0))
                values[m + step] = jnp.where(low, pltpu.roll(one, size - width, 0), two)
        step //= 2
    return values


def project_kernel(live_ref, normed_ref, cols_ref, weight_ref, *refs):
    out_ref, tmp_ref = refs[-2:]
    quads = normed_ref.shape[0] // QUAD
    dests, height, lanes = out_ref.shape
    each = height // quads
    count = dests * each
    unit = lanes // 12
    lane = lax.broadcasted_iota(jnp.int32, (1, lanes), 1)
    place = jnp.where(lane < 8 * unit, lane // (2 * unit), (lane - 8 * unit) // unit)
    group = max(1, 8 // each)
    for first in range(0, quads, group):
        values = []
        for m in range(first, first + group):
            packed = pack_rows([normed_ref[QUAD * m + a] for a in range(QUAD)])
            both = lax.dot_general(weight_ref[...], packed, NT, preferred_element_type=F32)
            row = (pl.program_id(0) * quads + m) * QUAD
            live = cols_ref[...]
            for a in range(QUAD):
                live = jnp.where(place == a, live * live_ref[row + a], live)
            values.append(sigmoid(both[:count]) * both[count:] * live)
        for b, value in enumerate(exchange_rows(values)):
            size = each * group
            for v in range(count // size):
                tmp_ref[v * group + b, first * each : first * each + size] = value[
                    v * size : (v + 1) * size
                ]
    out_ref[...] = tmp_ref[...].astype(BF16)


def project(live_rows, normed, live_cols, weight, after, dests):
    rows, cols, wide = normed.shape
    each = weight.shape[0] // (2 * dests)
    quads = max(8, 16 // each)
    lanes = QUAD * cols
    total = rows // QUAD
    return pl.pallas_call(
        project_kernel,
        grid=(total // quads,),
        in_specs=[
            pl.BlockSpec(memory_space=pltpu.SMEM),
            pl.BlockSpec((quads * QUAD, cols, wide), lambda i: (i, 0, 0)),
            whole(live_cols.shape),
            whole(weight.shape),
        ]
        + anywhere(after),
        out_specs=pl.BlockSpec((dests, quads * each, lanes), lambda i: (0, i, 0)),
        out_shape=jax.ShapeDtypeStruct((dests, total * each, lanes), BF16),
        scratch_shapes=[pltpu.VMEM((dests, quads * each, lanes), F32)],
        compiler_params=params(8 * dests * quads * each * lanes + 2 * MIB),
        cost_estimate=LIGHT,
        name="project",
    )(live_rows, normed, live_cols, weight, *after)


def assemble_kernel(half_ref, recv_ref, *refs, row_count, pos_count):
    left_ref, own_ref, send_ref, flat_ref, right_ref = refs[-5:]
    channel = pl.program_id(0)
    lanes = recv_ref.shape[2]
    unit = lanes // 12
    cols = 3 * unit
    each = send_ref.shape[1] // (row_count * QUAD)
    stride = recv_ref.shape[1] // each
    groups = pos_count // 4
    tiles = lanes // LANES
    per_row = each * QUAD // cols

    @pl.when(channel == 0)
    def _():
        for src in range(row_count * pos_count):
            value = recv_ref[src].astype(F32)
            for t in range(tiles):
                flat_ref[src, t] = value[:, t * LANES : (t + 1) * LANES]

    def block(row, group, index):
        packed = []
        for p in range(4):
            src = row * pos_count + group * 4 + p
            packed.append(
                [flat_ref[src, t, pl.ds(index, each, stride=stride), :] for t in range(tiles)]
            )
        return exchange_blocks(packed)

    for row in range(row_count):
        for group in range(groups):
            span = slice(group * lanes, (group + 1) * lanes)
            left = block(row, group, channel)
            for a in range(QUAD):
                start = (row * QUAD + a) * each
                left_ref[0, start : start + each, span] = jnp.concatenate(left[a], axis=1).astype(
                    BF16
                )
            right = block(row, group, channel + stride // 2)
            for a in range(QUAD):
                for piece in range(per_row):
                    place = row * per_row + piece
                    base = (place // 4) * lanes
                    low = piece * (cols // QUAD)
                    mid = low + 2 * unit // QUAD
                    high = low + cols // QUAD
                    first = base + (place % 4) * 2 * unit + a
                    second = base + 8 * unit + (place % 4) * unit + a
                    for t in range(tiles):
                        value = right[a][t]
                        at = group * tiles + t
                        right_ref[at, pl.ds(first, mid - low, stride=QUAD), :] = value[low:mid]
                        right_ref[at, pl.ds(second, high - mid, stride=QUAD), :] = value[mid:high]
    width = pos_count * cols
    own = pl.multiple_of(half_ref[0] * width, width)
    other = pl.multiple_of((1 - half_ref[0]) * width, width)
    theirs = []
    for at in range(groups * tiles):
        span = slice(at * LANES, (at + 1) * LANES)
        own_ref[0, :, span] = right_ref[at, pl.ds(own, width), :].astype(BF16)
        theirs.append(right_ref[at, pl.ds(other, width), :].astype(BF16))
    theirs = jnp.concatenate(theirs, axis=1)
    for row in range(row_count):
        span = slice(row * QUAD * each, (row + 1) * QUAD * each)
        send_ref[0, span] = lax.dot_general(
            left_ref[0, span], theirs, NT, preferred_element_type=F32
        ).astype(BF16)


def assemble(half, received, after, row_count, pos_count, cols):
    sources, height, lanes = received.shape
    each = (2 * pos_count * cols) // (row_count * QUAD)
    stride = height // each
    channels = stride // 2
    depth = pos_count * cols
    rows = 2 * depth
    return pl.pallas_call(
        functools.partial(assemble_kernel, row_count=row_count, pos_count=pos_count),
        grid=(channels,),
        in_specs=[pl.BlockSpec(memory_space=pltpu.SMEM), whole(received.shape)] + anywhere(after),
        out_specs=[
            pl.BlockSpec((1, rows, depth), lambda c: (c, 0, 0)),
            pl.BlockSpec((1, depth, depth), lambda c: (c, 0, 0)),
            pl.BlockSpec((1, rows, depth), lambda c: (c, 0, 0)),
        ],
        out_shape=[
            jax.ShapeDtypeStruct((channels, rows, depth), BF16),
            jax.ShapeDtypeStruct((channels, depth, depth), BF16),
            jax.ShapeDtypeStruct((channels, rows, depth), BF16),
        ],
        scratch_shapes=[
            pltpu.VMEM((sources, lanes // LANES, height, LANES), F32),
            pltpu.VMEM((depth // LANES, rows, LANES), F32),
        ],
        compiler_params=params(
            6 * received.size + 4 * rows * depth + 4 * (2 * rows + depth) * depth
        ),
        cost_estimate=LIGHT,
        name="assemble",
    )(half, received, *after)


def combine_kernel(left_ref, own_ref, recv_ref, *refs, row_count, pos_count):
    out_ref, tmp_ref = refs[-2:]
    channel = pl.program_id(0)
    channels = pl.num_programs(0)
    lanes = out_ref.shape[2]
    each = left_ref.shape[1] // (row_count * QUAD)
    stride = out_ref.shape[1] // each
    tiles = lanes // LANES
    for row in range(row_count):
        for group in range(pos_count // 4):
            cols = slice(group * lanes, (group + 1) * lanes)
            blocks = []
            for a in range(QUAD):
                span = slice((row * QUAD + a) * each, (row * QUAD + a + 1) * each)
                value = lax.dot_general(
                    left_ref[0, span], own_ref[0, cols], NT, preferred_element_type=F32
                )
                value = value + recv_ref[0, span, cols].astype(F32)
                blocks.append([value[:, t * LANES : (t + 1) * LANES] for t in range(tiles)])
            for p, value in enumerate(exchange_blocks(blocks)):
                dest = row * pos_count + group * 4 + p
                for t in range(tiles):
                    tmp_ref[dest, t, pl.ds(channel, each, stride=stride), :] = value[t]

    @pl.when(channel == channels - 1)
    def _():
        for dest in range(row_count * pos_count):
            for t in range(tiles):
                out_ref[dest, :, t * LANES : (t + 1) * LANES] = tmp_ref[dest, t].astype(BF16)


def combine(left, own, received, after, row_count, pos_count, cols):
    channels, rows, depth = left.shape
    each = rows // (row_count * QUAD)
    shape = (row_count * pos_count, each * channels, QUAD * cols)
    return pl.pallas_call(
        functools.partial(combine_kernel, row_count=row_count, pos_count=pos_count),
        grid=(channels,),
        in_specs=[
            pl.BlockSpec((1, rows, depth), lambda c: (c, 0, 0)),
            pl.BlockSpec((1, depth, depth), lambda c: (c, 0, 0)),
            pl.BlockSpec((1, rows, depth), lambda c: (c, 0, 0)),
        ]
        + anywhere(after),
        out_specs=whole(shape),
        out_shape=jax.ShapeDtypeStruct(shape, BF16),
        scratch_shapes=[pltpu.VMEM((shape[0], shape[2] // LANES, shape[1], LANES), F32)],
        compiler_params=params(
            4 * (2 * rows + depth) * depth + 6 * shape[0] * shape[1] * shape[2]
        ),
        cost_estimate=LIGHT,
        name="combine",
    )(left, own, received, *after)


def finish_kernel(*refs, chunks):
    parts = refs[:chunks]
    mid_ref, normed_ref, gate_ref, weight_ref, out_ref = refs[chunks : chunks + 5]
    flat = refs[chunks + 5 :]
    quads = mid_ref.shape[0] // QUAD
    sources, _, lanes = parts[0].shape
    tiles = range(lanes // LANES)
    for part, tmp in zip(parts, flat):
        height = part.shape[1]
        for src in range(sources):
            value = part[src].astype(F32)
            for t in tiles:
                tmp[t, src * height : (src + 1) * height] = value[:, t * LANES : (t + 1) * LANES]
    for m in range(quads):
        pieces = []
        for part, tmp in zip(parts, flat):
            height = part.shape[1]
            each = height // quads
            for k in range(each):
                pieces.append(
                    jnp.concatenate(
                        [tmp[t, pl.ds(m * each + k, sources, stride=height), :] for t in tiles], axis=1
                    )
                )
        normed = standardize_features(jnp.concatenate(pieces, axis=0), 0).astype(BF16)
        out = lax.dot_general(normed, weight_ref[...], TN, preferred_element_type=F32)
        for a, value in enumerate(unpack_rows(out)):
            i = QUAD * m + a
            gate = sigmoid(jnp.dot(normed_ref[i], gate_ref[...], preferred_element_type=F32))
            out_ref[i] = (mid_ref[i].astype(F32) + gate * value).astype(BF16)


def finish(parts, mid, normed, w_gate, w_final):
    rows, cols, wide = mid.shape
    sources, _, lanes = parts[0].shape
    total = rows // QUAD
    heights = [part.shape[1] // total for part in parts]
    quads = max(8, 16 // min(heights))
    tile = pl.BlockSpec((quads * QUAD, cols, wide), lambda i: (i, 0, 0))
    return pl.pallas_call(
        functools.partial(finish_kernel, chunks=len(parts)),
        grid=(total // quads,),
        in_specs=[
            pl.BlockSpec((sources, quads * each, lanes), lambda i: (0, i, 0)) for each in heights
        ]
        + [tile, tile, whole(w_gate.shape), whole(w_final.shape)],
        out_specs=tile,
        out_shape=jax.ShapeDtypeStruct(mid.shape, BF16),
        scratch_shapes=[
            pltpu.VMEM((lanes // LANES, sources * quads * each, LANES), F32) for each in heights
        ],
        compiler_params=params(
            8 * sources * quads * sum(heights) * lanes + 12 * quads * QUAD * cols * wide
        ),
        cost_estimate=LIGHT,
        name="finish",
    )(*parts, mid, normed, w_gate, w_final)


def chunk_sizes(channels):
    each = min(2, channels)
    return [each] * (channels // each)


def on_device(
    alignment_embedding,
    coupling_embedding,
    amino_validity,
    alignment_validity,
    alignment_matrix,
    tensor_final_matrix,
    coupling_logit_matrix,
    mean_final_matrix,
    trimul_matrices,
    trimul_final_matrix,
):
    seq_each, module_number, feature_count = alignment_embedding.shape
    rows, _, wide = coupling_embedding.shape
    row_count = lax.axis_size("row")
    pos_count = lax.axis_size("pos")
    col_count = 2 * pos_count
    row_index = lax.axis_index("row")
    half = lax.axis_index("half")
    col_index = half * pos_count + lax.axis_index("pos")
    seqs = seq_each * row_count
    active_entries = amino_validity.astype(F32)
    sequence_index = lax.broadcasted_iota(jnp.int32, alignment_validity.shape, 0)
    present_entries = (
        jnp.where(sequence_index == 0, F32(1.0), alignment_validity.astype(F32))
        * active_entries[None, :]
    )
    row_start = row_index * rows
    col_start = col_index * module_number
    present_rows = lax.dynamic_slice_in_dim(present_entries, row_start, rows, 1)
    present_cols = lax.dynamic_slice_in_dim(present_entries, col_start, module_number, 1)
    live_rows = lax.dynamic_slice_in_dim(active_entries, row_start, rows, 0)
    live_cols = lax.dynamic_slice_in_dim(active_entries, col_start, module_number, 0)

    own_start = (row_index * seq_each, col_start)
    present_own = lax.dynamic_slice(present_entries, own_start, (seq_each, module_number))
    own_normed = standardize_features(alignment_embedding.astype(F32), 2).astype(BF16)
    own_normed = own_normed.reshape(seq_each * module_number, feature_count)

    def project_msa(matrix):
        return jnp.dot(own_normed, matrix, preferred_element_type=F32).reshape(
            seq_each, module_number, -1
        )

    own_sides = project_msa(alignment_matrix[:, : 2 * TENSOR_FEATURES])
    own_sides = (own_sides * present_own[:, :, None]).astype(BF16)
    own_left = own_sides[:, :, :TENSOR_FEATURES]
    own_right = own_sides[:, :, TENSOR_FEATURES:]
    per_row = rows // module_number
    lefts = []
    for t in range(col_count):
        pairs = []
        for r in range(row_count):
            for q in range(col_count):
                to = (r * per_row + q % per_row - t) % col_count
                pairs.append((r * col_count + q, q // per_row * col_count + to))
        lefts.append(lax.ppermute(own_left, AXES, pairs))
    rights = [own_right]
    for t in range(1, row_count):
        pairs = [(r, (r - t) % row_count) for r in range(row_count)]
        rights.append(lax.ppermute(own_right, "row", pairs))

    w_tensor = tensor_final_matrix.reshape(TENSOR_FEATURES, TENSOR_FEATURES * wide)
    pair_mid, pair_normed = front(
        jnp.stack([row_index, col_index]).astype(jnp.int32),
        lefts,
        rights,
        present_rows,
        coupling_embedding,
        w_tensor,
        present_cols.T.astype(BF16),
    )

    unit = module_number // 3
    live_packed = jnp.concatenate(
        [live_cols[: 2 * unit]] * QUAD + [live_cols[2 * unit :]] * QUAD
    )[None]

    devices = row_count * pos_count
    sizes = chunk_sizes(CTRI // devices)
    w_kinds = trimul_matrices[:, : 4 * CTRI].T.reshape(2, 2, devices, -1, wide)
    half_scalar = half.astype(jnp.int32).reshape(1)
    swap = [(0, 1), (1, 0)]
    shape_of = (row_count, pos_count, module_number)
    stages = []
    start = 0
    for g, each in enumerate(sizes):
        weight = jnp.transpose(w_kinds[:, :, :, start : start + each], (1, 2, 0, 3, 4))
        start += each
        after = (stages[g - 2][3],) if g >= 2 else ()
        sent = project(
            live_rows, pair_normed, live_packed, weight.reshape(-1, wide), after, devices
        )
        received = lax.all_to_all(sent, GROUP, split_axis=0, concat_axis=0, tiled=True)
        after = (stages[g - 2][2],) if g >= 2 else ()
        left, own, theirs = assemble(half_scalar, received, after, *shape_of)
        stages.append((left, own, lax.ppermute(theirs, "half", swap), theirs))

    values = project_msa(
        alignment_matrix[:, 2 * TENSOR_FEATURES : 2 * TENSOR_FEATURES + MEAN_GROUPS * GROUP_FEATURES]
    ).astype(BF16)
    sequence_gate = jax.nn.sigmoid(
        project_msa(alignment_matrix[:, 2 * TENSOR_FEATURES + MEAN_GROUPS * GROUP_FEATURES :])
    )
    logits = (
        jnp.dot(
            pair_normed.reshape(rows * module_number, wide),
            coupling_logit_matrix,
            preferred_element_type=F32,
        ).reshape(rows, module_number, MEAN_GROUPS)
        + MASK_PENALTY * (live_rows - 1.0)[:, None, None]
    )
    logits_all = lax.all_gather(logits, "row", axis=0, tiled=True)
    values_all = lax.all_gather(values, ("half", "pos"), axis=1, tiled=True)
    top_all = jnp.max(logits_all, axis=0)
    expd = jnp.exp(logits_all - top_all[None])
    weights_all = (expd / jnp.sum(expd, axis=0)[None]).astype(BF16)
    value_all_heads = values_all.reshape(seq_each, -1, MEAN_GROUPS, GROUP_FEATURES)
    summed = jnp.einsum("jih,sjhd->sihd", weights_all, value_all_heads, preferred_element_type=F32)
    head_averaged = summed.reshape(seq_each, module_number, MEAN_GROUPS * GROUP_FEATURES)
    gated_result = (sequence_gate * head_averaged).astype(BF16)
    blended_update = jnp.dot(
        gated_result.reshape(seq_each * module_number, -1),
        mean_final_matrix,
        preferred_element_type=F32,
    ).reshape(seq_each, module_number, -1)
    alignment_updated_embedding = (alignment_embedding.astype(F32) + blended_update).astype(BF16)

    returned = []
    for g, (left, own, partial, _) in enumerate(stages):
        after = (stages[g + 1][3],) if g + 1 < len(stages) else (alignment_updated_embedding,)
        product = combine(left, own, partial, after, *shape_of)
        returned.append(lax.all_to_all(product, GROUP, split_axis=0, concat_axis=0, tiled=True))
    w_final = jnp.transpose(trimul_final_matrix.reshape(devices, -1, wide), (1, 0, 2))
    pair_output = finish(
        returned, pair_mid, pair_normed, trimul_matrices[:, 4 * CTRI :], w_final.reshape(-1, wide)
    )
    return (alignment_updated_embedding, pair_output)


def solution(mesh):
    rows, cols = mesh.devices.shape
    inner = Mesh(mesh.devices.reshape(rows, 2, cols // 2), AXES)
    tile = P("row", ("half", "pos"), None)
    in_specs = (tile, tile) + (P(),) * 8
    return jax.shard_map(
        on_device, mesh=inner, in_specs=in_specs, out_specs=(tile, tile), check_vma=False
    )
```

```python
import functools

import jax
import jax.numpy as jnp
from jax import lax
from jax.experimental import pallas as pl
from jax.experimental.pallas import tpu as pltpu
from jax.sharding import Mesh, PartitionSpec as P

TENSOR_FEATURES = 32
MEAN_GROUPS = 8
GROUP_FEATURES = 32
CTRI = 128

EPS = 1e-05
MASK_PENALTY = 10000.0
QUAD = 4
LANES = 128
MIB = 1024 * 1024
AXES = ("row", "half", "pos")
GROUP = ("row", "pos")
F32 = jnp.float32
BF16 = jnp.bfloat16
NT = (((1,), (1,)), ((), ()))
TN = (((0,), (0,)), ((), ()))


def standardize_features(values_in, axis):
    centre = values_in - jnp.mean(values_in, axis=axis, keepdims=True)
    spread = jnp.mean(centre * centre, axis=axis, keepdims=True)
    return centre * lax.rsqrt(spread + EPS)


def sigmoid(x):
    return 0.5 * jnp.tanh(0.5 * x) + 0.5


def params():
    return pltpu.CompilerParams(
        vmem_limit_bytes=60 * MIB, dimension_semantics=("arbitrary",)
    )


LIGHT = pl.CostEstimate(flops=1000, bytes_accessed=1000, transcendentals=0)


def whole(shape):
    zeros = (0,) * len(shape)
    return pl.BlockSpec(shape, lambda *_: zeros, pipeline_mode=pl.Buffered(1))


def anywhere(after):
    return [pl.BlockSpec(memory_space=pl.ANY)] * len(after)


def fence(values, after):
    return pl.pallas_call(
        lambda *refs: None,
        in_specs=anywhere(values) + anywhere(after),
        out_specs=anywhere(values),
        out_shape=[jax.ShapeDtypeStruct(v.shape, v.dtype) for v in values],
        input_output_aliases={i: i for i in range(len(values))},
        compiler_params=pltpu.CompilerParams(vmem_limit_bytes=60 * MIB),
        cost_estimate=LIGHT,
        name="fence",
    )(*values, *after)


def pack_rows(rows):
    unit = rows[0].shape[0] // 3
    return jnp.concatenate([r[: 2 * unit] for r in rows] + [r[2 * unit :] for r in rows], axis=0)


def unpack_rows(packed):
    unit = packed.shape[0] // 12
    return [
        jnp.concatenate(
            [
                packed[2 * unit * a : 2 * unit * (a + 1)],
                packed[8 * unit + unit * a : 8 * unit + unit * (a + 1)],
            ],
            axis=0,
        )
        for a in range(QUAD)
    ]


def swap_blocks(first, second, width, lane):
    low = (lane // width) % 2 == 0
    size = first.shape[1]
    return (
        jnp.where(low, first, pltpu.roll(second, width, 1)),
        jnp.where(low, pltpu.roll(first, size - width, 1), second),
    )


def exchange_blocks(packed):
    part = packed
    unit = LANES // 4
    lane = lax.broadcasted_iota(jnp.int32, part[0][0].shape, 1)
    out = [[None] * 3 for _ in range(4)]
    for pair in range(2):
        one, two = part[2 * pair], part[2 * pair + 1]
        for t in range(2):
            out[2 * t][pair], out[2 * t + 1][pair] = swap_blocks(one[t], two[t], 2 * unit, lane)
    u0, u2 = swap_blocks(part[0][2], part[2][2], 2 * unit, lane)
    u1, u3 = swap_blocks(part[1][2], part[3][2], 2 * unit, lane)
    out[0][2], out[1][2] = swap_blocks(u0, u1, unit, lane)
    out[2][2], out[3][2] = swap_blocks(u2, u3, unit, lane)
    return out


def front_kernel(place_ref, *refs, row_count, col_count):
    lefts, rights = refs[:col_count], refs[col_count : col_count + row_count]
    refs = refs[col_count + row_count :]
    prow_ref, coup_ref, weight_ref, pcol_ref, mid_ref, normed_ref = refs[:6]
    sides_ref, right_ref, tmp_ref = refs[6:]
    block, cols, wide = coup_ref.shape
    seq_each, _, width = lefts[0].shape
    seqs = seq_each * row_count
    per_row = col_count // row_count

    @pl.when(pl.program_id(0) == 0)
    def _():
        for t, part in enumerate(lefts):
            index = lax.rem(t + place_ref[1], col_count)
            first = lax.rem(index, per_row) * (cols * seqs) + index // per_row * seq_each
            for k in range(seq_each):
                sides_ref[pl.ds(first + k, cols, stride=seqs), 0:width] = part[k].astype(F32)
        right = jnp.zeros(right_ref.shape, F32)
        feature = lax.broadcasted_iota(jnp.int32, (width, width * seqs), 0)
        target = lax.broadcasted_iota(jnp.int32, (width, width * seqs), 1)
        for t, part in enumerate(rights):
            first = lax.rem(t + place_ref[0], row_count) * seq_each
            for k in range(seq_each):
                spread = (target == feature * seqs + (first + k)).astype(F32).astype(BF16)
                right += jnp.dot(part[k], spread, preferred_element_type=F32)
        right_ref[...] = right.astype(BF16)

    span = block * seqs
    start = pl.multiple_of(pl.program_id(0) * span, span)
    left = sides_ref[pl.ds(start, span), 0:width].astype(BF16)
    features = weight_ref.shape[1] // wide
    step = 4
    for low in range(0, features, step):
        part = jnp.dot(
            left, weight_ref[:, low * wide : (low + step) * wide], preferred_element_type=F32
        ).astype(BF16)
        for i in range(block):
            for d in range(step):
                tmp_ref[
                    i // 2,
                    (low + d) * seqs : (low + d + 1) * seqs,
                    (i % 2) * wide : (i % 2 + 1) * wide,
                ] = part[i * seqs : (i + 1) * seqs, d * wide : (d + 1) * wide]
    row_lane = lax.broadcasted_iota(jnp.int32, prow_ref.shape, 1)
    for pair in range(block // 2):
        update = jnp.dot(right_ref[...], tmp_ref[pair], preferred_element_type=F32)
        here = pl.program_id(0) * block + 2 * pair
        wanted = [jnp.where(row_lane == here + e, prow_ref[...], 0.0) for e in range(2)]
        wanted = [
            jnp.broadcast_to(jnp.sum(w, axis=1, keepdims=True), (seqs, wide)) for w in wanted
        ]
        count = jnp.dot(
            pcol_ref[...], jnp.concatenate(wanted, axis=1).astype(BF16), preferred_element_type=F32
        )
        update = update / jnp.maximum(count, 1.0)
        for e in range(2):
            i = 2 * pair + e
            mid = (coup_ref[i].astype(F32) + update[:, e * wide : (e + 1) * wide]).astype(BF16)
            mid_ref[i] = mid
            normed_ref[i] = standardize_features(mid.astype(F32), 1).astype(BF16)


def front(place, lefts, rights, present_rows, coupling, w_tensor, present_cols):
    rows, cols, wide = coupling.shape
    seqs, width = present_rows.shape[0], lefts[0].shape[2]
    block = 8
    tile = pl.BlockSpec((block, cols, wide), lambda i: (i, 0, 0))
    return pl.pallas_call(
        functools.partial(front_kernel, row_count=len(rights), col_count=len(lefts)),
        grid=(rows // block,),
        in_specs=[pl.BlockSpec(memory_space=pltpu.SMEM)]
        + [whole(part.shape) for part in lefts + rights]
        + [
            whole(present_rows.shape),
            tile,
            whole(w_tensor.shape),
            whole(present_cols.shape),
        ],
        out_specs=[tile, tile],
        out_shape=[jax.ShapeDtypeStruct(coupling.shape, BF16)] * 2,
        scratch_shapes=[
            pltpu.VMEM((rows * seqs, LANES), F32),
            pltpu.VMEM((cols, width * seqs), BF16),
            pltpu.VMEM((block // 2, width * seqs, 2 * wide), BF16),
        ],
        compiler_params=params(),
        cost_estimate=LIGHT,
        name="front",
    )(place, *lefts, *rights, present_rows, coupling, w_tensor, present_cols)


def exchange_rows(values):
    values = list(values)
    count = len(values)
    step = count // 2
    row = lax.broadcasted_iota(jnp.int32, values[0].shape, 0)
    size = values[0].shape[0]
    while step:
        width = 8 // count * step
        low = (row // width) % 2 == 0
        for m in range(count):
            if m & step == 0:
                one, two = values[m], values[m + step]
                values[m] = jnp.where(low, one, pltpu.roll(two, width, 0))
                values[m + step] = jnp.where(low, pltpu.roll(one, size - width, 0), two)
        step //= 2
    return values


def project_kernel(live_ref, normed_ref, cols_ref, weight_ref, *refs):
    out_ref, tmp_ref = refs[-2:]
    quads = normed_ref.shape[0] // QUAD
    dests, height, lanes = out_ref.shape
    each = height // quads
    count = dests * each
    unit = lanes // 12
    lane = lax.broadcasted_iota(jnp.int32, (1, lanes), 1)
    place = jnp.where(lane < 8 * unit, lane // (2 * unit), (lane - 8 * unit) // unit)
    group = max(1, 8 // each)
    for first in range(0, quads, group):
        values = []
        for m in range(first, first + group):
            packed = pack_rows([normed_ref[QUAD * m + a] for a in range(QUAD)])
            both = lax.dot_general(weight_ref[...], packed, NT, preferred_element_type=F32)
            row = (pl.program_id(0) * quads + m) * QUAD
            live = cols_ref[...]
            for a in range(QUAD):
                live = jnp.where(place == a, live * live_ref[row + a], live)
            values.append(sigmoid(both[:count]) * both[count:] * live)
        for b, value in enumerate(exchange_rows(values)):
            size = each * group
            for v in range(count // size):
                tmp_ref[v * group + b, first * each : first * each + size] = value[
                    v * size : (v + 1) * size
                ]
    out_ref[...] = tmp_ref[...].astype(BF16)


def project(live_rows, normed, live_cols, weight, after, dests):
    rows, cols, wide = normed.shape
    each = weight.shape[0] // (2 * dests)
    quads = max(8, 16 // each)
    lanes = QUAD * cols
    total = rows // QUAD
    return pl.pallas_call(
        project_kernel,
        grid=(total // quads,),
        in_specs=[
            pl.BlockSpec(memory_space=pltpu.SMEM),
            pl.BlockSpec((quads * QUAD, cols, wide), lambda i: (i, 0, 0)),
            whole(live_cols.shape),
            whole(weight.shape),
        ]
        + anywhere(after),
        out_specs=pl.BlockSpec((dests, quads * each, lanes), lambda i: (0, i, 0)),
        out_shape=jax.ShapeDtypeStruct((dests, total * each, lanes), BF16),
        scratch_shapes=[pltpu.VMEM((dests, quads * each, lanes), F32)],
        compiler_params=params(),
        cost_estimate=LIGHT,
        name="project",
    )(live_rows, normed, live_cols, weight, *after)


def assemble_kernel(half_ref, recv_ref, *refs, row_count, pos_count):
    left_ref, own_ref, send_ref, flat_ref, right_ref = refs[-5:]
    channel = pl.program_id(0)
    lanes = recv_ref.shape[2]
    unit = lanes // 12
    cols = 3 * unit
    each = send_ref.shape[1] // (row_count * QUAD)
    stride = recv_ref.shape[1] // each
    groups = pos_count // 4
    tiles = lanes // LANES
    per_row = each * QUAD // cols

    @pl.when(channel == 0)
    def _():
        for src in range(row_count * pos_count):
            value = recv_ref[src].astype(F32)
            for t in range(tiles):
                flat_ref[src, t] = value[:, t * LANES : (t + 1) * LANES]

    def block(row, group, index):
        packed = []
        for p in range(4):
            src = row * pos_count + group * 4 + p
            packed.append(
                [flat_ref[src, t, pl.ds(index, each, stride=stride), :] for t in range(tiles)]
            )
        return exchange_blocks(packed)

    for row in range(row_count):
        for group in range(groups):
            span = slice(group * lanes, (group + 1) * lanes)
            left = block(row, group, channel)
            for a in range(QUAD):
                start = (row * QUAD + a) * each
                left_ref[0, start : start + each, span] = jnp.concatenate(left[a], axis=1).astype(
                    BF16
                )
            right = block(row, group, channel + stride // 2)
            for a in range(QUAD):
                for piece in range(per_row):
                    place = row * per_row + piece
                    base = (place // 4) * lanes
                    low = piece * (cols // QUAD)
                    mid = low + 2 * unit // QUAD
                    high = low + cols // QUAD
                    first = base + (place % 4) * 2 * unit + a
                    second = base + 8 * unit + (place % 4) * unit + a
                    for t in range(tiles):
                        value = right[a][t]
                        at = group * tiles + t
                        right_ref[at, pl.ds(first, mid - low, stride=QUAD), :] = value[low:mid]
                        right_ref[at, pl.ds(second, high - mid, stride=QUAD), :] = value[mid:high]
    width = pos_count * cols
    own = pl.multiple_of(half_ref[0] * width, width)
    other = pl.multiple_of((1 - half_ref[0]) * width, width)
    theirs = []
    for at in range(groups * tiles):
        span = slice(at * LANES, (at + 1) * LANES)
        own_ref[0, :, span] = right_ref[at, pl.ds(own, width), :].astype(BF16)
        theirs.append(right_ref[at, pl.ds(other, width), :].astype(BF16))
    theirs = jnp.concatenate(theirs, axis=1)
    for row in range(row_count):
        span = slice(row * QUAD * each, (row + 1) * QUAD * each)
        send_ref[0, span] = lax.dot_general(
            left_ref[0, span], theirs, NT, preferred_element_type=F32
        ).astype(BF16)


def assemble(half, received, row_count, pos_count, cols):
    sources, height, lanes = received.shape
    each = (2 * pos_count * cols) // (row_count * QUAD)
    stride = height // each
    channels = stride // 2
    depth = pos_count * cols
    rows = 2 * depth
    return pl.pallas_call(
        functools.partial(assemble_kernel, row_count=row_count, pos_count=pos_count),
        grid=(channels,),
        in_specs=[pl.BlockSpec(memory_space=pltpu.SMEM), whole(received.shape)],
        out_specs=[
            pl.BlockSpec((1, rows, depth), lambda c: (c, 0, 0)),
            pl.BlockSpec((1, depth, depth), lambda c: (c, 0, 0)),
            pl.BlockSpec((1, rows, depth), lambda c: (c, 0, 0)),
        ],
        out_shape=[
            jax.ShapeDtypeStruct((channels, rows, depth), BF16),
            jax.ShapeDtypeStruct((channels, depth, depth), BF16),
            jax.ShapeDtypeStruct((channels, rows, depth), BF16),
        ],
        scratch_shapes=[
            pltpu.VMEM((sources, lanes // LANES, height, LANES), F32),
            pltpu.VMEM((depth // LANES, rows, LANES), F32),
        ],
        compiler_params=params(),
        cost_estimate=LIGHT,
        name="assemble",
    )(half, received)


def combine_kernel(left_ref, own_ref, recv_ref, *refs, row_count, pos_count):
    out_ref, tmp_ref = refs[-2:]
    channel = pl.program_id(0)
    channels = pl.num_programs(0)
    lanes = out_ref.shape[2]
    each = left_ref.shape[1] // (row_count * QUAD)
    stride = out_ref.shape[1] // each
    tiles = lanes // LANES
    for row in range(row_count):
        for group in range(pos_count // 4):
            cols = slice(group * lanes, (group + 1) * lanes)
            blocks = []
            for a in range(QUAD):
                span = slice((row * QUAD + a) * each, (row * QUAD + a + 1) * each)
                value = lax.dot_general(
                    left_ref[0, span], own_ref[0, cols], NT, preferred_element_type=F32
                )
                value = value + recv_ref[0, span, cols].astype(F32)
                blocks.append([value[:, t * LANES : (t + 1) * LANES] for t in range(tiles)])
            for p, value in enumerate(exchange_blocks(blocks)):
                dest = row * pos_count + group * 4 + p
                for t in range(tiles):
                    tmp_ref[dest, t, pl.ds(channel, each, stride=stride), :] = value[t]

    @pl.when(channel == channels - 1)
    def _():
        for dest in range(row_count * pos_count):
            for t in range(tiles):
                out_ref[dest, :, t * LANES : (t + 1) * LANES] = tmp_ref[dest, t].astype(BF16)


def combine(left, own, received, after, row_count, pos_count, cols):
    channels, rows, depth = left.shape
    each = rows // (row_count * QUAD)
    shape = (row_count * pos_count, each * channels, QUAD * cols)
    return pl.pallas_call(
        functools.partial(combine_kernel, row_count=row_count, pos_count=pos_count),
        grid=(channels,),
        in_specs=[
            pl.BlockSpec((1, rows, depth), lambda c: (c, 0, 0)),
            pl.BlockSpec((1, depth, depth), lambda c: (c, 0, 0)),
            pl.BlockSpec((1, rows, depth), lambda c: (c, 0, 0)),
        ]
        + anywhere(after),
        out_specs=whole(shape),
        out_shape=jax.ShapeDtypeStruct(shape, BF16),
        scratch_shapes=[pltpu.VMEM((shape[0], shape[2] // LANES, shape[1], LANES), F32)],
        compiler_params=params(),
        cost_estimate=LIGHT,
        name="combine",
    )(left, own, received, *after)


def finish_kernel(*refs, chunks):
    parts = refs[:chunks]
    mid_ref, normed_ref, gate_ref, weight_ref, out_ref = refs[chunks : chunks + 5]
    flat = refs[chunks + 5 :]
    quads = mid_ref.shape[0] // QUAD
    sources, _, lanes = parts[0].shape
    tiles = range(lanes // LANES)
    for part, tmp in zip(parts, flat):
        height = part.shape[1]
        for src in range(sources):
            value = part[src].astype(F32)
            for t in tiles:
                tmp[t, src * height : (src + 1) * height] = value[:, t * LANES : (t + 1) * LANES]
    for m in range(quads):
        pieces = []
        for part, tmp in zip(parts, flat):
            height = part.shape[1]
            each = height // quads
            for k in range(each):
                pieces.append(
                    jnp.concatenate(
                        [tmp[t, pl.ds(m * each + k, sources, stride=height), :] for t in tiles], axis=1
                    )
                )
        normed = standardize_features(jnp.concatenate(pieces, axis=0), 0).astype(BF16)
        out = lax.dot_general(normed, weight_ref[...], TN, preferred_element_type=F32)
        for a, value in enumerate(unpack_rows(out)):
            i = QUAD * m + a
            gate = sigmoid(jnp.dot(normed_ref[i], gate_ref[...], preferred_element_type=F32))
            out_ref[i] = (mid_ref[i].astype(F32) + gate * value).astype(BF16)


def finish(parts, mid, normed, w_gate, w_final):
    rows, cols, wide = mid.shape
    sources, _, lanes = parts[0].shape
    total = rows // QUAD
    heights = [part.shape[1] // total for part in parts]
    quads = max(8, 16 // min(heights))
    tile = pl.BlockSpec((quads * QUAD, cols, wide), lambda i: (i, 0, 0))
    return pl.pallas_call(
        functools.partial(finish_kernel, chunks=len(parts)),
        grid=(total // quads,),
        in_specs=[
            pl.BlockSpec((sources, quads * each, lanes), lambda i: (0, i, 0)) for each in heights
        ]
        + [tile, tile, whole(w_gate.shape), whole(w_final.shape)],
        out_specs=tile,
        out_shape=jax.ShapeDtypeStruct(mid.shape, BF16),
        scratch_shapes=[
            pltpu.VMEM((lanes // LANES, sources * quads * each, LANES), F32) for each in heights
        ],
        compiler_params=params(),
        cost_estimate=LIGHT,
        name="finish",
    )(*parts, mid, normed, w_gate, w_final)


def chunk_sizes(channels):
    each = min(2, channels)
    return [each] * (channels // each)


def on_device(
    alignment_embedding,
    coupling_embedding,
    amino_validity,
    alignment_validity,
    alignment_matrix,
    tensor_final_matrix,
    coupling_logit_matrix,
    mean_final_matrix,
    trimul_matrices,
    trimul_final_matrix,
):
    seq_each, module_number, feature_count = alignment_embedding.shape
    rows, _, wide = coupling_embedding.shape
    row_count = lax.axis_size("row")
    pos_count = lax.axis_size("pos")
    col_count = 2 * pos_count
    row_index = lax.axis_index("row")
    half = lax.axis_index("half")
    col_index = half * pos_count + lax.axis_index("pos")
    seqs = seq_each * row_count
    active_entries = amino_validity.astype(F32)
    sequence_index = lax.broadcasted_iota(jnp.int32, alignment_validity.shape, 0)
    present_entries = (
        jnp.where(sequence_index == 0, F32(1.0), alignment_validity.astype(F32))
        * active_entries[None, :]
    )
    row_start = row_index * rows
    col_start = col_index * module_number
    present_rows = lax.dynamic_slice_in_dim(present_entries, row_start, rows, 1)
    present_cols = lax.dynamic_slice_in_dim(present_entries, col_start, module_number, 1)
    live_rows = lax.dynamic_slice_in_dim(active_entries, row_start, rows, 0)
    live_cols = lax.dynamic_slice_in_dim(active_entries, col_start, module_number, 0)

    own_start = (row_index * seq_each, col_start)
    present_own = lax.dynamic_slice(present_entries, own_start, (seq_each, module_number))
    own_normed = standardize_features(alignment_embedding.astype(F32), 2).astype(BF16)
    own_normed = own_normed.reshape(seq_each * module_number, feature_count)

    def project_msa(matrix):
        return jnp.dot(own_normed, matrix, preferred_element_type=F32).reshape(
            seq_each, module_number, -1
        )

    own_sides = project_msa(alignment_matrix[:, : 2 * TENSOR_FEATURES])
    own_sides = (own_sides * present_own[:, :, None]).astype(BF16)
    own_left = own_sides[:, :, :TENSOR_FEATURES]
    own_right = own_sides[:, :, TENSOR_FEATURES:]
    per_row = rows // module_number
    lefts = []
    for t in range(col_count):
        pairs = []
        for r in range(row_count):
            for q in range(col_count):
                to = (r * per_row + q % per_row - t) % col_count
                pairs.append((r * col_count + q, q // per_row * col_count + to))
        lefts.append(lax.ppermute(own_left, AXES, pairs))
    rights = [own_right]
    for t in range(1, row_count):
        pairs = [(r, (r - t) % row_count) for r in range(row_count)]
        rights.append(lax.ppermute(own_right, "row", pairs))

    w_tensor = tensor_final_matrix.reshape(TENSOR_FEATURES, TENSOR_FEATURES * wide)
    pair_mid, pair_normed = front(
        jnp.stack([row_index, col_index]).astype(jnp.int32),
        lefts,
        rights,
        present_rows,
        coupling_embedding,
        w_tensor,
        present_cols.T.astype(BF16),
    )

    unit = module_number // 3
    live_packed = jnp.concatenate(
        [live_cols[: 2 * unit]] * QUAD + [live_cols[2 * unit :]] * QUAD
    )[None]

    devices = row_count * pos_count
    sizes = chunk_sizes(CTRI // devices)
    w_kinds = trimul_matrices[:, : 4 * CTRI].T.reshape(2, 2, devices, -1, wide)
    half_scalar = half.astype(jnp.int32).reshape(1)
    swap = [(0, 1), (1, 0)]
    shape_of = (row_count, pos_count, module_number)
    values = project_msa(
        alignment_matrix[:, 2 * TENSOR_FEATURES : 2 * TENSOR_FEATURES + MEAN_GROUPS * GROUP_FEATURES]
    ).astype(BF16)
    sequence_gate = jax.nn.sigmoid(
        project_msa(alignment_matrix[:, 2 * TENSOR_FEATURES + MEAN_GROUPS * GROUP_FEATURES :])
    )
    logits = (
        jnp.dot(
            pair_normed.reshape(rows * module_number, wide),
            coupling_logit_matrix,
            preferred_element_type=F32,
        ).reshape(rows, module_number, MEAN_GROUPS)
        + MASK_PENALTY * (live_rows - 1.0)[:, None, None]
    )
    chunks = len(sizes)

    def send(g, after):
        start = sum(sizes[:g])
        weight = jnp.transpose(w_kinds[:, :, :, start : start + sizes[g]], (1, 2, 0, 3, 4))
        return project(
            live_rows, pair_normed, live_packed, weight.reshape(-1, wide), after, devices
        )

    def exchange(block):
        return lax.all_to_all(block, GROUP, split_axis=0, concat_axis=0, tiled=True)

    stages = [assemble(half_scalar, exchange(send(0, ())), *shape_of)]
    ahead = send(1, ()) if chunks > 1 else None
    partials, returned = [], []

    def finish_chunk(g, partial, after):
        left, own, _ = stages[g]
        returned.append(exchange(combine(left, own, partial, after, *shape_of)))

    for g in range(chunks):
        carried = [stages[g][2]] + partials[g - 1 :][:1] * (g > 0)
        if g + 1 < chunks:
            carried.append(ahead)
        after = returned[g - 2 : g - 1] if g > 1 else []
        if g == 1:
            after = [logits, values]
        carried = fence(carried, after)
        partials.append(lax.ppermute(carried[0], "half", swap))
        if g + 1 < chunks:
            stages.append(assemble(half_scalar, exchange(carried[-1]), *shape_of))
        if g + 2 < chunks:
            ahead = send(g + 2, (stages[g][0],))
        if g > 0:
            finish_chunk(g - 1, carried[1], tuple(stages[g + 1][:1]) if g + 1 < chunks else ())

    logits_all = lax.all_gather(logits, "row", axis=0, tiled=True)
    values_all = lax.all_gather(values, ("half", "pos"), axis=1, tiled=True)
    top_all = jnp.max(logits_all, axis=0)
    expd = jnp.exp(logits_all - top_all[None])
    weights_all = (expd / jnp.sum(expd, axis=0)[None]).astype(BF16)
    value_all_heads = values_all.reshape(seq_each, -1, MEAN_GROUPS, GROUP_FEATURES)
    summed = jnp.einsum("jih,sjhd->sihd", weights_all, value_all_heads, preferred_element_type=F32)
    head_averaged = summed.reshape(seq_each, module_number, MEAN_GROUPS * GROUP_FEATURES)
    gated_result = (sequence_gate * head_averaged).astype(BF16)
    blended_update = jnp.dot(
        gated_result.reshape(seq_each * module_number, -1),
        mean_final_matrix,
        preferred_element_type=F32,
    ).reshape(seq_each, module_number, -1)
    alignment_updated_embedding = (alignment_embedding.astype(F32) + blended_update).astype(BF16)

    finish_chunk(chunks - 1, partials[-1], (alignment_updated_embedding,))
    w_final = jnp.transpose(trimul_final_matrix.reshape(devices, -1, wide), (1, 0, 2))
    pair_output = finish(
        returned, pair_mid, pair_normed, trimul_matrices[:, 4 * CTRI :], w_final.reshape(-1, wide)
    )
    return (alignment_updated_embedding, pair_output)


def solution(mesh):
    rows, cols = mesh.devices.shape
    inner = Mesh(mesh.devices.reshape(rows, 2, cols // 2), AXES)
    tile = P("row", ("half", "pos"), None)
    in_specs = (tile, tile) + (P(),) * 8
    return jax.shard_map(
        on_device, mesh=inner, in_specs=in_specs, out_specs=(tile, tile), check_vma=False
    )
```

```python
import functools

import jax
import jax.numpy as jnp
from jax import lax
from jax.experimental import pallas as pl
from jax.experimental.pallas import tpu as pltpu
from jax.sharding import Mesh, PartitionSpec as P

TENSOR_FEATURES = 32
MEAN_GROUPS = 8
GROUP_FEATURES = 32
CTRI = 128

EPS = 1e-05
MASK_PENALTY = 10000.0
QUAD = 4
LANES = 128
MIB = 1024 * 1024
AXES = ("row", "half", "pos")
GROUP = ("row", "pos")
F32 = jnp.float32
BF16 = jnp.bfloat16
NT = (((1,), (1,)), ((), ()))
TN = (((0,), (0,)), ((), ()))


def standardize_features(values_in, axis):
    centre = values_in - jnp.mean(values_in, axis=axis, keepdims=True)
    spread = jnp.mean(centre * centre, axis=axis, keepdims=True)
    return centre * lax.rsqrt(spread + EPS)


def sigmoid(x):
    return 0.5 * jnp.tanh(0.5 * x) + 0.5


def params():
    return pltpu.CompilerParams(
        vmem_limit_bytes=60 * MIB, dimension_semantics=("arbitrary",)
    )


LIGHT = pl.CostEstimate(flops=1000, bytes_accessed=1000, transcendentals=0)


def whole(shape):
    zeros = (0,) * len(shape)
    return pl.BlockSpec(shape, lambda *_: zeros, pipeline_mode=pl.Buffered(1))


def anywhere(after):
    return [pl.BlockSpec(memory_space=pl.ANY)] * len(after)


def fence(values, after):
    return pl.pallas_call(
        lambda *refs: None,
        in_specs=anywhere(values) + anywhere(after),
        out_specs=anywhere(values),
        out_shape=[jax.ShapeDtypeStruct(v.shape, v.dtype) for v in values],
        input_output_aliases={i: i for i in range(len(values))},
        compiler_params=pltpu.CompilerParams(vmem_limit_bytes=60 * MIB),
        cost_estimate=LIGHT,
        name="fence",
    )(*values, *after)


def pack_rows(rows):
    unit = rows[0].shape[0] // 3
    return jnp.concatenate([r[: 2 * unit] for r in rows] + [r[2 * unit :] for r in rows], axis=0)


def unpack_rows(packed):
    unit = packed.shape[0] // 12
    return [
        jnp.concatenate(
            [
                packed[2 * unit * a : 2 * unit * (a + 1)],
                packed[8 * unit + unit * a : 8 * unit + unit * (a + 1)],
            ],
            axis=0,
        )
        for a in range(QUAD)
    ]


def swap_blocks(first, second, width, lane):
    low = (lane // width) % 2 == 0
    size = first.shape[1]
    return (
        jnp.where(low, first, pltpu.roll(second, width, 1)),
        jnp.where(low, pltpu.roll(first, size - width, 1), second),
    )


def exchange_blocks(packed):
    part = packed
    unit = LANES // 4
    lane = lax.broadcasted_iota(jnp.int32, part[0][0].shape, 1)
    out = [[None] * 3 for _ in range(4)]
    for pair in range(2):
        one, two = part[2 * pair], part[2 * pair + 1]
        for t in range(2):
            out[2 * t][pair], out[2 * t + 1][pair] = swap_blocks(one[t], two[t], 2 * unit, lane)
    u0, u2 = swap_blocks(part[0][2], part[2][2], 2 * unit, lane)
    u1, u3 = swap_blocks(part[1][2], part[3][2], 2 * unit, lane)
    out[0][2], out[1][2] = swap_blocks(u0, u1, unit, lane)
    out[2][2], out[3][2] = swap_blocks(u2, u3, unit, lane)
    return out


def front_kernel(place_ref, *refs, row_count, col_count):
    lefts, rights = refs[:col_count], refs[col_count : col_count + row_count]
    refs = refs[col_count + row_count :]
    prow_ref, coup_ref, weight_ref, pcol_ref, mid_ref, normed_ref = refs[:6]
    sides_ref, right_ref, tmp_ref = refs[6:]
    block, cols, wide = coup_ref.shape
    seq_each, _, width = lefts[0].shape
    seqs = seq_each * row_count
    per_row = col_count // row_count

    @pl.when(pl.program_id(0) == 0)
    def _():
        for t, part in enumerate(lefts):
            index = lax.rem(t + place_ref[1], col_count)
            first = lax.rem(index, per_row) * (cols * seqs) + index // per_row * seq_each
            for k in range(seq_each):
                sides_ref[pl.ds(first + k, cols, stride=seqs), 0:width] = part[k].astype(F32)
        right = jnp.zeros(right_ref.shape, F32)
        feature = lax.broadcasted_iota(jnp.int32, (width, width * seqs), 0)
        target = lax.broadcasted_iota(jnp.int32, (width, width * seqs), 1)
        for t, part in enumerate(rights):
            first = lax.rem(t + place_ref[0], row_count) * seq_each
            for k in range(seq_each):
                spread = (target == feature * seqs + (first + k)).astype(F32).astype(BF16)
                right += jnp.dot(part[k], spread, preferred_element_type=F32)
        right_ref[...] = right.astype(BF16)

    span = block * seqs
    start = pl.multiple_of(pl.program_id(0) * span, span)
    left = sides_ref[pl.ds(start, span), 0:width].astype(BF16)
    features = weight_ref.shape[1] // wide
    step = 4
    for low in range(0, features, step):
        part = jnp.dot(
            left, weight_ref[:, low * wide : (low + step) * wide], preferred_element_type=F32
        ).astype(BF16)
        for i in range(block):
            for d in range(step):
                tmp_ref[
                    i // 2,
                    (low + d) * seqs : (low + d + 1) * seqs,
                    (i % 2) * wide : (i % 2 + 1) * wide,
                ] = part[i * seqs : (i + 1) * seqs, d * wide : (d + 1) * wide]
    row_lane = lax.broadcasted_iota(jnp.int32, prow_ref.shape, 1)
    for pair in range(block // 2):
        update = jnp.dot(right_ref[...], tmp_ref[pair], preferred_element_type=F32)
        here = pl.program_id(0) * block + 2 * pair
        wanted = [jnp.where(row_lane == here + e, prow_ref[...], 0.0) for e in range(2)]
        wanted = [
            jnp.broadcast_to(jnp.sum(w, axis=1, keepdims=True), (seqs, wide)) for w in wanted
        ]
        count = jnp.dot(
            pcol_ref[...], jnp.concatenate(wanted, axis=1).astype(BF16), preferred_element_type=F32
        )
        update = update / jnp.maximum(count, 1.0)
        for e in range(2):
            i = 2 * pair + e
            mid = (coup_ref[i].astype(F32) + update[:, e * wide : (e + 1) * wide]).astype(BF16)
            mid_ref[i] = mid
            normed_ref[i] = standardize_features(mid.astype(F32), 1).astype(BF16)


def front(place, lefts, rights, present_rows, coupling, w_tensor, present_cols):
    rows, cols, wide = coupling.shape
    seqs, width = present_rows.shape[0], lefts[0].shape[2]
    block = 8
    tile = pl.BlockSpec((block, cols, wide), lambda i: (i, 0, 0))
    return pl.pallas_call(
        functools.partial(front_kernel, row_count=len(rights), col_count=len(lefts)),
        grid=(rows // block,),
        in_specs=[pl.BlockSpec(memory_space=pltpu.SMEM)]
        + [whole(part.shape) for part in lefts + rights]
        + [
            whole(present_rows.shape),
            tile,
            whole(w_tensor.shape),
            whole(present_cols.shape),
        ],
        out_specs=[tile, tile],
        out_shape=[jax.ShapeDtypeStruct(coupling.shape, BF16)] * 2,
        scratch_shapes=[
            pltpu.VMEM((rows * seqs, LANES), F32),
            pltpu.VMEM((cols, width * seqs), BF16),
            pltpu.VMEM((block // 2, width * seqs, 2 * wide), BF16),
        ],
        compiler_params=params(),
        cost_estimate=LIGHT,
        name="front",
    )(place, *lefts, *rights, present_rows, coupling, w_tensor, present_cols)


def exchange_rows(values):
    values = list(values)
    count = len(values)
    step = count // 2
    row = lax.broadcasted_iota(jnp.int32, values[0].shape, 0)
    size = values[0].shape[0]
    while step:
        width = 8 // count * step
        low = (row // width) % 2 == 0
        for m in range(count):
            if m & step == 0:
                one, two = values[m], values[m + step]
                values[m] = jnp.where(low, one, pltpu.roll(two, width, 0))
                values[m + step] = jnp.where(low, pltpu.roll(one, size - width, 0), two)
        step //= 2
    return values


def project_kernel(live_ref, normed_ref, cols_ref, weight_ref, *refs):
    out_ref, tmp_ref = refs[-2:]
    quads = normed_ref.shape[0] // QUAD
    dests, height, lanes = out_ref.shape
    each = height // quads
    count = dests * each
    unit = lanes // 12
    lane = lax.broadcasted_iota(jnp.int32, (1, lanes), 1)
    place = jnp.where(lane < 8 * unit, lane // (2 * unit), (lane - 8 * unit) // unit)
    group = max(1, 8 // each)
    for first in range(0, quads, group):
        values = []
        for m in range(first, first + group):
            packed = pack_rows([normed_ref[QUAD * m + a] for a in range(QUAD)])
            both = lax.dot_general(weight_ref[...], packed, NT, preferred_element_type=F32)
            row = (pl.program_id(0) * quads + m) * QUAD
            live = cols_ref[...]
            for a in range(QUAD):
                live = jnp.where(place == a, live * live_ref[row + a], live)
            values.append(sigmoid(both[:count]) * both[count:] * live)
        for b, value in enumerate(exchange_rows(values)):
            size = each * group
            for v in range(count // size):
                tmp_ref[v * group + b, first * each : first * each + size] = value[
                    v * size : (v + 1) * size
                ]
    out_ref[...] = tmp_ref[...].astype(BF16)


def project(live_rows, normed, live_cols, weight, after, dests):
    rows, cols, wide = normed.shape
    each = weight.shape[0] // (2 * dests)
    quads = max(8, 16 // each)
    lanes = QUAD * cols
    total = rows // QUAD
    return pl.pallas_call(
        project_kernel,
        grid=(total // quads,),
        in_specs=[
            pl.BlockSpec(memory_space=pltpu.SMEM),
            pl.BlockSpec((quads * QUAD, cols, wide), lambda i: (i, 0, 0)),
            whole(live_cols.shape),
            whole(weight.shape),
        ]
        + anywhere(after),
        out_specs=pl.BlockSpec((dests, quads * each, lanes), lambda i: (0, i, 0)),
        out_shape=jax.ShapeDtypeStruct((dests, total * each, lanes), BF16),
        scratch_shapes=[pltpu.VMEM((dests, quads * each, lanes), F32)],
        compiler_params=params(),
        cost_estimate=LIGHT,
        name="project",
    )(live_rows, normed, live_cols, weight, *after)


def assemble_kernel(half_ref, recv_ref, *refs, row_count, pos_count):
    left_ref, own_ref, send_ref, flat_ref, right_ref = refs[-5:]
    channel = pl.program_id(0)
    lanes = recv_ref.shape[2]
    unit = lanes // 12
    cols = 3 * unit
    each = send_ref.shape[1] // (row_count * QUAD)
    stride = recv_ref.shape[1] // each
    groups = pos_count // 4
    tiles = lanes // LANES
    per_row = each * QUAD // cols

    @pl.when(channel == 0)
    def _():
        for src in range(row_count * pos_count):
            value = recv_ref[src].astype(F32)
            for t in range(tiles):
                flat_ref[src, t] = value[:, t * LANES : (t + 1) * LANES]

    def block(row, group, index):
        packed = []
        for p in range(4):
            src = row * pos_count + group * 4 + p
            packed.append(
                [flat_ref[src, t, pl.ds(index, each, stride=stride), :] for t in range(tiles)]
            )
        return exchange_blocks(packed)

    for row in range(row_count):
        for group in range(groups):
            span = slice(group * lanes, (group + 1) * lanes)
            left = block(row, group, channel)
            for a in range(QUAD):
                start = (row * QUAD + a) * each
                left_ref[0, start : start + each, span] = jnp.concatenate(left[a], axis=1).astype(
                    BF16
                )
            right = block(row, group, channel + stride // 2)
            for a in range(QUAD):
                for piece in range(per_row):
                    place = row * per_row + piece
                    base = (place // 4) * lanes
                    low = piece * (cols // QUAD)
                    mid = low + 2 * unit // QUAD
                    high = low + cols // QUAD
                    first = base + (place % 4) * 2 * unit + a
                    second = base + 8 * unit + (place % 4) * unit + a
                    for t in range(tiles):
                        value = right[a][t]
                        at = group * tiles + t
                        right_ref[at, pl.ds(first, mid - low, stride=QUAD), :] = value[low:mid]
                        right_ref[at, pl.ds(second, high - mid, stride=QUAD), :] = value[mid:high]
    width = pos_count * cols
    own = pl.multiple_of(half_ref[0] * width, width)
    other = pl.multiple_of((1 - half_ref[0]) * width, width)
    theirs = []
    for at in range(groups * tiles):
        span = slice(at * LANES, (at + 1) * LANES)
        own_ref[0, :, span] = right_ref[at, pl.ds(own, width), :].astype(BF16)
        theirs.append(right_ref[at, pl.ds(other, width), :].astype(BF16))
    theirs = jnp.concatenate(theirs, axis=1)
    for row in range(row_count):
        span = slice(row * QUAD * each, (row + 1) * QUAD * each)
        send_ref[0, span] = lax.dot_general(
            left_ref[0, span], theirs, NT, preferred_element_type=F32
        ).astype(BF16)


def assemble(half, received, after, row_count, pos_count, cols):
    sources, height, lanes = received.shape
    each = (2 * pos_count * cols) // (row_count * QUAD)
    stride = height // each
    channels = stride // 2
    depth = pos_count * cols
    rows = 2 * depth
    return pl.pallas_call(
        functools.partial(assemble_kernel, row_count=row_count, pos_count=pos_count),
        grid=(channels,),
        in_specs=[pl.BlockSpec(memory_space=pltpu.SMEM), whole(received.shape)] + anywhere(after),
        out_specs=[
            pl.BlockSpec((1, rows, depth), lambda c: (c, 0, 0)),
            pl.BlockSpec((1, depth, depth), lambda c: (c, 0, 0)),
            pl.BlockSpec((1, rows, depth), lambda c: (c, 0, 0)),
        ],
        out_shape=[
            jax.ShapeDtypeStruct((channels, rows, depth), BF16),
            jax.ShapeDtypeStruct((channels, depth, depth), BF16),
            jax.ShapeDtypeStruct((channels, rows, depth), BF16),
        ],
        scratch_shapes=[
            pltpu.VMEM((sources, lanes // LANES, height, LANES), F32),
            pltpu.VMEM((depth // LANES, rows, LANES), F32),
        ],
        compiler_params=params(),
        cost_estimate=LIGHT,
        name="assemble",
    )(half, received, *after)


def combine_kernel(left_ref, own_ref, recv_ref, *refs, row_count, pos_count):
    out_ref, tmp_ref = refs[-2:]
    channel = pl.program_id(0)
    channels = pl.num_programs(0)
    lanes = out_ref.shape[2]
    each = left_ref.shape[1] // (row_count * QUAD)
    stride = out_ref.shape[1] // each
    tiles = lanes // LANES
    for row in range(row_count):
        for group in range(pos_count // 4):
            cols = slice(group * lanes, (group + 1) * lanes)
            blocks = []
            for a in range(QUAD):
                span = slice((row * QUAD + a) * each, (row * QUAD + a + 1) * each)
                value = lax.dot_general(
                    left_ref[0, span], own_ref[0, cols], NT, preferred_element_type=F32
                )
                value = value + recv_ref[0, span, cols].astype(F32)
                blocks.append([value[:, t * LANES : (t + 1) * LANES] for t in range(tiles)])
            for p, value in enumerate(exchange_blocks(blocks)):
                dest = row * pos_count + group * 4 + p
                for t in range(tiles):
                    tmp_ref[dest, t, pl.ds(channel, each, stride=stride), :] = value[t]

    @pl.when(channel == channels - 1)
    def _():
        for dest in range(row_count * pos_count):
            for t in range(tiles):
                out_ref[dest, :, t * LANES : (t + 1) * LANES] = tmp_ref[dest, t].astype(BF16)


def combine(left, own, received, after, row_count, pos_count, cols):
    channels, rows, depth = left.shape
    each = rows // (row_count * QUAD)
    shape = (row_count * pos_count, each * channels, QUAD * cols)
    return pl.pallas_call(
        functools.partial(combine_kernel, row_count=row_count, pos_count=pos_count),
        grid=(channels,),
        in_specs=[
            pl.BlockSpec((1, rows, depth), lambda c: (c, 0, 0)),
            pl.BlockSpec((1, depth, depth), lambda c: (c, 0, 0)),
            pl.BlockSpec((1, rows, depth), lambda c: (c, 0, 0)),
        ]
        + anywhere(after),
        out_specs=whole(shape),
        out_shape=jax.ShapeDtypeStruct(shape, BF16),
        scratch_shapes=[pltpu.VMEM((shape[0], shape[2] // LANES, shape[1], LANES), F32)],
        compiler_params=params(),
        cost_estimate=LIGHT,
        name="combine",
    )(left, own, received, *after)


def finish_kernel(*refs, chunks):
    parts = refs[:chunks]
    mid_ref, normed_ref, gate_ref, weight_ref, out_ref = refs[chunks : chunks + 5]
    flat = refs[chunks + 5 :]
    quads = mid_ref.shape[0] // QUAD
    sources, _, lanes = parts[0].shape
    tiles = range(lanes // LANES)
    for part, tmp in zip(parts, flat):
        height = part.shape[1]
        for src in range(sources):
            value = part[src].astype(F32)
            for t in tiles:
                tmp[t, src * height : (src + 1) * height] = value[:, t * LANES : (t + 1) * LANES]
    for m in range(quads):
        pieces = []
        for part, tmp in zip(parts, flat):
            height = part.shape[1]
            each = height // quads
            for k in range(each):
                pieces.append(
                    jnp.concatenate(
                        [tmp[t, pl.ds(m * each + k, sources, stride=height), :] for t in tiles], axis=1
                    )
                )
        normed = standardize_features(jnp.concatenate(pieces, axis=0), 0).astype(BF16)
        out = lax.dot_general(normed, weight_ref[...], TN, preferred_element_type=F32)
        for a, value in enumerate(unpack_rows(out)):
            i = QUAD * m + a
            gate = sigmoid(jnp.dot(normed_ref[i], gate_ref[...], preferred_element_type=F32))
            out_ref[i] = (mid_ref[i].astype(F32) + gate * value).astype(BF16)


def finish(parts, mid, normed, w_gate, w_final):
    rows, cols, wide = mid.shape
    sources, _, lanes = parts[0].shape
    total = rows // QUAD
    heights = [part.shape[1] // total for part in parts]
    quads = max(8, 16 // min(heights))
    tile = pl.BlockSpec((quads * QUAD, cols, wide), lambda i: (i, 0, 0))
    return pl.pallas_call(
        functools.partial(finish_kernel, chunks=len(parts)),
        grid=(total // quads,),
        in_specs=[
            pl.BlockSpec((sources, quads * each, lanes), lambda i: (0, i, 0)) for each in heights
        ]
        + [tile, tile, whole(w_gate.shape), whole(w_final.shape)],
        out_specs=tile,
        out_shape=jax.ShapeDtypeStruct(mid.shape, BF16),
        scratch_shapes=[
            pltpu.VMEM((lanes // LANES, sources * quads * each, LANES), F32) for each in heights
        ],
        compiler_params=params(),
        cost_estimate=LIGHT,
        name="finish",
    )(*parts, mid, normed, w_gate, w_final)


def chunk_sizes(channels):
    each = min(4, channels)
    return [each] * (channels // each)


def on_device(
    alignment_embedding,
    coupling_embedding,
    amino_validity,
    alignment_validity,
    alignment_matrix,
    tensor_final_matrix,
    coupling_logit_matrix,
    mean_final_matrix,
    trimul_matrices,
    trimul_final_matrix,
):
    seq_each, module_number, feature_count = alignment_embedding.shape
    rows, _, wide = coupling_embedding.shape
    row_count = lax.axis_size("row")
    pos_count = lax.axis_size("pos")
    col_count = 2 * pos_count
    row_index = lax.axis_index("row")
    half = lax.axis_index("half")
    col_index = half * pos_count + lax.axis_index("pos")
    seqs = seq_each * row_count
    active_entries = amino_validity.astype(F32)
    sequence_index = lax.broadcasted_iota(jnp.int32, alignment_validity.shape, 0)
    present_entries = (
        jnp.where(sequence_index == 0, F32(1.0), alignment_validity.astype(F32))
        * active_entries[None, :]
    )
    row_start = row_index * rows
    col_start = col_index * module_number
    present_rows = lax.dynamic_slice_in_dim(present_entries, row_start, rows, 1)
    present_cols = lax.dynamic_slice_in_dim(present_entries, col_start, module_number, 1)
    live_rows = lax.dynamic_slice_in_dim(active_entries, row_start, rows, 0)
    live_cols = lax.dynamic_slice_in_dim(active_entries, col_start, module_number, 0)

    own_start = (row_index * seq_each, col_start)
    present_own = lax.dynamic_slice(present_entries, own_start, (seq_each, module_number))
    own_normed = standardize_features(alignment_embedding.astype(F32), 2).astype(BF16)
    own_normed = own_normed.reshape(seq_each * module_number, feature_count)

    def project_msa(matrix):
        return jnp.dot(own_normed, matrix, preferred_element_type=F32).reshape(
            seq_each, module_number, -1
        )

    own_sides = project_msa(alignment_matrix[:, : 2 * TENSOR_FEATURES])
    own_sides = (own_sides * present_own[:, :, None]).astype(BF16)
    own_left = own_sides[:, :, :TENSOR_FEATURES]
    own_right = own_sides[:, :, TENSOR_FEATURES:]
    per_row = rows // module_number
    lefts = []
    for t in range(col_count):
        pairs = []
        for r in range(row_count):
            for q in range(col_count):
                to = (r * per_row + q % per_row - t) % col_count
                pairs.append((r * col_count + q, q // per_row * col_count + to))
        lefts.append(lax.ppermute(own_left, AXES, pairs))
    rights = [own_right]
    for t in range(1, row_count):
        pairs = [(r, (r - t) % row_count) for r in range(row_count)]
        rights.append(lax.ppermute(own_right, "row", pairs))

    w_tensor = tensor_final_matrix.reshape(TENSOR_FEATURES, TENSOR_FEATURES * wide)
    pair_mid, pair_normed = front(
        jnp.stack([row_index, col_index]).astype(jnp.int32),
        lefts,
        rights,
        present_rows,
        coupling_embedding,
        w_tensor,
        present_cols.T.astype(BF16),
    )

    unit = module_number // 3
    live_packed = jnp.concatenate(
        [live_cols[: 2 * unit]] * QUAD + [live_cols[2 * unit :]] * QUAD
    )[None]

    devices = row_count * pos_count
    sizes = chunk_sizes(CTRI // devices)
    w_kinds = trimul_matrices[:, : 4 * CTRI].T.reshape(2, 2, devices, -1, wide)
    half_scalar = half.astype(jnp.int32).reshape(1)
    swap = [(0, 1), (1, 0)]
    shape_of = (row_count, pos_count, module_number)
    values = project_msa(
        alignment_matrix[:, 2 * TENSOR_FEATURES : 2 * TENSOR_FEATURES + MEAN_GROUPS * GROUP_FEATURES]
    ).astype(BF16)
    sequence_gate = jax.nn.sigmoid(
        project_msa(alignment_matrix[:, 2 * TENSOR_FEATURES + MEAN_GROUPS * GROUP_FEATURES :])
    )
    logits = (
        jnp.dot(
            pair_normed.reshape(rows * module_number, wide),
            coupling_logit_matrix,
            preferred_element_type=F32,
        ).reshape(rows, module_number, MEAN_GROUPS)
        + MASK_PENALTY * (live_rows - 1.0)[:, None, None]
    )
    chunks = len(sizes)

    def send(g, after):
        start = sum(sizes[:g])
        weight = jnp.transpose(w_kinds[:, :, :, start : start + sizes[g]], (1, 2, 0, 3, 4))
        return project(
            live_rows, pair_normed, live_packed, weight.reshape(-1, wide), after, devices
        )

    def exchange(block):
        return lax.all_to_all(block, GROUP, split_axis=0, concat_axis=0, tiled=True)

    sent = send(0, ())
    ahead = [send(1, ())] if chunks > 1 else []
    stages = [assemble(half_scalar, exchange(sent), (logits, values, *ahead), *shape_of)]
    partials, returned = [], []

    def finish_chunk(g, partial, after):
        left, own, _ = stages[g]
        returned.append(exchange(combine(left, own, partial, after, *shape_of)))

    logits_all = lax.all_gather(logits, "row", axis=0, tiled=True)
    values_all = lax.all_gather(values, ("half", "pos"), axis=1, tiled=True)
    top_all = jnp.max(logits_all, axis=0)
    expd = jnp.exp(logits_all - top_all[None])
    weights_all = (expd / jnp.sum(expd, axis=0)[None]).astype(BF16)
    value_all_heads = values_all.reshape(seq_each, -1, MEAN_GROUPS, GROUP_FEATURES)
    summed = jnp.einsum("jih,sjhd->sihd", weights_all, value_all_heads, preferred_element_type=F32)
    head_averaged = summed.reshape(seq_each, module_number, MEAN_GROUPS * GROUP_FEATURES)
    gated_result = (sequence_gate * head_averaged).astype(BF16)
    blended_update = jnp.dot(
        gated_result.reshape(seq_each * module_number, -1),
        mean_final_matrix,
        preferred_element_type=F32,
    ).reshape(seq_each, module_number, -1)
    alignment_updated_embedding = (alignment_embedding.astype(F32) + blended_update).astype(BF16)

    for g in range(chunks):
        carried = [stages[g][2], *partials[g - 1 : g], *ahead]
        after = returned[g - 2 : g - 1] if g > 1 else []
        if g == 1:
            after = [alignment_updated_embedding]
        carried = fence(carried, after)
        partials.append(lax.ppermute(carried[0], "half", swap))
        if g + 1 < chunks:
            stages.append(assemble(half_scalar, exchange(carried[-1]), (), *shape_of))
            ahead = [send(g + 2, (stages[g][0],))] if g + 2 < chunks else []
        if g > 0:
            finish_chunk(g - 1, carried[1], tuple(stages[g + 1][:1]) if g + 1 < chunks else ())

    finish_chunk(chunks - 1, partials[-1], (alignment_updated_embedding, *returned[-1:]))
    w_final = jnp.transpose(trimul_final_matrix.reshape(devices, -1, wide), (1, 0, 2))
    pair_output = finish(
        returned, pair_mid, pair_normed, trimul_matrices[:, 4 * CTRI :], w_final.reshape(-1, wide)
    )
    return (alignment_updated_embedding, pair_output)


def solution(mesh):
    rows, cols = mesh.devices.shape
    inner = Mesh(mesh.devices.reshape(rows, 2, cols // 2), AXES)
    tile = P("row", ("half", "pos"), None)
    in_specs = (tile, tile) + (P(),) * 8
    return jax.shard_map(
        on_device, mesh=inner, in_specs=in_specs, out_specs=(tile, tile), check_vma=False
    )
```

```python
import functools

import jax
import jax.numpy as jnp
from jax import lax
from jax.experimental import pallas as pl
from jax.experimental.pallas import tpu as pltpu
from jax.sharding import Mesh, PartitionSpec as P

TENSOR_FEATURES = 32
MEAN_GROUPS = 8
GROUP_FEATURES = 32
CTRI = 128

EPS = 1e-05
MASK_PENALTY = 10000.0
QUAD = 4
LANES = 128
MIB = 1024 * 1024
AXES = ("row", "half", "pos")
GROUP = ("row", "pos")
F32 = jnp.float32
BF16 = jnp.bfloat16
NT = (((1,), (1,)), ((), ()))
TN = (((0,), (0,)), ((), ()))


def standardize_features(values_in, axis):
    centre = values_in - jnp.mean(values_in, axis=axis, keepdims=True)
    spread = jnp.mean(centre * centre, axis=axis, keepdims=True)
    return centre * lax.rsqrt(spread + EPS)


def sigmoid(x):
    return 0.5 * jnp.tanh(0.5 * x) + 0.5


def params():
    return pltpu.CompilerParams(
        vmem_limit_bytes=60 * MIB, dimension_semantics=("arbitrary",)
    )


LIGHT = pl.CostEstimate(flops=1000, bytes_accessed=1000, transcendentals=0)


def whole(shape):
    zeros = (0,) * len(shape)
    return pl.BlockSpec(shape, lambda *_: zeros, pipeline_mode=pl.Buffered(1))


def anywhere(after):
    return [pl.BlockSpec(memory_space=pl.ANY)] * len(after)


def fence(values, after):
    return pl.pallas_call(
        lambda *refs: None,
        in_specs=anywhere(values) + anywhere(after),
        out_specs=anywhere(values),
        out_shape=[jax.ShapeDtypeStruct(v.shape, v.dtype) for v in values],
        input_output_aliases={i: i for i in range(len(values))},
        compiler_params=pltpu.CompilerParams(vmem_limit_bytes=60 * MIB),
        cost_estimate=LIGHT,
        name="fence",
    )(*values, *after)


def pack_rows(rows):
    unit = rows[0].shape[0] // 3
    return jnp.concatenate([r[: 2 * unit] for r in rows] + [r[2 * unit :] for r in rows], axis=0)


def unpack_rows(packed):
    unit = packed.shape[0] // 12
    return [
        jnp.concatenate(
            [
                packed[2 * unit * a : 2 * unit * (a + 1)],
                packed[8 * unit + unit * a : 8 * unit + unit * (a + 1)],
            ],
            axis=0,
        )
        for a in range(QUAD)
    ]


def swap_blocks(first, second, width, lane):
    low = (lane // width) % 2 == 0
    size = first.shape[1]
    return (
        jnp.where(low, first, pltpu.roll(second, width, 1)),
        jnp.where(low, pltpu.roll(first, size - width, 1), second),
    )


def exchange_blocks(packed):
    part = packed
    unit = LANES // 4
    lane = lax.broadcasted_iota(jnp.int32, part[0][0].shape, 1)
    out = [[None] * 3 for _ in range(4)]
    for pair in range(2):
        one, two = part[2 * pair], part[2 * pair + 1]
        for t in range(2):
            out[2 * t][pair], out[2 * t + 1][pair] = swap_blocks(one[t], two[t], 2 * unit, lane)
    u0, u2 = swap_blocks(part[0][2], part[2][2], 2 * unit, lane)
    u1, u3 = swap_blocks(part[1][2], part[3][2], 2 * unit, lane)
    out[0][2], out[1][2] = swap_blocks(u0, u1, unit, lane)
    out[2][2], out[3][2] = swap_blocks(u2, u3, unit, lane)
    return out


def front_kernel(place_ref, *refs, row_count, col_count, first_block):
    lefts, rights = refs[:col_count], refs[col_count : col_count + row_count]
    refs = refs[col_count + row_count :]
    prow_ref, coup_ref, weight_ref, pcol_ref = refs[:4]
    sides_ref, right_ref, tmp_ref = refs[-3:]
    mid_ref, normed_ref = refs[-5:-3]
    step_at = pl.program_id(0) + first_block
    block, cols, wide = coup_ref.shape
    seq_each, _, width = lefts[0].shape
    seqs = seq_each * row_count
    per_row = col_count // row_count

    @pl.when(pl.program_id(0) == 0)
    def _():
        for t, part in enumerate(lefts):
            index = lax.rem(t + place_ref[1], col_count)
            first = lax.rem(index, per_row) * (cols * seqs) + index // per_row * seq_each
            for k in range(seq_each):
                sides_ref[pl.ds(first + k, cols, stride=seqs), 0:width] = part[k].astype(F32)
        right = jnp.zeros(right_ref.shape, F32)
        feature = lax.broadcasted_iota(jnp.int32, (width, width * seqs), 0)
        target = lax.broadcasted_iota(jnp.int32, (width, width * seqs), 1)
        for t, part in enumerate(rights):
            first = lax.rem(t + place_ref[0], row_count) * seq_each
            for k in range(seq_each):
                spread = (target == feature * seqs + (first + k)).astype(F32).astype(BF16)
                right += jnp.dot(part[k], spread, preferred_element_type=F32)
        right_ref[...] = right.astype(BF16)

    span = block * seqs
    start = pl.multiple_of(step_at * span, span)
    left = sides_ref[pl.ds(start, span), 0:width].astype(BF16)
    features = weight_ref.shape[1] // wide
    step = 4
    for low in range(0, features, step):
        part = jnp.dot(
            left, weight_ref[:, low * wide : (low + step) * wide], preferred_element_type=F32
        ).astype(BF16)
        for i in range(block):
            for d in range(step):
                tmp_ref[
                    i // 2,
                    (low + d) * seqs : (low + d + 1) * seqs,
                    (i % 2) * wide : (i % 2 + 1) * wide,
                ] = part[i * seqs : (i + 1) * seqs, d * wide : (d + 1) * wide]
    row_lane = lax.broadcasted_iota(jnp.int32, prow_ref.shape, 1)
    for pair in range(block // 2):
        update = jnp.dot(right_ref[...], tmp_ref[pair], preferred_element_type=F32)
        here = step_at * block + 2 * pair
        wanted = [jnp.where(row_lane == here + e, prow_ref[...], 0.0) for e in range(2)]
        wanted = [
            jnp.broadcast_to(jnp.sum(w, axis=1, keepdims=True), (seqs, wide)) for w in wanted
        ]
        count = jnp.dot(
            pcol_ref[...], jnp.concatenate(wanted, axis=1).astype(BF16), preferred_element_type=F32
        )
        update = update / jnp.maximum(count, 1.0)
        for e in range(2):
            i = 2 * pair + e
            mid = (coup_ref[i].astype(F32) + update[:, e * wide : (e + 1) * wide]).astype(BF16)
            mid_ref[i] = mid
            normed_ref[i] = standardize_features(mid.astype(F32), 1).astype(BF16)


def front(chunk, chunks, place, lefts, rights, present_rows, coupling, w_tensor, present_cols, after):
    rows, cols, wide = coupling.shape
    seqs, width = present_rows.shape[0], lefts[0].shape[2]
    block = 8
    steps = rows // block // chunks
    tile = pl.BlockSpec((block, cols, wide), lambda i: (i, 0, 0))
    return pl.pallas_call(
        functools.partial(
            front_kernel,
            row_count=len(rights),
            col_count=len(lefts),
            first_block=chunk * steps,
        ),
        grid=(steps,),
        in_specs=[pl.BlockSpec(memory_space=pltpu.SMEM)]
        + [whole(part.shape) for part in lefts + rights]
        + [
            whole(present_rows.shape),
            pl.BlockSpec((block, cols, wide), lambda i: (i + chunk * steps, 0, 0)),
            whole(w_tensor.shape),
            whole(present_cols.shape),
        ]
        + anywhere(after),
        out_specs=[tile, tile],
        out_shape=[jax.ShapeDtypeStruct((rows // chunks, cols, wide), BF16)] * 2,
        scratch_shapes=[
            pltpu.VMEM((rows * seqs, LANES), F32),
            pltpu.VMEM((cols, width * seqs), BF16),
            pltpu.VMEM((block // 2, width * seqs, 2 * wide), BF16),
        ],
        compiler_params=params(),
        cost_estimate=LIGHT,
        name="front",
    )(place, *lefts, *rights, present_rows, coupling, w_tensor, present_cols, *after)


def exchange_rows(values):
    values = list(values)
    count = len(values)
    step = count // 2
    row = lax.broadcasted_iota(jnp.int32, values[0].shape, 0)
    size = values[0].shape[0]
    while step:
        width = 8 // count * step
        low = (row // width) % 2 == 0
        for m in range(count):
            if m & step == 0:
                one, two = values[m], values[m + step]
                values[m] = jnp.where(low, one, pltpu.roll(two, width, 0))
                values[m + step] = jnp.where(low, pltpu.roll(one, size - width, 0), two)
        step //= 2
    return values


def project_kernel(live_ref, normed_ref, cols_ref, weight_ref, *refs, first_row):
    out_ref, tmp_ref = refs[-2:]
    quads = normed_ref.shape[0] // QUAD
    dests, height, lanes = out_ref.shape
    each = height // quads
    count = dests * each
    unit = lanes // 12
    lane = lax.broadcasted_iota(jnp.int32, (1, lanes), 1)
    place = jnp.where(lane < 8 * unit, lane // (2 * unit), (lane - 8 * unit) // unit)
    group = max(1, 8 // each)
    for first in range(0, quads, group):
        values = []
        for m in range(first, first + group):
            packed = pack_rows([normed_ref[QUAD * m + a] for a in range(QUAD)])
            both = lax.dot_general(weight_ref[...], packed, NT, preferred_element_type=F32)
            row = first_row + (pl.program_id(0) * quads + m) * QUAD
            live = cols_ref[...]
            for a in range(QUAD):
                live = jnp.where(place == a, live * live_ref[row + a], live)
            values.append(sigmoid(both[:count]) * both[count:] * live)
        for b, value in enumerate(exchange_rows(values)):
            size = each * group
            for v in range(count // size):
                tmp_ref[v * group + b, first * each : first * each + size] = value[
                    v * size : (v + 1) * size
                ]
    out_ref[...] = tmp_ref[...].astype(BF16)


def project(first_row, live_rows, normed, live_cols, weight, dests):
    rows, cols, wide = normed.shape
    each = weight.shape[0] // (2 * dests)
    quads = max(8, 16 // each)
    lanes = QUAD * cols
    total = rows // QUAD
    return pl.pallas_call(
        functools.partial(project_kernel, first_row=first_row),
        grid=(total // quads,),
        in_specs=[
            pl.BlockSpec(memory_space=pltpu.SMEM),
            pl.BlockSpec((quads * QUAD, cols, wide), lambda i: (i, 0, 0)),
            whole(live_cols.shape),
            whole(weight.shape),
        ],
        out_specs=pl.BlockSpec((dests, quads * each, lanes), lambda i: (0, i, 0)),
        out_shape=jax.ShapeDtypeStruct((dests, total * each, lanes), BF16),
        scratch_shapes=[pltpu.VMEM((dests, quads * each, lanes), F32)],
        compiler_params=params(),
        cost_estimate=LIGHT,
        name="project",
    )(live_rows, normed, live_cols, weight)


def logit_kernel(live_ref, normed_ref, weight_ref, out_ref, *, first_row):
    block = normed_ref.shape[0]
    for i in range(block):
        live = live_ref[first_row + pl.program_id(0) * block + i]
        out_ref[i] = lax.dot_general(
            weight_ref[...], normed_ref[i], NT, preferred_element_type=F32
        ) + MASK_PENALTY * (live - 1.0)


def logit(first_row, live_rows, normed, weight):
    rows, cols, wide = normed.shape
    block = 16
    heads = weight.shape[0]
    return pl.pallas_call(
        functools.partial(logit_kernel, first_row=first_row),
        grid=(rows // block,),
        in_specs=[
            pl.BlockSpec(memory_space=pltpu.SMEM),
            pl.BlockSpec((block, cols, wide), lambda i: (i, 0, 0)),
            whole(weight.shape),
        ],
        out_specs=pl.BlockSpec((block, heads, cols), lambda i: (i, 0, 0)),
        out_shape=jax.ShapeDtypeStruct((rows, heads, cols), F32),
        compiler_params=params(),
        cost_estimate=LIGHT,
        name="logit",
    )(live_rows, normed, weight)


def assemble_kernel(recv_ref, *refs, row_count, pos_count):
    left_ref, right_ref, flat_ref, rows_ref = refs[-4:]
    channel = pl.program_id(0)
    lanes = recv_ref.shape[2]
    each = left_ref.shape[2]
    stride = recv_ref.shape[1] // each
    groups = pos_count // 4
    tiles = lanes // LANES

    @pl.when(channel == 0)
    def _():
        for src in range(row_count * pos_count):
            value = recv_ref[src].astype(F32)
            for t in range(tiles):
                flat_ref[src, t] = value[:, t * LANES : (t + 1) * LANES]

    def block(row, group, index):
        packed = []
        for p in range(4):
            src = row * pos_count + group * 4 + p
            packed.append(
                [flat_ref[src, t, pl.ds(index, each, stride=stride), :] for t in range(tiles)]
            )
        return exchange_blocks(packed)

    for row in range(row_count):
        for group in range(groups):
            span = slice(group * lanes, (group + 1) * lanes)
            left = block(row, group, channel)
            right = block(row, group, channel + stride // 2)
            for a in range(QUAD):
                left_ref[0, row * QUAD + a, :, span] = jnp.concatenate(left[a], axis=1).astype(BF16)
                for t in range(tiles):
                    rows_ref[t, pl.ds(a, each, stride=QUAD), :] = right[a][t]
            for t in range(tiles):
                at = slice(group * lanes + t * LANES, group * lanes + (t + 1) * LANES)
                right_ref[0, row, 0, :, at] = rows_ref[t].astype(BF16)


def assemble(chunk, chunks, received, sides, row_count, pos_count, cols):
    sources, height, lanes = received.shape
    depth = pos_count * cols
    each = depth // (row_count * QUAD * chunks)
    channels = height // each // 2
    blocks = row_count * QUAD
    shapes = [
        (channels, blocks, each * chunks, depth),
        (channels, row_count, chunks, QUAD * each, depth),
    ]
    return pl.pallas_call(
        functools.partial(assemble_kernel, row_count=row_count, pos_count=pos_count),
        grid=(channels,),
        in_specs=[whole(received.shape)] + anywhere(sides),
        out_specs=[
            pl.BlockSpec((1, blocks, each, depth), lambda c: (c, 0, chunk, 0)),
            pl.BlockSpec((1, row_count, 1, QUAD * each, depth), lambda c: (c, 0, chunk, 0, 0)),
        ],
        out_shape=[jax.ShapeDtypeStruct(shape, BF16) for shape in shapes],
        input_output_aliases={1: 0, 2: 1} if sides else {},
        scratch_shapes=[
            pltpu.VMEM((sources, lanes // LANES, height, LANES), F32),
            pltpu.VMEM((lanes // LANES, QUAD * each, LANES), F32),
        ],
        compiler_params=params(),
        cost_estimate=LIGHT,
        name="assemble",
    )(received, *sides)


def multiply_kernel(left_ref, right_ref, *refs, pos_count):
    out_ref, tmp_ref = refs[-2:]
    channel = pl.program_id(0)
    channels = pl.num_programs(0)
    lanes = out_ref.shape[2]
    _, blocks, each, depth = left_ref.shape
    row_count = blocks // QUAD
    unit = lanes // 12
    stride = out_ref.shape[1] // each
    tiles = lanes // LANES
    for group in range(pos_count // 4):
        starts = [(group * 4 + p) * 3 * unit for p in range(4)]
        wanted = jnp.concatenate(
            [right_ref[0, start : start + 2 * unit] for start in starts]
            + [right_ref[0, start + 2 * unit : start + 3 * unit] for start in starts],
            axis=0,
        )
        for row in range(row_count):
            left = left_ref[0, row * QUAD : (row + 1) * QUAD].reshape(QUAD * each, depth)
            value = lax.dot_general(left, wanted, NT, preferred_element_type=F32)
            packed = [
                [
                    value[a * each : (a + 1) * each, t * LANES : (t + 1) * LANES]
                    for t in range(tiles)
                ]
                for a in range(QUAD)
            ]
            for p, part in enumerate(exchange_blocks(packed)):
                dest = row * pos_count + group * 4 + p
                for t in range(tiles):
                    tmp_ref[dest, t, pl.ds(channel, each, stride=stride), :] = part[t]

    @pl.when(channel == channels - 1)
    def _():
        for dest in range(row_count * pos_count):
            for t in range(tiles):
                out_ref[dest, :, t * LANES : (t + 1) * LANES] = tmp_ref[dest, t].astype(BF16)


def multiply(first, count, left, right, after, pos_count, cols):
    _, blocks, each, depth = left.shape
    lanes = QUAD * cols
    shape = (blocks // QUAD * pos_count, each * count, lanes)
    return pl.pallas_call(
        functools.partial(multiply_kernel, pos_count=pos_count),
        grid=(count,),
        in_specs=[
            pl.BlockSpec((1, blocks, each, depth), lambda c: (c + first, 0, 0, 0)),
            pl.BlockSpec((1, depth, depth), lambda c: (c + first, 0, 0)),
        ]
        + anywhere(after),
        out_specs=whole(shape),
        out_shape=jax.ShapeDtypeStruct(shape, BF16),
        scratch_shapes=[pltpu.VMEM((shape[0], lanes // LANES, shape[1], LANES), F32)],
        compiler_params=params(),
        cost_estimate=LIGHT,
        name="multiply",
    )(left, right, *after)


def finish_kernel(*refs, parts, chunks):
    products = refs[:parts]
    mids = refs[parts : parts + chunks]
    normeds = refs[parts + chunks : parts + 2 * chunks]
    gate_ref, weight_ref, out_ref = refs[parts + 2 * chunks : parts + 2 * chunks + 3]
    flat = refs[parts + 2 * chunks + 3 :]
    quads = out_ref.shape[0] // QUAD
    sources, _, lanes = products[0].shape
    tiles = range(lanes // LANES)
    for product, tmp in zip(products, flat):
        height = product.shape[1]
        for src in range(sources):
            value = product[src].astype(F32)
            for t in tiles:
                tmp[t, src * height : (src + 1) * height] = value[:, t * LANES : (t + 1) * LANES]

    def rows(mid_ref, normed_ref):
        for m in range(quads):
            pieces = []
            for product, tmp in zip(products, flat):
                height = product.shape[1]
                each = height // quads
                for k in range(each):
                    pieces.append(
                        jnp.concatenate(
                            [tmp[t, pl.ds(m * each + k, sources, stride=height), :] for t in tiles],
                            axis=1,
                        )
                    )
            normed = standardize_features(jnp.concatenate(pieces, axis=0), 0).astype(BF16)
            out = lax.dot_general(normed, weight_ref[...], TN, preferred_element_type=F32)
            for a, value in enumerate(unpack_rows(out)):
                i = QUAD * m + a
                gate = sigmoid(jnp.dot(normed_ref[i], gate_ref[...], preferred_element_type=F32))
                out_ref[i] = (mid_ref[i].astype(F32) + gate * value).astype(BF16)

    steps = pl.num_programs(0) // chunks
    for chunk in range(chunks):
        pl.when(pl.program_id(0) // steps == chunk)(
            functools.partial(rows, mids[chunk], normeds[chunk])
        )


def finish(products, mids, normeds, w_gate, w_final):
    rows, cols, wide = mids[0].shape
    chunks = len(mids)
    sources, _, lanes = products[0].shape
    total = rows * chunks // QUAD
    heights = [part.shape[1] // total for part in products]
    quads = max(8, 16 // min(heights))
    steps = rows // QUAD // quads

    def tile(chunk):
        return pl.BlockSpec(
            (quads * QUAD, cols, wide),
            lambda i: (jnp.clip(i - chunk * steps, 0, steps - 1), 0, 0),
        )

    tiles = [tile(chunk) for chunk in range(chunks)]
    return pl.pallas_call(
        functools.partial(finish_kernel, parts=len(products), chunks=chunks),
        grid=(total // quads,),
        in_specs=[
            pl.BlockSpec((sources, quads * each, lanes), lambda i: (0, i, 0)) for each in heights
        ]
        + tiles * 2
        + [whole(w_gate.shape), whole(w_final.shape)],
        out_specs=pl.BlockSpec((quads * QUAD, cols, wide), lambda i: (i, 0, 0)),
        out_shape=jax.ShapeDtypeStruct((rows * chunks, cols, wide), BF16),
        scratch_shapes=[
            pltpu.VMEM((lanes // LANES, sources * quads * each, LANES), F32) for each in heights
        ],
        compiler_params=params(),
        cost_estimate=LIGHT,
        name="finish",
    )(*products, *mids, *normeds, w_gate, w_final)


def chunk_sizes(channels):
    each = min(2, channels)
    return [each] * (channels // each)


def on_device(
    alignment_embedding,
    coupling_embedding,
    amino_validity,
    alignment_validity,
    alignment_matrix,
    tensor_final_matrix,
    coupling_logit_matrix,
    mean_final_matrix,
    trimul_matrices,
    trimul_final_matrix,
):
    seq_each, module_number, feature_count = alignment_embedding.shape
    rows, _, wide = coupling_embedding.shape
    row_count = lax.axis_size("row")
    pos_count = lax.axis_size("pos")
    col_count = 2 * pos_count
    row_index = lax.axis_index("row")
    half = lax.axis_index("half")
    col_index = half * pos_count + lax.axis_index("pos")
    seqs = seq_each * row_count
    active_entries = amino_validity.astype(F32)
    sequence_index = lax.broadcasted_iota(jnp.int32, alignment_validity.shape, 0)
    present_entries = (
        jnp.where(sequence_index == 0, F32(1.0), alignment_validity.astype(F32))
        * active_entries[None, :]
    )
    row_start = row_index * rows
    col_start = col_index * module_number
    present_rows = lax.dynamic_slice_in_dim(present_entries, row_start, rows, 1)
    present_cols = lax.dynamic_slice_in_dim(present_entries, col_start, module_number, 1)
    live_rows = lax.dynamic_slice_in_dim(active_entries, row_start, rows, 0)
    live_cols = lax.dynamic_slice_in_dim(active_entries, col_start, module_number, 0)

    own_start = (row_index * seq_each, col_start)
    present_own = lax.dynamic_slice(present_entries, own_start, (seq_each, module_number))
    own_normed = standardize_features(alignment_embedding.astype(F32), 2).astype(BF16)
    own_normed = own_normed.reshape(seq_each * module_number, feature_count)

    def project_msa(matrix):
        return jnp.dot(own_normed, matrix, preferred_element_type=F32).reshape(
            seq_each, module_number, -1
        )

    own_sides = project_msa(alignment_matrix[:, : 2 * TENSOR_FEATURES])
    own_sides = (own_sides * present_own[:, :, None]).astype(BF16)
    own_left = own_sides[:, :, :TENSOR_FEATURES]
    own_right = own_sides[:, :, TENSOR_FEATURES:]
    per_row = rows // module_number
    lefts = []
    for t in range(col_count):
        pairs = []
        for r in range(row_count):
            for q in range(col_count):
                to = (r * per_row + q % per_row - t) % col_count
                pairs.append((r * col_count + q, q // per_row * col_count + to))
        lefts.append(lax.ppermute(own_left, AXES, pairs))
    rights = [own_right]
    for t in range(1, row_count):
        pairs = [(r, (r - t) % row_count) for r in range(row_count)]
        rights.append(lax.ppermute(own_right, "row", pairs))

    w_tensor = tensor_final_matrix.reshape(TENSOR_FEATURES, TENSOR_FEATURES * wide)
    unit = module_number // 3
    live_packed = jnp.concatenate(
        [live_cols[: 2 * unit]] * QUAD + [live_cols[2 * unit :]] * QUAD
    )[None]
    devices = row_count * col_count
    channels = CTRI // devices
    w_kinds = trimul_matrices[:, : 4 * CTRI].T.reshape(2, 2, devices, channels, wide)
    w_sides = jnp.transpose(w_kinds, (1, 2, 0, 3, 4)).reshape(-1, wide)
    w_logit = coupling_logit_matrix.T

    def exchange(block):
        return lax.all_to_all(block, AXES, split_axis=0, concat_axis=0, tiled=True)

    shape_of = (row_count, col_count, module_number)
    row_chunks = rows // QUAD // 16
    mids, normeds, logits = [], [], []
    sent, sides = (), ()
    for chunk in range(row_chunks):
        mid, normed = front(
            chunk,
            row_chunks,
            jnp.stack([row_index, col_index]).astype(jnp.int32),
            lefts,
            rights,
            present_rows,
            coupling_embedding,
            w_tensor,
            present_cols.T.astype(BF16),
            sent,
        )
        first_row = chunk * (rows // row_chunks)
        block = project(first_row, live_rows, normed, live_packed, w_sides, devices)
        sent = (block,)
        sides = assemble(chunk, row_chunks, exchange(block), sides, *shape_of)
        logits.append(logit(first_row, live_rows, normed, w_logit))
        mids.append(mid)
        normeds.append(normed)

    values = project_msa(
        alignment_matrix[:, 2 * TENSOR_FEATURES : 2 * TENSOR_FEATURES + MEAN_GROUPS * GROUP_FEATURES]
    ).astype(BF16)
    sequence_gate = jax.nn.sigmoid(
        project_msa(alignment_matrix[:, 2 * TENSOR_FEATURES + MEAN_GROUPS * GROUP_FEATURES :])
    )
    logits_all = lax.all_gather(jnp.concatenate(logits, axis=0), "row", axis=0, tiled=True)
    values_all = lax.all_gather(values, ("half", "pos"), axis=1, tiled=True)

    left, right = sides
    right = right.reshape(channels, -1, right.shape[-1])
    returned, first, after = [], 0, ()
    for count in chunk_sizes(channels):
        product = multiply(first, count, left, right, after, *shape_of[1:])
        returned.append(exchange(product))
        after = (product,)
        first += count
    logits_all, values_all = fence([logits_all, values_all], after)
    top_all = jnp.max(logits_all, axis=0)
    expd = jnp.exp(logits_all - top_all[None])
    weights_all = (expd / jnp.sum(expd, axis=0)[None]).astype(BF16)
    value_all_heads = values_all.reshape(seq_each, -1, MEAN_GROUPS, GROUP_FEATURES)
    summed = jnp.einsum("jhi,sjhd->sihd", weights_all, value_all_heads, preferred_element_type=F32)
    head_averaged = summed.reshape(seq_each, module_number, MEAN_GROUPS * GROUP_FEATURES)
    gated_result = (sequence_gate * head_averaged).astype(BF16)
    blended_update = jnp.dot(
        gated_result.reshape(seq_each * module_number, -1),
        mean_final_matrix,
        preferred_element_type=F32,
    ).reshape(seq_each, module_number, -1)
    alignment_updated_embedding = (alignment_embedding.astype(F32) + blended_update).astype(BF16)

    w_final = jnp.transpose(trimul_final_matrix.reshape(devices, -1, wide), (1, 0, 2))
    pair_output = finish(
        returned, mids, normeds, trimul_matrices[:, 4 * CTRI :], w_final.reshape(-1, wide)
    )
    return (alignment_updated_embedding, pair_output)


def solution(mesh):
    rows, cols = mesh.devices.shape
    inner = Mesh(mesh.devices.reshape(rows, 2, cols // 2), AXES)
    tile = P("row", ("half", "pos"), None)
    in_specs = (tile, tile) + (P(),) * 8
    return jax.shard_map(
        on_device, mesh=inner, in_specs=in_specs, out_specs=(tile, tile), check_vma=False
    )
```

```python
import functools

import jax
import jax.numpy as jnp
from jax import lax
from jax.experimental import pallas as pl
from jax.experimental.pallas import tpu as pltpu
from jax.sharding import Mesh, PartitionSpec as P

TENSOR_FEATURES = 32
MEAN_GROUPS = 8
GROUP_FEATURES = 32
CTRI = 128

EPS = 1e-05
MASK_PENALTY = 10000.0
QUAD = 4
LANES = 128
MIB = 1024 * 1024
AXES = ("row", "half", "pos")
GROUP = ("row", "pos")
F32 = jnp.float32
BF16 = jnp.bfloat16
NT = (((1,), (1,)), ((), ()))
TN = (((0,), (0,)), ((), ()))


def standardize_features(values_in, axis):
    centre = values_in - jnp.mean(values_in, axis=axis, keepdims=True)
    spread = jnp.mean(centre * centre, axis=axis, keepdims=True)
    return centre * lax.rsqrt(spread + EPS)


def sigmoid(x):
    return 0.5 * jnp.tanh(0.5 * x) + 0.5


def params():
    return pltpu.CompilerParams(
        vmem_limit_bytes=60 * MIB, dimension_semantics=("arbitrary",)
    )


LIGHT = pl.CostEstimate(flops=1000, bytes_accessed=1000, transcendentals=0)


def whole(shape):
    zeros = (0,) * len(shape)
    return pl.BlockSpec(shape, lambda *_: zeros, pipeline_mode=pl.Buffered(1))


def anywhere(after):
    return [pl.BlockSpec(memory_space=pl.ANY)] * len(after)


def fence(values, after):
    return pl.pallas_call(
        lambda *refs: None,
        in_specs=anywhere(values) + anywhere(after),
        out_specs=anywhere(values),
        out_shape=[jax.ShapeDtypeStruct(v.shape, v.dtype) for v in values],
        input_output_aliases={i: i for i in range(len(values))},
        compiler_params=pltpu.CompilerParams(vmem_limit_bytes=60 * MIB),
        cost_estimate=LIGHT,
        name="fence",
    )(*values, *after)


def pack_rows(rows):
    unit = rows[0].shape[0] // 3
    return jnp.concatenate([r[: 2 * unit] for r in rows] + [r[2 * unit :] for r in rows], axis=0)


def unpack_rows(packed):
    unit = packed.shape[0] // 12
    return [
        jnp.concatenate(
            [
                packed[2 * unit * a : 2 * unit * (a + 1)],
                packed[8 * unit + unit * a : 8 * unit + unit * (a + 1)],
            ],
            axis=0,
        )
        for a in range(QUAD)
    ]


def swap_blocks(first, second, width, lane):
    low = (lane // width) % 2 == 0
    size = first.shape[1]
    return (
        jnp.where(low, first, pltpu.roll(second, width, 1)),
        jnp.where(low, pltpu.roll(first, size - width, 1), second),
    )


def exchange_blocks(packed):
    part = packed
    unit = LANES // 4
    lane = lax.broadcasted_iota(jnp.int32, part[0][0].shape, 1)
    out = [[None] * 3 for _ in range(4)]
    for pair in range(2):
        one, two = part[2 * pair], part[2 * pair + 1]
        for t in range(2):
            out[2 * t][pair], out[2 * t + 1][pair] = swap_blocks(one[t], two[t], 2 * unit, lane)
    u0, u2 = swap_blocks(part[0][2], part[2][2], 2 * unit, lane)
    u1, u3 = swap_blocks(part[1][2], part[3][2], 2 * unit, lane)
    out[0][2], out[1][2] = swap_blocks(u0, u1, unit, lane)
    out[2][2], out[3][2] = swap_blocks(u2, u3, unit, lane)
    return out


def front_kernel(place_ref, *refs, row_count, col_count, first_block):
    lefts, rights = refs[:col_count], refs[col_count : col_count + row_count]
    refs = refs[col_count + row_count :]
    prow_ref, coup_ref, weight_ref, pcol_ref = refs[:4]
    sides_ref, right_ref, tmp_ref = refs[-3:]
    mid_ref, normed_ref = refs[-5:-3]
    step_at = pl.program_id(0) + first_block
    block, cols, wide = coup_ref.shape
    seq_each, _, width = lefts[0].shape
    seqs = seq_each * row_count
    per_row = col_count // row_count

    @pl.when(pl.program_id(0) == 0)
    def _():
        for t, part in enumerate(lefts):
            index = lax.rem(t + place_ref[1], col_count)
            first = lax.rem(index, per_row) * (cols * seqs) + index // per_row * seq_each
            for k in range(seq_each):
                sides_ref[pl.ds(first + k, cols, stride=seqs), 0:width] = part[k].astype(F32)
        right = jnp.zeros(right_ref.shape, F32)
        feature = lax.broadcasted_iota(jnp.int32, (width, width * seqs), 0)
        target = lax.broadcasted_iota(jnp.int32, (width, width * seqs), 1)
        for t, part in enumerate(rights):
            first = lax.rem(t + place_ref[0], row_count) * seq_each
            for k in range(seq_each):
                spread = (target == feature * seqs + (first + k)).astype(F32).astype(BF16)
                right += jnp.dot(part[k], spread, preferred_element_type=F32)
        right_ref[...] = right.astype(BF16)

    span = block * seqs
    start = pl.multiple_of(step_at * span, span)
    left = sides_ref[pl.ds(start, span), 0:width].astype(BF16)
    features = weight_ref.shape[1] // wide
    step = 4
    for low in range(0, features, step):
        part = jnp.dot(
            left, weight_ref[:, low * wide : (low + step) * wide], preferred_element_type=F32
        ).astype(BF16)
        for i in range(block):
            for d in range(step):
                tmp_ref[
                    i // 2,
                    (low + d) * seqs : (low + d + 1) * seqs,
                    (i % 2) * wide : (i % 2 + 1) * wide,
                ] = part[i * seqs : (i + 1) * seqs, d * wide : (d + 1) * wide]
    row_lane = lax.broadcasted_iota(jnp.int32, prow_ref.shape, 1)
    for pair in range(block // 2):
        update = jnp.dot(right_ref[...], tmp_ref[pair], preferred_element_type=F32)
        here = step_at * block + 2 * pair
        wanted = [jnp.where(row_lane == here + e, prow_ref[...], 0.0) for e in range(2)]
        wanted = [
            jnp.broadcast_to(jnp.sum(w, axis=1, keepdims=True), (seqs, wide)) for w in wanted
        ]
        count = jnp.dot(
            pcol_ref[...], jnp.concatenate(wanted, axis=1).astype(BF16), preferred_element_type=F32
        )
        update = update / jnp.maximum(count, 1.0)
        for e in range(2):
            i = 2 * pair + e
            mid = (coup_ref[i].astype(F32) + update[:, e * wide : (e + 1) * wide]).astype(BF16)
            mid_ref[i] = mid
            normed_ref[i] = standardize_features(mid.astype(F32), 1).astype(BF16)


def front(chunk, chunks, place, lefts, rights, present_rows, coupling, w_tensor, present_cols, after):
    rows, cols, wide = coupling.shape
    seqs, width = present_rows.shape[0], lefts[0].shape[2]
    block = 8
    steps = rows // block // chunks
    tile = pl.BlockSpec((block, cols, wide), lambda i: (i, 0, 0))
    return pl.pallas_call(
        functools.partial(
            front_kernel,
            row_count=len(rights),
            col_count=len(lefts),
            first_block=chunk * steps,
        ),
        grid=(steps,),
        in_specs=[pl.BlockSpec(memory_space=pltpu.SMEM)]
        + [whole(part.shape) for part in lefts + rights]
        + [
            whole(present_rows.shape),
            pl.BlockSpec((block, cols, wide), lambda i: (i + chunk * steps, 0, 0)),
            whole(w_tensor.shape),
            whole(present_cols.shape),
        ]
        + anywhere(after),
        out_specs=[tile, tile],
        out_shape=[jax.ShapeDtypeStruct((rows // chunks, cols, wide), BF16)] * 2,
        scratch_shapes=[
            pltpu.VMEM((rows * seqs, LANES), F32),
            pltpu.VMEM((cols, width * seqs), BF16),
            pltpu.VMEM((block // 2, width * seqs, 2 * wide), BF16),
        ],
        compiler_params=params(),
        cost_estimate=LIGHT,
        name="front",
    )(place, *lefts, *rights, present_rows, coupling, w_tensor, present_cols, *after)


def exchange_rows(values):
    values = list(values)
    count = len(values)
    step = count // 2
    row = lax.broadcasted_iota(jnp.int32, values[0].shape, 0)
    size = values[0].shape[0]
    while step:
        width = 8 // count * step
        low = (row // width) % 2 == 0
        for m in range(count):
            if m & step == 0:
                one, two = values[m], values[m + step]
                values[m] = jnp.where(low, one, pltpu.roll(two, width, 0))
                values[m + step] = jnp.where(low, pltpu.roll(one, size - width, 0), two)
        step //= 2
    return values


def project_kernel(live_ref, normed_ref, cols_ref, weight_ref, *refs, first_row):
    out_ref, tmp_ref = refs[-2:]
    quads = normed_ref.shape[0] // QUAD
    dests, height, lanes = out_ref.shape
    each = height // quads
    count = dests * each
    unit = lanes // 12
    lane = lax.broadcasted_iota(jnp.int32, (1, lanes), 1)
    place = jnp.where(lane < 8 * unit, lane // (2 * unit), (lane - 8 * unit) // unit)
    group = max(1, 8 // each)
    for first in range(0, quads, group):
        values = []
        for m in range(first, first + group):
            packed = pack_rows([normed_ref[QUAD * m + a] for a in range(QUAD)])
            both = lax.dot_general(weight_ref[...], packed, NT, preferred_element_type=F32)
            row = first_row + (pl.program_id(0) * quads + m) * QUAD
            live = cols_ref[...]
            for a in range(QUAD):
                live = jnp.where(place == a, live * live_ref[row + a], live)
            values.append(sigmoid(both[:count]) * both[count:] * live)
        for b, value in enumerate(exchange_rows(values)):
            size = each * group
            for v in range(count // size):
                tmp_ref[v * group + b, first * each : first * each + size] = value[
                    v * size : (v + 1) * size
                ]
    out_ref[...] = tmp_ref[...].astype(BF16)


def project(first_row, live_rows, normed, live_cols, weight, dests):
    rows, cols, wide = normed.shape
    each = weight.shape[0] // (2 * dests)
    quads = max(8, 16 // each)
    lanes = QUAD * cols
    total = rows // QUAD
    return pl.pallas_call(
        functools.partial(project_kernel, first_row=first_row),
        grid=(total // quads,),
        in_specs=[
            pl.BlockSpec(memory_space=pltpu.SMEM),
            pl.BlockSpec((quads * QUAD, cols, wide), lambda i: (i, 0, 0)),
            whole(live_cols.shape),
            whole(weight.shape),
        ],
        out_specs=pl.BlockSpec((dests, quads * each, lanes), lambda i: (0, i, 0)),
        out_shape=jax.ShapeDtypeStruct((dests, total * each, lanes), BF16),
        scratch_shapes=[pltpu.VMEM((dests, quads * each, lanes), F32)],
        compiler_params=params(),
        cost_estimate=LIGHT,
        name="project",
    )(live_rows, normed, live_cols, weight)


def logit_kernel(live_ref, normed_ref, weight_ref, *refs, first_row):
    out_ref = refs[-1]
    block = normed_ref.shape[0]
    for i in range(block):
        live = live_ref[first_row + pl.program_id(0) * block + i]
        out_ref[i] = lax.dot_general(
            weight_ref[...], normed_ref[i], NT, preferred_element_type=F32
        ) + MASK_PENALTY * (live - 1.0)


def logit(first_row, live_rows, normed, weight, after):
    rows, cols, wide = normed.shape
    block = 16
    heads = weight.shape[0]
    return pl.pallas_call(
        functools.partial(logit_kernel, first_row=first_row),
        grid=(rows // block,),
        in_specs=[
            pl.BlockSpec(memory_space=pltpu.SMEM),
            pl.BlockSpec((block, cols, wide), lambda i: (i, 0, 0)),
            whole(weight.shape),
        ]
        + anywhere(after),
        out_specs=pl.BlockSpec((block, heads, cols), lambda i: (i, 0, 0)),
        out_shape=jax.ShapeDtypeStruct((rows, heads, cols), F32),
        compiler_params=params(),
        cost_estimate=LIGHT,
        name="logit",
    )(live_rows, normed, weight, *after)


def assemble_kernel(recv_ref, *refs, row_count, pos_count, spans):
    left_ref, right_ref, flat_ref, rows_ref = refs[-4:]
    channel = pl.program_id(0)
    lanes = recv_ref.shape[2]
    each = left_ref.shape[2]
    height = recv_ref.shape[1] // spans
    stride = height // each
    groups = pos_count // 4
    tiles = lanes // LANES

    @pl.when(channel == 0)
    def _():
        for src in range(row_count * pos_count):
            value = recv_ref[src].astype(F32)
            for t in range(tiles):
                flat_ref[src, t] = value[:, t * LANES : (t + 1) * LANES]

    def block(row, group, index):
        packed = []
        index = index + group // groups * height
        for p in range(4):
            src = row * pos_count + group % groups * 4 + p
            packed.append(
                [flat_ref[src, t, pl.ds(index, each, stride=stride), :] for t in range(tiles)]
            )
        return exchange_blocks(packed)

    for row in range(row_count):
        for group in range(groups * spans):
            span = slice(group * lanes, (group + 1) * lanes)
            left = block(row, group, channel)
            right = block(row, group, channel + stride // 2)
            for a in range(QUAD):
                left_ref[0, row * QUAD + a, :, span] = jnp.concatenate(left[a], axis=1).astype(BF16)
                for t in range(tiles):
                    rows_ref[t, pl.ds(a, each, stride=QUAD), :] = right[a][t]
            for t in range(tiles):
                at = slice(group * lanes + t * LANES, group * lanes + (t + 1) * LANES)
                right_ref[0, row, 0, :, at] = rows_ref[t].astype(BF16)


def assemble(chunk, chunks, spans, received, sides, after, row_count, pos_count, cols):
    sources, height, lanes = received.shape
    depth = spans * pos_count * cols
    each = depth // (row_count * QUAD * chunks)
    channels = height // spans // each // 2
    blocks = row_count * QUAD
    shapes = [
        (channels, blocks, each * chunks, depth),
        (channels, row_count, chunks, QUAD * each, depth),
    ]
    return pl.pallas_call(
        functools.partial(
            assemble_kernel, row_count=row_count, pos_count=pos_count, spans=spans
        ),
        grid=(channels,),
        in_specs=[whole(received.shape)] + anywhere(sides) + anywhere(after),
        out_specs=[
            pl.BlockSpec((1, blocks, each, depth), lambda c: (c, 0, chunk, 0)),
            pl.BlockSpec((1, row_count, 1, QUAD * each, depth), lambda c: (c, 0, chunk, 0, 0)),
        ],
        out_shape=[jax.ShapeDtypeStruct(shape, BF16) for shape in shapes],
        input_output_aliases={1: 0, 2: 1} if sides else {},
        scratch_shapes=[
            pltpu.VMEM((sources, lanes // LANES, height, LANES), F32),
            pltpu.VMEM((lanes // LANES, QUAD * each, LANES), F32),
        ],
        compiler_params=params(),
        cost_estimate=LIGHT,
        name="assemble",
    )(received, *sides, *after)


def multiply_kernel(left_ref, right_ref, *refs, pos_count):
    out_ref, tmp_ref = refs[-2:]
    channel = pl.program_id(0)
    channels = pl.num_programs(0)
    lanes = out_ref.shape[2]
    _, blocks, each, depth = left_ref.shape
    row_count = blocks // QUAD
    unit = lanes // 12
    stride = out_ref.shape[1] // each
    tiles = lanes // LANES
    for group in range(pos_count // 4):
        starts = [(group * 4 + p) * 3 * unit for p in range(4)]
        wanted = jnp.concatenate(
            [right_ref[0, start : start + 2 * unit] for start in starts]
            + [right_ref[0, start + 2 * unit : start + 3 * unit] for start in starts],
            axis=0,
        )
        for row in range(row_count):
            left = left_ref[0, row * QUAD : (row + 1) * QUAD].reshape(QUAD * each, depth)
            value = lax.dot_general(left, wanted, NT, preferred_element_type=F32)
            packed = [
                [
                    value[a * each : (a + 1) * each, t * LANES : (t + 1) * LANES]
                    for t in range(tiles)
                ]
                for a in range(QUAD)
            ]
            for p, part in enumerate(exchange_blocks(packed)):
                dest = row * pos_count + group * 4 + p
                for t in range(tiles):
                    tmp_ref[dest, t, pl.ds(channel, each, stride=stride), :] = part[t]

    @pl.when(channel == channels - 1)
    def _():
        for dest in range(row_count * pos_count):
            for t in range(tiles):
                out_ref[dest, :, t * LANES : (t + 1) * LANES] = tmp_ref[dest, t].astype(BF16)


def multiply(left, right, after, pos_count, cols):
    count, blocks, each, depth = left.shape
    lanes = QUAD * cols
    shape = (blocks // QUAD * pos_count, each * count, lanes)
    return pl.pallas_call(
        functools.partial(multiply_kernel, pos_count=pos_count),
        grid=(count,),
        in_specs=[
            pl.BlockSpec((1, blocks, each, depth), lambda c: (c, 0, 0, 0)),
            pl.BlockSpec((1, depth, depth), lambda c: (c, 0, 0)),
        ]
        + anywhere(after),
        out_specs=whole(shape),
        out_shape=jax.ShapeDtypeStruct(shape, BF16),
        scratch_shapes=[pltpu.VMEM((shape[0], lanes // LANES, shape[1], LANES), F32)],
        compiler_params=params(),
        cost_estimate=LIGHT,
        name="multiply",
    )(left, right, *after)


def assemble_half_kernel(half_ref, *refs, row_count, pos_count, parts):
    recvs = refs[:parts]
    left_ref, own_ref, send_ref, flat_ref, right_ref = refs[-5:]
    channel = pl.program_id(0)
    lanes = recvs[0].shape[2]
    unit = lanes // 12
    cols = 3 * unit
    each = send_ref.shape[1] // (row_count * QUAD)
    stride = sum(recv.shape[1] for recv in recvs) // each
    groups = pos_count // 4
    tiles = lanes // LANES
    per_row = each * QUAD // cols

    @pl.when(channel == 0)
    def _():
        for src in range(row_count * pos_count):
            start = 0
            for recv in recvs:
                value = recv[src].astype(F32)
                end = start + recv.shape[1]
                for t in range(tiles):
                    flat_ref[src, t, start:end] = value[:, t * LANES : (t + 1) * LANES]
                start = end

    def block(row, group, index):
        packed = []
        for p in range(4):
            src = row * pos_count + group * 4 + p
            packed.append(
                [flat_ref[src, t, pl.ds(index, each, stride=stride), :] for t in range(tiles)]
            )
        return exchange_blocks(packed)

    for row in range(row_count):
        for group in range(groups):
            span = slice(group * lanes, (group + 1) * lanes)
            left = block(row, group, channel)
            for a in range(QUAD):
                start = (row * QUAD + a) * each
                left_ref[0, start : start + each, span] = jnp.concatenate(left[a], axis=1).astype(
                    BF16
                )
            right = block(row, group, channel + stride // 2)
            for a in range(QUAD):
                for piece in range(per_row):
                    place = row * per_row + piece
                    base = (place // 4) * lanes
                    low = piece * (cols // QUAD)
                    mid = low + 2 * unit // QUAD
                    high = low + cols // QUAD
                    first = base + (place % 4) * 2 * unit + a
                    second = base + 8 * unit + (place % 4) * unit + a
                    for t in range(tiles):
                        value = right[a][t]
                        at = group * tiles + t
                        right_ref[at, pl.ds(first, mid - low, stride=QUAD), :] = value[low:mid]
                        right_ref[at, pl.ds(second, high - mid, stride=QUAD), :] = value[mid:high]
    width = pos_count * cols
    own = pl.multiple_of(half_ref[0] * width, width)
    other = pl.multiple_of((1 - half_ref[0]) * width, width)
    theirs = []
    for at in range(groups * tiles):
        span = slice(at * LANES, (at + 1) * LANES)
        own_ref[0, :, span] = right_ref[at, pl.ds(own, width), :].astype(BF16)
        theirs.append(right_ref[at, pl.ds(other, width), :].astype(BF16))
    theirs = jnp.concatenate(theirs, axis=1)
    for row in range(row_count):
        span = slice(row * QUAD * each, (row + 1) * QUAD * each)
        send_ref[0, span] = lax.dot_general(
            left_ref[0, span], theirs, NT, preferred_element_type=F32
        ).astype(BF16)


def assemble_half(half, received, row_count, pos_count, cols):
    sources, _, lanes = received[0].shape
    height = sum(part.shape[1] for part in received)
    each = (2 * pos_count * cols) // (row_count * QUAD)
    channels = height // each // 2
    depth = pos_count * cols
    rows = 2 * depth
    return pl.pallas_call(
        functools.partial(
            assemble_half_kernel, row_count=row_count, pos_count=pos_count, parts=len(received)
        ),
        grid=(channels,),
        in_specs=[pl.BlockSpec(memory_space=pltpu.SMEM)] + [whole(part.shape) for part in received],
        out_specs=[
            pl.BlockSpec((1, rows, depth), lambda c: (c, 0, 0)),
            pl.BlockSpec((1, depth, depth), lambda c: (c, 0, 0)),
            pl.BlockSpec((1, rows, depth), lambda c: (c, 0, 0)),
        ],
        out_shape=[
            jax.ShapeDtypeStruct((channels, rows, depth), BF16),
            jax.ShapeDtypeStruct((channels, depth, depth), BF16),
            jax.ShapeDtypeStruct((channels, rows, depth), BF16),
        ],
        scratch_shapes=[
            pltpu.VMEM((sources, lanes // LANES, height, LANES), F32),
            pltpu.VMEM((depth // LANES, rows, LANES), F32),
        ],
        compiler_params=params(),
        cost_estimate=LIGHT,
        name="assemble_half",
    )(half, *received)


def combine_kernel(left_ref, own_ref, recv_ref, *refs, row_count, pos_count):
    out_ref, tmp_ref = refs[-2:]
    channel = pl.program_id(0)
    channels = pl.num_programs(0)
    lanes = out_ref.shape[2]
    each = left_ref.shape[1] // (row_count * QUAD)
    stride = out_ref.shape[1] // each
    tiles = lanes // LANES
    for row in range(row_count):
        for group in range(pos_count // 4):
            cols = slice(group * lanes, (group + 1) * lanes)
            blocks = []
            for a in range(QUAD):
                span = slice((row * QUAD + a) * each, (row * QUAD + a + 1) * each)
                value = lax.dot_general(
                    left_ref[0, span], own_ref[0, cols], NT, preferred_element_type=F32
                )
                value = value + recv_ref[0, span, cols].astype(F32)
                blocks.append([value[:, t * LANES : (t + 1) * LANES] for t in range(tiles)])
            for p, value in enumerate(exchange_blocks(blocks)):
                dest = row * pos_count + group * 4 + p
                for t in range(tiles):
                    tmp_ref[dest, t, pl.ds(channel, each, stride=stride), :] = value[t]

    @pl.when(channel == channels - 1)
    def _():
        for dest in range(row_count * pos_count):
            for t in range(tiles):
                out_ref[dest, :, t * LANES : (t + 1) * LANES] = tmp_ref[dest, t].astype(BF16)


def combine(left, own, received, after, row_count, pos_count, cols):
    channels, rows, depth = left.shape
    each = rows // (row_count * QUAD)
    shape = (row_count * pos_count, each * channels, QUAD * cols)
    return pl.pallas_call(
        functools.partial(combine_kernel, row_count=row_count, pos_count=pos_count),
        grid=(channels,),
        in_specs=[
            pl.BlockSpec((1, rows, depth), lambda c: (c, 0, 0)),
            pl.BlockSpec((1, depth, depth), lambda c: (c, 0, 0)),
            pl.BlockSpec((1, rows, depth), lambda c: (c, 0, 0)),
        ]
        + anywhere(after),
        out_specs=whole(shape),
        out_shape=jax.ShapeDtypeStruct(shape, BF16),
        scratch_shapes=[pltpu.VMEM((shape[0], shape[2] // LANES, shape[1], LANES), F32)],
        compiler_params=params(),
        cost_estimate=LIGHT,
        name="combine",
    )(left, own, received, *after)


def merge_kernel(*refs, parts, slots):
    pieces, (out_ref, sems) = refs[:parts], refs[-2:]
    copies = []
    for index, (piece, slot) in enumerate(zip(pieces, slots)):
        height = piece.shape[1]
        place = out_ref.at[:, pl.ds(slot * height, height), :]
        copies.append(pltpu.make_async_copy(piece, place, sems.at[index]))
    for copy in copies:
        copy.start()
    for copy in copies:
        copy.wait()


def merge(pieces, slots, count, into):
    sources, height, lanes = pieces[0].shape
    return pl.pallas_call(
        functools.partial(merge_kernel, parts=len(pieces), slots=slots),
        in_specs=anywhere(pieces) + anywhere(into),
        out_specs=pl.BlockSpec(memory_space=pl.ANY),
        out_shape=jax.ShapeDtypeStruct((sources, height * count, lanes), BF16),
        input_output_aliases={len(pieces): 0} if into else {},
        scratch_shapes=[pltpu.SemaphoreType.DMA((len(pieces),))],
        compiler_params=pltpu.CompilerParams(vmem_limit_bytes=60 * MIB),
        cost_estimate=LIGHT,
        name="merge",
    )(*pieces, *into)


def finish_kernel(*refs, parts, chunks):
    products = refs[:parts]
    mids = refs[parts : parts + chunks]
    normeds = refs[parts + chunks : parts + 2 * chunks]
    gate_ref, weight_ref, out_ref = refs[parts + 2 * chunks : parts + 2 * chunks + 3]
    flat = refs[parts + 2 * chunks + 3 :]
    quads = out_ref.shape[0] // QUAD
    lanes = products[0].shape[2]
    tiles = range(lanes // LANES)
    for product, tmp in zip(products, flat):
        sources, height, _ = product.shape
        for src in range(sources):
            value = product[src].astype(F32)
            for t in tiles:
                tmp[t, src * height : (src + 1) * height] = value[:, t * LANES : (t + 1) * LANES]

    def rows(mid_ref, normed_ref):
        for m in range(quads):
            pieces = []
            for product, tmp in zip(products, flat):
                sources, height, _ = product.shape
                each = height // quads
                for k in range(each):
                    pieces.append(
                        jnp.concatenate(
                            [tmp[t, pl.ds(m * each + k, sources, stride=height), :] for t in tiles],
                            axis=1,
                        )
                    )
            normed = standardize_features(jnp.concatenate(pieces, axis=0), 0).astype(BF16)
            out = lax.dot_general(normed, weight_ref[...], TN, preferred_element_type=F32)
            for a, value in enumerate(unpack_rows(out)):
                i = QUAD * m + a
                gate = sigmoid(jnp.dot(normed_ref[i], gate_ref[...], preferred_element_type=F32))
                out_ref[i] = (mid_ref[i].astype(F32) + gate * value).astype(BF16)

    steps = pl.num_programs(0) // chunks
    for chunk in range(chunks):
        pl.when(pl.program_id(0) // steps == chunk)(
            functools.partial(rows, mids[chunk], normeds[chunk])
        )


def finish(products, mids, normeds, w_gate, w_final):
    rows, cols, wide = mids[0].shape
    chunks = len(mids)
    lanes = products[0].shape[2]
    total = rows * chunks // QUAD
    heights = [part.shape[1] // total for part in products]
    quads = max(8, 16 // min(heights))
    steps = rows // QUAD // quads

    def tile(chunk):
        return pl.BlockSpec(
            (quads * QUAD, cols, wide),
            lambda i: (jnp.clip(i - chunk * steps, 0, steps - 1), 0, 0),
        )

    tiles = [tile(chunk) for chunk in range(chunks)]
    return pl.pallas_call(
        functools.partial(finish_kernel, parts=len(products), chunks=chunks),
        grid=(total // quads,),
        in_specs=[
            pl.BlockSpec((part.shape[0], quads * each, lanes), lambda i: (0, i, 0))
            for part, each in zip(products, heights)
        ]
        + tiles * 2
        + [whole(w_gate.shape), whole(w_final.shape)],
        out_specs=pl.BlockSpec((quads * QUAD, cols, wide), lambda i: (i, 0, 0)),
        out_shape=jax.ShapeDtypeStruct((rows * chunks, cols, wide), BF16),
        scratch_shapes=[
            pltpu.VMEM((lanes // LANES, part.shape[0] * quads * each, LANES), F32)
            for part, each in zip(products, heights)
        ],
        compiler_params=params(),
        cost_estimate=LIGHT,
        name="finish",
    )(*products, *mids, *normeds, w_gate, w_final)


def on_device(
    alignment_embedding,
    coupling_embedding,
    amino_validity,
    alignment_validity,
    alignment_matrix,
    tensor_final_matrix,
    coupling_logit_matrix,
    mean_final_matrix,
    trimul_matrices,
    trimul_final_matrix,
):
    seq_each, module_number, feature_count = alignment_embedding.shape
    rows, _, wide = coupling_embedding.shape
    row_count = lax.axis_size("row")
    pos_count = lax.axis_size("pos")
    col_count = 2 * pos_count
    row_index = lax.axis_index("row")
    half = lax.axis_index("half")
    col_index = half * pos_count + lax.axis_index("pos")
    seqs = seq_each * row_count
    active_entries = amino_validity.astype(F32)
    sequence_index = lax.broadcasted_iota(jnp.int32, alignment_validity.shape, 0)
    present_entries = (
        jnp.where(sequence_index == 0, F32(1.0), alignment_validity.astype(F32))
        * active_entries[None, :]
    )
    row_start = row_index * rows
    col_start = col_index * module_number
    present_rows = lax.dynamic_slice_in_dim(present_entries, row_start, rows, 1)
    present_cols = lax.dynamic_slice_in_dim(present_entries, col_start, module_number, 1)
    live_rows = lax.dynamic_slice_in_dim(active_entries, row_start, rows, 0)
    live_cols = lax.dynamic_slice_in_dim(active_entries, col_start, module_number, 0)

    own_start = (row_index * seq_each, col_start)
    present_own = lax.dynamic_slice(present_entries, own_start, (seq_each, module_number))
    own_normed = standardize_features(alignment_embedding.astype(F32), 2).astype(BF16)
    own_normed = own_normed.reshape(seq_each * module_number, feature_count)

    def project_msa(matrix):
        return jnp.dot(own_normed, matrix, preferred_element_type=F32).reshape(
            seq_each, module_number, -1
        )

    own_sides = project_msa(alignment_matrix[:, : 2 * TENSOR_FEATURES])
    own_sides = (own_sides * present_own[:, :, None]).astype(BF16)
    own_left = own_sides[:, :, :TENSOR_FEATURES]
    own_right = own_sides[:, :, TENSOR_FEATURES:]
    per_row = rows // module_number
    lefts = []
    for t in range(col_count):
        pairs = []
        for r in range(row_count):
            for q in range(col_count):
                to = (r * per_row + q % per_row - t) % col_count
                pairs.append((r * col_count + q, q // per_row * col_count + to))
        lefts.append(lax.ppermute(own_left, AXES, pairs))
    rights = [own_right]
    for t in range(1, row_count):
        pairs = [(r, (r - t) % row_count) for r in range(row_count)]
        rights.append(lax.ppermute(own_right, "row", pairs))

    w_tensor = tensor_final_matrix.reshape(TENSOR_FEATURES, TENSOR_FEATURES * wide)
    unit = module_number // 3
    live_packed = jnp.concatenate(
        [live_cols[: 2 * unit]] * QUAD + [live_cols[2 * unit :]] * QUAD
    )[None]
    devices = row_count * col_count
    w_kinds = trimul_matrices[:, : 4 * CTRI].T.reshape(2, 2, CTRI, wide)
    w_logit = coupling_logit_matrix.T

    def side_weights(part):
        return jnp.transpose(part, (1, 2, 0, 3, 4)).reshape(-1, wide)

    def exchange(block, axes):
        return lax.all_to_all(block, axes, split_axis=0, concat_axis=0, tiled=True)

    def front_rows(chunk, chunks, after):
        return front(
            chunk,
            chunks,
            jnp.stack([row_index, col_index]).astype(jnp.int32),
            lefts,
            rights,
            present_rows,
            coupling_embedding,
            w_tensor,
            present_cols.T.astype(BF16),
            after,
        )

    def project_rows(chunk, normed, weight, dests):
        first_row = chunk * normed.shape[0]
        return project(first_row, live_rows, normed, live_packed, weight, dests)

    group = devices // 2
    shape_of = (row_count, col_count, module_number)
    half_shape = (row_count, pos_count, module_number)
    mids, normeds, returned = [], [], []
    if CTRI // 2 % devices:
        row_chunks = rows // QUAD // 16
        sent, sides = (), ()
        weight = side_weights(w_kinds.reshape(2, 2, devices, -1, wide))
        for chunk in range(row_chunks):
            mid, normed = front_rows(chunk, row_chunks, sent)
            block = project_rows(chunk, normed, weight, devices)
            sent = (block,)
            sides = assemble(chunk, row_chunks, 1, exchange(block, AXES), sides, (), *shape_of)
            mids.append(mid)
            normeds.append(normed)
        left, right = sides
        right = right.reshape(right.shape[0], -1, right.shape[-1])
        last = multiply(left, right, (), *shape_of[1:])
        returned.append(exchange(last, AXES))
        after = (last,)
        orders = [(0, CTRI, devices)]
    else:
        cut = CTRI // 2
        row_chunks = 2
        w_half = side_weights(w_kinds[:, :, :cut].reshape(2, 2, group, -1, wide))
        w_both = w_kinds[:, :, cut:].reshape(2, 2, row_count, 2, pos_count, -1, wide)

        def half_weights(which):
            part = lax.dynamic_index_in_dim(w_both, which, 3, keepdims=False)
            return side_weights(part.reshape(2, 2, group, -1, wide))

        w_own, w_other = half_weights(half), half_weights(1 - half)
        swap = [(0, 1), (1, 0)]
        received, crossed, kept, ahead = [], [], [], ()
        for chunk in range(row_chunks):
            mid, normed = front_rows(chunk, row_chunks, ahead)
            mids.append(mid)
            normeds.append(normed)
            to_half = project_rows(chunk, normed, w_half, group)
            to_other = project_rows(chunk, normed, w_other, group)
            to_other, to_half, w_own = fence([to_other, to_half, w_own], received + crossed)
            crossed.append(lax.ppermute(to_other, "half", swap))
            received.append(exchange(to_half, GROUP))
            ahead = (w_own,)
            kept.append(project_rows(chunk, normed, w_own, group))
        half_scalar = half.astype(jnp.int32).reshape(1)
        left, own, theirs = assemble_half(half_scalar, received, *half_shape)
        merged = merge(kept + crossed[:-1], tuple(range(2 * row_chunks - 1)), 2 * row_chunks, ())
        merged = merge(crossed[-1:], (2 * row_chunks - 1,), 2 * row_chunks, (merged,))
        theirs, merged = fence([theirs, merged], ())
        partial = lax.ppermute(theirs, "half", swap)
        both = exchange(merged, GROUP)
        after = (both,)
        product = combine(left, own, partial, (both,), *half_shape)
        returned.append(exchange(product, GROUP))
        left, right = assemble(0, 1, 2, both, (), (product,), *half_shape)
        right = right.reshape(right.shape[0], -1, right.shape[-1])
        last = multiply(left, right, (), *shape_of[1:])
        returned.append(exchange(last, AXES))
        orders = [(0, cut, group), (cut, CTRI, devices)]
    logits = [
        logit(chunk * normed.shape[0], live_rows, normed, w_logit, after)
        for chunk, normed in enumerate(normeds)
    ]

    values = project_msa(
        alignment_matrix[:, 2 * TENSOR_FEATURES : 2 * TENSOR_FEATURES + MEAN_GROUPS * GROUP_FEATURES]
    ).astype(BF16)
    sequence_gate = jax.nn.sigmoid(
        project_msa(alignment_matrix[:, 2 * TENSOR_FEATURES + MEAN_GROUPS * GROUP_FEATURES :])
    )
    logits_all = lax.all_gather(jnp.concatenate(logits, axis=0), "row", axis=0, tiled=True)
    values_all = lax.all_gather(values, ("half", "pos"), axis=1, tiled=True)

    logits_all, values_all = fence([logits_all, values_all], (last,))
    top_all = jnp.max(logits_all, axis=0)
    expd = jnp.exp(logits_all - top_all[None])
    weights_all = (expd / jnp.sum(expd, axis=0)[None]).astype(BF16)
    value_all_heads = values_all.reshape(seq_each, -1, MEAN_GROUPS, GROUP_FEATURES)
    summed = jnp.einsum("jhi,sjhd->sihd", weights_all, value_all_heads, preferred_element_type=F32)
    head_averaged = summed.reshape(seq_each, module_number, MEAN_GROUPS * GROUP_FEATURES)
    gated_result = (sequence_gate * head_averaged).astype(BF16)
    blended_update = jnp.dot(
        gated_result.reshape(seq_each * module_number, -1),
        mean_final_matrix,
        preferred_element_type=F32,
    ).reshape(seq_each, module_number, -1)
    alignment_updated_embedding = (alignment_embedding.astype(F32) + blended_update).astype(BF16)

    w_final = jnp.concatenate(
        [
            jnp.transpose(
                trimul_final_matrix[low:high].reshape(sources, -1, wide), (1, 0, 2)
            ).reshape(-1, wide)
            for low, high, sources in orders
        ]
    )
    pair_output = finish(returned, mids, normeds, trimul_matrices[:, 4 * CTRI :], w_final)
    return (alignment_updated_embedding, pair_output)


def solution(mesh):
    rows, cols = mesh.devices.shape
    inner = Mesh(mesh.devices.reshape(rows, 2, cols // 2), AXES)
    tile = P("row", ("half", "pos"), None)
    in_specs = (tile, tile) + (P(),) * 8
    return jax.shard_map(
        on_device, mesh=inner, in_specs=in_specs, out_specs=(tile, tile), check_vma=False
    )
```

```python
import functools

import jax
import jax.numpy as jnp
from jax import lax
from jax.experimental import pallas as pl
from jax.experimental.pallas import tpu as pltpu
from jax.sharding import Mesh, PartitionSpec as P

TENSOR_FEATURES = 32
MEAN_GROUPS = 8
GROUP_FEATURES = 32
CTRI = 128

EPS = 1e-05
MASK_PENALTY = 10000.0
QUAD = 4
LANES = 128
MIB = 1024 * 1024
AXES = ("row", "half", "pos")
GROUP = ("row", "pos")
F32 = jnp.float32
BF16 = jnp.bfloat16
NT = (((1,), (1,)), ((), ()))
TN = (((0,), (0,)), ((), ()))


def standardize_features(values_in, axis):
    centre = values_in - jnp.mean(values_in, axis=axis, keepdims=True)
    spread = jnp.mean(centre * centre, axis=axis, keepdims=True)
    return centre * lax.rsqrt(spread + EPS)


def sigmoid(x):
    return 0.5 * jnp.tanh(0.5 * x) + 0.5


def params():
    return pltpu.CompilerParams(
        vmem_limit_bytes=60 * MIB, dimension_semantics=("arbitrary",)
    )


LIGHT = pl.CostEstimate(flops=1000, bytes_accessed=1000, transcendentals=0)


def whole(shape):
    zeros = (0,) * len(shape)
    return pl.BlockSpec(shape, lambda *_: zeros, pipeline_mode=pl.Buffered(1))


def anywhere(after):
    return [pl.BlockSpec(memory_space=pl.ANY)] * len(after)


def fence(values, after):
    return pl.pallas_call(
        lambda *refs: None,
        in_specs=anywhere(values) + anywhere(after),
        out_specs=anywhere(values),
        out_shape=[jax.ShapeDtypeStruct(v.shape, v.dtype) for v in values],
        input_output_aliases={i: i for i in range(len(values))},
        compiler_params=pltpu.CompilerParams(vmem_limit_bytes=60 * MIB),
        cost_estimate=LIGHT,
        name="fence",
    )(*values, *after)


def pack_rows(rows):
    unit = rows[0].shape[0] // 3
    return jnp.concatenate([r[: 2 * unit] for r in rows] + [r[2 * unit :] for r in rows], axis=0)


def unpack_rows(packed):
    unit = packed.shape[0] // 12
    return [
        jnp.concatenate(
            [
                packed[2 * unit * a : 2 * unit * (a + 1)],
                packed[8 * unit + unit * a : 8 * unit + unit * (a + 1)],
            ],
            axis=0,
        )
        for a in range(QUAD)
    ]


def swap_blocks(first, second, width, lane):
    low = (lane // width) % 2 == 0
    size = first.shape[1]
    return (
        jnp.where(low, first, pltpu.roll(second, width, 1)),
        jnp.where(low, pltpu.roll(first, size - width, 1), second),
    )


def exchange_blocks(packed):
    part = packed
    unit = LANES // 4
    lane = lax.broadcasted_iota(jnp.int32, part[0][0].shape, 1)
    out = [[None] * 3 for _ in range(4)]
    for pair in range(2):
        one, two = part[2 * pair], part[2 * pair + 1]
        for t in range(2):
            out[2 * t][pair], out[2 * t + 1][pair] = swap_blocks(one[t], two[t], 2 * unit, lane)
    u0, u2 = swap_blocks(part[0][2], part[2][2], 2 * unit, lane)
    u1, u3 = swap_blocks(part[1][2], part[3][2], 2 * unit, lane)
    out[0][2], out[1][2] = swap_blocks(u0, u1, unit, lane)
    out[2][2], out[3][2] = swap_blocks(u2, u3, unit, lane)
    return out


def front_kernel(place_ref, *refs, row_count, col_count, first_block):
    lefts, rights = refs[:col_count], refs[col_count : col_count + row_count]
    refs = refs[col_count + row_count :]
    prow_ref, coup_ref, weight_ref, pcol_ref = refs[:4]
    sides_ref, right_ref, tmp_ref = refs[-3:]
    mid_ref, normed_ref = refs[-5:-3]
    step_at = pl.program_id(0) + first_block
    block, cols, wide = coup_ref.shape
    seq_each, _, width = lefts[0].shape
    seqs = seq_each * row_count
    per_row = col_count // row_count

    @pl.when(pl.program_id(0) == 0)
    def _():
        for t, part in enumerate(lefts):
            index = lax.rem(t + place_ref[1], col_count)
            first = lax.rem(index, per_row) * (cols * seqs) + index // per_row * seq_each
            for k in range(seq_each):
                sides_ref[pl.ds(first + k, cols, stride=seqs), 0:width] = part[k].astype(F32)
        right = jnp.zeros(right_ref.shape, F32)
        feature = lax.broadcasted_iota(jnp.int32, (width, width * seqs), 0)
        target = lax.broadcasted_iota(jnp.int32, (width, width * seqs), 1)
        for t, part in enumerate(rights):
            first = lax.rem(t + place_ref[0], row_count) * seq_each
            for k in range(seq_each):
                spread = (target == feature * seqs + (first + k)).astype(F32).astype(BF16)
                right += jnp.dot(part[k], spread, preferred_element_type=F32)
        right_ref[...] = right.astype(BF16)

    span = block * seqs
    start = pl.multiple_of(step_at * span, span)
    left = sides_ref[pl.ds(start, span), 0:width].astype(BF16)
    features = weight_ref.shape[1] // wide
    step = 4
    for low in range(0, features, step):
        part = jnp.dot(
            left, weight_ref[:, low * wide : (low + step) * wide], preferred_element_type=F32
        ).astype(BF16)
        for i in range(block):
            for d in range(step):
                tmp_ref[
                    i // 2,
                    (low + d) * seqs : (low + d + 1) * seqs,
                    (i % 2) * wide : (i % 2 + 1) * wide,
                ] = part[i * seqs : (i + 1) * seqs, d * wide : (d + 1) * wide]
    row_lane = lax.broadcasted_iota(jnp.int32, prow_ref.shape, 1)
    for pair in range(block // 2):
        update = jnp.dot(right_ref[...], tmp_ref[pair], preferred_element_type=F32)
        here = step_at * block + 2 * pair
        wanted = [jnp.where(row_lane == here + e, prow_ref[...], 0.0) for e in range(2)]
        wanted = [
            jnp.broadcast_to(jnp.sum(w, axis=1, keepdims=True), (seqs, wide)) for w in wanted
        ]
        count = jnp.dot(
            pcol_ref[...], jnp.concatenate(wanted, axis=1).astype(BF16), preferred_element_type=F32
        )
        update = update / jnp.maximum(count, 1.0)
        for e in range(2):
            i = 2 * pair + e
            mid = (coup_ref[i].astype(F32) + update[:, e * wide : (e + 1) * wide]).astype(BF16)
            mid_ref[i] = mid
            normed_ref[i] = standardize_features(mid.astype(F32), 1).astype(BF16)


def front(chunk, chunks, place, lefts, rights, present_rows, coupling, w_tensor, present_cols, after):
    rows, cols, wide = coupling.shape
    seqs, width = present_rows.shape[0], lefts[0].shape[2]
    block = 8
    steps = rows // block // chunks
    tile = pl.BlockSpec((block, cols, wide), lambda i: (i, 0, 0))
    return pl.pallas_call(
        functools.partial(
            front_kernel,
            row_count=len(rights),
            col_count=len(lefts),
            first_block=chunk * steps,
        ),
        grid=(steps,),
        in_specs=[pl.BlockSpec(memory_space=pltpu.SMEM)]
        + [whole(part.shape) for part in lefts + rights]
        + [
            whole(present_rows.shape),
            pl.BlockSpec((block, cols, wide), lambda i: (i + chunk * steps, 0, 0)),
            whole(w_tensor.shape),
            whole(present_cols.shape),
        ]
        + anywhere(after),
        out_specs=[tile, tile],
        out_shape=[jax.ShapeDtypeStruct((rows // chunks, cols, wide), BF16)] * 2,
        scratch_shapes=[
            pltpu.VMEM((rows * seqs, LANES), F32),
            pltpu.VMEM((cols, width * seqs), BF16),
            pltpu.VMEM((block // 2, width * seqs, 2 * wide), BF16),
        ],
        compiler_params=params(),
        cost_estimate=LIGHT,
        name="front",
    )(place, *lefts, *rights, present_rows, coupling, w_tensor, present_cols, *after)


def exchange_rows(values):
    values = list(values)
    count = len(values)
    step = count // 2
    row = lax.broadcasted_iota(jnp.int32, values[0].shape, 0)
    size = values[0].shape[0]
    while step:
        width = 8 // count * step
        low = (row // width) % 2 == 0
        for m in range(count):
            if m & step == 0:
                one, two = values[m], values[m + step]
                values[m] = jnp.where(low, one, pltpu.roll(two, width, 0))
                values[m + step] = jnp.where(low, pltpu.roll(one, size - width, 0), two)
        step //= 2
    return values


def project_kernel(live_ref, normed_ref, cols_ref, weight_ref, *refs, first_row):
    out_ref, tmp_ref = refs[-2:]
    quads = normed_ref.shape[0] // QUAD
    dests, height, lanes = out_ref.shape
    each = height // quads
    count = dests * each
    unit = lanes // 12
    lane = lax.broadcasted_iota(jnp.int32, (1, lanes), 1)
    place = jnp.where(lane < 8 * unit, lane // (2 * unit), (lane - 8 * unit) // unit)
    group = max(1, 8 // each)
    for first in range(0, quads, group):
        values = []
        for m in range(first, first + group):
            packed = pack_rows([normed_ref[QUAD * m + a] for a in range(QUAD)])
            both = lax.dot_general(weight_ref[...], packed, NT, preferred_element_type=F32)
            row = first_row + (pl.program_id(0) * quads + m) * QUAD
            live = cols_ref[...]
            for a in range(QUAD):
                live = jnp.where(place == a, live * live_ref[row + a], live)
            values.append(sigmoid(both[:count]) * both[count:] * live)
        for b, value in enumerate(exchange_rows(values)):
            size = each * group
            for v in range(count // size):
                tmp_ref[v * group + b, first * each : first * each + size] = value[
                    v * size : (v + 1) * size
                ]
    out_ref[...] = tmp_ref[...].astype(BF16)


def project(first_row, live_rows, normed, live_cols, weight, dests):
    rows, cols, wide = normed.shape
    each = weight.shape[0] // (2 * dests)
    quads = max(8, 16 // each)
    lanes = QUAD * cols
    total = rows // QUAD
    return pl.pallas_call(
        functools.partial(project_kernel, first_row=first_row),
        grid=(total // quads,),
        in_specs=[
            pl.BlockSpec(memory_space=pltpu.SMEM),
            pl.BlockSpec((quads * QUAD, cols, wide), lambda i: (i, 0, 0)),
            whole(live_cols.shape),
            whole(weight.shape),
        ],
        out_specs=pl.BlockSpec((dests, quads * each, lanes), lambda i: (0, i, 0)),
        out_shape=jax.ShapeDtypeStruct((dests, total * each, lanes), BF16),
        scratch_shapes=[pltpu.VMEM((dests, quads * each, lanes), F32)],
        compiler_params=params(),
        cost_estimate=LIGHT,
        name="project",
    )(live_rows, normed, live_cols, weight)


def logit_kernel(live_ref, *refs, chunks):
    normeds, weight_ref, out_ref = refs[:chunks], refs[chunks], refs[-1]
    block = out_ref.shape[0]
    steps = pl.num_programs(0) // chunks

    def rows(normed_ref):
        for i in range(block):
            live = live_ref[pl.program_id(0) * block + i]
            out_ref[i] = lax.dot_general(
                weight_ref[...], normed_ref[i], NT, preferred_element_type=F32
            ) + MASK_PENALTY * (live - 1.0)

    for chunk in range(chunks):
        pl.when(pl.program_id(0) // steps == chunk)(functools.partial(rows, normeds[chunk]))


def chunk_tiles(shape, chunks, steps):
    def tile(chunk):
        return pl.BlockSpec(shape, lambda i: (jnp.clip(i - chunk * steps, 0, steps - 1), 0, 0))

    return [tile(chunk) for chunk in range(chunks)]


def logit(live_rows, normeds, weight, after):
    rows, cols, wide = normeds[0].shape
    block, chunks = 16, len(normeds)
    heads = weight.shape[0]
    return pl.pallas_call(
        functools.partial(logit_kernel, chunks=chunks),
        grid=(rows // block * chunks,),
        in_specs=[pl.BlockSpec(memory_space=pltpu.SMEM)]
        + chunk_tiles((block, cols, wide), chunks, rows // block)
        + [whole(weight.shape)]
        + anywhere(after),
        out_specs=pl.BlockSpec((block, heads, cols), lambda i: (i, 0, 0)),
        out_shape=jax.ShapeDtypeStruct((rows * chunks, heads, cols), F32),
        compiler_params=params(),
        cost_estimate=LIGHT,
        name="logit",
    )(live_rows, *normeds, weight, *after)


def assemble_kernel(recv_ref, *refs, row_count, pos_count, spans):
    left_ref, right_ref, flat_ref, rows_ref = refs[-4:]
    channel = pl.program_id(0)
    lanes = recv_ref.shape[2]
    each = left_ref.shape[2]
    height = recv_ref.shape[1] // spans
    stride = height // each
    groups = pos_count // 4
    tiles = lanes // LANES

    @pl.when(channel == 0)
    def _():
        for src in range(row_count * pos_count):
            value = recv_ref[src].astype(F32)
            for t in range(tiles):
                flat_ref[src, t] = value[:, t * LANES : (t + 1) * LANES]

    def block(row, group, index):
        packed = []
        index = index + group // groups * height
        for p in range(4):
            src = row * pos_count + group % groups * 4 + p
            packed.append(
                [flat_ref[src, t, pl.ds(index, each, stride=stride), :] for t in range(tiles)]
            )
        return exchange_blocks(packed)

    for row in range(row_count):
        for group in range(groups * spans):
            span = slice(group * lanes, (group + 1) * lanes)
            left = block(row, group, channel)
            right = block(row, group, channel + stride // 2)
            for a in range(QUAD):
                left_ref[0, row * QUAD + a, :, span] = jnp.concatenate(left[a], axis=1).astype(BF16)
                for t in range(tiles):
                    rows_ref[t, pl.ds(a, each, stride=QUAD), :] = right[a][t]
            for t in range(tiles):
                at = slice(group * lanes + t * LANES, group * lanes + (t + 1) * LANES)
                right_ref[0, row, 0, :, at] = rows_ref[t].astype(BF16)


def assemble(chunk, chunks, spans, received, sides, after, row_count, pos_count, cols):
    sources, height, lanes = received.shape
    depth = spans * pos_count * cols
    each = depth // (row_count * QUAD * chunks)
    channels = height // spans // each // 2
    blocks = row_count * QUAD
    shapes = [
        (channels, blocks, each * chunks, depth),
        (channels, row_count, chunks, QUAD * each, depth),
    ]
    return pl.pallas_call(
        functools.partial(
            assemble_kernel, row_count=row_count, pos_count=pos_count, spans=spans
        ),
        grid=(channels,),
        in_specs=[whole(received.shape)] + anywhere(sides) + anywhere(after),
        out_specs=[
            pl.BlockSpec((1, blocks, each, depth), lambda c: (c, 0, chunk, 0)),
            pl.BlockSpec((1, row_count, 1, QUAD * each, depth), lambda c: (c, 0, chunk, 0, 0)),
        ],
        out_shape=[jax.ShapeDtypeStruct(shape, BF16) for shape in shapes],
        input_output_aliases={1: 0, 2: 1} if sides else {},
        scratch_shapes=[
            pltpu.VMEM((sources, lanes // LANES, height, LANES), F32),
            pltpu.VMEM((lanes // LANES, QUAD * each, LANES), F32),
        ],
        compiler_params=params(),
        cost_estimate=LIGHT,
        name="assemble",
    )(received, *sides, *after)


def multiply_kernel(left_ref, right_ref, *refs, pos_count):
    out_ref, tmp_ref = refs[-2:]
    channel = pl.program_id(0)
    channels = pl.num_programs(0)
    lanes = out_ref.shape[2]
    _, blocks, each, depth = left_ref.shape
    row_count = blocks // QUAD
    unit = lanes // 12
    stride = out_ref.shape[1] // each
    tiles = lanes // LANES
    for group in range(pos_count // 4):
        starts = [(group * 4 + p) * 3 * unit for p in range(4)]
        wanted = jnp.concatenate(
            [right_ref[0, start : start + 2 * unit] for start in starts]
            + [right_ref[0, start + 2 * unit : start + 3 * unit] for start in starts],
            axis=0,
        )
        for row in range(row_count):
            left = left_ref[0, row * QUAD : (row + 1) * QUAD].reshape(QUAD * each, depth)
            value = lax.dot_general(left, wanted, NT, preferred_element_type=F32)
            packed = [
                [
                    value[a * each : (a + 1) * each, t * LANES : (t + 1) * LANES]
                    for t in range(tiles)
                ]
                for a in range(QUAD)
            ]
            for p, part in enumerate(exchange_blocks(packed)):
                dest = row * pos_count + group * 4 + p
                for t in range(tiles):
                    tmp_ref[dest, t, pl.ds(channel, each, stride=stride), :] = part[t]

    @pl.when(channel == channels - 1)
    def _():
        for dest in range(row_count * pos_count):
            for t in range(tiles):
                out_ref[dest, :, t * LANES : (t + 1) * LANES] = tmp_ref[dest, t].astype(BF16)


def multiply(left, right, after, pos_count, cols):
    count, blocks, each, depth = left.shape
    lanes = QUAD * cols
    shape = (blocks // QUAD * pos_count, each * count, lanes)
    return pl.pallas_call(
        functools.partial(multiply_kernel, pos_count=pos_count),
        grid=(count,),
        in_specs=[
            pl.BlockSpec((1, blocks, each, depth), lambda c: (c, 0, 0, 0)),
            pl.BlockSpec((1, depth, depth), lambda c: (c, 0, 0)),
        ]
        + anywhere(after),
        out_specs=whole(shape),
        out_shape=jax.ShapeDtypeStruct(shape, BF16),
        scratch_shapes=[pltpu.VMEM((shape[0], lanes // LANES, shape[1], LANES), F32)],
        compiler_params=params(),
        cost_estimate=LIGHT,
        name="multiply",
    )(left, right, *after)


def assemble_half_kernel(half_ref, *refs, row_count, pos_count, parts):
    recvs = refs[:parts]
    left_ref, own_ref, send_ref, flat_ref, right_ref = refs[-5:]
    channel = pl.program_id(0)
    lanes = recvs[0].shape[2]
    unit = lanes // 12
    cols = 3 * unit
    each = send_ref.shape[1] // (row_count * QUAD)
    stride = sum(recv.shape[1] for recv in recvs) // each
    groups = pos_count // 4
    tiles = lanes // LANES
    per_row = each * QUAD // cols

    @pl.when(channel == 0)
    def _():
        for src in range(row_count * pos_count):
            start = 0
            for recv in recvs:
                value = recv[src].astype(F32)
                end = start + recv.shape[1]
                for t in range(tiles):
                    flat_ref[src, t, start:end] = value[:, t * LANES : (t + 1) * LANES]
                start = end

    def block(row, group, index):
        packed = []
        for p in range(4):
            src = row * pos_count + group * 4 + p
            packed.append(
                [flat_ref[src, t, pl.ds(index, each, stride=stride), :] for t in range(tiles)]
            )
        return exchange_blocks(packed)

    for row in range(row_count):
        for group in range(groups):
            span = slice(group * lanes, (group + 1) * lanes)
            left = block(row, group, channel)
            for a in range(QUAD):
                start = (row * QUAD + a) * each
                left_ref[0, start : start + each, span] = jnp.concatenate(left[a], axis=1).astype(
                    BF16
                )
            right = block(row, group, channel + stride // 2)
            for a in range(QUAD):
                for piece in range(per_row):
                    place = row * per_row + piece
                    base = (place // 4) * lanes
                    low = piece * (cols // QUAD)
                    mid = low + 2 * unit // QUAD
                    high = low + cols // QUAD
                    first = base + (place % 4) * 2 * unit + a
                    second = base + 8 * unit + (place % 4) * unit + a
                    for t in range(tiles):
                        value = right[a][t]
                        at = group * tiles + t
                        right_ref[at, pl.ds(first, mid - low, stride=QUAD), :] = value[low:mid]
                        right_ref[at, pl.ds(second, high - mid, stride=QUAD), :] = value[mid:high]
    width = pos_count * cols
    own = pl.multiple_of(half_ref[0] * width, width)
    other = pl.multiple_of((1 - half_ref[0]) * width, width)
    theirs = []
    for at in range(groups * tiles):
        span = slice(at * LANES, (at + 1) * LANES)
        own_ref[0, :, span] = right_ref[at, pl.ds(own, width), :].astype(BF16)
        theirs.append(right_ref[at, pl.ds(other, width), :].astype(BF16))
    theirs = jnp.concatenate(theirs, axis=1)
    for row in range(row_count):
        span = slice(row * QUAD * each, (row + 1) * QUAD * each)
        send_ref[0, span] = lax.dot_general(
            left_ref[0, span], theirs, NT, preferred_element_type=F32
        ).astype(BF16)


def assemble_half(half, received, after, row_count, pos_count, cols):
    sources, _, lanes = received[0].shape
    height = sum(part.shape[1] for part in received)
    each = (2 * pos_count * cols) // (row_count * QUAD)
    channels = height // each // 2
    depth = pos_count * cols
    rows = 2 * depth
    return pl.pallas_call(
        functools.partial(
            assemble_half_kernel, row_count=row_count, pos_count=pos_count, parts=len(received)
        ),
        grid=(channels,),
        in_specs=[pl.BlockSpec(memory_space=pltpu.SMEM)]
        + [whole(part.shape) for part in received]
        + anywhere(after),
        out_specs=[
            pl.BlockSpec((1, rows, depth), lambda c: (c, 0, 0)),
            pl.BlockSpec((1, depth, depth), lambda c: (c, 0, 0)),
            pl.BlockSpec((1, rows, depth), lambda c: (c, 0, 0)),
        ],
        out_shape=[
            jax.ShapeDtypeStruct((channels, rows, depth), BF16),
            jax.ShapeDtypeStruct((channels, depth, depth), BF16),
            jax.ShapeDtypeStruct((channels, rows, depth), BF16),
        ],
        scratch_shapes=[
            pltpu.VMEM((sources, lanes // LANES, height, LANES), F32),
            pltpu.VMEM((depth // LANES, rows, LANES), F32),
        ],
        compiler_params=params(),
        cost_estimate=LIGHT,
        name="assemble_half",
    )(half, *received, *after)


def combine_kernel(left_ref, own_ref, recv_ref, *refs, row_count, pos_count):
    out_ref, tmp_ref = refs[-2:]
    channel = pl.program_id(0)
    channels = pl.num_programs(0)
    lanes = out_ref.shape[2]
    each = left_ref.shape[1] // (row_count * QUAD)
    stride = out_ref.shape[1] // each
    tiles = lanes // LANES
    for row in range(row_count):
        for group in range(pos_count // 4):
            cols = slice(group * lanes, (group + 1) * lanes)
            blocks = []
            for a in range(QUAD):
                span = slice((row * QUAD + a) * each, (row * QUAD + a + 1) * each)
                value = lax.dot_general(
                    left_ref[0, span], own_ref[0, cols], NT, preferred_element_type=F32
                )
                value = value + recv_ref[0, span, cols].astype(F32)
                blocks.append([value[:, t * LANES : (t + 1) * LANES] for t in range(tiles)])
            for p, value in enumerate(exchange_blocks(blocks)):
                dest = row * pos_count + group * 4 + p
                for t in range(tiles):
                    tmp_ref[dest, t, pl.ds(channel, each, stride=stride), :] = value[t]

    @pl.when(channel == channels - 1)
    def _():
        for dest in range(row_count * pos_count):
            for t in range(tiles):
                out_ref[dest, :, t * LANES : (t + 1) * LANES] = tmp_ref[dest, t].astype(BF16)


def combine(left, own, received, after, row_count, pos_count, cols):
    channels, rows, depth = left.shape
    each = rows // (row_count * QUAD)
    shape = (row_count * pos_count, each * channels, QUAD * cols)
    return pl.pallas_call(
        functools.partial(combine_kernel, row_count=row_count, pos_count=pos_count),
        grid=(channels,),
        in_specs=[
            pl.BlockSpec((1, rows, depth), lambda c: (c, 0, 0)),
            pl.BlockSpec((1, depth, depth), lambda c: (c, 0, 0)),
            pl.BlockSpec((1, rows, depth), lambda c: (c, 0, 0)),
        ]
        + anywhere(after),
        out_specs=whole(shape),
        out_shape=jax.ShapeDtypeStruct(shape, BF16),
        scratch_shapes=[pltpu.VMEM((shape[0], shape[2] // LANES, shape[1], LANES), F32)],
        compiler_params=params(),
        cost_estimate=LIGHT,
        name="combine",
    )(left, own, received, *after)


def merge_kernel(*refs, parts):
    for index, piece in enumerate(refs[:parts]):

        @pl.when(pl.program_id(0) == index)
        def _():
            refs[-1][...] = piece[...]


def merge(pieces, first, count, into):
    sources, height, lanes = pieces[0].shape
    return pl.pallas_call(
        functools.partial(merge_kernel, parts=len(pieces)),
        grid=(len(pieces),),
        in_specs=[whole(piece.shape) for piece in pieces] + anywhere(into),
        out_specs=pl.BlockSpec((sources, height, lanes), lambda i: (0, i + first, 0)),
        out_shape=jax.ShapeDtypeStruct((sources, height * count, lanes), BF16),
        input_output_aliases={len(pieces): 0} if into else {},
        compiler_params=params(),
        cost_estimate=LIGHT,
        name="merge",
    )(*pieces, *into)


def average_kernel(place_ref, *refs, row_count, col_count):
    logits, values = refs[:row_count], refs[row_count : row_count + col_count]
    gate_ref, align_ref, weight_ref, out_ref, exp_ref, value_ref = refs[row_count + col_count :]
    rows, heads, cols = logits[0].shape
    per_row = col_count // row_count
    for u, value in enumerate(values):
        value_ref[lax.rem(place_ref[1] + u, col_count)] = value[...]
    top = jnp.max(logits[0][...], axis=0)
    for block in logits[1:]:
        top = jnp.maximum(top, jnp.max(block[...], axis=0))
    total = jnp.zeros((heads, cols), F32)
    size = rows * heads
    for t, block in enumerate(logits):
        powers = jnp.exp(block[...] - top[None])
        total = total + jnp.sum(powers, axis=0)
        exp_ref[t * size : (t + 1) * size, 0:cols] = powers.reshape(size, cols)
    out = align_ref[...].astype(F32)
    for h in range(heads):
        summed = jnp.zeros(gate_ref.shape[1:], F32)
        for t in range(row_count):
            first = lax.rem(place_ref[0] + t, row_count) * per_row
            powers = exp_ref[pl.ds(t * size + h, rows, stride=heads), :][:, :cols]
            weights = (powers / total[h : h + 1]).astype(BF16)
            value = jnp.concatenate([value_ref[first + k, h] for k in range(per_row)], axis=0)
            summed += lax.dot_general(weights, value, TN, preferred_element_type=F32)
        gated = (gate_ref[h] * summed).astype(BF16)
        out += jnp.dot(gated, weight_ref[h], preferred_element_type=F32)
    out_ref[...] = out.astype(BF16)


def average(place, logits, values, gate, align, weight):
    rows, heads, cols = logits[0].shape
    operands = [*logits, *values, gate, align, weight]
    return pl.pallas_call(
        functools.partial(average_kernel, row_count=len(logits), col_count=len(values)),
        grid=(1,),
        in_specs=[pl.BlockSpec(memory_space=pltpu.SMEM)] + [whole(v.shape) for v in operands],
        out_specs=whole(align.shape),
        out_shape=jax.ShapeDtypeStruct(align.shape, BF16),
        scratch_shapes=[
            pltpu.VMEM((len(logits) * rows * heads, LANES), F32),
            pltpu.VMEM((len(values), *values[0].shape), BF16),
        ],
        compiler_params=params(),
        cost_estimate=LIGHT,
        name="average",
    )(place, *operands)


def finish_kernel(*refs, parts, chunks):
    products = refs[:parts]
    mids = refs[parts : parts + chunks]
    normeds = refs[parts + chunks : parts + 2 * chunks]
    gate_ref, weight_ref, out_ref = refs[parts + 2 * chunks : parts + 2 * chunks + 3]
    flat = refs[parts + 2 * chunks + 3 :]
    quads = out_ref.shape[0] // QUAD
    lanes = products[0].shape[2]
    tiles = range(lanes // LANES)
    for product, tmp in zip(products, flat):
        sources, height, _ = product.shape
        for src in range(sources):
            value = product[src].astype(F32)
            for t in tiles:
                tmp[t, src * height : (src + 1) * height] = value[:, t * LANES : (t + 1) * LANES]

    def rows(mid_ref, normed_ref):
        for m in range(quads):
            pieces = []
            for product, tmp in zip(products, flat):
                sources, height, _ = product.shape
                each = height // quads
                for k in range(each):
                    pieces.append(
                        jnp.concatenate(
                            [tmp[t, pl.ds(m * each + k, sources, stride=height), :] for t in tiles],
                            axis=1,
                        )
                    )
            normed = standardize_features(jnp.concatenate(pieces, axis=0), 0).astype(BF16)
            out = lax.dot_general(normed, weight_ref[...], TN, preferred_element_type=F32)
            for a, value in enumerate(unpack_rows(out)):
                i = QUAD * m + a
                gate = sigmoid(jnp.dot(normed_ref[i], gate_ref[...], preferred_element_type=F32))
                out_ref[i] = (mid_ref[i].astype(F32) + gate * value).astype(BF16)

    steps = pl.num_programs(0) // chunks
    for chunk in range(chunks):
        pl.when(pl.program_id(0) // steps == chunk)(
            functools.partial(rows, mids[chunk], normeds[chunk])
        )


def finish(products, mids, normeds, w_gate, w_final):
    rows, cols, wide = mids[0].shape
    chunks = len(mids)
    lanes = products[0].shape[2]
    total = rows * chunks // QUAD
    heights = [part.shape[1] // total for part in products]
    quads = max(8, 16 // min(heights))
    steps = rows // QUAD // quads

    tiles = chunk_tiles((quads * QUAD, cols, wide), chunks, steps)
    return pl.pallas_call(
        functools.partial(finish_kernel, parts=len(products), chunks=chunks),
        grid=(total // quads,),
        in_specs=[
            pl.BlockSpec((part.shape[0], quads * each, lanes), lambda i: (0, i, 0))
            for part, each in zip(products, heights)
        ]
        + tiles * 2
        + [whole(w_gate.shape), whole(w_final.shape)],
        out_specs=pl.BlockSpec((quads * QUAD, cols, wide), lambda i: (i, 0, 0)),
        out_shape=jax.ShapeDtypeStruct((rows * chunks, cols, wide), BF16),
        scratch_shapes=[
            pltpu.VMEM((lanes // LANES, part.shape[0] * quads * each, LANES), F32)
            for part, each in zip(products, heights)
        ],
        compiler_params=params(),
        cost_estimate=LIGHT,
        name="finish",
    )(*products, *mids, *normeds, w_gate, w_final)


def on_device(
    alignment_embedding,
    coupling_embedding,
    amino_validity,
    alignment_validity,
    alignment_matrix,
    tensor_final_matrix,
    coupling_logit_matrix,
    mean_final_matrix,
    trimul_matrices,
    trimul_final_matrix,
):
    seq_each, module_number, feature_count = alignment_embedding.shape
    rows, _, wide = coupling_embedding.shape
    row_count = lax.axis_size("row")
    pos_count = lax.axis_size("pos")
    col_count = 2 * pos_count
    row_index = lax.axis_index("row")
    half = lax.axis_index("half")
    col_index = half * pos_count + lax.axis_index("pos")
    seqs = seq_each * row_count
    active_entries = amino_validity.astype(F32)
    sequence_index = lax.broadcasted_iota(jnp.int32, alignment_validity.shape, 0)
    present_entries = (
        jnp.where(sequence_index == 0, F32(1.0), alignment_validity.astype(F32))
        * active_entries[None, :]
    )
    row_start = row_index * rows
    col_start = col_index * module_number
    present_rows = lax.dynamic_slice_in_dim(present_entries, row_start, rows, 1)
    present_cols = lax.dynamic_slice_in_dim(present_entries, col_start, module_number, 1)
    live_rows = lax.dynamic_slice_in_dim(active_entries, row_start, rows, 0)
    live_cols = lax.dynamic_slice_in_dim(active_entries, col_start, module_number, 0)

    own_start = (row_index * seq_each, col_start)
    present_own = lax.dynamic_slice(present_entries, own_start, (seq_each, module_number))
    own_normed = standardize_features(alignment_embedding.astype(F32), 2).astype(BF16)
    own_normed = own_normed.reshape(seq_each * module_number, feature_count)

    def project_msa(matrix):
        return jnp.dot(own_normed, matrix, preferred_element_type=F32).reshape(
            seq_each, module_number, -1
        )

    own_sides = project_msa(alignment_matrix[:, : 2 * TENSOR_FEATURES])
    own_sides = (own_sides * present_own[:, :, None]).astype(BF16)
    own_left = own_sides[:, :, :TENSOR_FEATURES]
    own_right = own_sides[:, :, TENSOR_FEATURES:]
    per_row = rows // module_number
    lefts = []
    for t in range(col_count):
        pairs = []
        for r in range(row_count):
            for q in range(col_count):
                to = (r * per_row + q % per_row - t) % col_count
                pairs.append((r * col_count + q, q // per_row * col_count + to))
        lefts.append(lax.ppermute(own_left, AXES, pairs))
    rights = [own_right]
    for t in range(1, row_count):
        pairs = [(r, (r - t) % row_count) for r in range(row_count)]
        rights.append(lax.ppermute(own_right, "row", pairs))

    w_tensor = tensor_final_matrix.reshape(TENSOR_FEATURES, TENSOR_FEATURES * wide)
    unit = module_number // 3
    live_packed = jnp.concatenate(
        [live_cols[: 2 * unit]] * QUAD + [live_cols[2 * unit :]] * QUAD
    )[None]
    devices = row_count * col_count
    w_kinds = trimul_matrices[:, : 4 * CTRI].T.reshape(2, 2, CTRI, wide)
    w_logit = coupling_logit_matrix.T

    def side_weights(part):
        return jnp.transpose(part, (1, 2, 0, 3, 4)).reshape(-1, wide)

    def exchange(block, axes):
        return lax.all_to_all(block, axes, split_axis=0, concat_axis=0, tiled=True)

    def front_rows(chunk, chunks, after):
        return front(
            chunk,
            chunks,
            place,
            lefts,
            rights,
            present_rows,
            coupling_embedding,
            w_tensor,
            present_cols.T.astype(BF16),
            after,
        )

    def project_rows(chunk, normed, weight, dests):
        first_row = chunk * normed.shape[0]
        return project(first_row, live_rows, normed, live_packed, weight, dests)

    place = jnp.stack([row_index, col_index]).astype(jnp.int32)

    def by_head(part):
        part = part.reshape(seq_each, module_number, MEAN_GROUPS, GROUP_FEATURES)
        return jnp.transpose(part, (2, 1, 0, 3)).reshape(MEAN_GROUPS, module_number, -1)

    first = 2 * TENSOR_FEATURES
    middle = first + MEAN_GROUPS * GROUP_FEATURES
    values = by_head(project_msa(alignment_matrix[:, first:middle]).astype(BF16))
    sequence_gate = by_head(jax.nn.sigmoid(project_msa(alignment_matrix[:, middle:])))
    w_mean = mean_final_matrix.reshape(MEAN_GROUPS, 1, GROUP_FEATURES, 1, feature_count)
    same = jnp.eye(seq_each, dtype=BF16).reshape(1, seq_each, 1, seq_each, 1)
    w_mean = (w_mean * same).reshape(
        MEAN_GROUPS, seq_each * GROUP_FEATURES, seq_each * feature_count
    )
    align = jnp.transpose(alignment_embedding, (1, 0, 2)).reshape(module_number, -1)

    def update_alignment(logits, values):
        logit_blocks, value_blocks = [logits], [values]
        for t in range(1, row_count):
            pairs = [(r, (r - t) % row_count) for r in range(row_count)]
            logit_blocks.append(lax.ppermute(logits, "row", pairs))
        for t in range(1, col_count):
            pairs = [(q, (q - t) % col_count) for q in range(col_count)]
            value_blocks.append(lax.ppermute(values, ("half", "pos"), pairs))
        return average(place, logit_blocks, value_blocks, sequence_gate, align, w_mean)

    group = devices // 2
    shape_of = (row_count, col_count, module_number)
    half_shape = (row_count, pos_count, module_number)
    mids, normeds, returned = [], [], []
    if CTRI // 2 % devices:
        row_chunks = rows // QUAD // 16
        sent, sides = (), ()
        weight = side_weights(w_kinds.reshape(2, 2, devices, -1, wide))
        for chunk in range(row_chunks):
            mid, normed = front_rows(chunk, row_chunks, sent)
            block = project_rows(chunk, normed, weight, devices)
            sent = (block,)
            sides = assemble(chunk, row_chunks, 1, exchange(block, AXES), sides, (), *shape_of)
            mids.append(mid)
            normeds.append(normed)
        left, right = sides
        right = right.reshape(right.shape[0], -1, right.shape[-1])
        last = multiply(left, right, (), *shape_of[1:])
        returned.append(exchange(last, AXES))
        logits = logit(live_rows, normeds, w_logit, ())
        orders = [(0, CTRI, devices)]
    else:
        cut = CTRI // 2
        row_chunks = 2
        w_half = side_weights(w_kinds[:, :, :cut].reshape(2, 2, group, -1, wide))
        w_both = w_kinds[:, :, cut:].reshape(2, 2, row_count, 2, pos_count, -1, wide)

        def half_weights(which):
            part = lax.dynamic_index_in_dim(w_both, which, 3, keepdims=False)
            return side_weights(part.reshape(2, 2, group, -1, wide))

        w_own, w_other = half_weights(half), half_weights(1 - half)
        swap = [(0, 1), (1, 0)]
        received, crossed, kept, ahead = [], [], [], ()
        for chunk in range(row_chunks):
            mid, normed = front_rows(chunk, row_chunks, ahead)
            mids.append(mid)
            normeds.append(normed)
            to_half = project_rows(chunk, normed, w_half, group)
            to_other = project_rows(chunk, normed, w_other, group)
            to_other, to_half, w_own = fence([to_other, to_half, w_own], received + crossed)
            crossed.append(lax.ppermute(to_other, "half", swap))
            received.append(exchange(to_half, GROUP))
            ahead = (w_own,)
            kept.append(project_rows(chunk, normed, w_own, group))
        half_scalar = half.astype(jnp.int32).reshape(1)
        logits = logit(live_rows, normeds, w_logit, tuple(kept))
        merged = merge(kept + crossed[:-1], 0, 2 * row_chunks, ())
        left, own, theirs = assemble_half(
            half_scalar, received, (logits, values, merged), *half_shape
        )
        merged = merge(crossed[-1:], 2 * row_chunks - 1, 2 * row_chunks, (merged,))
        theirs, merged = fence([theirs, merged], ())
        partial = lax.ppermute(theirs, "half", swap)
        both = exchange(merged, GROUP)
        product = combine(left, own, partial, (both,), *half_shape)
        returned.append(exchange(product, GROUP))
        left, right = assemble(0, 1, 2, both, (), (product,), *half_shape)
        right = right.reshape(right.shape[0], -1, right.shape[-1])
        last = multiply(left, right, (), *shape_of[1:])
        returned.append(exchange(last, AXES))
        orders = [(0, cut, group), (cut, CTRI, devices)]
    logits, values = fence([logits, values], (last,))
    aligned = update_alignment(logits, values)
    alignment_updated_embedding = jnp.transpose(
        aligned.reshape(module_number, seq_each, feature_count), (1, 0, 2)
    )
    w_final = jnp.concatenate(
        [
            jnp.transpose(
                trimul_final_matrix[low:high].reshape(sources, -1, wide), (1, 0, 2)
            ).reshape(-1, wide)
            for low, high, sources in orders
        ]
    )
    pair_output = finish(returned, mids, normeds, trimul_matrices[:, 4 * CTRI :], w_final)
    return (alignment_updated_embedding, pair_output)


def solution(mesh):
    rows, cols = mesh.devices.shape
    inner = Mesh(mesh.devices.reshape(rows, 2, cols // 2), AXES)
    tile = P("row", ("half", "pos"), None)
    in_specs = (tile, tile) + (P(),) * 8
    return jax.shard_map(
        on_device, mesh=inner, in_specs=in_specs, out_specs=(tile, tile), check_vma=False
    )
```

```python
import functools

import jax
import jax.numpy as jnp
from jax import lax
from jax.experimental import pallas as pl
from jax.experimental.pallas import tpu as pltpu
from jax.sharding import Mesh, PartitionSpec as P

TENSOR_FEATURES = 32
MEAN_GROUPS = 8
GROUP_FEATURES = 32
CTRI = 128

EPS = 1e-05
MASK_PENALTY = 10000.0
QUAD = 4
LANES = 128
MIB = 1024 * 1024
AXES = ("row", "half", "pos")
GROUP = ("row", "pos")
F32 = jnp.float32
BF16 = jnp.bfloat16
NT = (((1,), (1,)), ((), ()))
TN = (((0,), (0,)), ((), ()))


def standardize_features(values_in, axis):
    centre = values_in - jnp.mean(values_in, axis=axis, keepdims=True)
    spread = jnp.mean(centre * centre, axis=axis, keepdims=True)
    return centre * lax.rsqrt(spread + EPS)


def sigmoid(x):
    return 0.5 * jnp.tanh(0.5 * x) + 0.5


def params():
    return pltpu.CompilerParams(
        vmem_limit_bytes=60 * MIB, dimension_semantics=("arbitrary",)
    )


LIGHT = pl.CostEstimate(flops=1000, bytes_accessed=1000, transcendentals=0)


def whole(shape):
    zeros = (0,) * len(shape)
    return pl.BlockSpec(shape, lambda *_: zeros, pipeline_mode=pl.Buffered(1))


def anywhere(after):
    return [pl.BlockSpec(memory_space=pl.ANY)] * len(after)


def fence(values, after):
    return pl.pallas_call(
        lambda *refs: None,
        in_specs=anywhere(values) + anywhere(after),
        out_specs=anywhere(values),
        out_shape=[jax.ShapeDtypeStruct(v.shape, v.dtype) for v in values],
        input_output_aliases={i: i for i in range(len(values))},
        compiler_params=pltpu.CompilerParams(vmem_limit_bytes=60 * MIB),
        cost_estimate=LIGHT,
        name="fence",
    )(*values, *after)


def pack_rows(rows):
    unit = rows[0].shape[0] // 3
    return jnp.concatenate([r[: 2 * unit] for r in rows] + [r[2 * unit :] for r in rows], axis=0)


def unpack_rows(packed):
    unit = packed.shape[0] // 12
    return [
        jnp.concatenate(
            [
                packed[2 * unit * a : 2 * unit * (a + 1)],
                packed[8 * unit + unit * a : 8 * unit + unit * (a + 1)],
            ],
            axis=0,
        )
        for a in range(QUAD)
    ]


def swap_blocks(first, second, width, lane):
    low = (lane // width) % 2 == 0
    size = first.shape[1]
    return (
        jnp.where(low, first, pltpu.roll(second, width, 1)),
        jnp.where(low, pltpu.roll(first, size - width, 1), second),
    )


def exchange_blocks(packed):
    part = packed
    unit = LANES // 4
    lane = lax.broadcasted_iota(jnp.int32, part[0][0].shape, 1)
    out = [[None] * 3 for _ in range(4)]
    for pair in range(2):
        one, two = part[2 * pair], part[2 * pair + 1]
        for t in range(2):
            out[2 * t][pair], out[2 * t + 1][pair] = swap_blocks(one[t], two[t], 2 * unit, lane)
    u0, u2 = swap_blocks(part[0][2], part[2][2], 2 * unit, lane)
    u1, u3 = swap_blocks(part[1][2], part[3][2], 2 * unit, lane)
    out[0][2], out[1][2] = swap_blocks(u0, u1, unit, lane)
    out[2][2], out[3][2] = swap_blocks(u2, u3, unit, lane)
    return out


def front_kernel(place_ref, *refs, row_count, col_count, first_block):
    lefts, rights = refs[:col_count], refs[col_count : col_count + row_count]
    refs = refs[col_count + row_count :]
    prow_ref, coup_ref, weight_ref, pcol_ref = refs[:4]
    sides_ref, right_ref, tmp_ref = refs[-3:]
    mid_ref, normed_ref = refs[-5:-3]
    step_at = pl.program_id(0) + first_block
    block, cols, wide = coup_ref.shape
    seq_each, _, width = lefts[0].shape
    seqs = seq_each * row_count
    per_row = col_count // row_count

    @pl.when(pl.program_id(0) == 0)
    def _():
        for t, part in enumerate(lefts):
            index = lax.rem(t + place_ref[1], col_count)
            first = lax.rem(index, per_row) * (cols * seqs) + index // per_row * seq_each
            for k in range(seq_each):
                sides_ref[pl.ds(first + k, cols, stride=seqs), 0:width] = part[k].astype(F32)
        right = jnp.zeros(right_ref.shape, F32)
        feature = lax.broadcasted_iota(jnp.int32, (width, width * seqs), 0)
        target = lax.broadcasted_iota(jnp.int32, (width, width * seqs), 1)
        for t, part in enumerate(rights):
            first = lax.rem(t + place_ref[0], row_count) * seq_each
            for k in range(seq_each):
                spread = (target == feature * seqs + (first + k)).astype(F32).astype(BF16)
                right += jnp.dot(part[k], spread, preferred_element_type=F32)
        right_ref[...] = right.astype(BF16)

    span = block * seqs
    start = pl.multiple_of(step_at * span, span)
    left = sides_ref[pl.ds(start, span), 0:width].astype(BF16)
    features = weight_ref.shape[1] // wide
    step = 4
    for low in range(0, features, step):
        part = jnp.dot(
            left, weight_ref[:, low * wide : (low + step) * wide], preferred_element_type=F32
        ).astype(BF16)
        for i in range(block):
            for d in range(step):
                tmp_ref[
                    i // 2,
                    (low + d) * seqs : (low + d + 1) * seqs,
                    (i % 2) * wide : (i % 2 + 1) * wide,
                ] = part[i * seqs : (i + 1) * seqs, d * wide : (d + 1) * wide]
    row_lane = lax.broadcasted_iota(jnp.int32, prow_ref.shape, 1)
    for pair in range(block // 2):
        update = jnp.dot(right_ref[...], tmp_ref[pair], preferred_element_type=F32)
        here = step_at * block + 2 * pair
        wanted = [jnp.where(row_lane == here + e, prow_ref[...], 0.0) for e in range(2)]
        wanted = [
            jnp.broadcast_to(jnp.sum(w, axis=1, keepdims=True), (seqs, wide)) for w in wanted
        ]
        count = jnp.dot(
            pcol_ref[...], jnp.concatenate(wanted, axis=1).astype(BF16), preferred_element_type=F32
        )
        update = update / jnp.maximum(count, 1.0)
        for e in range(2):
            i = 2 * pair + e
            mid = (coup_ref[i].astype(F32) + update[:, e * wide : (e + 1) * wide]).astype(BF16)
            mid_ref[i] = mid
            normed_ref[i] = standardize_features(mid.astype(F32), 1).astype(BF16)


def front(chunk, chunks, place, lefts, rights, present_rows, coupling, w_tensor, present_cols, after):
    rows, cols, wide = coupling.shape
    seqs, width = present_rows.shape[0], lefts[0].shape[2]
    block = 8
    steps = rows // block // chunks
    tile = pl.BlockSpec((block, cols, wide), lambda i: (i, 0, 0))
    return pl.pallas_call(
        functools.partial(
            front_kernel,
            row_count=len(rights),
            col_count=len(lefts),
            first_block=chunk * steps,
        ),
        grid=(steps,),
        in_specs=[pl.BlockSpec(memory_space=pltpu.SMEM)]
        + [whole(part.shape) for part in lefts + rights]
        + [
            whole(present_rows.shape),
            pl.BlockSpec((block, cols, wide), lambda i: (i + chunk * steps, 0, 0)),
            whole(w_tensor.shape),
            whole(present_cols.shape),
        ]
        + anywhere(after),
        out_specs=[tile, tile],
        out_shape=[jax.ShapeDtypeStruct((rows // chunks, cols, wide), BF16)] * 2,
        scratch_shapes=[
            pltpu.VMEM((rows * seqs, LANES), F32),
            pltpu.VMEM((cols, width * seqs), BF16),
            pltpu.VMEM((block // 2, width * seqs, 2 * wide), BF16),
        ],
        compiler_params=params(),
        cost_estimate=LIGHT,
        name="front",
    )(place, *lefts, *rights, present_rows, coupling, w_tensor, present_cols, *after)


def exchange_rows(values):
    values = list(values)
    count = len(values)
    step = count // 2
    row = lax.broadcasted_iota(jnp.int32, values[0].shape, 0)
    size = values[0].shape[0]
    while step:
        width = 8 // count * step
        low = (row // width) % 2 == 0
        for m in range(count):
            if m & step == 0:
                one, two = values[m], values[m + step]
                values[m] = jnp.where(low, one, pltpu.roll(two, width, 0))
                values[m + step] = jnp.where(low, pltpu.roll(one, size - width, 0), two)
        step //= 2
    return values


def project_kernel(live_ref, normed_ref, cols_ref, weight_ref, *refs, first_row):
    out_ref, tmp_ref = refs[-2:]
    quads = normed_ref.shape[0] // QUAD
    dests, height, lanes = out_ref.shape
    each = height // quads
    count = dests * each
    unit = lanes // 12
    lane = lax.broadcasted_iota(jnp.int32, (1, lanes), 1)
    place = jnp.where(lane < 8 * unit, lane // (2 * unit), (lane - 8 * unit) // unit)
    group = max(1, 8 // each)
    for first in range(0, quads, group):
        values = []
        for m in range(first, first + group):
            packed = pack_rows([normed_ref[QUAD * m + a] for a in range(QUAD)])
            both = lax.dot_general(weight_ref[...], packed, NT, preferred_element_type=F32)
            row = first_row + (pl.program_id(0) * quads + m) * QUAD
            live = cols_ref[...]
            for a in range(QUAD):
                live = jnp.where(place == a, live * live_ref[row + a], live)
            values.append(sigmoid(both[:count]) * both[count:] * live)
        for b, value in enumerate(exchange_rows(values)):
            size = each * group
            for v in range(count // size):
                tmp_ref[v * group + b, first * each : first * each + size] = value[
                    v * size : (v + 1) * size
                ]
    out_ref[...] = tmp_ref[...].astype(BF16)


def project(first_row, live_rows, normed, live_cols, weight, dests):
    rows, cols, wide = normed.shape
    each = weight.shape[0] // (2 * dests)
    quads = max(8, 16 // each)
    lanes = QUAD * cols
    total = rows // QUAD
    return pl.pallas_call(
        functools.partial(project_kernel, first_row=first_row),
        grid=(total // quads,),
        in_specs=[
            pl.BlockSpec(memory_space=pltpu.SMEM),
            pl.BlockSpec((quads * QUAD, cols, wide), lambda i: (i, 0, 0)),
            whole(live_cols.shape),
            whole(weight.shape),
        ],
        out_specs=pl.BlockSpec((dests, quads * each, lanes), lambda i: (0, i, 0)),
        out_shape=jax.ShapeDtypeStruct((dests, total * each, lanes), BF16),
        scratch_shapes=[pltpu.VMEM((dests, quads * each, lanes), F32)],
        compiler_params=params(),
        cost_estimate=LIGHT,
        name="project",
    )(live_rows, normed, live_cols, weight)


def logit_kernel(live_ref, *refs, chunks):
    normeds, weight_ref, out_ref = refs[:chunks], refs[chunks], refs[-1]
    block = out_ref.shape[0]
    steps = pl.num_programs(0) // chunks

    def rows(normed_ref):
        for i in range(block):
            live = live_ref[pl.program_id(0) * block + i]
            out_ref[i] = lax.dot_general(
                weight_ref[...], normed_ref[i], NT, preferred_element_type=F32
            ) + MASK_PENALTY * (live - 1.0)

    for chunk in range(chunks):
        pl.when(pl.program_id(0) // steps == chunk)(functools.partial(rows, normeds[chunk]))


def chunk_tiles(shape, chunks, steps):
    def tile(chunk):
        return pl.BlockSpec(shape, lambda i: (jnp.clip(i - chunk * steps, 0, steps - 1), 0, 0))

    return [tile(chunk) for chunk in range(chunks)]


def logit(live_rows, normeds, weight, after):
    rows, cols, wide = normeds[0].shape
    block, chunks = 16, len(normeds)
    heads = weight.shape[0]
    return pl.pallas_call(
        functools.partial(logit_kernel, chunks=chunks),
        grid=(rows // block * chunks,),
        in_specs=[pl.BlockSpec(memory_space=pltpu.SMEM)]
        + chunk_tiles((block, cols, wide), chunks, rows // block)
        + [whole(weight.shape)]
        + anywhere(after),
        out_specs=pl.BlockSpec((block, heads, cols), lambda i: (i, 0, 0)),
        out_shape=jax.ShapeDtypeStruct((rows * chunks, heads, cols), F32),
        compiler_params=params(),
        cost_estimate=LIGHT,
        name="logit",
    )(live_rows, *normeds, weight, *after)


def assemble_kernel(recv_ref, *refs, row_count, pos_count, spans):
    left_ref, right_ref, flat_ref, rows_ref = refs[-4:]
    channel = pl.program_id(0)
    lanes = recv_ref.shape[2]
    each = left_ref.shape[2]
    height = recv_ref.shape[1] // spans
    stride = height // each
    groups = pos_count // 4
    tiles = lanes // LANES

    @pl.when(channel == 0)
    def _():
        for src in range(row_count * pos_count):
            value = recv_ref[src].astype(F32)
            for t in range(tiles):
                flat_ref[src, t] = value[:, t * LANES : (t + 1) * LANES]

    def block(row, group, index):
        packed = []
        index = index + group // groups * height
        for p in range(4):
            src = row * pos_count + group % groups * 4 + p
            packed.append(
                [flat_ref[src, t, pl.ds(index, each, stride=stride), :] for t in range(tiles)]
            )
        return exchange_blocks(packed)

    for row in range(row_count):
        for group in range(groups * spans):
            span = slice(group * lanes, (group + 1) * lanes)
            left = block(row, group, channel)
            right = block(row, group, channel + stride // 2)
            for a in range(QUAD):
                left_ref[0, row * QUAD + a, :, span] = jnp.concatenate(left[a], axis=1).astype(BF16)
                for t in range(tiles):
                    rows_ref[t, pl.ds(a, each, stride=QUAD), :] = right[a][t]
            for t in range(tiles):
                at = slice(group * lanes + t * LANES, group * lanes + (t + 1) * LANES)
                right_ref[0, row, 0, :, at] = rows_ref[t].astype(BF16)


def assemble(chunk, chunks, spans, received, sides, after, row_count, pos_count, cols):
    sources, height, lanes = received.shape
    depth = spans * pos_count * cols
    each = depth // (row_count * QUAD * chunks)
    channels = height // spans // each // 2
    blocks = row_count * QUAD
    shapes = [
        (channels, blocks, each * chunks, depth),
        (channels, row_count, chunks, QUAD * each, depth),
    ]
    return pl.pallas_call(
        functools.partial(
            assemble_kernel, row_count=row_count, pos_count=pos_count, spans=spans
        ),
        grid=(channels,),
        in_specs=[whole(received.shape)] + anywhere(sides) + anywhere(after),
        out_specs=[
            pl.BlockSpec((1, blocks, each, depth), lambda c: (c, 0, chunk, 0)),
            pl.BlockSpec((1, row_count, 1, QUAD * each, depth), lambda c: (c, 0, chunk, 0, 0)),
        ],
        out_shape=[jax.ShapeDtypeStruct(shape, BF16) for shape in shapes],
        input_output_aliases={1: 0, 2: 1} if sides else {},
        scratch_shapes=[
            pltpu.VMEM((sources, lanes // LANES, height, LANES), F32),
            pltpu.VMEM((lanes // LANES, QUAD * each, LANES), F32),
        ],
        compiler_params=params(),
        cost_estimate=LIGHT,
        name="assemble",
    )(received, *sides, *after)


def multiply_kernel(left_ref, right_ref, *refs, pos_count):
    out_ref, tmp_ref = refs[-2:]
    channel = pl.program_id(0)
    channels = pl.num_programs(0)
    lanes = out_ref.shape[2]
    _, blocks, each, depth = left_ref.shape
    row_count = blocks // QUAD
    unit = lanes // 12
    stride = out_ref.shape[1] // each
    tiles = lanes // LANES
    for group in range(pos_count // 4):
        starts = [(group * 4 + p) * 3 * unit for p in range(4)]
        wanted = jnp.concatenate(
            [right_ref[0, start : start + 2 * unit] for start in starts]
            + [right_ref[0, start + 2 * unit : start + 3 * unit] for start in starts],
            axis=0,
        )
        for row in range(row_count):
            left = left_ref[0, row * QUAD : (row + 1) * QUAD].reshape(QUAD * each, depth)
            value = lax.dot_general(left, wanted, NT, preferred_element_type=F32)
            packed = [
                [
                    value[a * each : (a + 1) * each, t * LANES : (t + 1) * LANES]
                    for t in range(tiles)
                ]
                for a in range(QUAD)
            ]
            for p, part in enumerate(exchange_blocks(packed)):
                dest = row * pos_count + group * 4 + p
                for t in range(tiles):
                    tmp_ref[dest, t, pl.ds(channel, each, stride=stride), :] = part[t]

    @pl.when(channel == channels - 1)
    def _():
        for dest in range(row_count * pos_count):
            for t in range(tiles):
                out_ref[dest, :, t * LANES : (t + 1) * LANES] = tmp_ref[dest, t].astype(BF16)


def multiply(left, right, after, pos_count, cols):
    count, blocks, each, depth = left.shape
    lanes = QUAD * cols
    shape = (blocks // QUAD * pos_count, each * count, lanes)
    return pl.pallas_call(
        functools.partial(multiply_kernel, pos_count=pos_count),
        grid=(count,),
        in_specs=[
            pl.BlockSpec((1, blocks, each, depth), lambda c: (c, 0, 0, 0)),
            pl.BlockSpec((1, depth, depth), lambda c: (c, 0, 0)),
        ]
        + anywhere(after),
        out_specs=whole(shape),
        out_shape=jax.ShapeDtypeStruct(shape, BF16),
        scratch_shapes=[pltpu.VMEM((shape[0], lanes // LANES, shape[1], LANES), F32)],
        compiler_params=params(),
        cost_estimate=LIGHT,
        name="multiply",
    )(left, right, *after)


def assemble_half_kernel(half_ref, *refs, row_count, pos_count, parts):
    recvs = refs[:parts]
    left_ref, own_ref, send_ref, flat_ref, right_ref = refs[-5:]
    channel = pl.program_id(0)
    lanes = recvs[0].shape[2]
    unit = lanes // 12
    cols = 3 * unit
    each = send_ref.shape[1] // (row_count * QUAD)
    stride = sum(recv.shape[1] for recv in recvs) // each
    groups = pos_count // 4
    tiles = lanes // LANES
    per_row = each * QUAD // cols

    @pl.when(channel == 0)
    def _():
        for src in range(row_count * pos_count):
            start = 0
            for recv in recvs:
                value = recv[src].astype(F32)
                end = start + recv.shape[1]
                for t in range(tiles):
                    flat_ref[src, t, start:end] = value[:, t * LANES : (t + 1) * LANES]
                start = end

    def block(row, group, index):
        packed = []
        for p in range(4):
            src = row * pos_count + group * 4 + p
            packed.append(
                [flat_ref[src, t, pl.ds(index, each, stride=stride), :] for t in range(tiles)]
            )
        return exchange_blocks(packed)

    for row in range(row_count):
        for group in range(groups):
            span = slice(group * lanes, (group + 1) * lanes)
            left = block(row, group, channel)
            for a in range(QUAD):
                start = (row * QUAD + a) * each
                left_ref[0, start : start + each, span] = jnp.concatenate(left[a], axis=1).astype(
                    BF16
                )
            right = block(row, group, channel + stride // 2)
            for a in range(QUAD):
                for piece in range(per_row):
                    place = row * per_row + piece
                    base = (place // 4) * lanes
                    low = piece * (cols // QUAD)
                    mid = low + 2 * unit // QUAD
                    high = low + cols // QUAD
                    first = base + (place % 4) * 2 * unit + a
                    second = base + 8 * unit + (place % 4) * unit + a
                    for t in range(tiles):
                        value = right[a][t]
                        at = group * tiles + t
                        right_ref[at, pl.ds(first, mid - low, stride=QUAD), :] = value[low:mid]
                        right_ref[at, pl.ds(second, high - mid, stride=QUAD), :] = value[mid:high]
    width = pos_count * cols
    own = pl.multiple_of(half_ref[0] * width, width)
    other = pl.multiple_of((1 - half_ref[0]) * width, width)
    theirs = []
    for at in range(groups * tiles):
        span = slice(at * LANES, (at + 1) * LANES)
        own_ref[0, :, span] = right_ref[at, pl.ds(own, width), :].astype(BF16)
        theirs.append(right_ref[at, pl.ds(other, width), :].astype(BF16))
    theirs = jnp.concatenate(theirs, axis=1)
    for row in range(row_count):
        span = slice(row * QUAD * each, (row + 1) * QUAD * each)
        send_ref[0, span] = lax.dot_general(
            left_ref[0, span], theirs, NT, preferred_element_type=F32
        ).astype(BF16)


def assemble_half(half, received, after, row_count, pos_count, cols):
    sources, _, lanes = received[0].shape
    height = sum(part.shape[1] for part in received)
    each = (2 * pos_count * cols) // (row_count * QUAD)
    channels = height // each // 2
    depth = pos_count * cols
    rows = 2 * depth
    return pl.pallas_call(
        functools.partial(
            assemble_half_kernel, row_count=row_count, pos_count=pos_count, parts=len(received)
        ),
        grid=(channels,),
        in_specs=[pl.BlockSpec(memory_space=pltpu.SMEM)]
        + [whole(part.shape) for part in received]
        + anywhere(after),
        out_specs=[
            pl.BlockSpec((1, rows, depth), lambda c: (c, 0, 0)),
            pl.BlockSpec((1, depth, depth), lambda c: (c, 0, 0)),
            pl.BlockSpec((1, rows, depth), lambda c: (c, 0, 0)),
        ],
        out_shape=[
            jax.ShapeDtypeStruct((channels, rows, depth), BF16),
            jax.ShapeDtypeStruct((channels, depth, depth), BF16),
            jax.ShapeDtypeStruct((channels, rows, depth), BF16),
        ],
        scratch_shapes=[
            pltpu.VMEM((sources, lanes // LANES, height, LANES), F32),
            pltpu.VMEM((depth // LANES, rows, LANES), F32),
        ],
        compiler_params=params(),
        cost_estimate=LIGHT,
        name="assemble_half",
    )(half, *received, *after)


def combine_kernel(left_ref, own_ref, recv_ref, *refs, row_count, pos_count):
    out_ref, tmp_ref = refs[-2:]
    channel = pl.program_id(0)
    channels = pl.num_programs(0)
    lanes = out_ref.shape[2]
    each = left_ref.shape[1] // (row_count * QUAD)
    stride = out_ref.shape[1] // each
    tiles = lanes // LANES
    for row in range(row_count):
        for group in range(pos_count // 4):
            cols = slice(group * lanes, (group + 1) * lanes)
            span = slice(row * QUAD * each, (row + 1) * QUAD * each)
            value = lax.dot_general(
                left_ref[0, span], own_ref[0, cols], NT, preferred_element_type=F32
            )
            value = value + recv_ref[0, span, cols].astype(F32)
            blocks = [
                [
                    value[a * each : (a + 1) * each, t * LANES : (t + 1) * LANES]
                    for t in range(tiles)
                ]
                for a in range(QUAD)
            ]
            for p, value in enumerate(exchange_blocks(blocks)):
                dest = row * pos_count + group * 4 + p
                for t in range(tiles):
                    tmp_ref[dest, t, pl.ds(channel, each, stride=stride), :] = value[t]

    @pl.when(channel == channels - 1)
    def _():
        for dest in range(row_count * pos_count):
            for t in range(tiles):
                out_ref[dest, :, t * LANES : (t + 1) * LANES] = tmp_ref[dest, t].astype(BF16)


def combine(left, own, received, after, row_count, pos_count, cols):
    channels, rows, depth = left.shape
    each = rows // (row_count * QUAD)
    shape = (row_count * pos_count, each * channels, QUAD * cols)
    return pl.pallas_call(
        functools.partial(combine_kernel, row_count=row_count, pos_count=pos_count),
        grid=(channels,),
        in_specs=[
            pl.BlockSpec((1, rows, depth), lambda c: (c, 0, 0)),
            pl.BlockSpec((1, depth, depth), lambda c: (c, 0, 0)),
            pl.BlockSpec((1, rows, depth), lambda c: (c, 0, 0)),
        ]
        + anywhere(after),
        out_specs=whole(shape),
        out_shape=jax.ShapeDtypeStruct(shape, BF16),
        scratch_shapes=[pltpu.VMEM((shape[0], shape[2] // LANES, shape[1], LANES), F32)],
        compiler_params=params(),
        cost_estimate=LIGHT,
        name="combine",
    )(left, own, received, *after)


def merge_kernel(*refs, parts):
    for index, piece in enumerate(refs[:parts]):

        @pl.when(pl.program_id(0) == index)
        def _():
            refs[-1][...] = piece[...]


def merge(pieces, first, count, into):
    sources, height, lanes = pieces[0].shape
    return pl.pallas_call(
        functools.partial(merge_kernel, parts=len(pieces)),
        grid=(len(pieces),),
        in_specs=[whole(piece.shape) for piece in pieces] + anywhere(into),
        out_specs=pl.BlockSpec((sources, height, lanes), lambda i: (0, i + first, 0)),
        out_shape=jax.ShapeDtypeStruct((sources, height * count, lanes), BF16),
        input_output_aliases={len(pieces): 0} if into else {},
        compiler_params=params(),
        cost_estimate=LIGHT,
        name="merge",
    )(*pieces, *into)


def average_kernel(place_ref, *refs, row_count, col_count):
    logits, values = refs[:row_count], refs[row_count : row_count + col_count]
    refs = refs[row_count + col_count :]
    gate_ref, align_ref, weight_ref, project_ref, out_ref, exp_ref, value_ref = refs
    rows, heads, cols = logits[0].shape
    wide = gate_ref.shape[2]
    per_row = col_count // row_count
    for u, value in enumerate(values):
        value_ref[lax.rem(place_ref[1] + u, col_count)] = jnp.dot(
            value[...], project_ref[...], preferred_element_type=F32
        ).astype(BF16)
    top = jnp.max(logits[0][...], axis=0)
    for block in logits[1:]:
        top = jnp.maximum(top, jnp.max(block[...], axis=0))
    total = jnp.zeros((heads, cols), F32)
    size = rows * heads
    for t, block in enumerate(logits):
        powers = jnp.exp(block[...] - top[None])
        total = total + jnp.sum(powers, axis=0)
        exp_ref[t * size : (t + 1) * size, 0:cols] = powers.reshape(size, cols)
    out = align_ref[...].astype(F32)
    for h in range(heads):
        summed = jnp.zeros(gate_ref.shape[1:], F32)
        for t in range(row_count):
            first = lax.rem(place_ref[0] + t, row_count) * per_row
            powers = exp_ref[pl.ds(t * size + h, rows, stride=heads), :][:, :cols]
            weights = (powers / total[h : h + 1]).astype(BF16)
            value = jnp.concatenate(
                [value_ref[first + k, :, h * wide : (h + 1) * wide] for k in range(per_row)], axis=0
            )
            summed += lax.dot_general(weights, value, TN, preferred_element_type=F32)
        gated = (gate_ref[h] * summed).astype(BF16)
        out += jnp.dot(gated, weight_ref[h], preferred_element_type=F32)
    out_ref[...] = out.astype(BF16)


def average(place, logits, values, gate, align, weight, w_value):
    rows, heads, cols = logits[0].shape
    operands = [*logits, *values, gate, align, weight, w_value]
    return pl.pallas_call(
        functools.partial(average_kernel, row_count=len(logits), col_count=len(values)),
        grid=(1,),
        in_specs=[pl.BlockSpec(memory_space=pltpu.SMEM)] + [whole(v.shape) for v in operands],
        out_specs=whole(align.shape),
        out_shape=jax.ShapeDtypeStruct(align.shape, BF16),
        scratch_shapes=[
            pltpu.VMEM((len(logits) * rows * heads, LANES), F32),
            pltpu.VMEM((len(values), cols, w_value.shape[1]), BF16),
        ],
        compiler_params=params(),
        cost_estimate=LIGHT,
        name="average",
    )(place, *operands)


def finish_kernel(*refs, parts, chunks):
    products = refs[:parts]
    mids = refs[parts : parts + chunks]
    normeds = refs[parts + chunks : parts + 2 * chunks]
    gate_ref, weight_ref, out_ref = refs[parts + 2 * chunks : parts + 2 * chunks + 3]
    flat = refs[parts + 2 * chunks + 3 :]
    quads = out_ref.shape[0] // QUAD
    lanes = products[0].shape[2]
    tiles = range(lanes // LANES)
    for product, tmp in zip(products, flat):
        sources, height, _ = product.shape
        for src in range(sources):
            value = product[src].astype(F32)
            for t in tiles:
                tmp[t, src * height : (src + 1) * height] = value[:, t * LANES : (t + 1) * LANES]

    def rows(mid_ref, normed_ref):
        for m in range(quads):
            pieces = []
            for product, tmp in zip(products, flat):
                sources, height, _ = product.shape
                each = height // quads
                for k in range(each):
                    pieces.append(
                        jnp.concatenate(
                            [tmp[t, pl.ds(m * each + k, sources, stride=height), :] for t in tiles],
                            axis=1,
                        )
                    )
            normed = standardize_features(jnp.concatenate(pieces, axis=0), 0).astype(BF16)
            out = lax.dot_general(normed, weight_ref[...], TN, preferred_element_type=F32)
            for a, value in enumerate(unpack_rows(out)):
                i = QUAD * m + a
                gate = sigmoid(jnp.dot(normed_ref[i], gate_ref[...], preferred_element_type=F32))
                out_ref[i] = (mid_ref[i].astype(F32) + gate * value).astype(BF16)

    steps = pl.num_programs(0) // chunks
    for chunk in range(chunks):
        pl.when(pl.program_id(0) // steps == chunk)(
            functools.partial(rows, mids[chunk], normeds[chunk])
        )


def finish(products, mids, normeds, w_gate, w_final):
    rows, cols, wide = mids[0].shape
    chunks = len(mids)
    lanes = products[0].shape[2]
    total = rows * chunks // QUAD
    heights = [part.shape[1] // total for part in products]
    quads = max(8, 16 // min(heights))
    steps = rows // QUAD // quads

    tiles = chunk_tiles((quads * QUAD, cols, wide), chunks, steps)
    return pl.pallas_call(
        functools.partial(finish_kernel, parts=len(products), chunks=chunks),
        grid=(total // quads,),
        in_specs=[
            pl.BlockSpec((part.shape[0], quads * each, lanes), lambda i: (0, i, 0))
            for part, each in zip(products, heights)
        ]
        + tiles * 2
        + [whole(w_gate.shape), whole(w_final.shape)],
        out_specs=pl.BlockSpec((quads * QUAD, cols, wide), lambda i: (i, 0, 0)),
        out_shape=jax.ShapeDtypeStruct((rows * chunks, cols, wide), BF16),
        scratch_shapes=[
            pltpu.VMEM((lanes // LANES, part.shape[0] * quads * each, LANES), F32)
            for part, each in zip(products, heights)
        ],
        compiler_params=params(),
        cost_estimate=LIGHT,
        name="finish",
    )(*products, *mids, *normeds, w_gate, w_final)


def on_device(
    alignment_embedding,
    coupling_embedding,
    amino_validity,
    alignment_validity,
    alignment_matrix,
    tensor_final_matrix,
    coupling_logit_matrix,
    mean_final_matrix,
    trimul_matrices,
    trimul_final_matrix,
):
    seq_each, module_number, feature_count = alignment_embedding.shape
    rows, _, wide = coupling_embedding.shape
    row_count = lax.axis_size("row")
    pos_count = lax.axis_size("pos")
    col_count = 2 * pos_count
    row_index = lax.axis_index("row")
    half = lax.axis_index("half")
    col_index = half * pos_count + lax.axis_index("pos")
    seqs = seq_each * row_count
    active_entries = amino_validity.astype(F32)
    sequence_index = lax.broadcasted_iota(jnp.int32, alignment_validity.shape, 0)
    present_entries = (
        jnp.where(sequence_index == 0, F32(1.0), alignment_validity.astype(F32))
        * active_entries[None, :]
    )
    row_start = row_index * rows
    col_start = col_index * module_number
    present_rows = lax.dynamic_slice_in_dim(present_entries, row_start, rows, 1)
    present_cols = lax.dynamic_slice_in_dim(present_entries, col_start, module_number, 1)
    live_rows = lax.dynamic_slice_in_dim(active_entries, row_start, rows, 0)
    live_cols = lax.dynamic_slice_in_dim(active_entries, col_start, module_number, 0)

    own_start = (row_index * seq_each, col_start)
    present_own = lax.dynamic_slice(present_entries, own_start, (seq_each, module_number))
    own_normed = standardize_features(alignment_embedding.astype(F32), 2).astype(BF16)
    own_normed = own_normed.reshape(seq_each * module_number, feature_count)

    def project_msa(matrix):
        return jnp.dot(own_normed, matrix, preferred_element_type=F32).reshape(
            seq_each, module_number, -1
        )

    own_sides = project_msa(alignment_matrix[:, : 2 * TENSOR_FEATURES])
    own_sides = (own_sides * present_own[:, :, None]).astype(BF16)
    own_left = own_sides[:, :, :TENSOR_FEATURES]
    own_right = own_sides[:, :, TENSOR_FEATURES:]
    per_row = rows // module_number
    lefts = []
    for t in range(col_count):
        pairs = []
        for r in range(row_count):
            for q in range(col_count):
                to = (r * per_row + q % per_row - t) % col_count
                pairs.append((r * col_count + q, q // per_row * col_count + to))
        lefts.append(lax.ppermute(own_left, AXES, pairs))
    rights = [own_right]
    for t in range(1, row_count):
        pairs = [(r, (r - t) % row_count) for r in range(row_count)]
        rights.append(lax.ppermute(own_right, "row", pairs))

    w_tensor = tensor_final_matrix.reshape(TENSOR_FEATURES, TENSOR_FEATURES * wide)
    unit = module_number // 3
    live_packed = jnp.concatenate(
        [live_cols[: 2 * unit]] * QUAD + [live_cols[2 * unit :]] * QUAD
    )[None]
    devices = row_count * col_count
    w_kinds = trimul_matrices[:, : 4 * CTRI].T.reshape(2, 2, CTRI, wide)
    w_logit = coupling_logit_matrix.T

    def side_weights(part):
        return jnp.transpose(part, (1, 2, 0, 3, 4)).reshape(-1, wide)

    def exchange(block, axes):
        return lax.all_to_all(block, axes, split_axis=0, concat_axis=0, tiled=True)

    def front_rows(chunk, chunks, after):
        return front(
            chunk,
            chunks,
            place,
            lefts,
            rights,
            present_rows,
            coupling_embedding,
            w_tensor,
            present_cols.T.astype(BF16),
            after,
        )

    def project_rows(chunk, normed, weight, dests):
        first_row = chunk * normed.shape[0]
        return project(first_row, live_rows, normed, live_packed, weight, dests)

    place = jnp.stack([row_index, col_index]).astype(jnp.int32)

    def by_head(part):
        part = part.reshape(seq_each, module_number, MEAN_GROUPS, GROUP_FEATURES)
        return jnp.transpose(part, (2, 1, 0, 3)).reshape(MEAN_GROUPS, module_number, -1)

    first = 2 * TENSOR_FEATURES
    middle = first + MEAN_GROUPS * GROUP_FEATURES
    w_value = alignment_matrix[:, first:middle].reshape(
        1, feature_count, MEAN_GROUPS, 1, GROUP_FEATURES
    )
    apart = jnp.eye(seq_each, dtype=BF16).reshape(seq_each, 1, 1, seq_each, 1)
    w_value = (w_value * apart).reshape(seq_each * feature_count, -1)
    own_rows = jnp.transpose(
        own_normed.reshape(seq_each, module_number, feature_count), (1, 0, 2)
    ).reshape(module_number, -1)
    sequence_gate = by_head(jax.nn.sigmoid(project_msa(alignment_matrix[:, middle:])))
    w_mean = mean_final_matrix.reshape(MEAN_GROUPS, 1, GROUP_FEATURES, 1, feature_count)
    same = jnp.eye(seq_each, dtype=BF16).reshape(1, seq_each, 1, seq_each, 1)
    w_mean = (w_mean * same).reshape(
        MEAN_GROUPS, seq_each * GROUP_FEATURES, seq_each * feature_count
    )
    align = jnp.transpose(alignment_embedding, (1, 0, 2)).reshape(module_number, -1)

    def blocks_of(own, axes, count):
        blocks = [own]
        for t in range(1, count):
            pairs = [(at, (at - t) % count) for at in range(count)]
            blocks.append(lax.ppermute(own, axes, pairs))
        return blocks

    group = devices // 2
    shape_of = (row_count, col_count, module_number)
    half_shape = (row_count, pos_count, module_number)
    mids, normeds, returned = [], [], []
    if CTRI // 2 % devices:
        row_chunks = rows // QUAD // 16
        sent, sides = (), ()
        weight = side_weights(w_kinds.reshape(2, 2, devices, -1, wide))
        for chunk in range(row_chunks):
            mid, normed = front_rows(chunk, row_chunks, sent)
            block = project_rows(chunk, normed, weight, devices)
            sent = (block,)
            sides = assemble(chunk, row_chunks, 1, exchange(block, AXES), sides, (), *shape_of)
            mids.append(mid)
            normeds.append(normed)
        left, right = sides
        right = right.reshape(right.shape[0], -1, right.shape[-1])
        last = multiply(left, right, (), *shape_of[1:])
        returned.append(exchange(last, AXES))
        logits = logit(live_rows, normeds, w_logit, ())
        (logits,) = fence([logits], (last,))
        logits = blocks_of(logits, "row", row_count)
        orders = [(0, CTRI, devices)]
    else:
        cut = CTRI // 2
        row_chunks = 2
        w_half = side_weights(w_kinds[:, :, :cut].reshape(2, 2, group, -1, wide))
        w_both = w_kinds[:, :, cut:].reshape(2, 2, row_count, 2, pos_count, -1, wide)

        def half_weights(which):
            part = lax.dynamic_index_in_dim(w_both, which, 3, keepdims=False)
            return side_weights(part.reshape(2, 2, group, -1, wide))

        w_own, w_other = half_weights(half), half_weights(1 - half)
        swap = [(0, 1), (1, 0)]
        received, crossed, kept, ahead = [], [], [], ()
        for chunk in range(row_chunks):
            mid, normed = front_rows(chunk, row_chunks, ahead)
            mids.append(mid)
            normeds.append(normed)
            to_half = project_rows(chunk, normed, w_half, group)
            to_other = project_rows(chunk, normed, w_other, group)
            to_other, to_half, w_own = fence([to_other, to_half, w_own], received + crossed)
            crossed.append(lax.ppermute(to_other, "half", swap))
            received.append(exchange(to_half, GROUP))
            ahead = (w_own,)
            kept.append(project_rows(chunk, normed, w_own, group))
        half_scalar = half.astype(jnp.int32).reshape(1)
        logits = logit(live_rows, normeds, w_logit, tuple(kept))
        merged = merge(kept + crossed[:-1], 0, 2 * row_chunks, ())
        left, own, theirs = assemble_half(
            half_scalar, received, (logits, merged), *half_shape
        )
        merged = merge(crossed[-1:], 2 * row_chunks - 1, 2 * row_chunks, (merged,))
        theirs, merged = fence([theirs, merged], ())
        partial = lax.ppermute(theirs, "half", swap)
        both = exchange(merged, GROUP)
        product = combine(left, own, partial, (both,), *half_shape)
        (logits,) = fence([logits], (product,))
        logits = blocks_of(logits, "row", row_count)
        returned.append(exchange(product, GROUP))
        left, right = assemble(0, 1, 2, both, (), (product,), *half_shape)
        right = right.reshape(right.shape[0], -1, right.shape[-1])
        last = multiply(left, right, tuple(logits[1:]), *shape_of[1:])
        returned.append(exchange(last, AXES))
        orders = [(0, cut, group), (cut, CTRI, devices)]
    (own_rows,) = fence([own_rows], (last,))
    values = blocks_of(own_rows, ("half", "pos"), col_count)
    aligned = average(place, logits, values, sequence_gate, align, w_mean, w_value)
    alignment_updated_embedding = jnp.transpose(
        aligned.reshape(module_number, seq_each, feature_count), (1, 0, 2)
    )
    w_final = jnp.concatenate(
        [
            jnp.transpose(
                trimul_final_matrix[low:high].reshape(sources, -1, wide), (1, 0, 2)
            ).reshape(-1, wide)
            for low, high, sources in orders
        ]
    )
    pair_output = finish(returned, mids, normeds, trimul_matrices[:, 4 * CTRI :], w_final)
    return (alignment_updated_embedding, pair_output)


def solution(mesh):
    rows, cols = mesh.devices.shape
    inner = Mesh(mesh.devices.reshape(rows, 2, cols // 2), AXES)
    tile = P("row", ("half", "pos"), None)
    in_specs = (tile, tile) + (P(),) * 8
    return jax.shard_map(
        on_device, mesh=inner, in_specs=in_specs, out_specs=(tile, tile), check_vma=False
    )
```

```python
import functools

import jax
import jax.numpy as jnp
from jax import lax
from jax.experimental import pallas as pl
from jax.experimental.pallas import tpu as pltpu
from jax.sharding import Mesh, PartitionSpec as P

TENSOR_FEATURES = 32
MEAN_GROUPS = 8
GROUP_FEATURES = 32
CTRI = 128

EPS = 1e-05
MASK_PENALTY = 10000.0
QUAD = 4
LANES = 128
MIB = 1024 * 1024
AXES = ("row", "half", "pos")
GROUP = ("row", "pos")
F32 = jnp.float32
BF16 = jnp.bfloat16
NT = (((1,), (1,)), ((), ()))
TN = (((0,), (0,)), ((), ()))


def standardize_features(values_in, axis):
    centre = values_in - jnp.mean(values_in, axis=axis, keepdims=True)
    spread = jnp.mean(centre * centre, axis=axis, keepdims=True)
    return centre * lax.rsqrt(spread + EPS)


def sigmoid(x):
    return 0.5 * jnp.tanh(0.5 * x) + 0.5


def params():
    return pltpu.CompilerParams(
        vmem_limit_bytes=60 * MIB, dimension_semantics=("arbitrary",)
    )


LIGHT = pl.CostEstimate(flops=1000, bytes_accessed=1000, transcendentals=0)


def whole(shape):
    zeros = (0,) * len(shape)
    return pl.BlockSpec(shape, lambda *_: zeros, pipeline_mode=pl.Buffered(1))


def anywhere(after):
    return [pl.BlockSpec(memory_space=pl.ANY)] * len(after)


def fence(values, after):
    return pl.pallas_call(
        lambda *refs: None,
        in_specs=anywhere(values) + anywhere(after),
        out_specs=anywhere(values),
        out_shape=[jax.ShapeDtypeStruct(v.shape, v.dtype) for v in values],
        input_output_aliases={i: i for i in range(len(values))},
        compiler_params=pltpu.CompilerParams(vmem_limit_bytes=60 * MIB),
        cost_estimate=LIGHT,
        name="fence",
    )(*values, *after)


def pack_rows(rows):
    unit = rows[0].shape[0] // 3
    return jnp.concatenate([r[: 2 * unit] for r in rows] + [r[2 * unit :] for r in rows], axis=0)


def unpack_rows(packed):
    unit = packed.shape[0] // 12
    return [
        jnp.concatenate(
            [
                packed[2 * unit * a : 2 * unit * (a + 1)],
                packed[8 * unit + unit * a : 8 * unit + unit * (a + 1)],
            ],
            axis=0,
        )
        for a in range(QUAD)
    ]


def swap_blocks(first, second, width, lane):
    low = (lane // width) % 2 == 0
    size = first.shape[1]
    return (
        jnp.where(low, first, pltpu.roll(second, width, 1)),
        jnp.where(low, pltpu.roll(first, size - width, 1), second),
    )


def exchange_blocks(packed):
    part = packed
    unit = LANES // 4
    lane = lax.broadcasted_iota(jnp.int32, part[0][0].shape, 1)
    out = [[None] * 3 for _ in range(4)]
    for pair in range(2):
        one, two = part[2 * pair], part[2 * pair + 1]
        for t in range(2):
            out[2 * t][pair], out[2 * t + 1][pair] = swap_blocks(one[t], two[t], 2 * unit, lane)
    u0, u2 = swap_blocks(part[0][2], part[2][2], 2 * unit, lane)
    u1, u3 = swap_blocks(part[1][2], part[3][2], 2 * unit, lane)
    out[0][2], out[1][2] = swap_blocks(u0, u1, unit, lane)
    out[2][2], out[3][2] = swap_blocks(u2, u3, unit, lane)
    return out


def front_kernel(place_ref, *refs, row_count, col_count, first_block):
    lefts, rights = refs[:col_count], refs[col_count : col_count + row_count]
    refs = refs[col_count + row_count :]
    prow_ref, coup_ref, weight_ref, pcol_ref, wleft_ref, pside_ref = refs[:6]
    sides_ref, right_ref, tmp_ref = refs[-3:]
    mid_ref, normed_ref = refs[-5:-3]
    step_at = pl.program_id(0) + first_block
    block, cols, wide = coup_ref.shape
    seq_each, _, width = wleft_ref.shape
    seqs = seq_each * row_count
    per_row = col_count // row_count

    @pl.when(pl.program_id(0) == 0)
    def _():
        for t, part in enumerate(lefts):
            index = lax.rem(t + place_ref[1], col_count)
            span = pl.multiple_of(lax.rem(index, per_row) * cols, cols)
            first = index // per_row * seq_each
            present = pside_ref[pl.ds(span, cols), :]
            seq_lane = lax.broadcasted_iota(jnp.int32, present.shape, 1)
            for k in range(seq_each):
                mask = jnp.sum(
                    jnp.where(seq_lane == first + k, present, 0.0), axis=1, keepdims=True
                )
                left = jnp.dot(part[...], wleft_ref[k], preferred_element_type=F32) * mask
                sides_ref[pl.ds(span * seqs + first + k, cols, stride=seqs), 0:width] = left
        right = jnp.zeros(right_ref.shape, F32)
        feature = lax.broadcasted_iota(jnp.int32, (width, width * seqs), 0)
        target = lax.broadcasted_iota(jnp.int32, (width, width * seqs), 1)
        for t, part in enumerate(rights):
            first = lax.rem(t + place_ref[0], row_count) * seq_each
            for k in range(seq_each):
                spread = (target == feature * seqs + (first + k)).astype(F32).astype(BF16)
                right += jnp.dot(part[k], spread, preferred_element_type=F32)
        right_ref[...] = right.astype(BF16)

    span = block * seqs
    start = pl.multiple_of(step_at * span, span)
    left = sides_ref[pl.ds(start, span), 0:width].astype(BF16)
    features = weight_ref.shape[1] // wide
    step = 4
    for low in range(0, features, step):
        part = jnp.dot(
            left, weight_ref[:, low * wide : (low + step) * wide], preferred_element_type=F32
        ).astype(BF16)
        for i in range(block):
            for d in range(step):
                tmp_ref[
                    i // 2,
                    (low + d) * seqs : (low + d + 1) * seqs,
                    (i % 2) * wide : (i % 2 + 1) * wide,
                ] = part[i * seqs : (i + 1) * seqs, d * wide : (d + 1) * wide]
    row_lane = lax.broadcasted_iota(jnp.int32, prow_ref.shape, 1)
    for pair in range(block // 2):
        update = jnp.dot(right_ref[...], tmp_ref[pair], preferred_element_type=F32)
        here = step_at * block + 2 * pair
        wanted = [jnp.where(row_lane == here + e, prow_ref[...], 0.0) for e in range(2)]
        wanted = [
            jnp.broadcast_to(jnp.sum(w, axis=1, keepdims=True), (seqs, wide)) for w in wanted
        ]
        count = jnp.dot(
            pcol_ref[...], jnp.concatenate(wanted, axis=1).astype(BF16), preferred_element_type=F32
        )
        update = update / jnp.maximum(count, 1.0)
        for e in range(2):
            i = 2 * pair + e
            mid = (coup_ref[i].astype(F32) + update[:, e * wide : (e + 1) * wide]).astype(BF16)
            mid_ref[i] = mid
            normed_ref[i] = standardize_features(mid.astype(F32), 1).astype(BF16)


def front(
    chunk, chunks, place, lefts, rights, present_rows, coupling, w_tensor, present_cols, w_left, after
):
    rows, cols, wide = coupling.shape
    seqs, width = present_rows.shape[0], w_left.shape[2]
    present_sides = present_rows.T
    block = 8
    steps = rows // block // chunks
    tile = pl.BlockSpec((block, cols, wide), lambda i: (i, 0, 0))
    return pl.pallas_call(
        functools.partial(
            front_kernel,
            row_count=len(rights),
            col_count=len(lefts),
            first_block=chunk * steps,
        ),
        grid=(steps,),
        in_specs=[pl.BlockSpec(memory_space=pltpu.SMEM)]
        + [whole(part.shape) for part in lefts + rights]
        + [
            whole(present_rows.shape),
            pl.BlockSpec((block, cols, wide), lambda i: (i + chunk * steps, 0, 0)),
            whole(w_tensor.shape),
            whole(present_cols.shape),
            whole(w_left.shape),
            whole(present_sides.shape),
        ]
        + anywhere(after),
        out_specs=[tile, tile],
        out_shape=[jax.ShapeDtypeStruct((rows // chunks, cols, wide), BF16)] * 2,
        scratch_shapes=[
            pltpu.VMEM((rows * seqs, LANES), F32),
            pltpu.VMEM((cols, width * seqs), BF16),
            pltpu.VMEM((block // 2, width * seqs, 2 * wide), BF16),
        ],
        compiler_params=params(),
        cost_estimate=LIGHT,
        name="front",
    )(
        place,
        *lefts,
        *rights,
        present_rows,
        coupling,
        w_tensor,
        present_cols,
        w_left,
        present_sides,
        *after,
    )


def exchange_rows(values):
    values = list(values)
    count = len(values)
    step = count // 2
    row = lax.broadcasted_iota(jnp.int32, values[0].shape, 0)
    size = values[0].shape[0]
    while step:
        width = 8 // count * step
        low = (row // width) % 2 == 0
        for m in range(count):
            if m & step == 0:
                one, two = values[m], values[m + step]
                values[m] = jnp.where(low, one, pltpu.roll(two, width, 0))
                values[m + step] = jnp.where(low, pltpu.roll(one, size - width, 0), two)
        step //= 2
    return values


def project_kernel(live_ref, normed_ref, cols_ref, weight_ref, *refs, first_row):
    out_ref, tmp_ref = refs[-2:]
    quads = normed_ref.shape[0] // QUAD
    dests, height, lanes = out_ref.shape
    each = height // quads
    count = dests * each
    unit = lanes // 12
    lane = lax.broadcasted_iota(jnp.int32, (1, lanes), 1)
    place = jnp.where(lane < 8 * unit, lane // (2 * unit), (lane - 8 * unit) // unit)
    group = max(1, 8 // each)
    for first in range(0, quads, group):
        values = []
        for m in range(first, first + group):
            packed = pack_rows([normed_ref[QUAD * m + a] for a in range(QUAD)])
            both = lax.dot_general(weight_ref[...], packed, NT, preferred_element_type=F32)
            row = first_row + (pl.program_id(0) * quads + m) * QUAD
            live = cols_ref[...]
            for a in range(QUAD):
                live = jnp.where(place == a, live * live_ref[row + a], live)
            values.append(sigmoid(both[:count]) * both[count:] * live)
        for b, value in enumerate(exchange_rows(values)):
            size = each * group
            for v in range(count // size):
                tmp_ref[v * group + b, first * each : first * each + size] = value[
                    v * size : (v + 1) * size
                ]
    out_ref[...] = tmp_ref[...].astype(BF16)


def project(first_row, live_rows, normed, live_cols, weight, dests):
    rows, cols, wide = normed.shape
    each = weight.shape[0] // (2 * dests)
    quads = max(8, 16 // each)
    lanes = QUAD * cols
    total = rows // QUAD
    return pl.pallas_call(
        functools.partial(project_kernel, first_row=first_row),
        grid=(total // quads,),
        in_specs=[
            pl.BlockSpec(memory_space=pltpu.SMEM),
            pl.BlockSpec((quads * QUAD, cols, wide), lambda i: (i, 0, 0)),
            whole(live_cols.shape),
            whole(weight.shape),
        ],
        out_specs=pl.BlockSpec((dests, quads * each, lanes), lambda i: (0, i, 0)),
        out_shape=jax.ShapeDtypeStruct((dests, total * each, lanes), BF16),
        scratch_shapes=[pltpu.VMEM((dests, quads * each, lanes), F32)],
        compiler_params=params(),
        cost_estimate=LIGHT,
        name="project",
    )(live_rows, normed, live_cols, weight)


def logit_kernel(live_ref, *refs, chunks):
    normeds, weight_ref, out_ref = refs[:chunks], refs[chunks], refs[-1]
    block = out_ref.shape[0]
    steps = pl.num_programs(0) // chunks

    def rows(normed_ref):
        for i in range(block):
            live = live_ref[pl.program_id(0) * block + i]
            out_ref[i] = lax.dot_general(
                weight_ref[...], normed_ref[i], NT, preferred_element_type=F32
            ) + MASK_PENALTY * (live - 1.0)

    for chunk in range(chunks):
        pl.when(pl.program_id(0) // steps == chunk)(functools.partial(rows, normeds[chunk]))


def chunk_tiles(shape, chunks, steps):
    def tile(chunk):
        return pl.BlockSpec(shape, lambda i: (jnp.clip(i - chunk * steps, 0, steps - 1), 0, 0))

    return [tile(chunk) for chunk in range(chunks)]


def logit(live_rows, normeds, weight, after):
    rows, cols, wide = normeds[0].shape
    block, chunks = 16, len(normeds)
    heads = weight.shape[0]
    return pl.pallas_call(
        functools.partial(logit_kernel, chunks=chunks),
        grid=(rows // block * chunks,),
        in_specs=[pl.BlockSpec(memory_space=pltpu.SMEM)]
        + chunk_tiles((block, cols, wide), chunks, rows // block)
        + [whole(weight.shape)]
        + anywhere(after),
        out_specs=pl.BlockSpec((block, heads, cols), lambda i: (i, 0, 0)),
        out_shape=jax.ShapeDtypeStruct((rows * chunks, heads, cols), F32),
        compiler_params=params(),
        cost_estimate=LIGHT,
        name="logit",
    )(live_rows, *normeds, weight, *after)


def assemble_kernel(recv_ref, *refs, row_count, pos_count, spans):
    left_ref, right_ref, flat_ref, rows_ref = refs[-4:]
    channel = pl.program_id(0)
    lanes = recv_ref.shape[2]
    each = left_ref.shape[2]
    height = recv_ref.shape[1] // spans
    stride = height // each
    groups = pos_count // 4
    tiles = lanes // LANES

    @pl.when(channel == 0)
    def _():
        for src in range(row_count * pos_count):
            value = recv_ref[src].astype(F32)
            for t in range(tiles):
                flat_ref[src, t] = value[:, t * LANES : (t + 1) * LANES]

    def block(row, group, index):
        packed = []
        index = index + group // groups * height
        for p in range(4):
            src = row * pos_count + group % groups * 4 + p
            packed.append(
                [flat_ref[src, t, pl.ds(index, each, stride=stride), :] for t in range(tiles)]
            )
        return exchange_blocks(packed)

    for row in range(row_count):
        for group in range(groups * spans):
            span = slice(group * lanes, (group + 1) * lanes)
            left = block(row, group, channel)
            right = block(row, group, channel + stride // 2)
            for a in range(QUAD):
                left_ref[0, row * QUAD + a, :, span] = jnp.concatenate(left[a], axis=1).astype(BF16)
                for t in range(tiles):
                    rows_ref[t, pl.ds(a, each, stride=QUAD), :] = right[a][t]
            for t in range(tiles):
                at = slice(group * lanes + t * LANES, group * lanes + (t + 1) * LANES)
                right_ref[0, row, 0, :, at] = rows_ref[t].astype(BF16)


def assemble(chunk, chunks, spans, received, sides, after, row_count, pos_count, cols):
    sources, height, lanes = received.shape
    depth = spans * pos_count * cols
    each = depth // (row_count * QUAD * chunks)
    channels = height // spans // each // 2
    blocks = row_count * QUAD
    shapes = [
        (channels, blocks, each * chunks, depth),
        (channels, row_count, chunks, QUAD * each, depth),
    ]
    return pl.pallas_call(
        functools.partial(
            assemble_kernel, row_count=row_count, pos_count=pos_count, spans=spans
        ),
        grid=(channels,),
        in_specs=[whole(received.shape)] + anywhere(sides) + anywhere(after),
        out_specs=[
            pl.BlockSpec((1, blocks, each, depth), lambda c: (c, 0, chunk, 0)),
            pl.BlockSpec((1, row_count, 1, QUAD * each, depth), lambda c: (c, 0, chunk, 0, 0)),
        ],
        out_shape=[jax.ShapeDtypeStruct(shape, BF16) for shape in shapes],
        input_output_aliases={1: 0, 2: 1} if sides else {},
        scratch_shapes=[
            pltpu.VMEM((sources, lanes // LANES, height, LANES), F32),
            pltpu.VMEM((lanes // LANES, QUAD * each, LANES), F32),
        ],
        compiler_params=params(),
        cost_estimate=LIGHT,
        name="assemble",
    )(received, *sides, *after)


def multiply_kernel(left_ref, right_ref, *refs, pos_count):
    out_ref, tmp_ref = refs[-2:]
    channel = pl.program_id(0)
    channels = pl.num_programs(0)
    lanes = out_ref.shape[2]
    _, blocks, each, depth = left_ref.shape
    row_count = blocks // QUAD
    unit = lanes // 12
    stride = out_ref.shape[1] // each
    tiles = lanes // LANES
    for group in range(pos_count // 4):
        starts = [(group * 4 + p) * 3 * unit for p in range(4)]
        wanted = jnp.concatenate(
            [right_ref[0, start : start + 2 * unit] for start in starts]
            + [right_ref[0, start + 2 * unit : start + 3 * unit] for start in starts],
            axis=0,
        )
        for row in range(row_count):
            left = left_ref[0, row * QUAD : (row + 1) * QUAD].reshape(QUAD * each, depth)
            value = lax.dot_general(left, wanted, NT, preferred_element_type=F32)
            packed = [
                [
                    value[a * each : (a + 1) * each, t * LANES : (t + 1) * LANES]
                    for t in range(tiles)
                ]
                for a in range(QUAD)
            ]
            for p, part in enumerate(exchange_blocks(packed)):
                dest = row * pos_count + group * 4 + p
                for t in range(tiles):
                    tmp_ref[dest, t, pl.ds(channel, each, stride=stride), :] = part[t]

    @pl.when(channel == channels - 1)
    def _():
        for dest in range(row_count * pos_count):
            for t in range(tiles):
                out_ref[dest, :, t * LANES : (t + 1) * LANES] = tmp_ref[dest, t].astype(BF16)


def multiply(left, right, after, pos_count, cols):
    count, blocks, each, depth = left.shape
    lanes = QUAD * cols
    shape = (blocks // QUAD * pos_count, each * count, lanes)
    return pl.pallas_call(
        functools.partial(multiply_kernel, pos_count=pos_count),
        grid=(count,),
        in_specs=[
            pl.BlockSpec((1, blocks, each, depth), lambda c: (c, 0, 0, 0)),
            pl.BlockSpec((1, depth, depth), lambda c: (c, 0, 0)),
        ]
        + anywhere(after),
        out_specs=whole(shape),
        out_shape=jax.ShapeDtypeStruct(shape, BF16),
        scratch_shapes=[pltpu.VMEM((shape[0], lanes // LANES, shape[1], LANES), F32)],
        compiler_params=params(),
        cost_estimate=LIGHT,
        name="multiply",
    )(left, right, *after)


def assemble_half_kernel(half_ref, *refs, row_count, pos_count, parts):
    recvs = refs[:parts]
    left_ref, own_ref, send_ref, flat_ref, right_ref = refs[-5:]
    channel = pl.program_id(0)
    lanes = recvs[0].shape[2]
    unit = lanes // 12
    cols = 3 * unit
    each = send_ref.shape[1] // (row_count * QUAD)
    stride = sum(recv.shape[1] for recv in recvs) // each
    groups = pos_count // 4
    tiles = lanes // LANES
    per_row = each * QUAD // cols

    @pl.when(channel == 0)
    def _():
        for src in range(row_count * pos_count):
            start = 0
            for recv in recvs:
                value = recv[src].astype(F32)
                end = start + recv.shape[1]
                for t in range(tiles):
                    flat_ref[src, t, start:end] = value[:, t * LANES : (t + 1) * LANES]
                start = end

    def block(row, group, index):
        packed = []
        for p in range(4):
            src = row * pos_count + group * 4 + p
            packed.append(
                [flat_ref[src, t, pl.ds(index, each, stride=stride), :] for t in range(tiles)]
            )
        return exchange_blocks(packed)

    for row in range(row_count):
        for group in range(groups):
            span = slice(group * lanes, (group + 1) * lanes)
            left = block(row, group, channel)
            for a in range(QUAD):
                start = (row * QUAD + a) * each
                left_ref[0, start : start + each, span] = jnp.concatenate(left[a], axis=1).astype(
                    BF16
                )
            right = block(row, group, channel + stride // 2)
            for a in range(QUAD):
                for piece in range(per_row):
                    place = row * per_row + piece
                    base = (place // 4) * lanes
                    low = piece * (cols // QUAD)
                    mid = low + 2 * unit // QUAD
                    high = low + cols // QUAD
                    first = base + (place % 4) * 2 * unit + a
                    second = base + 8 * unit + (place % 4) * unit + a
                    for t in range(tiles):
                        value = right[a][t]
                        at = group * tiles + t
                        right_ref[at, pl.ds(first, mid - low, stride=QUAD), :] = value[low:mid]
                        right_ref[at, pl.ds(second, high - mid, stride=QUAD), :] = value[mid:high]
    width = pos_count * cols
    own = pl.multiple_of(half_ref[0] * width, width)
    other = pl.multiple_of((1 - half_ref[0]) * width, width)
    theirs = []
    for at in range(groups * tiles):
        span = slice(at * LANES, (at + 1) * LANES)
        own_ref[0, :, span] = right_ref[at, pl.ds(own, width), :].astype(BF16)
        theirs.append(right_ref[at, pl.ds(other, width), :].astype(BF16))
    theirs = jnp.concatenate(theirs, axis=1)
    for row in range(row_count):
        span = slice(row * QUAD * each, (row + 1) * QUAD * each)
        send_ref[0, span] = lax.dot_general(
            left_ref[0, span], theirs, NT, preferred_element_type=F32
        ).astype(BF16)


def assemble_half(half, received, after, row_count, pos_count, cols):
    sources, _, lanes = received[0].shape
    height = sum(part.shape[1] for part in received)
    each = (2 * pos_count * cols) // (row_count * QUAD)
    channels = height // each // 2
    depth = pos_count * cols
    rows = 2 * depth
    return pl.pallas_call(
        functools.partial(
            assemble_half_kernel, row_count=row_count, pos_count=pos_count, parts=len(received)
        ),
        grid=(channels,),
        in_specs=[pl.BlockSpec(memory_space=pltpu.SMEM)]
        + [whole(part.shape) for part in received]
        + anywhere(after),
        out_specs=[
            pl.BlockSpec((1, rows, depth), lambda c: (c, 0, 0)),
            pl.BlockSpec((1, depth, depth), lambda c: (c, 0, 0)),
            pl.BlockSpec((1, rows, depth), lambda c: (c, 0, 0)),
        ],
        out_shape=[
            jax.ShapeDtypeStruct((channels, rows, depth), BF16),
            jax.ShapeDtypeStruct((channels, depth, depth), BF16),
            jax.ShapeDtypeStruct((channels, rows, depth), BF16),
        ],
        scratch_shapes=[
            pltpu.VMEM((sources, lanes // LANES, height, LANES), F32),
            pltpu.VMEM((depth // LANES, rows, LANES), F32),
        ],
        compiler_params=params(),
        cost_estimate=LIGHT,
        name="assemble_half",
    )(half, *received, *after)


def combine_kernel(left_ref, own_ref, recv_ref, *refs, row_count, pos_count):
    out_ref, tmp_ref = refs[-2:]
    channel = pl.program_id(0)
    channels = pl.num_programs(0)
    lanes = out_ref.shape[2]
    each = left_ref.shape[1] // (row_count * QUAD)
    stride = out_ref.shape[1] // each
    tiles = lanes // LANES
    for row in range(row_count):
        for group in range(pos_count // 4):
            cols = slice(group * lanes, (group + 1) * lanes)
            span = slice(row * QUAD * each, (row + 1) * QUAD * each)
            value = lax.dot_general(
                left_ref[0, span], own_ref[0, cols], NT, preferred_element_type=F32
            )
            value = value + recv_ref[0, span, cols].astype(F32)
            blocks = [
                [
                    value[a * each : (a + 1) * each, t * LANES : (t + 1) * LANES]
                    for t in range(tiles)
                ]
                for a in range(QUAD)
            ]
            for p, value in enumerate(exchange_blocks(blocks)):
                dest = row * pos_count + group * 4 + p
                for t in range(tiles):
                    tmp_ref[dest, t, pl.ds(channel, each, stride=stride), :] = value[t]

    @pl.when(channel == channels - 1)
    def _():
        for dest in range(row_count * pos_count):
            for t in range(tiles):
                out_ref[dest, :, t * LANES : (t + 1) * LANES] = tmp_ref[dest, t].astype(BF16)


def combine(left, own, received, after, row_count, pos_count, cols):
    channels, rows, depth = left.shape
    each = rows // (row_count * QUAD)
    shape = (row_count * pos_count, each * channels, QUAD * cols)
    return pl.pallas_call(
        functools.partial(combine_kernel, row_count=row_count, pos_count=pos_count),
        grid=(channels,),
        in_specs=[
            pl.BlockSpec((1, rows, depth), lambda c: (c, 0, 0)),
            pl.BlockSpec((1, depth, depth), lambda c: (c, 0, 0)),
            pl.BlockSpec((1, rows, depth), lambda c: (c, 0, 0)),
        ]
        + anywhere(after),
        out_specs=whole(shape),
        out_shape=jax.ShapeDtypeStruct(shape, BF16),
        scratch_shapes=[pltpu.VMEM((shape[0], shape[2] // LANES, shape[1], LANES), F32)],
        compiler_params=params(),
        cost_estimate=LIGHT,
        name="combine",
    )(left, own, received, *after)


def merge_kernel(*refs, parts):
    for index, piece in enumerate(refs[:parts]):

        @pl.when(pl.program_id(0) == index)
        def _():
            refs[-1][...] = piece[...]


def merge(pieces, first, count, into):
    sources, height, lanes = pieces[0].shape
    return pl.pallas_call(
        functools.partial(merge_kernel, parts=len(pieces)),
        grid=(len(pieces),),
        in_specs=[whole(piece.shape) for piece in pieces] + anywhere(into),
        out_specs=pl.BlockSpec((sources, height, lanes), lambda i: (0, i + first, 0)),
        out_shape=jax.ShapeDtypeStruct((sources, height * count, lanes), BF16),
        input_output_aliases={len(pieces): 0} if into else {},
        compiler_params=params(),
        cost_estimate=LIGHT,
        name="merge",
    )(*pieces, *into)


def partial_kernel(place_ref, logit_ref, *refs, row_count, col_count):
    sides, refs = refs[:col_count], refs[col_count:]
    project_ref, outs, exp_ref, value_ref = refs[0], refs[1 : 1 + row_count], *refs[-2:]
    rows, heads, cols = logit_ref.shape
    wide = value_ref.shape[2] // heads
    per_row = col_count // row_count
    for u, side in enumerate(sides):
        index = lax.rem(place_ref[1] + u, col_count)
        part = lax.rem(place_ref[0] + row_count - index // per_row, row_count)
        span = pl.multiple_of(lax.rem(index, per_row) * cols, cols)
        value_ref[part, pl.ds(span, cols), :] = jnp.dot(
            side[...], project_ref[...], preferred_element_type=F32
        ).astype(BF16)
    top = jnp.max(logit_ref[...], axis=0)
    powers = jnp.exp(logit_ref[...] - top[None])
    total = jnp.sum(powers, axis=0)
    exp_ref[:, 0:cols] = powers.reshape(rows * heads, cols)
    for h in range(heads):
        weights = exp_ref[pl.ds(h, rows, stride=heads), :][:, :cols].astype(BF16)
        for t, out in enumerate(outs):
            out[h, :cols] = lax.dot_general(
                weights,
                value_ref[t, :, h * wide : (h + 1) * wide],
                TN,
                preferred_element_type=F32,
            )
            out[h, cols:] = jnp.zeros((out.shape[1] - cols, wide), F32)
            out[h, cols : cols + 1, 0:cols] = top[h : h + 1]
            out[h, cols + 1 : cols + 2, 0:cols] = total[h : h + 1]


def partial_average(place, logits, sides, w_value):
    rows, heads, cols = logits.shape
    wide = w_value.shape[1] // heads
    row_count = len(sides) * cols // rows
    shape = (heads, cols + 8, wide)
    return pl.pallas_call(
        functools.partial(partial_kernel, row_count=row_count, col_count=len(sides)),
        grid=(1,),
        in_specs=[pl.BlockSpec(memory_space=pltpu.SMEM)]
        + [whole(v.shape) for v in (logits, *sides, w_value)],
        out_specs=[whole(shape)] * row_count,
        out_shape=[jax.ShapeDtypeStruct(shape, F32)] * row_count,
        scratch_shapes=[
            pltpu.VMEM((rows * heads, LANES), F32),
            pltpu.VMEM((row_count, rows, w_value.shape[1]), BF16),
        ],
        compiler_params=params(),
        cost_estimate=LIGHT,
        name="partial",
    )(place, logits, *sides, w_value)


def average_kernel(*refs):
    parts, (gate_ref, align_ref, weight_ref, out_ref) = refs[:-4], refs[-4:]
    heads, cols, _ = gate_ref.shape
    here = lax.broadcasted_iota(jnp.int32, (cols, cols), 0)
    there = lax.broadcasted_iota(jnp.int32, (cols, cols), 1)
    out = align_ref[...].astype(F32)
    for h in range(heads):
        tops = [part[h, cols : cols + 1, 0:cols] for part in parts]
        sums = [part[h, cols + 1 : cols + 2, 0:cols] for part in parts]
        top = functools.reduce(jnp.maximum, tops)
        scales = [jnp.exp(t - top) for t in tops]
        total = sum(scale * each for scale, each in zip(scales, sums))
        summed = jnp.zeros(gate_ref.shape[1:], F32)
        for part, scale in zip(parts, scales):
            factor = jnp.where(here == there, scale / total, 0.0)
            summed += jnp.dot(
                factor,
                part[h, :cols],
                precision=lax.Precision.HIGHEST,
                preferred_element_type=F32,
            )
        gated = (gate_ref[h] * summed).astype(BF16)
        out += jnp.dot(gated, weight_ref[h], preferred_element_type=F32)
    out_ref[...] = out.astype(BF16)


def average(parts, gate, align, weight):
    operands = [*parts, gate, align, weight]
    return pl.pallas_call(
        average_kernel,
        grid=(1,),
        in_specs=[whole(v.shape) for v in operands],
        out_specs=whole(align.shape),
        out_shape=jax.ShapeDtypeStruct(align.shape, BF16),
        compiler_params=params(),
        cost_estimate=LIGHT,
        name="average",
    )(*operands)


def finish_kernel(*refs, parts, chunks):
    products = refs[:parts]
    mids = refs[parts : parts + chunks]
    normeds = refs[parts + chunks : parts + 2 * chunks]
    gate_ref, weight_ref, out_ref = refs[parts + 2 * chunks : parts + 2 * chunks + 3]
    flat = refs[parts + 2 * chunks + 3 :]
    quads = out_ref.shape[0] // QUAD
    lanes = products[0].shape[2]
    tiles = range(lanes // LANES)
    for product, tmp in zip(products, flat):
        sources, height, _ = product.shape
        for src in range(sources):
            value = product[src].astype(F32)
            for t in tiles:
                tmp[t, src * height : (src + 1) * height] = value[:, t * LANES : (t + 1) * LANES]

    def rows(mid_ref, normed_ref):
        for m in range(quads):
            pieces = []
            for product, tmp in zip(products, flat):
                sources, height, _ = product.shape
                each = height // quads
                for k in range(each):
                    pieces.append(
                        jnp.concatenate(
                            [tmp[t, pl.ds(m * each + k, sources, stride=height), :] for t in tiles],
                            axis=1,
                        )
                    )
            normed = standardize_features(jnp.concatenate(pieces, axis=0), 0).astype(BF16)
            out = lax.dot_general(normed, weight_ref[...], TN, preferred_element_type=F32)
            for a, value in enumerate(unpack_rows(out)):
                i = QUAD * m + a
                gate = sigmoid(jnp.dot(normed_ref[i], gate_ref[...], preferred_element_type=F32))
                out_ref[i] = (mid_ref[i].astype(F32) + gate * value).astype(BF16)

    steps = pl.num_programs(0) // chunks
    for chunk in range(chunks):
        pl.when(pl.program_id(0) // steps == chunk)(
            functools.partial(rows, mids[chunk], normeds[chunk])
        )


def finish(products, mids, normeds, w_gate, w_final):
    rows, cols, wide = mids[0].shape
    chunks = len(mids)
    lanes = products[0].shape[2]
    total = rows * chunks // QUAD
    heights = [part.shape[1] // total for part in products]
    quads = max(8, 16 // min(heights))
    steps = rows // QUAD // quads

    tiles = chunk_tiles((quads * QUAD, cols, wide), chunks, steps)
    return pl.pallas_call(
        functools.partial(finish_kernel, parts=len(products), chunks=chunks),
        grid=(total // quads,),
        in_specs=[
            pl.BlockSpec((part.shape[0], quads * each, lanes), lambda i: (0, i, 0))
            for part, each in zip(products, heights)
        ]
        + tiles * 2
        + [whole(w_gate.shape), whole(w_final.shape)],
        out_specs=pl.BlockSpec((quads * QUAD, cols, wide), lambda i: (i, 0, 0)),
        out_shape=jax.ShapeDtypeStruct((rows * chunks, cols, wide), BF16),
        scratch_shapes=[
            pltpu.VMEM((lanes // LANES, part.shape[0] * quads * each, LANES), F32)
            for part, each in zip(products, heights)
        ],
        compiler_params=params(),
        cost_estimate=LIGHT,
        name="finish",
    )(*products, *mids, *normeds, w_gate, w_final)


def on_device(
    alignment_embedding,
    coupling_embedding,
    amino_validity,
    alignment_validity,
    alignment_matrix,
    tensor_final_matrix,
    coupling_logit_matrix,
    mean_final_matrix,
    trimul_matrices,
    trimul_final_matrix,
):
    seq_each, module_number, feature_count = alignment_embedding.shape
    rows, _, wide = coupling_embedding.shape
    row_count = lax.axis_size("row")
    pos_count = lax.axis_size("pos")
    col_count = 2 * pos_count
    row_index = lax.axis_index("row")
    half = lax.axis_index("half")
    col_index = half * pos_count + lax.axis_index("pos")
    seqs = seq_each * row_count
    active_entries = amino_validity.astype(F32)
    sequence_index = lax.broadcasted_iota(jnp.int32, alignment_validity.shape, 0)
    present_entries = (
        jnp.where(sequence_index == 0, F32(1.0), alignment_validity.astype(F32))
        * active_entries[None, :]
    )
    row_start = row_index * rows
    col_start = col_index * module_number
    present_rows = lax.dynamic_slice_in_dim(present_entries, row_start, rows, 1)
    present_cols = lax.dynamic_slice_in_dim(present_entries, col_start, module_number, 1)
    live_rows = lax.dynamic_slice_in_dim(active_entries, row_start, rows, 0)
    live_cols = lax.dynamic_slice_in_dim(active_entries, col_start, module_number, 0)

    own_start = (row_index * seq_each, col_start)
    present_own = lax.dynamic_slice(present_entries, own_start, (seq_each, module_number))
    own_normed = standardize_features(alignment_embedding.astype(F32), 2).astype(BF16)
    own_normed = own_normed.reshape(seq_each * module_number, feature_count)

    def project_msa(matrix):
        return jnp.dot(own_normed, matrix, preferred_element_type=F32).reshape(
            seq_each, module_number, -1
        )

    own_right = project_msa(alignment_matrix[:, TENSOR_FEATURES : 2 * TENSOR_FEATURES])
    own_right = (own_right * present_own[:, :, None]).astype(BF16)
    own_rows = jnp.transpose(
        own_normed.reshape(seq_each, module_number, feature_count), (1, 0, 2)
    ).reshape(module_number, -1)
    apart = jnp.eye(seq_each, dtype=BF16)
    w_left = apart[:, :, None, None] * alignment_matrix[:, :TENSOR_FEATURES]
    w_left = w_left.reshape(seq_each, seq_each * feature_count, TENSOR_FEATURES)
    per_row = rows // module_number
    lefts = []
    for t in range(col_count):
        pairs = []
        for r in range(row_count):
            for q in range(col_count):
                to = (r * per_row + q % per_row - t) % col_count
                pairs.append((r * col_count + q, q // per_row * col_count + to))
        lefts.append(lax.ppermute(own_rows, AXES, pairs))
    rights = [own_right]
    for t in range(1, row_count):
        pairs = [(r, (r - t) % row_count) for r in range(row_count)]
        rights.append(lax.ppermute(own_right, "row", pairs))

    w_tensor = tensor_final_matrix.reshape(TENSOR_FEATURES, TENSOR_FEATURES * wide)
    unit = module_number // 3
    live_packed = jnp.concatenate(
        [live_cols[: 2 * unit]] * QUAD + [live_cols[2 * unit :]] * QUAD
    )[None]
    devices = row_count * col_count
    w_kinds = trimul_matrices[:, : 4 * CTRI].T.reshape(2, 2, CTRI, wide)
    w_logit = coupling_logit_matrix.T

    def side_weights(part):
        return jnp.transpose(part, (1, 2, 0, 3, 4)).reshape(-1, wide)

    def exchange(block, axes):
        return lax.all_to_all(block, axes, split_axis=0, concat_axis=0, tiled=True)

    def front_rows(chunk, chunks, after):
        return front(
            chunk,
            chunks,
            place,
            lefts,
            rights,
            present_rows,
            coupling_embedding,
            w_tensor,
            present_cols.T.astype(BF16),
            w_left,
            after,
        )

    def project_rows(chunk, normed, weight, dests):
        first_row = chunk * normed.shape[0]
        return project(first_row, live_rows, normed, live_packed, weight, dests)

    place = jnp.stack([row_index, col_index]).astype(jnp.int32)

    def by_head(part):
        part = part.reshape(seq_each, module_number, MEAN_GROUPS, GROUP_FEATURES)
        return jnp.transpose(part, (2, 1, 0, 3)).reshape(MEAN_GROUPS, module_number, -1)

    first = 2 * TENSOR_FEATURES
    middle = first + MEAN_GROUPS * GROUP_FEATURES
    w_value = alignment_matrix[:, first:middle].reshape(
        1, feature_count, MEAN_GROUPS, 1, GROUP_FEATURES
    )
    w_value = (w_value * apart.reshape(seq_each, 1, 1, seq_each, 1)).reshape(
        seq_each * feature_count, -1
    )
    sequence_gate = by_head(jax.nn.sigmoid(project_msa(alignment_matrix[:, middle:])))
    w_mean = mean_final_matrix.reshape(MEAN_GROUPS, 1, GROUP_FEATURES, 1, feature_count)
    w_mean = (w_mean * apart.reshape(1, seq_each, 1, seq_each, 1)).reshape(
        MEAN_GROUPS, seq_each * GROUP_FEATURES, seq_each * feature_count
    )
    align = jnp.transpose(alignment_embedding, (1, 0, 2)).reshape(module_number, -1)

    def gather_parts(parts):
        gathered = list(parts[:1])
        for t in range(1, row_count):
            pairs = [(r, (r - t) % row_count) for r in range(row_count)]
            gathered.append(lax.ppermute(parts[t], "row", pairs))
        return gathered

    group = devices // 2
    shape_of = (row_count, col_count, module_number)
    half_shape = (row_count, pos_count, module_number)
    mids, normeds, returned = [], [], []
    if CTRI // 2 % devices:
        row_chunks = rows // QUAD // 16
        sent, sides = (), ()
        weight = side_weights(w_kinds.reshape(2, 2, devices, -1, wide))
        for chunk in range(row_chunks):
            mid, normed = front_rows(chunk, row_chunks, sent)
            block = project_rows(chunk, normed, weight, devices)
            sent = (block,)
            sides = assemble(chunk, row_chunks, 1, exchange(block, AXES), sides, (), *shape_of)
            mids.append(mid)
            normeds.append(normed)
        left, right = sides
        right = right.reshape(right.shape[0], -1, right.shape[-1])
        last = multiply(left, right, (), *shape_of[1:])
        returned.append(exchange(last, AXES))
        logits = logit(live_rows, normeds, w_logit, ())
        parts = partial_average(place, logits, lefts, w_value)
        parts = gather_parts(fence(parts, (last,)))
        orders = [(0, CTRI, devices)]
    else:
        cut = CTRI // 2
        row_chunks = 2
        w_half = side_weights(w_kinds[:, :, :cut].reshape(2, 2, group, -1, wide))
        w_both = w_kinds[:, :, cut:].reshape(2, 2, row_count, 2, pos_count, -1, wide)

        def half_weights(which):
            part = lax.dynamic_index_in_dim(w_both, which, 3, keepdims=False)
            return side_weights(part.reshape(2, 2, group, -1, wide))

        w_own, w_other = half_weights(half), half_weights(1 - half)
        swap = [(0, 1), (1, 0)]
        received, crossed, kept, ahead = [], [], [], ()
        for chunk in range(row_chunks):
            mid, normed = front_rows(chunk, row_chunks, ahead)
            mids.append(mid)
            normeds.append(normed)
            to_half = project_rows(chunk, normed, w_half, group)
            to_other = project_rows(chunk, normed, w_other, group)
            to_other, to_half, w_own = fence([to_other, to_half, w_own], received + crossed)
            crossed.append(lax.ppermute(to_other, "half", swap))
            received.append(exchange(to_half, GROUP))
            ahead = (w_own,)
            kept.append(project_rows(chunk, normed, w_own, group))
        half_scalar = half.astype(jnp.int32).reshape(1)
        logits = logit(live_rows, normeds, w_logit, tuple(kept))
        parts = partial_average(place, logits, lefts, w_value)
        merged = merge(kept + crossed[:-1], 0, 2 * row_chunks, ())
        left, own, theirs = assemble_half(
            half_scalar, received, (parts[0], merged), *half_shape
        )
        merged = merge(crossed[-1:], 2 * row_chunks - 1, 2 * row_chunks, (merged,))
        theirs, merged, *parts = fence([theirs, merged, *parts], ())
        partial = lax.ppermute(theirs, "half", swap)
        both = exchange(merged, GROUP)
        parts = gather_parts(parts)
        product = combine(left, own, partial, (both, *parts[1:]), *half_shape)
        returned.append(exchange(product, GROUP))
        left, right = assemble(0, 1, 2, both, (), (product,), *half_shape)
        right = right.reshape(right.shape[0], -1, right.shape[-1])
        last = multiply(left, right, (), *shape_of[1:])
        returned.append(exchange(last, AXES))
        orders = [(0, cut, group), (cut, CTRI, devices)]
    parts = fence(parts, (last,))
    aligned = average(parts, sequence_gate, align, w_mean)
    alignment_updated_embedding = jnp.transpose(
        aligned.reshape(module_number, seq_each, feature_count), (1, 0, 2)
    )
    w_final = jnp.concatenate(
        [
            jnp.transpose(
                trimul_final_matrix[low:high].reshape(sources, -1, wide), (1, 0, 2)
            ).reshape(-1, wide)
            for low, high, sources in orders
        ]
    )
    pair_output = finish(returned, mids, normeds, trimul_matrices[:, 4 * CTRI :], w_final)
    return (alignment_updated_embedding, pair_output)


def solution(mesh):
    rows, cols = mesh.devices.shape
    inner = Mesh(mesh.devices.reshape(rows, 2, cols // 2), AXES)
    tile = P("row", ("half", "pos"), None)
    in_specs = (tile, tile) + (P(),) * 8
    return jax.shard_map(
        on_device, mesh=inner, in_specs=in_specs, out_specs=(tile, tile), check_vma=False
    )
```

```python
import functools

import jax
import jax.numpy as jnp
from jax import lax
from jax.experimental import pallas as pl
from jax.experimental.pallas import tpu as pltpu
from jax.sharding import Mesh, PartitionSpec as P

TENSOR_FEATURES = 32
MEAN_GROUPS = 8
GROUP_FEATURES = 32
CTRI = 128

EPS = 1e-05
MASK_PENALTY = 10000.0
QUAD = 4
LANES = 128
MIB = 1024 * 1024
AXES = ("row", "half", "pos")
GROUP = ("row", "pos")
F32 = jnp.float32
BF16 = jnp.bfloat16
NT = (((1,), (1,)), ((), ()))
TN = (((0,), (0,)), ((), ()))


def standardize_features(values_in, axis):
    centre = values_in - jnp.mean(values_in, axis=axis, keepdims=True)
    spread = jnp.mean(centre * centre, axis=axis, keepdims=True)
    return centre * lax.rsqrt(spread + EPS)


def sigmoid(x):
    return 0.5 * jnp.tanh(0.5 * x) + 0.5


def params():
    return pltpu.CompilerParams(
        vmem_limit_bytes=60 * MIB, dimension_semantics=("arbitrary",)
    )


LIGHT = pl.CostEstimate(flops=1000, bytes_accessed=1000, transcendentals=0)


def whole(shape):
    zeros = (0,) * len(shape)
    return pl.BlockSpec(shape, lambda *_: zeros, pipeline_mode=pl.Buffered(1))


def anywhere(after):
    return [pl.BlockSpec(memory_space=pl.ANY)] * len(after)


def fence(values, after):
    return pl.pallas_call(
        lambda *refs: None,
        in_specs=anywhere(values) + anywhere(after),
        out_specs=anywhere(values),
        out_shape=[jax.ShapeDtypeStruct(v.shape, v.dtype) for v in values],
        input_output_aliases={i: i for i in range(len(values))},
        compiler_params=pltpu.CompilerParams(vmem_limit_bytes=60 * MIB),
        cost_estimate=LIGHT,
        name="fence",
    )(*values, *after)


def pack_rows(rows):
    unit = rows[0].shape[0] // 3
    return jnp.concatenate([r[: 2 * unit] for r in rows] + [r[2 * unit :] for r in rows], axis=0)


def unpack_rows(packed):
    unit = packed.shape[0] // 12
    return [
        jnp.concatenate(
            [
                packed[2 * unit * a : 2 * unit * (a + 1)],
                packed[8 * unit + unit * a : 8 * unit + unit * (a + 1)],
            ],
            axis=0,
        )
        for a in range(QUAD)
    ]


def swap_blocks(first, second, width, lane):
    low = (lane // width) % 2 == 0
    size = first.shape[1]
    return (
        jnp.where(low, first, pltpu.roll(second, width, 1)),
        jnp.where(low, pltpu.roll(first, size - width, 1), second),
    )


def exchange_blocks(packed):
    part = packed
    unit = LANES // 4
    lane = lax.broadcasted_iota(jnp.int32, part[0][0].shape, 1)
    out = [[None] * 3 for _ in range(4)]
    for pair in range(2):
        one, two = part[2 * pair], part[2 * pair + 1]
        for t in range(2):
            out[2 * t][pair], out[2 * t + 1][pair] = swap_blocks(one[t], two[t], 2 * unit, lane)
    u0, u2 = swap_blocks(part[0][2], part[2][2], 2 * unit, lane)
    u1, u3 = swap_blocks(part[1][2], part[3][2], 2 * unit, lane)
    out[0][2], out[1][2] = swap_blocks(u0, u1, unit, lane)
    out[2][2], out[3][2] = swap_blocks(u2, u3, unit, lane)
    return out


def front_kernel(place_ref, *refs, row_count, col_count, first_block):
    lefts, rights = refs[:col_count], refs[col_count : col_count + row_count]
    refs = refs[col_count + row_count :]
    prow_ref, coup_ref, weight_ref, pcol_ref, wleft_ref, pside_ref = refs[:6]
    sides_ref, right_ref, tmp_ref = refs[-3:]
    mid_ref, normed_ref = refs[-5:-3]
    step_at = pl.program_id(0) + first_block
    block, cols, wide = coup_ref.shape
    seq_each, _, width = wleft_ref.shape
    seqs = seq_each * row_count
    per_row = col_count // row_count

    @pl.when(pl.program_id(0) == 0)
    def _():
        for t, part in enumerate(lefts):
            index = lax.rem(t + place_ref[1], col_count)
            span = pl.multiple_of(lax.rem(index, per_row) * cols, cols)
            first = index // per_row * seq_each
            present = pside_ref[pl.ds(span, cols), :]
            seq_lane = lax.broadcasted_iota(jnp.int32, present.shape, 1)
            for k in range(seq_each):
                mask = jnp.sum(
                    jnp.where(seq_lane == first + k, present, 0.0), axis=1, keepdims=True
                )
                left = jnp.dot(part[...], wleft_ref[k], preferred_element_type=F32) * mask
                sides_ref[pl.ds(span * seqs + first + k, cols, stride=seqs), 0:width] = left
        right = jnp.zeros(right_ref.shape, F32)
        feature = lax.broadcasted_iota(jnp.int32, (width, width * seqs), 0)
        target = lax.broadcasted_iota(jnp.int32, (width, width * seqs), 1)
        for t, part in enumerate(rights):
            first = lax.rem(t + place_ref[0], row_count) * seq_each
            for k in range(seq_each):
                spread = (target == feature * seqs + (first + k)).astype(F32).astype(BF16)
                right += jnp.dot(part[k], spread, preferred_element_type=F32)
        right_ref[...] = right.astype(BF16)

    span = block * seqs
    start = pl.multiple_of(step_at * span, span)
    left = sides_ref[pl.ds(start, span), 0:width].astype(BF16)
    features = weight_ref.shape[1] // wide
    step = 4
    for low in range(0, features, step):
        part = jnp.dot(
            left, weight_ref[:, low * wide : (low + step) * wide], preferred_element_type=F32
        ).astype(BF16)
        for i in range(block):
            for d in range(step):
                tmp_ref[
                    i // 2,
                    (low + d) * seqs : (low + d + 1) * seqs,
                    (i % 2) * wide : (i % 2 + 1) * wide,
                ] = part[i * seqs : (i + 1) * seqs, d * wide : (d + 1) * wide]
    row_lane = lax.broadcasted_iota(jnp.int32, prow_ref.shape, 1)
    for pair in range(block // 2):
        update = jnp.dot(right_ref[...], tmp_ref[pair], preferred_element_type=F32)
        here = step_at * block + 2 * pair
        wanted = [jnp.where(row_lane == here + e, prow_ref[...], 0.0) for e in range(2)]
        wanted = [
            jnp.broadcast_to(jnp.sum(w, axis=1, keepdims=True), (seqs, wide)) for w in wanted
        ]
        count = jnp.dot(
            pcol_ref[...], jnp.concatenate(wanted, axis=1).astype(BF16), preferred_element_type=F32
        )
        update = update / jnp.maximum(count, 1.0)
        for e in range(2):
            i = 2 * pair + e
            mid = (coup_ref[i].astype(F32) + update[:, e * wide : (e + 1) * wide]).astype(BF16)
            mid_ref[i] = mid
            normed_ref[i] = standardize_features(mid.astype(F32), 1).astype(BF16)


def front(
    first_row, count, place, lefts, rights, present_rows, coupling, w_tensor, present_cols, w_left, after
):
    rows, cols, wide = coupling.shape
    seqs, width = present_rows.shape[0], w_left.shape[2]
    present_sides = present_rows.T
    block = 8
    steps, offset = count // block, first_row // block
    tile = pl.BlockSpec((block, cols, wide), lambda i: (i, 0, 0))
    return pl.pallas_call(
        functools.partial(
            front_kernel,
            row_count=len(rights),
            col_count=len(lefts),
            first_block=offset,
        ),
        grid=(steps,),
        in_specs=[pl.BlockSpec(memory_space=pltpu.SMEM)]
        + [whole(part.shape) for part in lefts + rights]
        + [
            whole(present_rows.shape),
            pl.BlockSpec((block, cols, wide), lambda i: (i + offset, 0, 0)),
            whole(w_tensor.shape),
            whole(present_cols.shape),
            whole(w_left.shape),
            whole(present_sides.shape),
        ]
        + anywhere(after),
        out_specs=[tile, tile],
        out_shape=[jax.ShapeDtypeStruct((count, cols, wide), BF16)] * 2,
        scratch_shapes=[
            pltpu.VMEM((rows * seqs, LANES), F32),
            pltpu.VMEM((cols, width * seqs), BF16),
            pltpu.VMEM((block // 2, width * seqs, 2 * wide), BF16),
        ],
        compiler_params=params(),
        cost_estimate=LIGHT,
        name="front",
    )(
        place,
        *lefts,
        *rights,
        present_rows,
        coupling,
        w_tensor,
        present_cols,
        w_left,
        present_sides,
        *after,
    )


def exchange_rows(values):
    values = list(values)
    count = len(values)
    step = count // 2
    row = lax.broadcasted_iota(jnp.int32, values[0].shape, 0)
    size = values[0].shape[0]
    while step:
        width = 8 // count * step
        low = (row // width) % 2 == 0
        for m in range(count):
            if m & step == 0:
                one, two = values[m], values[m + step]
                values[m] = jnp.where(low, one, pltpu.roll(two, width, 0))
                values[m + step] = jnp.where(low, pltpu.roll(one, size - width, 0), two)
        step //= 2
    return values


def project_kernel(live_ref, normed_ref, cols_ref, weight_ref, *refs, first_row):
    out_ref, tmp_ref = refs[-2:]
    quads = normed_ref.shape[0] // QUAD
    dests, height, lanes = out_ref.shape
    each = height // quads
    count = dests * each
    unit = lanes // 12
    lane = lax.broadcasted_iota(jnp.int32, (1, lanes), 1)
    place = jnp.where(lane < 8 * unit, lane // (2 * unit), (lane - 8 * unit) // unit)
    group = max(1, 8 // each)
    for first in range(0, quads, group):
        values = []
        for m in range(first, first + group):
            packed = pack_rows([normed_ref[QUAD * m + a] for a in range(QUAD)])
            both = lax.dot_general(weight_ref[...], packed, NT, preferred_element_type=F32)
            row = first_row + (pl.program_id(0) * quads + m) * QUAD
            live = cols_ref[...]
            for a in range(QUAD):
                live = jnp.where(place == a, live * live_ref[row + a], live)
            values.append(sigmoid(both[:count]) * both[count:] * live)
        for b, value in enumerate(exchange_rows(values)):
            size = each * group
            for v in range(count // size):
                tmp_ref[v * group + b, first * each : first * each + size] = value[
                    v * size : (v + 1) * size
                ]
    out_ref[...] = tmp_ref[...].astype(BF16)


def project(first_row, live_rows, normed, live_cols, weight, dests):
    rows, cols, wide = normed.shape
    each = weight.shape[0] // (2 * dests)
    quads = max(8, 16 // each)
    lanes = QUAD * cols
    total = rows // QUAD
    return pl.pallas_call(
        functools.partial(project_kernel, first_row=first_row),
        grid=(total // quads,),
        in_specs=[
            pl.BlockSpec(memory_space=pltpu.SMEM),
            pl.BlockSpec((quads * QUAD, cols, wide), lambda i: (i, 0, 0)),
            whole(live_cols.shape),
            whole(weight.shape),
        ],
        out_specs=pl.BlockSpec((dests, quads * each, lanes), lambda i: (0, i, 0)),
        out_shape=jax.ShapeDtypeStruct((dests, total * each, lanes), BF16),
        scratch_shapes=[pltpu.VMEM((dests, quads * each, lanes), F32)],
        compiler_params=params(),
        cost_estimate=LIGHT,
        name="project",
    )(live_rows, normed, live_cols, weight)


def at_chunk(steps, body, *groups):
    start = 0
    for chunk, count in enumerate(steps):
        here = (pl.program_id(0) >= start) & (pl.program_id(0) < start + count)
        pl.when(here)(functools.partial(body, *[group[chunk] for group in groups]))
        start += count


def chunk_tiles(shape, steps):
    def tile(start, count):
        return pl.BlockSpec(shape, lambda i: (jnp.clip(i - start, 0, count - 1), 0, 0))

    return [tile(sum(steps[:chunk]), count) for chunk, count in enumerate(steps)]


def logit_kernel(live_ref, *refs, steps):
    normeds, weight_ref, out_ref = refs[: len(steps)], refs[len(steps)], refs[-1]
    block = out_ref.shape[0]

    def rows(normed_ref):
        for i in range(block):
            live = live_ref[pl.program_id(0) * block + i]
            out_ref[i] = lax.dot_general(
                weight_ref[...], normed_ref[i], NT, preferred_element_type=F32
            ) + MASK_PENALTY * (live - 1.0)

    at_chunk(steps, rows, normeds)


def logit(live_rows, normeds, weight, after):
    _, cols, wide = normeds[0].shape
    block = 16
    steps = [normed.shape[0] // block for normed in normeds]
    heads = weight.shape[0]
    return pl.pallas_call(
        functools.partial(logit_kernel, steps=steps),
        grid=(sum(steps),),
        in_specs=[pl.BlockSpec(memory_space=pltpu.SMEM)]
        + chunk_tiles((block, cols, wide), steps)
        + [whole(weight.shape)]
        + anywhere(after),
        out_specs=pl.BlockSpec((block, heads, cols), lambda i: (i, 0, 0)),
        out_shape=jax.ShapeDtypeStruct((sum(steps) * block, heads, cols), F32),
        compiler_params=params(),
        cost_estimate=LIGHT,
        name="logit",
    )(live_rows, *normeds, weight, *after)


def assemble_kernel(recv_ref, *refs, row_count, pos_count, spans):
    left_ref, right_ref, flat_ref, rows_ref = refs[-4:]
    channel = pl.program_id(0)
    lanes = recv_ref.shape[2]
    each = left_ref.shape[2]
    height = recv_ref.shape[1] // spans
    stride = height // each
    groups = pos_count // 4
    tiles = lanes // LANES

    @pl.when(channel == 0)
    def _():
        for src in range(row_count * pos_count):
            value = recv_ref[src].astype(F32)
            for t in range(tiles):
                flat_ref[src, t] = value[:, t * LANES : (t + 1) * LANES]

    def block(row, group, index):
        packed = []
        index = index + group // groups * height
        for p in range(4):
            src = row * pos_count + group % groups * 4 + p
            packed.append(
                [flat_ref[src, t, pl.ds(index, each, stride=stride), :] for t in range(tiles)]
            )
        return exchange_blocks(packed)

    for row in range(row_count):
        for group in range(groups * spans):
            span = slice(group * lanes, (group + 1) * lanes)
            left = block(row, group, channel)
            right = block(row, group, channel + stride // 2)
            for a in range(QUAD):
                left_ref[0, row * QUAD + a, :, span] = jnp.concatenate(left[a], axis=1).astype(BF16)
                for t in range(tiles):
                    rows_ref[t, pl.ds(a, each, stride=QUAD), :] = right[a][t]
            for t in range(tiles):
                at = slice(group * lanes + t * LANES, group * lanes + (t + 1) * LANES)
                right_ref[0, row, 0, :, at] = rows_ref[t].astype(BF16)


def assemble(chunk, chunks, spans, received, sides, after, row_count, pos_count, cols):
    sources, height, lanes = received.shape
    depth = spans * pos_count * cols
    each = depth // (row_count * QUAD * chunks)
    channels = height // spans // each // 2
    blocks = row_count * QUAD
    shapes = [
        (channels, blocks, each * chunks, depth),
        (channels, row_count, chunks, QUAD * each, depth),
    ]
    return pl.pallas_call(
        functools.partial(
            assemble_kernel, row_count=row_count, pos_count=pos_count, spans=spans
        ),
        grid=(channels,),
        in_specs=[whole(received.shape)] + anywhere(sides) + anywhere(after),
        out_specs=[
            pl.BlockSpec((1, blocks, each, depth), lambda c: (c, 0, chunk, 0)),
            pl.BlockSpec((1, row_count, 1, QUAD * each, depth), lambda c: (c, 0, chunk, 0, 0)),
        ],
        out_shape=[jax.ShapeDtypeStruct(shape, BF16) for shape in shapes],
        input_output_aliases={1: 0, 2: 1} if sides else {},
        scratch_shapes=[
            pltpu.VMEM((sources, lanes // LANES, height, LANES), F32),
            pltpu.VMEM((lanes // LANES, QUAD * each, LANES), F32),
        ],
        compiler_params=params(),
        cost_estimate=LIGHT,
        name="assemble",
    )(received, *sides, *after)


def multiply_kernel(left_ref, right_ref, *refs, pos_count):
    out_ref, tmp_ref = refs[-2:]
    channel = pl.program_id(0)
    channels = pl.num_programs(0)
    lanes = out_ref.shape[2]
    _, blocks, each, depth = left_ref.shape
    row_count = blocks // QUAD
    unit = lanes // 12
    stride = out_ref.shape[1] // each
    tiles = lanes // LANES
    for group in range(pos_count // 4):
        starts = [(group * 4 + p) * 3 * unit for p in range(4)]
        wanted = jnp.concatenate(
            [right_ref[0, start : start + 2 * unit] for start in starts]
            + [right_ref[0, start + 2 * unit : start + 3 * unit] for start in starts],
            axis=0,
        )
        for row in range(row_count):
            left = left_ref[0, row * QUAD : (row + 1) * QUAD].reshape(QUAD * each, depth)
            value = lax.dot_general(left, wanted, NT, preferred_element_type=F32)
            packed = [
                [
                    value[a * each : (a + 1) * each, t * LANES : (t + 1) * LANES]
                    for t in range(tiles)
                ]
                for a in range(QUAD)
            ]
            for p, part in enumerate(exchange_blocks(packed)):
                dest = row * pos_count + group * 4 + p
                for t in range(tiles):
                    tmp_ref[dest, t, pl.ds(channel, each, stride=stride), :] = part[t]

    @pl.when(channel == channels - 1)
    def _():
        for dest in range(row_count * pos_count):
            for t in range(tiles):
                out_ref[dest, :, t * LANES : (t + 1) * LANES] = tmp_ref[dest, t].astype(BF16)


def multiply(left, right, after, pos_count, cols):
    count, blocks, each, depth = left.shape
    lanes = QUAD * cols
    shape = (blocks // QUAD * pos_count, each * count, lanes)
    return pl.pallas_call(
        functools.partial(multiply_kernel, pos_count=pos_count),
        grid=(count,),
        in_specs=[
            pl.BlockSpec((1, blocks, each, depth), lambda c: (c, 0, 0, 0)),
            pl.BlockSpec((1, depth, depth), lambda c: (c, 0, 0)),
        ]
        + anywhere(after),
        out_specs=whole(shape),
        out_shape=jax.ShapeDtypeStruct(shape, BF16),
        scratch_shapes=[pltpu.VMEM((shape[0], lanes // LANES, shape[1], LANES), F32)],
        compiler_params=params(),
        cost_estimate=LIGHT,
        name="multiply",
    )(left, right, *after)


def assemble_half_kernel(half_ref, *refs, row_count, pos_count, parts):
    recvs = refs[:parts]
    left_ref, own_ref, send_ref, flat_ref, right_ref = refs[-5:]
    channel = pl.program_id(0)
    lanes = recvs[0].shape[2]
    unit = lanes // 12
    cols = 3 * unit
    each = send_ref.shape[1] // (row_count * QUAD)
    stride = sum(recv.shape[1] for recv in recvs) // each
    groups = pos_count // 4
    tiles = lanes // LANES
    per_row = each * QUAD // cols

    @pl.when(channel == 0)
    def _():
        for src in range(row_count * pos_count):
            start = 0
            for recv in recvs:
                value = recv[src].astype(F32)
                end = start + recv.shape[1]
                for t in range(tiles):
                    flat_ref[src, t, start:end] = value[:, t * LANES : (t + 1) * LANES]
                start = end

    def block(row, group, index):
        packed = []
        for p in range(4):
            src = row * pos_count + group * 4 + p
            packed.append(
                [flat_ref[src, t, pl.ds(index, each, stride=stride), :] for t in range(tiles)]
            )
        return exchange_blocks(packed)

    for row in range(row_count):
        for group in range(groups):
            span = slice(group * lanes, (group + 1) * lanes)
            left = block(row, group, channel)
            for a in range(QUAD):
                start = (row * QUAD + a) * each
                left_ref[0, start : start + each, span] = jnp.concatenate(left[a], axis=1).astype(
                    BF16
                )
            right = block(row, group, channel + stride // 2)
            for a in range(QUAD):
                for piece in range(per_row):
                    place = row * per_row + piece
                    base = (place // 4) * lanes
                    low = piece * (cols // QUAD)
                    mid = low + 2 * unit // QUAD
                    high = low + cols // QUAD
                    first = base + (place % 4) * 2 * unit + a
                    second = base + 8 * unit + (place % 4) * unit + a
                    for t in range(tiles):
                        value = right[a][t]
                        at = group * tiles + t
                        right_ref[at, pl.ds(first, mid - low, stride=QUAD), :] = value[low:mid]
                        right_ref[at, pl.ds(second, high - mid, stride=QUAD), :] = value[mid:high]
    width = pos_count * cols
    own = pl.multiple_of(half_ref[0] * width, width)
    other = pl.multiple_of((1 - half_ref[0]) * width, width)
    theirs = []
    for at in range(groups * tiles):
        span = slice(at * LANES, (at + 1) * LANES)
        own_ref[0, :, span] = right_ref[at, pl.ds(own, width), :].astype(BF16)
        theirs.append(right_ref[at, pl.ds(other, width), :].astype(BF16))
    theirs = jnp.concatenate(theirs, axis=1)
    for row in range(row_count):
        span = slice(row * QUAD * each, (row + 1) * QUAD * each)
        send_ref[0, span] = lax.dot_general(
            left_ref[0, span], theirs, NT, preferred_element_type=F32
        ).astype(BF16)


def assemble_half(half, received, after, row_count, pos_count, cols):
    sources, _, lanes = received[0].shape
    height = sum(part.shape[1] for part in received)
    each = (2 * pos_count * cols) // (row_count * QUAD)
    channels = height // each // 2
    depth = pos_count * cols
    rows = 2 * depth
    return pl.pallas_call(
        functools.partial(
            assemble_half_kernel, row_count=row_count, pos_count=pos_count, parts=len(received)
        ),
        grid=(channels,),
        in_specs=[pl.BlockSpec(memory_space=pltpu.SMEM)]
        + [whole(part.shape) for part in received]
        + anywhere(after),
        out_specs=[
            pl.BlockSpec((1, rows, depth), lambda c: (c, 0, 0)),
            pl.BlockSpec((1, depth, depth), lambda c: (c, 0, 0)),
            pl.BlockSpec((1, rows, depth), lambda c: (c, 0, 0)),
        ],
        out_shape=[
            jax.ShapeDtypeStruct((channels, rows, depth), BF16),
            jax.ShapeDtypeStruct((channels, depth, depth), BF16),
            jax.ShapeDtypeStruct((channels, rows, depth), BF16),
        ],
        scratch_shapes=[
            pltpu.VMEM((sources, lanes // LANES, height, LANES), F32),
            pltpu.VMEM((depth // LANES, rows, LANES), F32),
        ],
        compiler_params=params(),
        cost_estimate=LIGHT,
        name="assemble_half",
    )(half, *received, *after)


def combine_kernel(left_ref, own_ref, recv_ref, *refs, row_count, pos_count):
    out_ref, tmp_ref = refs[-2:]
    channel = pl.program_id(0)
    channels = pl.num_programs(0)
    lanes = out_ref.shape[2]
    each = left_ref.shape[1] // (row_count * QUAD)
    stride = out_ref.shape[1] // each
    tiles = lanes // LANES
    for row in range(row_count):
        for group in range(pos_count // 4):
            cols = slice(group * lanes, (group + 1) * lanes)
            span = slice(row * QUAD * each, (row + 1) * QUAD * each)
            value = lax.dot_general(
                left_ref[0, span], own_ref[0, cols], NT, preferred_element_type=F32
            )
            value = value + recv_ref[0, span, cols].astype(F32)
            blocks = [
                [
                    value[a * each : (a + 1) * each, t * LANES : (t + 1) * LANES]
                    for t in range(tiles)
                ]
                for a in range(QUAD)
            ]
            for p, value in enumerate(exchange_blocks(blocks)):
                dest = row * pos_count + group * 4 + p
                for t in range(tiles):
                    tmp_ref[dest, t, pl.ds(channel, each, stride=stride), :] = value[t]

    @pl.when(channel == channels - 1)
    def _():
        for dest in range(row_count * pos_count):
            for t in range(tiles):
                out_ref[dest, :, t * LANES : (t + 1) * LANES] = tmp_ref[dest, t].astype(BF16)


def combine(left, own, received, after, row_count, pos_count, cols):
    channels, rows, depth = left.shape
    each = rows // (row_count * QUAD)
    shape = (row_count * pos_count, each * channels, QUAD * cols)
    return pl.pallas_call(
        functools.partial(combine_kernel, row_count=row_count, pos_count=pos_count),
        grid=(channels,),
        in_specs=[
            pl.BlockSpec((1, rows, depth), lambda c: (c, 0, 0)),
            pl.BlockSpec((1, depth, depth), lambda c: (c, 0, 0)),
            pl.BlockSpec((1, rows, depth), lambda c: (c, 0, 0)),
        ]
        + anywhere(after),
        out_specs=whole(shape),
        out_shape=jax.ShapeDtypeStruct(shape, BF16),
        scratch_shapes=[pltpu.VMEM((shape[0], shape[2] // LANES, shape[1], LANES), F32)],
        compiler_params=params(),
        cost_estimate=LIGHT,
        name="combine",
    )(left, own, received, *after)


def merge_kernel(*refs, steps):
    def put(piece):
        refs[-1][...] = piece[...]

    at_chunk(steps, put, refs[: len(steps)])


def merge(pieces, first, height, unit, into):
    sources, _, lanes = pieces[0].shape
    steps = [piece.shape[1] // unit for piece in pieces]

    def block(start, count):
        return pl.BlockSpec(
            (sources, unit, lanes), lambda i: (0, jnp.clip(i - start, 0, count - 1), 0)
        )

    return pl.pallas_call(
        functools.partial(merge_kernel, steps=steps),
        grid=(sum(steps),),
        in_specs=[block(sum(steps[:at]), count) for at, count in enumerate(steps)] + anywhere(into),
        out_specs=pl.BlockSpec((sources, unit, lanes), lambda i: (0, i + first // unit, 0)),
        out_shape=jax.ShapeDtypeStruct((sources, height, lanes), BF16),
        input_output_aliases={len(pieces): 0} if into else {},
        compiler_params=params(),
        cost_estimate=LIGHT,
        name="merge",
    )(*pieces, *into)


def partial_kernel(place_ref, logit_ref, *refs, row_count, col_count):
    sides, refs = refs[:col_count], refs[col_count:]
    project_ref, outs, exp_ref, value_ref = refs[0], refs[1 : 1 + row_count], *refs[-2:]
    rows, heads, cols = logit_ref.shape
    wide = value_ref.shape[2] // heads
    per_row = col_count // row_count
    for u, side in enumerate(sides):
        index = lax.rem(place_ref[1] + u, col_count)
        part = lax.rem(place_ref[0] + row_count - index // per_row, row_count)
        span = pl.multiple_of(lax.rem(index, per_row) * cols, cols)
        value_ref[part, pl.ds(span, cols), :] = jnp.dot(
            side[...], project_ref[...], preferred_element_type=F32
        ).astype(BF16)
    top = jnp.max(logit_ref[...], axis=0)
    powers = jnp.exp(logit_ref[...] - top[None])
    total = jnp.sum(powers, axis=0)
    exp_ref[:, 0:cols] = powers.reshape(rows * heads, cols)
    for h in range(heads):
        weights = exp_ref[pl.ds(h, rows, stride=heads), :][:, :cols].astype(BF16)
        for t, out in enumerate(outs):
            out[h, :cols] = lax.dot_general(
                weights,
                value_ref[t, :, h * wide : (h + 1) * wide],
                TN,
                preferred_element_type=F32,
            )
            out[h, cols:] = jnp.zeros((out.shape[1] - cols, wide), F32)
            out[h, cols : cols + 1, 0:cols] = top[h : h + 1]
            out[h, cols + 1 : cols + 2, 0:cols] = total[h : h + 1]


def partial_average(place, logits, sides, w_value):
    rows, heads, cols = logits.shape
    wide = w_value.shape[1] // heads
    row_count = len(sides) * cols // rows
    shape = (heads, cols + 8, wide)
    return pl.pallas_call(
        functools.partial(partial_kernel, row_count=row_count, col_count=len(sides)),
        grid=(1,),
        in_specs=[pl.BlockSpec(memory_space=pltpu.SMEM)]
        + [whole(v.shape) for v in (logits, *sides, w_value)],
        out_specs=[whole(shape)] * row_count,
        out_shape=[jax.ShapeDtypeStruct(shape, F32)] * row_count,
        scratch_shapes=[
            pltpu.VMEM((rows * heads, LANES), F32),
            pltpu.VMEM((row_count, rows, w_value.shape[1]), BF16),
        ],
        compiler_params=params(),
        cost_estimate=LIGHT,
        name="partial",
    )(place, logits, *sides, w_value)


def average_kernel(*refs):
    parts, (gate_ref, align_ref, weight_ref, out_ref) = refs[:-4], refs[-4:]
    heads, cols, _ = gate_ref.shape
    here = lax.broadcasted_iota(jnp.int32, (cols, cols), 0)
    there = lax.broadcasted_iota(jnp.int32, (cols, cols), 1)
    out = align_ref[...].astype(F32)
    for h in range(heads):
        tops = [part[h, cols : cols + 1, 0:cols] for part in parts]
        sums = [part[h, cols + 1 : cols + 2, 0:cols] for part in parts]
        top = functools.reduce(jnp.maximum, tops)
        scales = [jnp.exp(t - top) for t in tops]
        total = sum(scale * each for scale, each in zip(scales, sums))
        summed = jnp.zeros(gate_ref.shape[1:], F32)
        for part, scale in zip(parts, scales):
            factor = jnp.where(here == there, scale / total, 0.0)
            summed += jnp.dot(
                factor,
                part[h, :cols],
                precision=lax.Precision.HIGHEST,
                preferred_element_type=F32,
            )
        gated = (gate_ref[h] * summed).astype(BF16)
        out += jnp.dot(gated, weight_ref[h], preferred_element_type=F32)
    out_ref[...] = out.astype(BF16)


def average(parts, gate, align, weight):
    operands = [*parts, gate, align, weight]
    return pl.pallas_call(
        average_kernel,
        grid=(1,),
        in_specs=[whole(v.shape) for v in operands],
        out_specs=whole(align.shape),
        out_shape=jax.ShapeDtypeStruct(align.shape, BF16),
        compiler_params=params(),
        cost_estimate=LIGHT,
        name="average",
    )(*operands)


def finish_kernel(*refs, parts, steps):
    chunks = len(steps)
    products = refs[:parts]
    mids = refs[parts : parts + chunks]
    normeds = refs[parts + chunks : parts + 2 * chunks]
    gate_ref, weight_ref, out_ref = refs[parts + 2 * chunks : parts + 2 * chunks + 3]
    flat = refs[parts + 2 * chunks + 3 :]
    quads = out_ref.shape[0] // QUAD
    lanes = products[0].shape[2]
    tiles = range(lanes // LANES)
    for product, tmp in zip(products, flat):
        sources, height, _ = product.shape
        for src in range(sources):
            value = product[src].astype(F32)
            for t in tiles:
                tmp[t, src * height : (src + 1) * height] = value[:, t * LANES : (t + 1) * LANES]

    def rows(mid_ref, normed_ref):
        for m in range(quads):
            pieces = []
            for product, tmp in zip(products, flat):
                sources, height, _ = product.shape
                each = height // quads
                for k in range(each):
                    pieces.append(
                        jnp.concatenate(
                            [tmp[t, pl.ds(m * each + k, sources, stride=height), :] for t in tiles],
                            axis=1,
                        )
                    )
            normed = standardize_features(jnp.concatenate(pieces, axis=0), 0).astype(BF16)
            out = lax.dot_general(normed, weight_ref[...], TN, preferred_element_type=F32)
            for a, value in enumerate(unpack_rows(out)):
                i = QUAD * m + a
                gate = sigmoid(jnp.dot(normed_ref[i], gate_ref[...], preferred_element_type=F32))
                out_ref[i] = (mid_ref[i].astype(F32) + gate * value).astype(BF16)

    at_chunk(steps, rows, mids, normeds)


def finish(products, mids, normeds, w_gate, w_final):
    _, cols, wide = mids[0].shape
    lanes = products[0].shape[2]
    total = sum(mid.shape[0] for mid in mids) // QUAD
    heights = [part.shape[1] // total for part in products]
    quads = max(8, 16 // min(heights))
    steps = [mid.shape[0] // QUAD // quads for mid in mids]
    tiles = chunk_tiles((quads * QUAD, cols, wide), steps)
    return pl.pallas_call(
        functools.partial(finish_kernel, parts=len(products), steps=steps),
        grid=(total // quads,),
        in_specs=[
            pl.BlockSpec((part.shape[0], quads * each, lanes), lambda i: (0, i, 0))
            for part, each in zip(products, heights)
        ]
        + tiles * 2
        + [whole(w_gate.shape), whole(w_final.shape)],
        out_specs=pl.BlockSpec((quads * QUAD, cols, wide), lambda i: (i, 0, 0)),
        out_shape=jax.ShapeDtypeStruct((total * QUAD, cols, wide), BF16),
        scratch_shapes=[
            pltpu.VMEM((lanes // LANES, part.shape[0] * quads * each, LANES), F32)
            for part, each in zip(products, heights)
        ],
        compiler_params=params(),
        cost_estimate=LIGHT,
        name="finish",
    )(*products, *mids, *normeds, w_gate, w_final)


def on_device(
    alignment_embedding,
    coupling_embedding,
    amino_validity,
    alignment_validity,
    alignment_matrix,
    tensor_final_matrix,
    coupling_logit_matrix,
    mean_final_matrix,
    trimul_matrices,
    trimul_final_matrix,
):
    seq_each, module_number, feature_count = alignment_embedding.shape
    rows, _, wide = coupling_embedding.shape
    row_count = lax.axis_size("row")
    pos_count = lax.axis_size("pos")
    col_count = 2 * pos_count
    row_index = lax.axis_index("row")
    half = lax.axis_index("half")
    col_index = half * pos_count + lax.axis_index("pos")
    seqs = seq_each * row_count
    active_entries = amino_validity.astype(F32)
    sequence_index = lax.broadcasted_iota(jnp.int32, alignment_validity.shape, 0)
    present_entries = (
        jnp.where(sequence_index == 0, F32(1.0), alignment_validity.astype(F32))
        * active_entries[None, :]
    )
    row_start = row_index * rows
    col_start = col_index * module_number
    present_rows = lax.dynamic_slice_in_dim(present_entries, row_start, rows, 1)
    present_cols = lax.dynamic_slice_in_dim(present_entries, col_start, module_number, 1)
    live_rows = lax.dynamic_slice_in_dim(active_entries, row_start, rows, 0)
    live_cols = lax.dynamic_slice_in_dim(active_entries, col_start, module_number, 0)

    own_start = (row_index * seq_each, col_start)
    present_own = lax.dynamic_slice(present_entries, own_start, (seq_each, module_number))
    own_normed = standardize_features(alignment_embedding.astype(F32), 2).astype(BF16)
    own_normed = own_normed.reshape(seq_each * module_number, feature_count)

    def project_msa(matrix):
        return jnp.dot(own_normed, matrix, preferred_element_type=F32).reshape(
            seq_each, module_number, -1
        )

    own_right = project_msa(alignment_matrix[:, TENSOR_FEATURES : 2 * TENSOR_FEATURES])
    own_right = (own_right * present_own[:, :, None]).astype(BF16)
    own_rows = jnp.transpose(
        own_normed.reshape(seq_each, module_number, feature_count), (1, 0, 2)
    ).reshape(module_number, -1)
    apart = jnp.eye(seq_each, dtype=BF16)
    w_left = apart[:, :, None, None] * alignment_matrix[:, :TENSOR_FEATURES]
    w_left = w_left.reshape(seq_each, seq_each * feature_count, TENSOR_FEATURES)
    per_row = rows // module_number
    lefts = []
    for t in range(col_count):
        pairs = []
        for r in range(row_count):
            for q in range(col_count):
                to = (r * per_row + q % per_row - t) % col_count
                pairs.append((r * col_count + q, q // per_row * col_count + to))
        lefts.append(lax.ppermute(own_rows, AXES, pairs))
    rights = [own_right]
    for t in range(1, row_count):
        pairs = [(r, (r - t) % row_count) for r in range(row_count)]
        rights.append(lax.ppermute(own_right, "row", pairs))

    w_tensor = tensor_final_matrix.reshape(TENSOR_FEATURES, TENSOR_FEATURES * wide)
    unit = module_number // 3
    live_packed = jnp.concatenate(
        [live_cols[: 2 * unit]] * QUAD + [live_cols[2 * unit :]] * QUAD
    )[None]
    devices = row_count * col_count
    w_kinds = trimul_matrices[:, : 4 * CTRI].T.reshape(2, 2, CTRI, wide)
    w_logit = coupling_logit_matrix.T

    def side_weights(part):
        return jnp.transpose(part, (1, 2, 0, 3, 4)).reshape(-1, wide)

    def exchange(block, axes):
        return lax.all_to_all(block, axes, split_axis=0, concat_axis=0, tiled=True)

    def front_rows(first_row, count, after):
        return front(
            first_row,
            count,
            place,
            lefts,
            rights,
            present_rows,
            coupling_embedding,
            w_tensor,
            present_cols.T.astype(BF16),
            w_left,
            after,
        )

    def project_rows(first_row, normed, weight, dests):
        return project(first_row, live_rows, normed, live_packed, weight, dests)

    place = jnp.stack([row_index, col_index]).astype(jnp.int32)

    def by_head(part):
        part = part.reshape(seq_each, module_number, MEAN_GROUPS, GROUP_FEATURES)
        return jnp.transpose(part, (2, 1, 0, 3)).reshape(MEAN_GROUPS, module_number, -1)

    first = 2 * TENSOR_FEATURES
    middle = first + MEAN_GROUPS * GROUP_FEATURES
    w_value = alignment_matrix[:, first:middle].reshape(
        1, feature_count, MEAN_GROUPS, 1, GROUP_FEATURES
    )
    w_value = (w_value * apart.reshape(seq_each, 1, 1, seq_each, 1)).reshape(
        seq_each * feature_count, -1
    )
    sequence_gate = by_head(jax.nn.sigmoid(project_msa(alignment_matrix[:, middle:])))
    w_mean = mean_final_matrix.reshape(MEAN_GROUPS, 1, GROUP_FEATURES, 1, feature_count)
    w_mean = (w_mean * apart.reshape(1, seq_each, 1, seq_each, 1)).reshape(
        MEAN_GROUPS, seq_each * GROUP_FEATURES, seq_each * feature_count
    )
    align = jnp.transpose(alignment_embedding, (1, 0, 2)).reshape(module_number, -1)

    def gather_parts(parts):
        gathered = list(parts[:1])
        for t in range(1, row_count):
            pairs = [(r, (r - t) % row_count) for r in range(row_count)]
            gathered.append(lax.ppermute(parts[t], "row", pairs))
        return gathered

    group = devices // 2
    shape_of = (row_count, col_count, module_number)
    half_shape = (row_count, pos_count, module_number)
    mids, normeds, returned = [], [], []
    if CTRI // 2 % devices:
        row_chunks = rows // QUAD // 16
        sent, sides = (), ()
        weight = side_weights(w_kinds.reshape(2, 2, devices, -1, wide))
        for chunk in range(row_chunks):
            first_row = chunk * (rows // row_chunks)
            mid, normed = front_rows(first_row, rows // row_chunks, sent)
            block = project_rows(first_row, normed, weight, devices)
            sent = (block,)
            sides = assemble(chunk, row_chunks, 1, exchange(block, AXES), sides, (), *shape_of)
            mids.append(mid)
            normeds.append(normed)
        left, right = sides
        right = right.reshape(right.shape[0], -1, right.shape[-1])
        last = multiply(left, right, (), *shape_of[1:])
        returned.append(exchange(last, AXES))
        logits = logit(live_rows, normeds, w_logit, ())
        parts = partial_average(place, logits, lefts, w_value)
        parts = gather_parts(fence(parts, (last,)))
        orders = [(0, CTRI, devices)]
    else:
        cut = CTRI // 2
        row_chunks = [rows // 3, rows - rows // 3]
        w_half = side_weights(w_kinds[:, :, :cut].reshape(2, 2, group, -1, wide))
        w_both = w_kinds[:, :, cut:].reshape(2, 2, row_count, 2, pos_count, -1, wide)

        def half_weights(which):
            part = lax.dynamic_index_in_dim(w_both, which, 3, keepdims=False)
            return side_weights(part.reshape(2, 2, group, -1, wide))

        w_own, w_other = half_weights(half), half_weights(1 - half)
        swap = [(0, 1), (1, 0)]
        received, crossed, kept, ahead = [], [], [], ()
        for chunk, count in enumerate(row_chunks):
            first_row = sum(row_chunks[:chunk])
            mid, normed = front_rows(first_row, count, ahead)
            mids.append(mid)
            normeds.append(normed)
            to_half = project_rows(first_row, normed, w_half, group)
            to_other = project_rows(first_row, normed, w_other, group)
            to_other, to_half, w_own = fence([to_other, to_half, w_own], received + crossed)
            crossed.append(lax.ppermute(to_other, "half", swap))
            received.append(exchange(to_half, GROUP))
            ahead = (w_own,)
            kept.append(project_rows(first_row, normed, w_own, group))
        half_scalar = half.astype(jnp.int32).reshape(1)
        logits = logit(live_rows, normeds, w_logit, tuple(kept))
        parts = partial_average(place, logits, lefts, w_value)
        height = 2 * sum(part.shape[1] for part in kept)
        unit, last = kept[0].shape[1], height - kept[-1].shape[1]
        merged = merge(kept + crossed[:-1], 0, height, unit, ())
        left, own, theirs = assemble_half(
            half_scalar, received, (parts[0], merged), *half_shape
        )
        merged = merge(crossed[-1:], last, height, unit, (merged,))
        theirs, *parts = fence([theirs, *parts], ())
        partial = lax.ppermute(theirs, "half", swap)
        both = exchange(merged, GROUP)
        parts = gather_parts(parts)
        product = combine(left, own, partial, (both, *parts[1:]), *half_shape)
        returned.append(exchange(product, GROUP))
        left, right = assemble(0, 1, 2, both, (), (product,), *half_shape)
        right = right.reshape(right.shape[0], -1, right.shape[-1])
        last = multiply(left, right, (), *shape_of[1:])
        returned.append(exchange(last, AXES))
        orders = [(0, cut, group), (cut, CTRI, devices)]
    parts = fence(parts, (last,))
    aligned = average(parts, sequence_gate, align, w_mean)
    alignment_updated_embedding = jnp.transpose(
        aligned.reshape(module_number, seq_each, feature_count), (1, 0, 2)
    )
    w_final = jnp.concatenate(
        [
            jnp.transpose(
                trimul_final_matrix[low:high].reshape(sources, -1, wide), (1, 0, 2)
            ).reshape(-1, wide)
            for low, high, sources in orders
        ]
    )
    pair_output = finish(returned, mids, normeds, trimul_matrices[:, 4 * CTRI :], w_final)
    return (alignment_updated_embedding, pair_output)


def solution(mesh):
    rows, cols = mesh.devices.shape
    inner = Mesh(mesh.devices.reshape(rows, 2, cols // 2), AXES)
    tile = P("row", ("half", "pos"), None)
    in_specs = (tile, tile) + (P(),) * 8
    return jax.shard_map(
        on_device, mesh=inner, in_specs=in_specs, out_specs=(tile, tile), check_vma=False
    )
```

```python
import functools

import jax
import jax.numpy as jnp
from jax import lax
from jax.experimental import pallas as pl
from jax.experimental.pallas import tpu as pltpu
from jax.sharding import Mesh, PartitionSpec as P

TENSOR_FEATURES = 32
MEAN_GROUPS = 8
GROUP_FEATURES = 32
CTRI = 128

EPS = 1e-05
MASK_PENALTY = 10000.0
QUAD = 4
LANES = 128
MIB = 1024 * 1024
AXES = ("row", "half", "pos")
GROUP = ("row", "pos")
F32 = jnp.float32
BF16 = jnp.bfloat16
NT = (((1,), (1,)), ((), ()))
TN = (((0,), (0,)), ((), ()))


def standardize_features(values_in, axis):
    centre = values_in - jnp.mean(values_in, axis=axis, keepdims=True)
    spread = jnp.mean(centre * centre, axis=axis, keepdims=True)
    return centre * lax.rsqrt(spread + EPS)


def sigmoid(x):
    return 0.5 * jnp.tanh(0.5 * x) + 0.5


def params():
    return pltpu.CompilerParams(
        vmem_limit_bytes=60 * MIB, dimension_semantics=("arbitrary",)
    )


LIGHT = pl.CostEstimate(flops=1000, bytes_accessed=1000, transcendentals=0)


def whole(shape):
    zeros = (0,) * len(shape)
    return pl.BlockSpec(shape, lambda *_: zeros, pipeline_mode=pl.Buffered(1))


def anywhere(after):
    return [pl.BlockSpec(memory_space=pl.ANY)] * len(after)


def fence(values, after):
    return pl.pallas_call(
        lambda *refs: None,
        in_specs=anywhere(values) + anywhere(after),
        out_specs=anywhere(values),
        out_shape=[jax.ShapeDtypeStruct(v.shape, v.dtype) for v in values],
        input_output_aliases={i: i for i in range(len(values))},
        compiler_params=pltpu.CompilerParams(vmem_limit_bytes=60 * MIB),
        cost_estimate=LIGHT,
        name="fence",
    )(*values, *after)


def pack_rows(rows):
    unit = rows[0].shape[0] // 3
    return jnp.concatenate([r[: 2 * unit] for r in rows] + [r[2 * unit :] for r in rows], axis=0)


def unpack_rows(packed):
    unit = packed.shape[0] // 12
    return [
        jnp.concatenate(
            [
                packed[2 * unit * a : 2 * unit * (a + 1)],
                packed[8 * unit + unit * a : 8 * unit + unit * (a + 1)],
            ],
            axis=0,
        )
        for a in range(QUAD)
    ]


def swap_blocks(first, second, width, lane):
    low = (lane // width) % 2 == 0
    size = first.shape[1]
    return (
        jnp.where(low, first, pltpu.roll(second, width, 1)),
        jnp.where(low, pltpu.roll(first, size - width, 1), second),
    )


def exchange_blocks(packed):
    part = packed
    unit = LANES // 4
    lane = lax.broadcasted_iota(jnp.int32, part[0][0].shape, 1)
    out = [[None] * 3 for _ in range(4)]
    for pair in range(2):
        one, two = part[2 * pair], part[2 * pair + 1]
        for t in range(2):
            out[2 * t][pair], out[2 * t + 1][pair] = swap_blocks(one[t], two[t], 2 * unit, lane)
    u0, u2 = swap_blocks(part[0][2], part[2][2], 2 * unit, lane)
    u1, u3 = swap_blocks(part[1][2], part[3][2], 2 * unit, lane)
    out[0][2], out[1][2] = swap_blocks(u0, u1, unit, lane)
    out[2][2], out[3][2] = swap_blocks(u2, u3, unit, lane)
    return out


def front_kernel(place_ref, *refs, row_count, col_count, first_block):
    lefts, rights = refs[:col_count], refs[col_count : col_count + row_count]
    refs = refs[col_count + row_count :]
    prow_ref, coup_ref, weight_ref, pcol_ref, wleft_ref, pside_ref = refs[:6]
    sides_ref, right_ref, tmp_ref = refs[-3:]
    mid_ref, normed_ref = refs[-5:-3]
    step_at = pl.program_id(0) + first_block
    block, cols, wide = coup_ref.shape
    seq_each, _, width = wleft_ref.shape
    seqs = seq_each * row_count
    per_row = col_count // row_count

    @pl.when(pl.program_id(0) == 0)
    def _():
        for t, part in enumerate(lefts):
            index = lax.rem(t + place_ref[1], col_count)
            span = pl.multiple_of(lax.rem(index, per_row) * cols, cols)
            first = index // per_row * seq_each
            present = pside_ref[pl.ds(span, cols), :]
            seq_lane = lax.broadcasted_iota(jnp.int32, present.shape, 1)
            for k in range(seq_each):
                mask = jnp.sum(
                    jnp.where(seq_lane == first + k, present, 0.0), axis=1, keepdims=True
                )
                left = jnp.dot(part[...], wleft_ref[k], preferred_element_type=F32) * mask
                sides_ref[pl.ds(span * seqs + first + k, cols, stride=seqs), 0:width] = left
        right = jnp.zeros(right_ref.shape, F32)
        feature = lax.broadcasted_iota(jnp.int32, (width, width * seqs), 0)
        target = lax.broadcasted_iota(jnp.int32, (width, width * seqs), 1)
        for t, part in enumerate(rights):
            first = lax.rem(t + place_ref[0], row_count) * seq_each
            for k in range(seq_each):
                spread = (target == feature * seqs + (first + k)).astype(F32).astype(BF16)
                right += jnp.dot(part[k], spread, preferred_element_type=F32)
        right_ref[...] = right.astype(BF16)

    span = block * seqs
    start = pl.multiple_of(step_at * span, span)
    left = sides_ref[pl.ds(start, span), 0:width].astype(BF16)
    features = weight_ref.shape[1] // wide
    step = 4
    for low in range(0, features, step):
        part = jnp.dot(
            left, weight_ref[:, low * wide : (low + step) * wide], preferred_element_type=F32
        ).astype(BF16)
        for i in range(block):
            for d in range(step):
                tmp_ref[
                    i // 2,
                    (low + d) * seqs : (low + d + 1) * seqs,
                    (i % 2) * wide : (i % 2 + 1) * wide,
                ] = part[i * seqs : (i + 1) * seqs, d * wide : (d + 1) * wide]
    row_lane = lax.broadcasted_iota(jnp.int32, prow_ref.shape, 1)
    for pair in range(block // 2):
        update = jnp.dot(right_ref[...], tmp_ref[pair], preferred_element_type=F32)
        here = step_at * block + 2 * pair
        wanted = [jnp.where(row_lane == here + e, prow_ref[...], 0.0) for e in range(2)]
        wanted = [
            jnp.broadcast_to(jnp.sum(w, axis=1, keepdims=True), (seqs, wide)) for w in wanted
        ]
        count = jnp.dot(
            pcol_ref[...], jnp.concatenate(wanted, axis=1).astype(BF16), preferred_element_type=F32
        )
        update = update / jnp.maximum(count, 1.0)
        for e in range(2):
            i = 2 * pair + e
            mid = (coup_ref[i].astype(F32) + update[:, e * wide : (e + 1) * wide]).astype(BF16)
            mid_ref[i] = mid
            normed_ref[i] = standardize_features(mid.astype(F32), 1).astype(BF16)


def front(
    first_row, count, place, lefts, rights, present_rows, coupling, w_tensor, present_cols, w_left, after
):
    rows, cols, wide = coupling.shape
    seqs, width = present_rows.shape[0], w_left.shape[2]
    present_sides = present_rows.T
    block = 8
    steps, offset = count // block, first_row // block
    tile = pl.BlockSpec((block, cols, wide), lambda i: (i, 0, 0))
    return pl.pallas_call(
        functools.partial(
            front_kernel,
            row_count=len(rights),
            col_count=len(lefts),
            first_block=offset,
        ),
        grid=(steps,),
        in_specs=[pl.BlockSpec(memory_space=pltpu.SMEM)]
        + [whole(part.shape) for part in lefts + rights]
        + [
            whole(present_rows.shape),
            pl.BlockSpec((block, cols, wide), lambda i: (i + offset, 0, 0)),
            whole(w_tensor.shape),
            whole(present_cols.shape),
            whole(w_left.shape),
            whole(present_sides.shape),
        ]
        + anywhere(after),
        out_specs=[tile, tile],
        out_shape=[jax.ShapeDtypeStruct((count, cols, wide), BF16)] * 2,
        scratch_shapes=[
            pltpu.VMEM((rows * seqs, LANES), F32),
            pltpu.VMEM((cols, width * seqs), BF16),
            pltpu.VMEM((block // 2, width * seqs, 2 * wide), BF16),
        ],
        compiler_params=params(),
        cost_estimate=LIGHT,
        name="front",
    )(
        place,
        *lefts,
        *rights,
        present_rows,
        coupling,
        w_tensor,
        present_cols,
        w_left,
        present_sides,
        *after,
    )


def exchange_rows(values):
    values = list(values)
    count = len(values)
    step = count // 2
    row = lax.broadcasted_iota(jnp.int32, values[0].shape, 0)
    size = values[0].shape[0]
    while step:
        width = 8 // count * step
        low = (row // width) % 2 == 0
        for m in range(count):
            if m & step == 0:
                one, two = values[m], values[m + step]
                values[m] = jnp.where(low, one, pltpu.roll(two, width, 0))
                values[m + step] = jnp.where(low, pltpu.roll(one, size - width, 0), two)
        step //= 2
    return values


def project_kernel(live_ref, normed_ref, cols_ref, weight_ref, *refs, first_row):
    out_ref, tmp_ref = refs[-2:]
    quads = normed_ref.shape[0] // QUAD
    dests, height, lanes = out_ref.shape
    each = height // quads
    count = dests * each
    unit = lanes // 12
    lane = lax.broadcasted_iota(jnp.int32, (1, lanes), 1)
    place = jnp.where(lane < 8 * unit, lane // (2 * unit), (lane - 8 * unit) // unit)
    group = max(1, 8 // each)
    for first in range(0, quads, group):
        values = []
        for m in range(first, first + group):
            packed = pack_rows([normed_ref[QUAD * m + a] for a in range(QUAD)])
            both = lax.dot_general(weight_ref[...], packed, NT, preferred_element_type=F32)
            row = first_row + (pl.program_id(0) * quads + m) * QUAD
            live = cols_ref[...]
            for a in range(QUAD):
                live = jnp.where(place == a, live * live_ref[row + a], live)
            values.append(sigmoid(both[:count]) * both[count:] * live)
        for b, value in enumerate(exchange_rows(values)):
            size = each * group
            for v in range(count // size):
                tmp_ref[v * group + b, first * each : first * each + size] = value[
                    v * size : (v + 1) * size
                ]
    out_ref[...] = tmp_ref[...].astype(BF16)


def project(first_row, live_rows, normed, live_cols, weight, dests):
    rows, cols, wide = normed.shape
    each = weight.shape[0] // (2 * dests)
    quads = max(8, 16 // each)
    lanes = QUAD * cols
    total = rows // QUAD
    return pl.pallas_call(
        functools.partial(project_kernel, first_row=first_row),
        grid=(total // quads,),
        in_specs=[
            pl.BlockSpec(memory_space=pltpu.SMEM),
            pl.BlockSpec((quads * QUAD, cols, wide), lambda i: (i, 0, 0)),
            whole(live_cols.shape),
            whole(weight.shape),
        ],
        out_specs=pl.BlockSpec((dests, quads * each, lanes), lambda i: (0, i, 0)),
        out_shape=jax.ShapeDtypeStruct((dests, total * each, lanes), BF16),
        scratch_shapes=[pltpu.VMEM((dests, quads * each, lanes), F32)],
        compiler_params=params(),
        cost_estimate=LIGHT,
        name="project",
    )(live_rows, normed, live_cols, weight)


def at_chunk(steps, body, *groups):
    start = 0
    for chunk, count in enumerate(steps):
        here = (pl.program_id(0) >= start) & (pl.program_id(0) < start + count)
        pl.when(here)(functools.partial(body, *[group[chunk] for group in groups]))
        start += count


def chunk_tiles(shape, steps):
    def tile(start, count):
        return pl.BlockSpec(shape, lambda i: (jnp.clip(i - start, 0, count - 1), 0, 0))

    return [tile(sum(steps[:chunk]), count) for chunk, count in enumerate(steps)]


def logit_kernel(live_ref, *refs, steps):
    normeds, weight_ref, out_ref = refs[: len(steps)], refs[len(steps)], refs[-1]
    block = out_ref.shape[0]

    def rows(normed_ref):
        for i in range(block):
            live = live_ref[pl.program_id(0) * block + i]
            out_ref[i] = lax.dot_general(
                weight_ref[...], normed_ref[i], NT, preferred_element_type=F32
            ) + MASK_PENALTY * (live - 1.0)

    at_chunk(steps, rows, normeds)


def logit(live_rows, normeds, weight, after):
    _, cols, wide = normeds[0].shape
    block = 16
    steps = [normed.shape[0] // block for normed in normeds]
    heads = weight.shape[0]
    return pl.pallas_call(
        functools.partial(logit_kernel, steps=steps),
        grid=(sum(steps),),
        in_specs=[pl.BlockSpec(memory_space=pltpu.SMEM)]
        + chunk_tiles((block, cols, wide), steps)
        + [whole(weight.shape)]
        + anywhere(after),
        out_specs=pl.BlockSpec((block, heads, cols), lambda i: (i, 0, 0)),
        out_shape=jax.ShapeDtypeStruct((sum(steps) * block, heads, cols), F32),
        compiler_params=params(),
        cost_estimate=LIGHT,
        name="logit",
    )(live_rows, *normeds, weight, *after)


def assemble_kernel(recv_ref, *refs, row_count, pos_count, spans):
    left_ref, right_ref, flat_ref, rows_ref = refs[-4:]
    channel = pl.program_id(0)
    lanes = recv_ref.shape[2]
    each = left_ref.shape[2]
    height = recv_ref.shape[1] // spans
    stride = height // each
    groups = pos_count // 4
    tiles = lanes // LANES

    @pl.when(channel == 0)
    def _():
        for src in range(row_count * pos_count):
            value = recv_ref[src].astype(F32)
            for t in range(tiles):
                flat_ref[src, t] = value[:, t * LANES : (t + 1) * LANES]

    def block(row, group, index):
        packed = []
        index = index + group // groups * height
        for p in range(4):
            src = row * pos_count + group % groups * 4 + p
            packed.append(
                [flat_ref[src, t, pl.ds(index, each, stride=stride), :] for t in range(tiles)]
            )
        return exchange_blocks(packed)

    for row in range(row_count):
        for group in range(groups * spans):
            span = slice(group * lanes, (group + 1) * lanes)
            left = block(row, group, channel)
            right = block(row, group, channel + stride // 2)
            for a in range(QUAD):
                left_ref[0, row * QUAD + a, :, span] = jnp.concatenate(left[a], axis=1).astype(BF16)
                for t in range(tiles):
                    rows_ref[t, pl.ds(a, each, stride=QUAD), :] = right[a][t]
            for t in range(tiles):
                at = slice(group * lanes + t * LANES, group * lanes + (t + 1) * LANES)
                right_ref[0, row, 0, :, at] = rows_ref[t].astype(BF16)


def assemble(chunk, chunks, spans, received, sides, after, row_count, pos_count, cols):
    sources, height, lanes = received.shape
    depth = spans * pos_count * cols
    each = depth // (row_count * QUAD * chunks)
    channels = height // spans // each // 2
    blocks = row_count * QUAD
    shapes = [
        (channels, blocks, each * chunks, depth),
        (channels, row_count, chunks, QUAD * each, depth),
    ]
    return pl.pallas_call(
        functools.partial(
            assemble_kernel, row_count=row_count, pos_count=pos_count, spans=spans
        ),
        grid=(channels,),
        in_specs=[whole(received.shape)] + anywhere(sides) + anywhere(after),
        out_specs=[
            pl.BlockSpec((1, blocks, each, depth), lambda c: (c, 0, chunk, 0)),
            pl.BlockSpec((1, row_count, 1, QUAD * each, depth), lambda c: (c, 0, chunk, 0, 0)),
        ],
        out_shape=[jax.ShapeDtypeStruct(shape, BF16) for shape in shapes],
        input_output_aliases={1: 0, 2: 1} if sides else {},
        scratch_shapes=[
            pltpu.VMEM((sources, lanes // LANES, height, LANES), F32),
            pltpu.VMEM((lanes // LANES, QUAD * each, LANES), F32),
        ],
        compiler_params=params(),
        cost_estimate=LIGHT,
        name="assemble",
    )(received, *sides, *after)


def multiply_kernel(left_ref, right_ref, *refs, pos_count):
    out_ref, tmp_ref = refs[-2:]
    channel = pl.program_id(0)
    channels = pl.num_programs(0)
    lanes = out_ref.shape[2]
    _, blocks, each, depth = left_ref.shape
    row_count = blocks // QUAD
    unit = lanes // 12
    stride = out_ref.shape[1] // each
    tiles = lanes // LANES
    for group in range(pos_count // 4):
        starts = [(group * 4 + p) * 3 * unit for p in range(4)]
        wanted = jnp.concatenate(
            [right_ref[0, start : start + 2 * unit] for start in starts]
            + [right_ref[0, start + 2 * unit : start + 3 * unit] for start in starts],
            axis=0,
        )
        for row in range(row_count):
            left = left_ref[0, row * QUAD : (row + 1) * QUAD].reshape(QUAD * each, depth)
            value = lax.dot_general(left, wanted, NT, preferred_element_type=F32)
            packed = [
                [
                    value[a * each : (a + 1) * each, t * LANES : (t + 1) * LANES]
                    for t in range(tiles)
                ]
                for a in range(QUAD)
            ]
            for p, part in enumerate(exchange_blocks(packed)):
                dest = row * pos_count + group * 4 + p
                for t in range(tiles):
                    tmp_ref[dest, t, pl.ds(channel, each, stride=stride), :] = part[t]

    @pl.when(channel == channels - 1)
    def _():
        for dest in range(row_count * pos_count):
            for t in range(tiles):
                out_ref[dest, :, t * LANES : (t + 1) * LANES] = tmp_ref[dest, t].astype(BF16)


def multiply(left, right, after, pos_count, cols):
    count, blocks, each, depth = left.shape
    lanes = QUAD * cols
    shape = (blocks // QUAD * pos_count, each * count, lanes)
    return pl.pallas_call(
        functools.partial(multiply_kernel, pos_count=pos_count),
        grid=(count,),
        in_specs=[
            pl.BlockSpec((1, blocks, each, depth), lambda c: (c, 0, 0, 0)),
            pl.BlockSpec((1, depth, depth), lambda c: (c, 0, 0)),
        ]
        + anywhere(after),
        out_specs=whole(shape),
        out_shape=jax.ShapeDtypeStruct(shape, BF16),
        scratch_shapes=[pltpu.VMEM((shape[0], lanes // LANES, shape[1], LANES), F32)],
        compiler_params=params(),
        cost_estimate=LIGHT,
        name="multiply",
    )(left, right, *after)


def assemble_half_kernel(half_ref, *refs, row_count, pos_count, parts):
    recvs = refs[:parts]
    left_ref, own_ref, send_ref, flat_ref, right_ref = refs[-5:]
    channel = pl.program_id(0)
    lanes = recvs[0].shape[2]
    unit = lanes // 12
    cols = 3 * unit
    each = send_ref.shape[1] // (row_count * QUAD)
    stride = sum(recv.shape[1] for recv in recvs) // each
    groups = pos_count // 4
    tiles = lanes // LANES
    per_row = each * QUAD // cols

    @pl.when(channel == 0)
    def _():
        for src in range(row_count * pos_count):
            start = 0
            for recv in recvs:
                value = recv[src].astype(F32)
                end = start + recv.shape[1]
                for t in range(tiles):
                    flat_ref[src, t, start:end] = value[:, t * LANES : (t + 1) * LANES]
                start = end

    def block(row, group, index):
        packed = []
        for p in range(4):
            src = row * pos_count + group * 4 + p
            packed.append(
                [flat_ref[src, t, pl.ds(index, each, stride=stride), :] for t in range(tiles)]
            )
        return exchange_blocks(packed)

    for row in range(row_count):
        for group in range(groups):
            span = slice(group * lanes, (group + 1) * lanes)
            left = block(row, group, channel)
            for a in range(QUAD):
                start = (row * QUAD + a) * each
                left_ref[0, start : start + each, span] = jnp.concatenate(left[a], axis=1).astype(
                    BF16
                )
            right = block(row, group, channel + stride // 2)
            for a in range(QUAD):
                for piece in range(per_row):
                    place = row * per_row + piece
                    base = (place // 4) * lanes
                    low = piece * (cols // QUAD)
                    mid = low + 2 * unit // QUAD
                    high = low + cols // QUAD
                    first = base + (place % 4) * 2 * unit + a
                    second = base + 8 * unit + (place % 4) * unit + a
                    for t in range(tiles):
                        value = right[a][t]
                        at = group * tiles + t
                        right_ref[at, pl.ds(first, mid - low, stride=QUAD), :] = value[low:mid]
                        right_ref[at, pl.ds(second, high - mid, stride=QUAD), :] = value[mid:high]
    width = pos_count * cols
    own = pl.multiple_of(half_ref[0] * width, width)
    other = pl.multiple_of((1 - half_ref[0]) * width, width)
    theirs = []
    for at in range(groups * tiles):
        span = slice(at * LANES, (at + 1) * LANES)
        own_ref[0, :, span] = right_ref[at, pl.ds(own, width), :].astype(BF16)
        theirs.append(right_ref[at, pl.ds(other, width), :].astype(BF16))
    theirs = jnp.concatenate(theirs, axis=1)
    send_ref[0] = lax.dot_general(
        left_ref[0], theirs, NT, preferred_element_type=F32
    ).astype(BF16)


def assemble_half(half, received, after, row_count, pos_count, cols):
    sources, _, lanes = received[0].shape
    height = sum(part.shape[1] for part in received)
    each = (2 * pos_count * cols) // (row_count * QUAD)
    channels = height // each // 2
    depth = pos_count * cols
    rows = 2 * depth
    return pl.pallas_call(
        functools.partial(
            assemble_half_kernel, row_count=row_count, pos_count=pos_count, parts=len(received)
        ),
        grid=(channels,),
        in_specs=[pl.BlockSpec(memory_space=pltpu.SMEM)]
        + [whole(part.shape) for part in received]
        + anywhere(after),
        out_specs=[
            pl.BlockSpec((1, rows, depth), lambda c: (c, 0, 0)),
            pl.BlockSpec((1, depth, depth), lambda c: (c, 0, 0)),
            pl.BlockSpec((1, rows, depth), lambda c: (c, 0, 0)),
        ],
        out_shape=[
            jax.ShapeDtypeStruct((channels, rows, depth), BF16),
            jax.ShapeDtypeStruct((channels, depth, depth), BF16),
            jax.ShapeDtypeStruct((channels, rows, depth), BF16),
        ],
        scratch_shapes=[
            pltpu.VMEM((sources, lanes // LANES, height, LANES), F32),
            pltpu.VMEM((depth // LANES, rows, LANES), F32),
        ],
        compiler_params=params(),
        cost_estimate=LIGHT,
        name="assemble_half",
    )(half, *received, *after)


def combine_kernel(left_ref, own_ref, recv_ref, *refs, row_count, pos_count):
    out_ref, tmp_ref = refs[-2:]
    channel = pl.program_id(0)
    channels = pl.num_programs(0)
    lanes = out_ref.shape[2]
    each = left_ref.shape[1] // (row_count * QUAD)
    stride = out_ref.shape[1] // each
    tiles = lanes // LANES
    for group in range(pos_count // 4):
        cols = slice(group * lanes, (group + 1) * lanes)
        whole_value = lax.dot_general(
            left_ref[0], own_ref[0, cols], NT, preferred_element_type=F32
        )
        for row in range(row_count):
            span = slice(row * QUAD * each, (row + 1) * QUAD * each)
            value = whole_value[span] + recv_ref[0, span, cols].astype(F32)
            blocks = [
                [
                    value[a * each : (a + 1) * each, t * LANES : (t + 1) * LANES]
                    for t in range(tiles)
                ]
                for a in range(QUAD)
            ]
            for p, value in enumerate(exchange_blocks(blocks)):
                dest = row * pos_count + group * 4 + p
                for t in range(tiles):
                    tmp_ref[dest, t, pl.ds(channel, each, stride=stride), :] = value[t]

    @pl.when(channel == channels - 1)
    def _():
        for dest in range(row_count * pos_count):
            for t in range(tiles):
                out_ref[dest, :, t * LANES : (t + 1) * LANES] = tmp_ref[dest, t].astype(BF16)


def combine(left, own, received, after, row_count, pos_count, cols):
    channels, rows, depth = left.shape
    each = rows // (row_count * QUAD)
    shape = (row_count * pos_count, each * channels, QUAD * cols)
    return pl.pallas_call(
        functools.partial(combine_kernel, row_count=row_count, pos_count=pos_count),
        grid=(channels,),
        in_specs=[
            pl.BlockSpec((1, rows, depth), lambda c: (c, 0, 0)),
            pl.BlockSpec((1, depth, depth), lambda c: (c, 0, 0)),
            pl.BlockSpec((1, rows, depth), lambda c: (c, 0, 0)),
        ]
        + anywhere(after),
        out_specs=whole(shape),
        out_shape=jax.ShapeDtypeStruct(shape, BF16),
        scratch_shapes=[pltpu.VMEM((shape[0], shape[2] // LANES, shape[1], LANES), F32)],
        compiler_params=params(),
        cost_estimate=LIGHT,
        name="combine",
    )(left, own, received, *after)


def merge_kernel(*refs, steps):
    def put(piece):
        refs[-1][...] = piece[...]

    at_chunk(steps, put, refs[: len(steps)])


def merge(pieces, first, height, unit, into, after):
    sources, _, lanes = pieces[0].shape
    steps = [piece.shape[1] // unit for piece in pieces]

    def block(start, count):
        return pl.BlockSpec(
            (sources, unit, lanes), lambda i: (0, jnp.clip(i - start, 0, count - 1), 0)
        )

    return pl.pallas_call(
        functools.partial(merge_kernel, steps=steps),
        grid=(sum(steps),),
        in_specs=[block(sum(steps[:at]), count) for at, count in enumerate(steps)]
        + anywhere(into)
        + anywhere(after),
        out_specs=pl.BlockSpec((sources, unit, lanes), lambda i: (0, i + first // unit, 0)),
        out_shape=jax.ShapeDtypeStruct((sources, height, lanes), BF16),
        input_output_aliases={len(pieces): 0} if into else {},
        compiler_params=params(),
        cost_estimate=LIGHT,
        name="merge",
    )(*pieces, *into, *after)


def partial_kernel(place_ref, logit_ref, *refs, row_count, col_count):
    sides, refs = refs[:col_count], refs[col_count:]
    project_ref, outs, exp_ref, value_ref = refs[0], refs[1 : 1 + row_count], *refs[-2:]
    rows, heads, cols = logit_ref.shape
    wide = value_ref.shape[2] // heads
    per_row = col_count // row_count
    for u, side in enumerate(sides):
        index = lax.rem(place_ref[1] + u, col_count)
        part = lax.rem(place_ref[0] + row_count - index // per_row, row_count)
        span = pl.multiple_of(lax.rem(index, per_row) * cols, cols)
        value_ref[part, pl.ds(span, cols), :] = jnp.dot(
            side[...], project_ref[...], preferred_element_type=F32
        ).astype(BF16)
    top = jnp.max(logit_ref[...], axis=0)
    powers = jnp.exp(logit_ref[...] - top[None])
    total = jnp.sum(powers, axis=0)
    exp_ref[:, 0:cols] = powers.reshape(rows * heads, cols)
    for h in range(heads):
        weights = exp_ref[pl.ds(h, rows, stride=heads), :][:, :cols].astype(BF16)
        for t, out in enumerate(outs):
            out[h, :cols] = lax.dot_general(
                weights,
                value_ref[t, :, h * wide : (h + 1) * wide],
                TN,
                preferred_element_type=F32,
            )
            out[h, cols:] = jnp.zeros((out.shape[1] - cols, wide), F32)
            out[h, cols : cols + 1, 0:cols] = top[h : h + 1]
            out[h, cols + 1 : cols + 2, 0:cols] = total[h : h + 1]


def partial_average(place, logits, sides, w_value):
    rows, heads, cols = logits.shape
    wide = w_value.shape[1] // heads
    row_count = len(sides) * cols // rows
    shape = (heads, cols + 8, wide)
    return pl.pallas_call(
        functools.partial(partial_kernel, row_count=row_count, col_count=len(sides)),
        grid=(1,),
        in_specs=[pl.BlockSpec(memory_space=pltpu.SMEM)]
        + [whole(v.shape) for v in (logits, *sides, w_value)],
        out_specs=[whole(shape)] * row_count,
        out_shape=[jax.ShapeDtypeStruct(shape, F32)] * row_count,
        scratch_shapes=[
            pltpu.VMEM((rows * heads, LANES), F32),
            pltpu.VMEM((row_count, rows, w_value.shape[1]), BF16),
        ],
        compiler_params=params(),
        cost_estimate=LIGHT,
        name="partial",
    )(place, logits, *sides, w_value)


def average_kernel(*refs):
    parts, (gate_ref, align_ref, weight_ref, out_ref) = refs[:-4], refs[-4:]
    heads, cols, _ = gate_ref.shape
    here = lax.broadcasted_iota(jnp.int32, (cols, cols), 0)
    there = lax.broadcasted_iota(jnp.int32, (cols, cols), 1)
    out = align_ref[...].astype(F32)
    for h in range(heads):
        tops = [part[h, cols : cols + 1, 0:cols] for part in parts]
        sums = [part[h, cols + 1 : cols + 2, 0:cols] for part in parts]
        top = functools.reduce(jnp.maximum, tops)
        scales = [jnp.exp(t - top) for t in tops]
        total = sum(scale * each for scale, each in zip(scales, sums))
        summed = jnp.zeros(gate_ref.shape[1:], F32)
        for part, scale in zip(parts, scales):
            factor = jnp.where(here == there, scale / total, 0.0)
            summed += jnp.dot(
                factor,
                part[h, :cols],
                precision=lax.Precision.HIGHEST,
                preferred_element_type=F32,
            )
        gated = (gate_ref[h] * summed).astype(BF16)
        out += jnp.dot(gated, weight_ref[h], preferred_element_type=F32)
    out_ref[...] = out.astype(BF16)


def average(parts, gate, align, weight):
    operands = [*parts, gate, align, weight]
    return pl.pallas_call(
        average_kernel,
        grid=(1,),
        in_specs=[whole(v.shape) for v in operands],
        out_specs=whole(align.shape),
        out_shape=jax.ShapeDtypeStruct(align.shape, BF16),
        compiler_params=params(),
        cost_estimate=LIGHT,
        name="average",
    )(*operands)


def finish_kernel(*refs, parts, steps):
    chunks = len(steps)
    products = refs[:parts]
    mids = refs[parts : parts + chunks]
    normeds = refs[parts + chunks : parts + 2 * chunks]
    gate_ref, weight_ref, out_ref = refs[parts + 2 * chunks : parts + 2 * chunks + 3]
    flat = refs[parts + 2 * chunks + 3 :]
    quads = out_ref.shape[0] // QUAD
    lanes = products[0].shape[2]
    tiles = range(lanes // LANES)
    for product, tmp in zip(products, flat):
        sources, height, _ = product.shape
        for src in range(sources):
            value = product[src].astype(F32)
            for t in tiles:
                tmp[t, src * height : (src + 1) * height] = value[:, t * LANES : (t + 1) * LANES]

    def rows(mid_ref, normed_ref):
        count, cols, wide = normed_ref.shape
        gates = sigmoid(
            jnp.dot(
                normed_ref[...].reshape(count * cols, wide),
                gate_ref[...],
                preferred_element_type=F32,
            )
        )
        for m in range(quads):
            pieces = []
            for product, tmp in zip(products, flat):
                sources, height, _ = product.shape
                each = height // quads
                for k in range(each):
                    pieces.append(
                        jnp.concatenate(
                            [tmp[t, pl.ds(m * each + k, sources, stride=height), :] for t in tiles],
                            axis=1,
                        )
                    )
            normed = standardize_features(jnp.concatenate(pieces, axis=0), 0).astype(BF16)
            out = lax.dot_general(normed, weight_ref[...], TN, preferred_element_type=F32)
            for a, value in enumerate(unpack_rows(out)):
                i = QUAD * m + a
                gate = gates[i * cols : (i + 1) * cols]
                out_ref[i] = (mid_ref[i].astype(F32) + gate * value).astype(BF16)

    at_chunk(steps, rows, mids, normeds)


def finish(products, mids, normeds, w_gate, w_final):
    _, cols, wide = mids[0].shape
    lanes = products[0].shape[2]
    total = sum(mid.shape[0] for mid in mids) // QUAD
    heights = [part.shape[1] // total for part in products]
    quads = max(8, 16 // min(heights))
    steps = [mid.shape[0] // QUAD // quads for mid in mids]
    tiles = chunk_tiles((quads * QUAD, cols, wide), steps)
    return pl.pallas_call(
        functools.partial(finish_kernel, parts=len(products), steps=steps),
        grid=(total // quads,),
        in_specs=[
            pl.BlockSpec((part.shape[0], quads * each, lanes), lambda i: (0, i, 0))
            for part, each in zip(products, heights)
        ]
        + tiles * 2
        + [whole(w_gate.shape), whole(w_final.shape)],
        out_specs=pl.BlockSpec((quads * QUAD, cols, wide), lambda i: (i, 0, 0)),
        out_shape=jax.ShapeDtypeStruct((total * QUAD, cols, wide), BF16),
        scratch_shapes=[
            pltpu.VMEM((lanes // LANES, part.shape[0] * quads * each, LANES), F32)
            for part, each in zip(products, heights)
        ],
        compiler_params=params(),
        cost_estimate=LIGHT,
        name="finish",
    )(*products, *mids, *normeds, w_gate, w_final)


def on_device(
    alignment_embedding,
    coupling_embedding,
    amino_validity,
    alignment_validity,
    alignment_matrix,
    tensor_final_matrix,
    coupling_logit_matrix,
    mean_final_matrix,
    trimul_matrices,
    trimul_final_matrix,
):
    seq_each, module_number, feature_count = alignment_embedding.shape
    rows, _, wide = coupling_embedding.shape
    row_count = lax.axis_size("row")
    pos_count = lax.axis_size("pos")
    col_count = 2 * pos_count
    row_index = lax.axis_index("row")
    half = lax.axis_index("half")
    col_index = half * pos_count + lax.axis_index("pos")
    seqs = seq_each * row_count
    active_entries = amino_validity.astype(F32)
    sequence_index = lax.broadcasted_iota(jnp.int32, alignment_validity.shape, 0)
    present_entries = (
        jnp.where(sequence_index == 0, F32(1.0), alignment_validity.astype(F32))
        * active_entries[None, :]
    )
    row_start = row_index * rows
    col_start = col_index * module_number
    present_rows = lax.dynamic_slice_in_dim(present_entries, row_start, rows, 1)
    present_cols = lax.dynamic_slice_in_dim(present_entries, col_start, module_number, 1)
    live_rows = lax.dynamic_slice_in_dim(active_entries, row_start, rows, 0)
    live_cols = lax.dynamic_slice_in_dim(active_entries, col_start, module_number, 0)

    own_start = (row_index * seq_each, col_start)
    present_own = lax.dynamic_slice(present_entries, own_start, (seq_each, module_number))
    own_normed = standardize_features(alignment_embedding.astype(F32), 2).astype(BF16)
    own_normed = own_normed.reshape(seq_each * module_number, feature_count)

    def project_msa(matrix):
        return jnp.dot(own_normed, matrix, preferred_element_type=F32).reshape(
            seq_each, module_number, -1
        )

    own_right = project_msa(alignment_matrix[:, TENSOR_FEATURES : 2 * TENSOR_FEATURES])
    own_right = (own_right * present_own[:, :, None]).astype(BF16)
    own_rows = jnp.transpose(
        own_normed.reshape(seq_each, module_number, feature_count), (1, 0, 2)
    ).reshape(module_number, -1)
    apart = jnp.eye(seq_each, dtype=BF16)
    w_left = apart[:, :, None, None] * alignment_matrix[:, :TENSOR_FEATURES]
    w_left = w_left.reshape(seq_each, seq_each * feature_count, TENSOR_FEATURES)
    per_row = rows // module_number
    lefts = []
    for t in range(col_count):
        pairs = []
        for r in range(row_count):
            for q in range(col_count):
                to = (r * per_row + q % per_row - t) % col_count
                pairs.append((r * col_count + q, q // per_row * col_count + to))
        lefts.append(lax.ppermute(own_rows, AXES, pairs))
    rights = [own_right]
    for t in range(1, row_count):
        pairs = [(r, (r - t) % row_count) for r in range(row_count)]
        rights.append(lax.ppermute(own_right, "row", pairs))

    w_tensor = tensor_final_matrix.reshape(TENSOR_FEATURES, TENSOR_FEATURES * wide)
    unit = module_number // 3
    live_packed = jnp.concatenate(
        [live_cols[: 2 * unit]] * QUAD + [live_cols[2 * unit :]] * QUAD
    )[None]
    devices = row_count * col_count
    w_kinds = trimul_matrices[:, : 4 * CTRI].T.reshape(2, 2, CTRI, wide)
    w_logit = coupling_logit_matrix.T

    def side_weights(part):
        return jnp.transpose(part, (1, 2, 0, 3, 4)).reshape(-1, wide)

    def exchange(block, axes):
        return lax.all_to_all(block, axes, split_axis=0, concat_axis=0, tiled=True)

    def front_rows(first_row, count, after):
        return front(
            first_row,
            count,
            place,
            lefts,
            rights,
            present_rows,
            coupling_embedding,
            w_tensor,
            present_cols.T.astype(BF16),
            w_left,
            after,
        )

    def project_rows(first_row, normed, weight, dests):
        return project(first_row, live_rows, normed, live_packed, weight, dests)

    place = jnp.stack([row_index, col_index]).astype(jnp.int32)

    def by_head(part):
        part = part.reshape(seq_each, module_number, MEAN_GROUPS, GROUP_FEATURES)
        return jnp.transpose(part, (2, 1, 0, 3)).reshape(MEAN_GROUPS, module_number, -1)

    first = 2 * TENSOR_FEATURES
    middle = first + MEAN_GROUPS * GROUP_FEATURES
    w_value = alignment_matrix[:, first:middle].reshape(
        1, feature_count, MEAN_GROUPS, 1, GROUP_FEATURES
    )
    w_value = (w_value * apart.reshape(seq_each, 1, 1, seq_each, 1)).reshape(
        seq_each * feature_count, -1
    )
    sequence_gate = by_head(jax.nn.sigmoid(project_msa(alignment_matrix[:, middle:])))
    w_mean = mean_final_matrix.reshape(MEAN_GROUPS, 1, GROUP_FEATURES, 1, feature_count)
    w_mean = (w_mean * apart.reshape(1, seq_each, 1, seq_each, 1)).reshape(
        MEAN_GROUPS, seq_each * GROUP_FEATURES, seq_each * feature_count
    )
    align = jnp.transpose(alignment_embedding, (1, 0, 2)).reshape(module_number, -1)

    def gather_parts(parts):
        gathered = list(parts[:1])
        for t in range(1, row_count):
            pairs = [(r, (r - t) % row_count) for r in range(row_count)]
            gathered.append(lax.ppermute(parts[t], "row", pairs))
        return gathered

    group = devices // 2
    shape_of = (row_count, col_count, module_number)
    half_shape = (row_count, pos_count, module_number)
    mids, normeds, returned = [], [], []
    if CTRI // 2 % devices:
        row_chunks = rows // QUAD // 16
        sent, sides = (), ()
        weight = side_weights(w_kinds.reshape(2, 2, devices, -1, wide))
        for chunk in range(row_chunks):
            first_row = chunk * (rows // row_chunks)
            mid, normed = front_rows(first_row, rows // row_chunks, sent)
            block = project_rows(first_row, normed, weight, devices)
            sent = (block,)
            sides = assemble(chunk, row_chunks, 1, exchange(block, AXES), sides, (), *shape_of)
            mids.append(mid)
            normeds.append(normed)
        left, right = sides
        right = right.reshape(right.shape[0], -1, right.shape[-1])
        last = multiply(left, right, (), *shape_of[1:])
        returned.append(exchange(last, AXES))
        logits = logit(live_rows, normeds, w_logit, ())
        parts = partial_average(place, logits, lefts, w_value)
        parts = gather_parts(fence(parts, (last,)))
        orders = [(0, CTRI, devices)]
    else:
        cut = CTRI // 2
        row_chunks = [rows // 3, rows - rows // 3]
        w_half = side_weights(w_kinds[:, :, :cut].reshape(2, 2, group, -1, wide))
        w_both = w_kinds[:, :, cut:].reshape(2, 2, row_count, 2, pos_count, -1, wide)

        def half_weights(which):
            part = lax.dynamic_index_in_dim(w_both, which, 3, keepdims=False)
            return side_weights(part.reshape(2, 2, group, -1, wide))

        w_own, w_other = half_weights(half), half_weights(1 - half)
        swap = [(0, 1), (1, 0)]
        received, crossed, kept, ahead = [], [], [], ()
        for chunk, count in enumerate(row_chunks):
            first_row = sum(row_chunks[:chunk])
            mid, normed = front_rows(first_row, count, ahead)
            mids.append(mid)
            normeds.append(normed)
            to_half = project_rows(first_row, normed, w_half, group)
            to_other = project_rows(first_row, normed, w_other, group)
            to_other, to_half, w_own = fence([to_other, to_half, w_own], received + crossed)
            crossed.append(lax.ppermute(to_other, "half", swap))
            received.append(exchange(to_half, GROUP))
            ahead = (w_own,)
            kept.append(project_rows(first_row, normed, w_own, group))
        half_scalar = half.astype(jnp.int32).reshape(1)
        logits = logit(live_rows, normeds, w_logit, tuple(kept))
        parts = partial_average(place, logits, lefts, w_value)
        height = 2 * sum(part.shape[1] for part in kept)
        unit, last = kept[0].shape[1], height - kept[-1].shape[1]
        merged = merge(kept + crossed[:-1], 0, height, unit, (), ())
        left, own, theirs = assemble_half(
            half_scalar, received, (parts[0], merged), *half_shape
        )
        merged = merge(crossed[-1:], last, height, unit, (merged,), (left,))
        theirs, *parts = fence([theirs, *parts], ())
        partial = lax.ppermute(theirs, "half", swap)
        both = exchange(merged, GROUP)
        parts = gather_parts(parts)
        product = combine(left, own, partial, (both, *parts[1:]), *half_shape)
        returned.append(exchange(product, GROUP))
        left, right = assemble(0, 1, 2, both, (), (product,), *half_shape)
        right = right.reshape(right.shape[0], -1, right.shape[-1])
        last = multiply(left, right, (), *shape_of[1:])
        returned.append(exchange(last, AXES))
        orders = [(0, cut, group), (cut, CTRI, devices)]
    parts = fence(parts, (last,))
    aligned = average(parts, sequence_gate, align, w_mean)
    alignment_updated_embedding = jnp.transpose(
        aligned.reshape(module_number, seq_each, feature_count), (1, 0, 2)
    )
    w_final = jnp.concatenate(
        [
            jnp.transpose(
                trimul_final_matrix[low:high].reshape(sources, -1, wide), (1, 0, 2)
            ).reshape(-1, wide)
            for low, high, sources in orders
        ]
    )
    pair_output = finish(returned, mids, normeds, trimul_matrices[:, 4 * CTRI :], w_final)
    return (alignment_updated_embedding, pair_output)


def solution(mesh):
    rows, cols = mesh.devices.shape
    inner = Mesh(mesh.devices.reshape(rows, 2, cols // 2), AXES)
    tile = P("row", ("half", "pos"), None)
    in_specs = (tile, tile) + (P(),) * 8
    return jax.shard_map(
        on_device, mesh=inner, in_specs=in_specs, out_specs=(tile, tile), check_vma=False
    )
```

```python
import functools

import jax
import jax.numpy as jnp
from jax import lax
from jax.experimental import pallas as pl
from jax.experimental.pallas import tpu as pltpu
from jax.sharding import Mesh, PartitionSpec as P

TENSOR_FEATURES = 32
MEAN_GROUPS = 8
GROUP_FEATURES = 32
CTRI = 128

EPS = 1e-05
MASK_PENALTY = 10000.0
QUAD = 4
LANES = 128
MIB = 1024 * 1024
AXES = ("row", "half", "pos")
GROUP = ("row", "pos")
F32 = jnp.float32
BF16 = jnp.bfloat16
NT = (((1,), (1,)), ((), ()))
TN = (((0,), (0,)), ((), ()))


def standardize_features(values_in, axis):
    centre = values_in - jnp.mean(values_in, axis=axis, keepdims=True)
    spread = jnp.mean(centre * centre, axis=axis, keepdims=True)
    return centre * lax.rsqrt(spread + EPS)


def sigmoid(x):
    return 0.5 * jnp.tanh(0.5 * x) + 0.5


def params():
    return pltpu.CompilerParams(
        vmem_limit_bytes=60 * MIB, dimension_semantics=("arbitrary",)
    )


LIGHT = pl.CostEstimate(flops=1000, bytes_accessed=1000, transcendentals=0)


def whole(shape):
    zeros = (0,) * len(shape)
    return pl.BlockSpec(shape, lambda *_: zeros, pipeline_mode=pl.Buffered(1))


def anywhere(after):
    return [pl.BlockSpec(memory_space=pl.ANY)] * len(after)


def fence(values, after):
    return pl.pallas_call(
        lambda *refs: None,
        in_specs=anywhere(values) + anywhere(after),
        out_specs=anywhere(values),
        out_shape=[jax.ShapeDtypeStruct(v.shape, v.dtype) for v in values],
        input_output_aliases={i: i for i in range(len(values))},
        compiler_params=pltpu.CompilerParams(vmem_limit_bytes=60 * MIB),
        cost_estimate=LIGHT,
        name="fence",
    )(*values, *after)


def pack_rows(rows):
    unit = rows[0].shape[0] // 3
    return jnp.concatenate([r[: 2 * unit] for r in rows] + [r[2 * unit :] for r in rows], axis=0)


def unpack_rows(packed):
    unit = packed.shape[0] // 12
    return [
        jnp.concatenate(
            [
                packed[2 * unit * a : 2 * unit * (a + 1)],
                packed[8 * unit + unit * a : 8 * unit + unit * (a + 1)],
            ],
            axis=0,
        )
        for a in range(QUAD)
    ]


def swap_blocks(first, second, width, lane):
    low = (lane // width) % 2 == 0
    size = first.shape[1]
    return (
        jnp.where(low, first, pltpu.roll(second, width, 1)),
        jnp.where(low, pltpu.roll(first, size - width, 1), second),
    )


def exchange_blocks(packed):
    part = packed
    unit = LANES // 4
    lane = lax.broadcasted_iota(jnp.int32, part[0][0].shape, 1)
    out = [[None] * 3 for _ in range(4)]
    for pair in range(2):
        one, two = part[2 * pair], part[2 * pair + 1]
        for t in range(2):
            out[2 * t][pair], out[2 * t + 1][pair] = swap_blocks(one[t], two[t], 2 * unit, lane)
    u0, u2 = swap_blocks(part[0][2], part[2][2], 2 * unit, lane)
    u1, u3 = swap_blocks(part[1][2], part[3][2], 2 * unit, lane)
    out[0][2], out[1][2] = swap_blocks(u0, u1, unit, lane)
    out[2][2], out[3][2] = swap_blocks(u2, u3, unit, lane)
    return out


def front_kernel(place_ref, *refs, row_count, col_count, first_block):
    lefts, rights = refs[:col_count], refs[col_count : col_count + row_count]
    refs = refs[col_count + row_count :]
    prow_ref, coup_ref, weight_ref, pcol_ref, wleft_ref, pside_ref = refs[:6]
    sides_ref, right_ref, tmp_ref = refs[-3:]
    mid_ref, normed_ref = refs[-5:-3]
    step_at = pl.program_id(0) + first_block
    block, cols, wide = coup_ref.shape
    seq_each, _, width = wleft_ref.shape
    seqs = seq_each * row_count
    per_row = col_count // row_count

    @pl.when(pl.program_id(0) == 0)
    def _():
        for t, part in enumerate(lefts):
            index = lax.rem(t + place_ref[1], col_count)
            span = pl.multiple_of(lax.rem(index, per_row) * cols, cols)
            first = index // per_row * seq_each
            present = pside_ref[pl.ds(span, cols), :]
            seq_lane = lax.broadcasted_iota(jnp.int32, present.shape, 1)
            for k in range(seq_each):
                mask = jnp.sum(
                    jnp.where(seq_lane == first + k, present, 0.0), axis=1, keepdims=True
                )
                left = jnp.dot(part[...], wleft_ref[k], preferred_element_type=F32) * mask
                sides_ref[pl.ds(span * seqs + first + k, cols, stride=seqs), 0:width] = left
        right = jnp.zeros(right_ref.shape, F32)
        feature = lax.broadcasted_iota(jnp.int32, (width, width * seqs), 0)
        target = lax.broadcasted_iota(jnp.int32, (width, width * seqs), 1)
        for t, part in enumerate(rights):
            first = lax.rem(t + place_ref[0], row_count) * seq_each
            for k in range(seq_each):
                spread = (target == feature * seqs + (first + k)).astype(F32).astype(BF16)
                right += jnp.dot(part[k], spread, preferred_element_type=F32)
        right_ref[...] = right.astype(BF16)

    span = block * seqs
    start = pl.multiple_of(step_at * span, span)
    left = sides_ref[pl.ds(start, span), 0:width].astype(BF16)
    features = weight_ref.shape[1] // wide
    step = 4
    for low in range(0, features, step):
        part = jnp.dot(
            left, weight_ref[:, low * wide : (low + step) * wide], preferred_element_type=F32
        ).astype(BF16)
        for i in range(block):
            for d in range(step):
                tmp_ref[
                    i // 2,
                    (low + d) * seqs : (low + d + 1) * seqs,
                    (i % 2) * wide : (i % 2 + 1) * wide,
                ] = part[i * seqs : (i + 1) * seqs, d * wide : (d + 1) * wide]
    row_lane = lax.broadcasted_iota(jnp.int32, prow_ref.shape, 1)
    for pair in range(block // 2):
        update = jnp.dot(right_ref[...], tmp_ref[pair], preferred_element_type=F32)
        here = step_at * block + 2 * pair
        wanted = [jnp.where(row_lane == here + e, prow_ref[...], 0.0) for e in range(2)]
        wanted = [
            jnp.broadcast_to(jnp.sum(w, axis=1, keepdims=True), (seqs, wide)) for w in wanted
        ]
        count = jnp.dot(
            pcol_ref[...], jnp.concatenate(wanted, axis=1).astype(BF16), preferred_element_type=F32
        )
        update = update / jnp.maximum(count, 1.0)
        for e in range(2):
            i = 2 * pair + e
            mid = (coup_ref[i].astype(F32) + update[:, e * wide : (e + 1) * wide]).astype(BF16)
            mid_ref[i] = mid
            normed_ref[i] = standardize_features(mid.astype(F32), 1).astype(BF16)


def front(
    first_row, count, place, lefts, rights, present_rows, coupling, w_tensor, present_cols, w_left, after
):
    rows, cols, wide = coupling.shape
    seqs, width = present_rows.shape[0], w_left.shape[2]
    present_sides = present_rows.T
    block = 8
    steps, offset = count // block, first_row // block
    tile = pl.BlockSpec((block, cols, wide), lambda i: (i, 0, 0))
    return pl.pallas_call(
        functools.partial(
            front_kernel,
            row_count=len(rights),
            col_count=len(lefts),
            first_block=offset,
        ),
        grid=(steps,),
        in_specs=[pl.BlockSpec(memory_space=pltpu.SMEM)]
        + [whole(part.shape) for part in lefts + rights]
        + [
            whole(present_rows.shape),
            pl.BlockSpec((block, cols, wide), lambda i: (i + offset, 0, 0)),
            whole(w_tensor.shape),
            whole(present_cols.shape),
            whole(w_left.shape),
            whole(present_sides.shape),
        ]
        + anywhere(after),
        out_specs=[tile, tile],
        out_shape=[jax.ShapeDtypeStruct((count, cols, wide), BF16)] * 2,
        scratch_shapes=[
            pltpu.VMEM((rows * seqs, LANES), F32),
            pltpu.VMEM((cols, width * seqs), BF16),
            pltpu.VMEM((block // 2, width * seqs, 2 * wide), BF16),
        ],
        compiler_params=params(),
        cost_estimate=LIGHT,
        name="front",
    )(
        place,
        *lefts,
        *rights,
        present_rows,
        coupling,
        w_tensor,
        present_cols,
        w_left,
        present_sides,
        *after,
    )


def exchange_rows(values):
    values = list(values)
    count = len(values)
    step = count // 2
    row = lax.broadcasted_iota(jnp.int32, values[0].shape, 0)
    size = values[0].shape[0]
    while step:
        width = 8 // count * step
        low = (row // width) % 2 == 0
        for m in range(count):
            if m & step == 0:
                one, two = values[m], values[m + step]
                values[m] = jnp.where(low, one, pltpu.roll(two, width, 0))
                values[m + step] = jnp.where(low, pltpu.roll(one, size - width, 0), two)
        step //= 2
    return values


def project_kernel(live_ref, normed_ref, cols_ref, weight_ref, *refs, first_row):
    out_ref, tmp_ref = refs[-2:]
    quads = normed_ref.shape[0] // QUAD
    dests, height, lanes = out_ref.shape
    each = height // quads
    count = dests * each
    unit = lanes // 12
    lane = lax.broadcasted_iota(jnp.int32, (1, lanes), 1)
    place = jnp.where(lane < 8 * unit, lane // (2 * unit), (lane - 8 * unit) // unit)
    group = max(1, 8 // each)
    for first in range(0, quads, group):
        values = []
        for m in range(first, first + group):
            packed = pack_rows([normed_ref[QUAD * m + a] for a in range(QUAD)])
            both = lax.dot_general(weight_ref[...], packed, NT, preferred_element_type=F32)
            row = first_row + (pl.program_id(0) * quads + m) * QUAD
            live = cols_ref[...]
            for a in range(QUAD):
                live = jnp.where(place == a, live * live_ref[row + a], live)
            values.append(sigmoid(both[:count]) * both[count:] * live)
        for b, value in enumerate(exchange_rows(values)):
            size = each * group
            for v in range(count // size):
                tmp_ref[v * group + b, first * each : first * each + size] = value[
                    v * size : (v + 1) * size
                ]
    out_ref[...] = tmp_ref[...].astype(BF16)


def project(first_row, live_rows, normed, live_cols, weight, dests):
    rows, cols, wide = normed.shape
    each = weight.shape[0] // (2 * dests)
    quads = max(8, 16 // each)
    lanes = QUAD * cols
    total = rows // QUAD
    return pl.pallas_call(
        functools.partial(project_kernel, first_row=first_row),
        grid=(total // quads,),
        in_specs=[
            pl.BlockSpec(memory_space=pltpu.SMEM),
            pl.BlockSpec((quads * QUAD, cols, wide), lambda i: (i, 0, 0)),
            whole(live_cols.shape),
            whole(weight.shape),
        ],
        out_specs=pl.BlockSpec((dests, quads * each, lanes), lambda i: (0, i, 0)),
        out_shape=jax.ShapeDtypeStruct((dests, total * each, lanes), BF16),
        scratch_shapes=[pltpu.VMEM((dests, quads * each, lanes), F32)],
        compiler_params=params(),
        cost_estimate=LIGHT,
        name="project",
    )(live_rows, normed, live_cols, weight)


def at_chunk(steps, body, *groups):
    start = 0
    for chunk, count in enumerate(steps):
        here = (pl.program_id(0) >= start) & (pl.program_id(0) < start + count)
        pl.when(here)(functools.partial(body, *[group[chunk] for group in groups]))
        start += count


def chunk_tiles(shape, steps):
    def tile(start, count):
        return pl.BlockSpec(shape, lambda i: (jnp.clip(i - start, 0, count - 1), 0, 0))

    return [tile(sum(steps[:chunk]), count) for chunk, count in enumerate(steps)]


def logit_kernel(live_ref, *refs, steps):
    normeds, weight_ref, out_ref = refs[: len(steps)], refs[len(steps)], refs[-1]
    block = out_ref.shape[0]

    def rows(normed_ref):
        for i in range(block):
            live = live_ref[pl.program_id(0) * block + i]
            out_ref[i] = lax.dot_general(
                weight_ref[...], normed_ref[i], NT, preferred_element_type=F32
            ) + MASK_PENALTY * (live - 1.0)

    at_chunk(steps, rows, normeds)


def logit(live_rows, normeds, weight, after):
    _, cols, wide = normeds[0].shape
    block = 16
    steps = [normed.shape[0] // block for normed in normeds]
    heads = weight.shape[0]
    return pl.pallas_call(
        functools.partial(logit_kernel, steps=steps),
        grid=(sum(steps),),
        in_specs=[pl.BlockSpec(memory_space=pltpu.SMEM)]
        + chunk_tiles((block, cols, wide), steps)
        + [whole(weight.shape)]
        + anywhere(after),
        out_specs=pl.BlockSpec((block, heads, cols), lambda i: (i, 0, 0)),
        out_shape=jax.ShapeDtypeStruct((sum(steps) * block, heads, cols), F32),
        compiler_params=params(),
        cost_estimate=LIGHT,
        name="logit",
    )(live_rows, *normeds, weight, *after)


def assemble_kernel(recv_ref, *refs, row_count, pos_count, spans):
    left_ref, right_ref, flat_ref, rows_ref = refs[-4:]
    channel = pl.program_id(0)
    lanes = recv_ref.shape[2]
    each = left_ref.shape[2]
    height = recv_ref.shape[1] // spans
    stride = height // each
    groups = pos_count // 4
    tiles = lanes // LANES

    @pl.when(channel == 0)
    def _():
        for src in range(row_count * pos_count):
            value = recv_ref[src].astype(F32)
            for t in range(tiles):
                flat_ref[src, t] = value[:, t * LANES : (t + 1) * LANES]

    def block(row, group, index):
        packed = []
        index = index + group // groups * height
        for p in range(4):
            src = row * pos_count + group % groups * 4 + p
            packed.append(
                [flat_ref[src, t, pl.ds(index, each, stride=stride), :] for t in range(tiles)]
            )
        return exchange_blocks(packed)

    for row in range(row_count):
        for group in range(groups * spans):
            span = slice(group * lanes, (group + 1) * lanes)
            left = block(row, group, channel)
            right = block(row, group, channel + stride // 2)
            for a in range(QUAD):
                left_ref[0, row * QUAD + a, :, span] = jnp.concatenate(left[a], axis=1).astype(BF16)
                for t in range(tiles):
                    rows_ref[t, pl.ds(a, each, stride=QUAD), :] = right[a][t]
            for t in range(tiles):
                at = slice(group * lanes + t * LANES, group * lanes + (t + 1) * LANES)
                right_ref[0, row, 0, :, at] = rows_ref[t].astype(BF16)


def assemble(chunk, chunks, spans, received, sides, after, row_count, pos_count, cols):
    sources, height, lanes = received.shape
    depth = spans * pos_count * cols
    each = depth // (row_count * QUAD * chunks)
    channels = height // spans // each // 2
    blocks = row_count * QUAD
    shapes = [
        (channels, blocks, each * chunks, depth),
        (channels, row_count, chunks, QUAD * each, depth),
    ]
    return pl.pallas_call(
        functools.partial(
            assemble_kernel, row_count=row_count, pos_count=pos_count, spans=spans
        ),
        grid=(channels,),
        in_specs=[whole(received.shape)] + anywhere(sides) + anywhere(after),
        out_specs=[
            pl.BlockSpec((1, blocks, each, depth), lambda c: (c, 0, chunk, 0)),
            pl.BlockSpec((1, row_count, 1, QUAD * each, depth), lambda c: (c, 0, chunk, 0, 0)),
        ],
        out_shape=[jax.ShapeDtypeStruct(shape, BF16) for shape in shapes],
        input_output_aliases={1: 0, 2: 1} if sides else {},
        scratch_shapes=[
            pltpu.VMEM((sources, lanes // LANES, height, LANES), F32),
            pltpu.VMEM((lanes // LANES, QUAD * each, LANES), F32),
        ],
        compiler_params=params(),
        cost_estimate=LIGHT,
        name="assemble",
    )(received, *sides, *after)


def multiply_kernel(left_ref, right_ref, *refs, pos_count):
    out_ref, tmp_ref = refs[-2:]
    channel = pl.program_id(0)
    channels = pl.num_programs(0)
    lanes = out_ref.shape[2]
    _, blocks, each, depth = left_ref.shape
    row_count = blocks // QUAD
    unit = lanes // 12
    stride = out_ref.shape[1] // each
    tiles = lanes // LANES
    for group in range(pos_count // 4):
        starts = [(group * 4 + p) * 3 * unit for p in range(4)]
        wanted = jnp.concatenate(
            [right_ref[0, start : start + 2 * unit] for start in starts]
            + [right_ref[0, start + 2 * unit : start + 3 * unit] for start in starts],
            axis=0,
        )
        for row in range(row_count):
            left = left_ref[0, row * QUAD : (row + 1) * QUAD].reshape(QUAD * each, depth)
            value = lax.dot_general(left, wanted, NT, preferred_element_type=F32)
            packed = [
                [
                    value[a * each : (a + 1) * each, t * LANES : (t + 1) * LANES]
                    for t in range(tiles)
                ]
                for a in range(QUAD)
            ]
            for p, part in enumerate(exchange_blocks(packed)):
                dest = row * pos_count + group * 4 + p
                for t in range(tiles):
                    tmp_ref[dest, t, pl.ds(channel, each, stride=stride), :] = part[t]

    @pl.when(channel == channels - 1)
    def _():
        for dest in range(row_count * pos_count):
            for t in range(tiles):
                out_ref[dest, :, t * LANES : (t + 1) * LANES] = tmp_ref[dest, t].astype(BF16)


def multiply(left, right, after, pos_count, cols):
    count, blocks, each, depth = left.shape
    lanes = QUAD * cols
    shape = (blocks // QUAD * pos_count, each * count, lanes)
    return pl.pallas_call(
        functools.partial(multiply_kernel, pos_count=pos_count),
        grid=(count,),
        in_specs=[
            pl.BlockSpec((1, blocks, each, depth), lambda c: (c, 0, 0, 0)),
            pl.BlockSpec((1, depth, depth), lambda c: (c, 0, 0)),
        ]
        + anywhere(after),
        out_specs=whole(shape),
        out_shape=jax.ShapeDtypeStruct(shape, BF16),
        scratch_shapes=[pltpu.VMEM((shape[0], lanes // LANES, shape[1], LANES), F32)],
        compiler_params=params(),
        cost_estimate=LIGHT,
        name="multiply",
    )(left, right, *after)


def assemble_half_kernel(half_ref, *refs, row_count, pos_count, parts):
    recvs = refs[:parts]
    left_ref, own_ref, send_ref, flat_ref, right_ref = refs[-5:]
    channel = pl.program_id(0)
    lanes = recvs[0].shape[2]
    unit = lanes // 12
    cols = 3 * unit
    each = send_ref.shape[1] // (row_count * QUAD)
    stride = sum(recv.shape[1] for recv in recvs) // each
    groups = pos_count // 4
    tiles = lanes // LANES
    per_row = each * QUAD // cols

    sorted_rows = stride == 8

    def sort(src, carry):
        start = 0
        for recv in recvs:
            for low in range(0, recv.shape[1], 64):
                value = recv[src, low : low + 64].astype(F32)
                values = exchange_rows([value[8 * i : 8 * i + 8] for i in range(8)])
                for index, part in enumerate(values):
                    at = index * each + start
                    for t in range(tiles):
                        flat_ref[src, t, at : at + 8] = part[:, t * LANES : (t + 1) * LANES]
                start += 8
        return carry

    @pl.when(channel == 0)
    def _():
        if sorted_rows:
            lax.fori_loop(0, row_count * pos_count, sort, 0)
            return
        for src in range(row_count * pos_count):
            start = 0
            for recv in recvs:
                value = recv[src].astype(F32)
                end = start + recv.shape[1]
                for t in range(tiles):
                    flat_ref[src, t, start:end] = value[:, t * LANES : (t + 1) * LANES]
                start = end

    def block(row, group, index):
        if sorted_rows:
            place = pl.ds(pl.multiple_of(index * each, each), each)
        else:
            place = pl.ds(index, each, stride=stride)
        packed = []
        for p in range(4):
            src = row * pos_count + group * 4 + p
            packed.append([flat_ref[src, t, place, :] for t in range(tiles)])
        return exchange_blocks(packed)

    for row in range(row_count):
        for group in range(groups):
            span = slice(group * lanes, (group + 1) * lanes)
            left = block(row, group, channel)
            for a in range(QUAD):
                start = (row * QUAD + a) * each
                left_ref[0, start : start + each, span] = jnp.concatenate(left[a], axis=1).astype(
                    BF16
                )
            right = block(row, group, channel + stride // 2)
            for a in range(QUAD):
                for piece in range(per_row):
                    place = row * per_row + piece
                    base = (place // 4) * lanes
                    low = piece * (cols // QUAD)
                    mid = low + 2 * unit // QUAD
                    high = low + cols // QUAD
                    first = base + (place % 4) * 2 * unit + a
                    second = base + 8 * unit + (place % 4) * unit + a
                    for t in range(tiles):
                        value = right[a][t]
                        at = group * tiles + t
                        right_ref[at, pl.ds(first, mid - low, stride=QUAD), :] = value[low:mid]
                        right_ref[at, pl.ds(second, high - mid, stride=QUAD), :] = value[mid:high]
    width = pos_count * cols
    own = pl.multiple_of(half_ref[0] * width, width)
    other = pl.multiple_of((1 - half_ref[0]) * width, width)
    theirs = []
    for at in range(groups * tiles):
        span = slice(at * LANES, (at + 1) * LANES)
        own_ref[0, :, span] = right_ref[at, pl.ds(own, width), :].astype(BF16)
        theirs.append(right_ref[at, pl.ds(other, width), :].astype(BF16))
    theirs = jnp.concatenate(theirs, axis=1)
    send_ref[0] = lax.dot_general(
        left_ref[0], theirs, NT, preferred_element_type=F32
    ).astype(BF16)


def assemble_half(half, received, after, row_count, pos_count, cols):
    sources, _, lanes = received[0].shape
    height = sum(part.shape[1] for part in received)
    each = (2 * pos_count * cols) // (row_count * QUAD)
    channels = height // each // 2
    depth = pos_count * cols
    rows = 2 * depth
    return pl.pallas_call(
        functools.partial(
            assemble_half_kernel, row_count=row_count, pos_count=pos_count, parts=len(received)
        ),
        grid=(channels,),
        in_specs=[pl.BlockSpec(memory_space=pltpu.SMEM)]
        + [whole(part.shape) for part in received]
        + anywhere(after),
        out_specs=[
            pl.BlockSpec((1, rows, depth), lambda c: (c, 0, 0)),
            pl.BlockSpec((1, depth, depth), lambda c: (c, 0, 0)),
            pl.BlockSpec((1, rows, depth), lambda c: (c, 0, 0)),
        ],
        out_shape=[
            jax.ShapeDtypeStruct((channels, rows, depth), BF16),
            jax.ShapeDtypeStruct((channels, depth, depth), BF16),
            jax.ShapeDtypeStruct((channels, rows, depth), BF16),
        ],
        scratch_shapes=[
            pltpu.VMEM((sources, lanes // LANES, height, LANES), F32),
            pltpu.VMEM((depth // LANES, rows, LANES), F32),
        ],
        compiler_params=params(),
        cost_estimate=LIGHT,
        name="assemble_half",
    )(half, *received, *after)


def combine_kernel(left_ref, own_ref, recv_ref, *refs, row_count, pos_count):
    out_ref, tmp_ref = refs[-2:]
    channel = pl.program_id(0)
    channels = pl.num_programs(0)
    lanes = out_ref.shape[2]
    each = left_ref.shape[1] // (row_count * QUAD)
    stride = out_ref.shape[1] // each
    tiles = lanes // LANES
    for group in range(pos_count // 4):
        cols = slice(group * lanes, (group + 1) * lanes)
        whole_value = lax.dot_general(
            left_ref[0], own_ref[0, cols], NT, preferred_element_type=F32
        )
        for row in range(row_count):
            span = slice(row * QUAD * each, (row + 1) * QUAD * each)
            value = whole_value[span] + recv_ref[0, span, cols].astype(F32)
            blocks = [
                [
                    value[a * each : (a + 1) * each, t * LANES : (t + 1) * LANES]
                    for t in range(tiles)
                ]
                for a in range(QUAD)
            ]
            for p, value in enumerate(exchange_blocks(blocks)):
                dest = row * pos_count + group * 4 + p
                for t in range(tiles):
                    tmp_ref[dest, t, pl.ds(channel, each, stride=stride), :] = value[t]

    @pl.when(channel == channels - 1)
    def _():
        for dest in range(row_count * pos_count):
            for t in range(tiles):
                out_ref[dest, :, t * LANES : (t + 1) * LANES] = tmp_ref[dest, t].astype(BF16)


def combine(left, own, received, after, row_count, pos_count, cols):
    channels, rows, depth = left.shape
    each = rows // (row_count * QUAD)
    shape = (row_count * pos_count, each * channels, QUAD * cols)
    return pl.pallas_call(
        functools.partial(combine_kernel, row_count=row_count, pos_count=pos_count),
        grid=(channels,),
        in_specs=[
            pl.BlockSpec((1, rows, depth), lambda c: (c, 0, 0)),
            pl.BlockSpec((1, depth, depth), lambda c: (c, 0, 0)),
            pl.BlockSpec((1, rows, depth), lambda c: (c, 0, 0)),
        ]
        + anywhere(after),
        out_specs=whole(shape),
        out_shape=jax.ShapeDtypeStruct(shape, BF16),
        scratch_shapes=[pltpu.VMEM((shape[0], shape[2] // LANES, shape[1], LANES), F32)],
        compiler_params=params(),
        cost_estimate=LIGHT,
        name="combine",
    )(left, own, received, *after)


def merge_kernel(*refs, steps):
    def put(piece):
        refs[-1][...] = piece[...]

    at_chunk(steps, put, refs[: len(steps)])


def merge(pieces, first, height, unit, into, after):
    sources, _, lanes = pieces[0].shape
    steps = [piece.shape[1] // unit for piece in pieces]

    def block(start, count):
        return pl.BlockSpec(
            (sources, unit, lanes), lambda i: (0, jnp.clip(i - start, 0, count - 1), 0)
        )

    return pl.pallas_call(
        functools.partial(merge_kernel, steps=steps),
        grid=(sum(steps),),
        in_specs=[block(sum(steps[:at]), count) for at, count in enumerate(steps)]
        + anywhere(into)
        + anywhere(after),
        out_specs=pl.BlockSpec((sources, unit, lanes), lambda i: (0, i + first // unit, 0)),
        out_shape=jax.ShapeDtypeStruct((sources, height, lanes), BF16),
        input_output_aliases={len(pieces): 0} if into else {},
        compiler_params=params(),
        cost_estimate=LIGHT,
        name="merge",
    )(*pieces, *into, *after)


def partial_kernel(place_ref, logit_ref, *refs, row_count, col_count):
    sides, refs = refs[:col_count], refs[col_count:]
    project_ref, outs, exp_ref, value_ref = refs[0], refs[1 : 1 + row_count], *refs[-2:]
    rows, heads, cols = logit_ref.shape
    wide = value_ref.shape[2] // heads
    per_row = col_count // row_count
    for u, side in enumerate(sides):
        index = lax.rem(place_ref[1] + u, col_count)
        part = lax.rem(place_ref[0] + row_count - index // per_row, row_count)
        span = pl.multiple_of(lax.rem(index, per_row) * cols, cols)
        value_ref[part, pl.ds(span, cols), :] = jnp.dot(
            side[...], project_ref[...], preferred_element_type=F32
        ).astype(BF16)
    top = jnp.max(logit_ref[...], axis=0)
    powers = jnp.exp(logit_ref[...] - top[None])
    total = jnp.sum(powers, axis=0)
    exp_ref[:, 0:cols] = powers.reshape(rows * heads, cols)
    for h in range(heads):
        weights = exp_ref[pl.ds(h, rows, stride=heads), :][:, :cols].astype(BF16)
        for t, out in enumerate(outs):
            out[h, :cols] = lax.dot_general(
                weights,
                value_ref[t, :, h * wide : (h + 1) * wide],
                TN,
                preferred_element_type=F32,
            )
            out[h, cols:] = jnp.zeros((out.shape[1] - cols, wide), F32)
            out[h, cols : cols + 1, 0:cols] = top[h : h + 1]
            out[h, cols + 1 : cols + 2, 0:cols] = total[h : h + 1]


def partial_average(place, logits, sides, w_value):
    rows, heads, cols = logits.shape
    wide = w_value.shape[1] // heads
    row_count = len(sides) * cols // rows
    shape = (heads, cols + 8, wide)
    return pl.pallas_call(
        functools.partial(partial_kernel, row_count=row_count, col_count=len(sides)),
        grid=(1,),
        in_specs=[pl.BlockSpec(memory_space=pltpu.SMEM)]
        + [whole(v.shape) for v in (logits, *sides, w_value)],
        out_specs=[whole(shape)] * row_count,
        out_shape=[jax.ShapeDtypeStruct(shape, F32)] * row_count,
        scratch_shapes=[
            pltpu.VMEM((rows * heads, LANES), F32),
            pltpu.VMEM((row_count, rows, w_value.shape[1]), BF16),
        ],
        compiler_params=params(),
        cost_estimate=LIGHT,
        name="partial",
    )(place, logits, *sides, w_value)


def average_kernel(*refs):
    parts, (gate_ref, align_ref, weight_ref, out_ref) = refs[:-4], refs[-4:]
    heads, cols, _ = gate_ref.shape
    here = lax.broadcasted_iota(jnp.int32, (cols, cols), 0)
    there = lax.broadcasted_iota(jnp.int32, (cols, cols), 1)
    out = align_ref[...].astype(F32)
    for h in range(heads):
        tops = [part[h, cols : cols + 1, 0:cols] for part in parts]
        sums = [part[h, cols + 1 : cols + 2, 0:cols] for part in parts]
        top = functools.reduce(jnp.maximum, tops)
        scales = [jnp.exp(t - top) for t in tops]
        total = sum(scale * each for scale, each in zip(scales, sums))
        summed = jnp.zeros(gate_ref.shape[1:], F32)
        for part, scale in zip(parts, scales):
            factor = jnp.where(here == there, scale / total, 0.0)
            summed += jnp.dot(
                factor,
                part[h, :cols],
                precision=lax.Precision.HIGHEST,
                preferred_element_type=F32,
            )
        gated = (gate_ref[h] * summed).astype(BF16)
        out += jnp.dot(gated, weight_ref[h], preferred_element_type=F32)
    out_ref[...] = out.astype(BF16)


def average(parts, gate, align, weight):
    operands = [*parts, gate, align, weight]
    return pl.pallas_call(
        average_kernel,
        grid=(1,),
        in_specs=[whole(v.shape) for v in operands],
        out_specs=whole(align.shape),
        out_shape=jax.ShapeDtypeStruct(align.shape, BF16),
        compiler_params=params(),
        cost_estimate=LIGHT,
        name="average",
    )(*operands)


def finish_kernel(*refs, parts, steps):
    chunks = len(steps)
    products = refs[:parts]
    mids = refs[parts : parts + chunks]
    normeds = refs[parts + chunks : parts + 2 * chunks]
    gate_ref, weight_ref, out_ref, tmp_ref = refs[parts + 2 * chunks :]
    quads = out_ref.shape[0] // QUAD
    total = tmp_ref.shape[0] // quads
    first = 0
    for product in products:
        sources, height, _ = product.shape
        group = 8 // (height // quads)
        for low in range(0, sources, group):
            values = [product[src].astype(F32) for src in range(low, low + group)]
            for b, value in enumerate(exchange_rows(values)):
                for v in range(height // 8):
                    start = (v * group + b) * total + first
                    tmp_ref[start : start + 8] = value[8 * v : 8 * v + 8]
            first += 8

    def rows(mid_ref, normed_ref):
        count, cols, wide = normed_ref.shape
        gates = sigmoid(
            jnp.dot(
                normed_ref[...].reshape(count * cols, wide),
                gate_ref[...],
                preferred_element_type=F32,
            )
        )
        for m in range(quads):
            product = tmp_ref[m * total : (m + 1) * total]
            normed = standardize_features(product, 0).astype(BF16)
            out = lax.dot_general(normed, weight_ref[...], TN, preferred_element_type=F32)
            for a, value in enumerate(unpack_rows(out)):
                i = QUAD * m + a
                gate = gates[i * cols : (i + 1) * cols]
                out_ref[i] = (mid_ref[i].astype(F32) + gate * value).astype(BF16)

    at_chunk(steps, rows, mids, normeds)


def finish(products, mids, normeds, w_gate, w_final):
    _, cols, wide = mids[0].shape
    lanes = products[0].shape[2]
    total = sum(mid.shape[0] for mid in mids) // QUAD
    heights = [part.shape[1] // total for part in products]
    quads = max(8, 16 // min(heights))
    steps = [mid.shape[0] // QUAD // quads for mid in mids]
    tiles = chunk_tiles((quads * QUAD, cols, wide), steps)
    return pl.pallas_call(
        functools.partial(finish_kernel, parts=len(products), steps=steps),
        grid=(total // quads,),
        in_specs=[
            pl.BlockSpec((part.shape[0], quads * each, lanes), lambda i: (0, i, 0))
            for part, each in zip(products, heights)
        ]
        + tiles * 2
        + [whole(w_gate.shape), whole(w_final.shape)],
        out_specs=pl.BlockSpec((quads * QUAD, cols, wide), lambda i: (i, 0, 0)),
        out_shape=jax.ShapeDtypeStruct((total * QUAD, cols, wide), BF16),
        scratch_shapes=[pltpu.VMEM((quads * w_final.shape[0], lanes), F32)],
        compiler_params=params(),
        cost_estimate=LIGHT,
        name="finish",
    )(*products, *mids, *normeds, w_gate, w_final)


def on_device(
    alignment_embedding,
    coupling_embedding,
    amino_validity,
    alignment_validity,
    alignment_matrix,
    tensor_final_matrix,
    coupling_logit_matrix,
    mean_final_matrix,
    trimul_matrices,
    trimul_final_matrix,
):
    seq_each, module_number, feature_count = alignment_embedding.shape
    rows, _, wide = coupling_embedding.shape
    row_count = lax.axis_size("row")
    pos_count = lax.axis_size("pos")
    col_count = 2 * pos_count
    row_index = lax.axis_index("row")
    half = lax.axis_index("half")
    col_index = half * pos_count + lax.axis_index("pos")
    seqs = seq_each * row_count
    active_entries = amino_validity.astype(F32)
    sequence_index = lax.broadcasted_iota(jnp.int32, alignment_validity.shape, 0)
    present_entries = (
        jnp.where(sequence_index == 0, F32(1.0), alignment_validity.astype(F32))
        * active_entries[None, :]
    )
    row_start = row_index * rows
    col_start = col_index * module_number
    present_rows = lax.dynamic_slice_in_dim(present_entries, row_start, rows, 1)
    present_cols = lax.dynamic_slice_in_dim(present_entries, col_start, module_number, 1)
    live_rows = lax.dynamic_slice_in_dim(active_entries, row_start, rows, 0)
    live_cols = lax.dynamic_slice_in_dim(active_entries, col_start, module_number, 0)

    own_start = (row_index * seq_each, col_start)
    present_own = lax.dynamic_slice(present_entries, own_start, (seq_each, module_number))
    own_normed = standardize_features(alignment_embedding.astype(F32), 2).astype(BF16)
    own_normed = own_normed.reshape(seq_each * module_number, feature_count)

    def project_msa(matrix):
        return jnp.dot(own_normed, matrix, preferred_element_type=F32).reshape(
            seq_each, module_number, -1
        )

    own_right = project_msa(alignment_matrix[:, TENSOR_FEATURES : 2 * TENSOR_FEATURES])
    own_right = (own_right * present_own[:, :, None]).astype(BF16)
    own_rows = jnp.transpose(
        own_normed.reshape(seq_each, module_number, feature_count), (1, 0, 2)
    ).reshape(module_number, -1)
    apart = jnp.eye(seq_each, dtype=BF16)
    w_left = apart[:, :, None, None] * alignment_matrix[:, :TENSOR_FEATURES]
    w_left = w_left.reshape(seq_each, seq_each * feature_count, TENSOR_FEATURES)
    per_row = rows // module_number
    lefts = []
    for t in range(col_count):
        pairs = []
        for r in range(row_count):
            for q in range(col_count):
                to = (r * per_row + q % per_row - t) % col_count
                pairs.append((r * col_count + q, q // per_row * col_count + to))
        lefts.append(lax.ppermute(own_rows, AXES, pairs))
    rights = [own_right]
    for t in range(1, row_count):
        pairs = [(r, (r - t) % row_count) for r in range(row_count)]
        rights.append(lax.ppermute(own_right, "row", pairs))

    w_tensor = tensor_final_matrix.reshape(TENSOR_FEATURES, TENSOR_FEATURES * wide)
    unit = module_number // 3
    live_packed = jnp.concatenate(
        [live_cols[: 2 * unit]] * QUAD + [live_cols[2 * unit :]] * QUAD
    )[None]
    devices = row_count * col_count
    w_kinds = trimul_matrices[:, : 4 * CTRI].T.reshape(2, 2, CTRI, wide)
    w_logit = coupling_logit_matrix.T

    def side_weights(part):
        return jnp.transpose(part, (1, 2, 0, 3, 4)).reshape(-1, wide)

    def exchange(block, axes):
        return lax.all_to_all(block, axes, split_axis=0, concat_axis=0, tiled=True)

    def front_rows(first_row, count, after):
        return front(
            first_row,
            count,
            place,
            lefts,
            rights,
            present_rows,
            coupling_embedding,
            w_tensor,
            present_cols.T.astype(BF16),
            w_left,
            after,
        )

    def project_rows(first_row, normed, weight, dests):
        return project(first_row, live_rows, normed, live_packed, weight, dests)

    place = jnp.stack([row_index, col_index]).astype(jnp.int32)

    def by_head(part):
        part = part.reshape(seq_each, module_number, MEAN_GROUPS, GROUP_FEATURES)
        return jnp.transpose(part, (2, 1, 0, 3)).reshape(MEAN_GROUPS, module_number, -1)

    first = 2 * TENSOR_FEATURES
    middle = first + MEAN_GROUPS * GROUP_FEATURES
    w_value = alignment_matrix[:, first:middle].reshape(
        1, feature_count, MEAN_GROUPS, 1, GROUP_FEATURES
    )
    w_value = (w_value * apart.reshape(seq_each, 1, 1, seq_each, 1)).reshape(
        seq_each * feature_count, -1
    )
    sequence_gate = by_head(jax.nn.sigmoid(project_msa(alignment_matrix[:, middle:])))
    w_mean = mean_final_matrix.reshape(MEAN_GROUPS, 1, GROUP_FEATURES, 1, feature_count)
    w_mean = (w_mean * apart.reshape(1, seq_each, 1, seq_each, 1)).reshape(
        MEAN_GROUPS, seq_each * GROUP_FEATURES, seq_each * feature_count
    )
    align = jnp.transpose(alignment_embedding, (1, 0, 2)).reshape(module_number, -1)

    def gather_parts(parts):
        gathered = list(parts[:1])
        for t in range(1, row_count):
            pairs = [(r, (r - t) % row_count) for r in range(row_count)]
            gathered.append(lax.ppermute(parts[t], "row", pairs))
        return gathered

    group = devices // 2
    shape_of = (row_count, col_count, module_number)
    half_shape = (row_count, pos_count, module_number)
    mids, normeds, returned = [], [], []
    if CTRI // 2 % devices:
        row_chunks = rows // QUAD // 16
        sent, sides = (), ()
        weight = side_weights(w_kinds.reshape(2, 2, devices, -1, wide))
        for chunk in range(row_chunks):
            first_row = chunk * (rows // row_chunks)
            mid, normed = front_rows(first_row, rows // row_chunks, sent)
            block = project_rows(first_row, normed, weight, devices)
            sent = (block,)
            sides = assemble(chunk, row_chunks, 1, exchange(block, AXES), sides, (), *shape_of)
            mids.append(mid)
            normeds.append(normed)
        left, right = sides
        right = right.reshape(right.shape[0], -1, right.shape[-1])
        last = multiply(left, right, (), *shape_of[1:])
        returned.append(exchange(last, AXES))
        logits = logit(live_rows, normeds, w_logit, ())
        parts = partial_average(place, logits, lefts, w_value)
        parts = gather_parts(fence(parts, (last,)))
    else:
        cut = CTRI // 2
        row_chunks = [rows // 3, rows - rows // 3]
        w_half = side_weights(w_kinds[:, :, :cut].reshape(2, 2, group, -1, wide))
        w_both = w_kinds[:, :, cut:].reshape(2, 2, row_count, 2, pos_count, -1, wide)

        def half_weights(which):
            part = lax.dynamic_index_in_dim(w_both, which, 3, keepdims=False)
            return side_weights(part.reshape(2, 2, group, -1, wide))

        w_own, w_other = half_weights(half), half_weights(1 - half)
        swap = [(0, 1), (1, 0)]
        received, crossed, kept, ahead = [], [], [], ()
        for chunk, count in enumerate(row_chunks):
            first_row = sum(row_chunks[:chunk])
            mid, normed = front_rows(first_row, count, ahead)
            mids.append(mid)
            normeds.append(normed)
            to_half = project_rows(first_row, normed, w_half, group)
            to_other = project_rows(first_row, normed, w_other, group)
            to_other, to_half, w_own = fence([to_other, to_half, w_own], received + crossed)
            crossed.append(lax.ppermute(to_other, "half", swap))
            received.append(exchange(to_half, GROUP))
            ahead = (w_own,)
            kept.append(project_rows(first_row, normed, w_own, group))
        half_scalar = half.astype(jnp.int32).reshape(1)
        logits = logit(live_rows, normeds, w_logit, tuple(kept))
        parts = partial_average(place, logits, lefts, w_value)
        height = 2 * sum(part.shape[1] for part in kept)
        unit, last = kept[0].shape[1], height - kept[-1].shape[1]
        merged = merge(kept + crossed[:-1], 0, height, unit, (), ())
        left, own, theirs = assemble_half(
            half_scalar, received, (parts[0], merged), *half_shape
        )
        merged = merge(crossed[-1:], last, height, unit, (merged,), (left,))
        theirs, *parts = fence([theirs, *parts], ())
        partial = lax.ppermute(theirs, "half", swap)
        both = exchange(merged, GROUP)
        parts = gather_parts(parts)
        product = combine(left, own, partial, (both, *parts[1:]), *half_shape)
        returned.append(exchange(product, GROUP))
        left, right = assemble(0, 1, 2, both, (), (product,), *half_shape)
        right = right.reshape(right.shape[0], -1, right.shape[-1])
        last = multiply(left, right, (), *shape_of[1:])
        returned.append(exchange(last, AXES))
    parts = fence(parts, (last,))
    aligned = average(parts, sequence_gate, align, w_mean)
    alignment_updated_embedding = jnp.transpose(
        aligned.reshape(module_number, seq_each, feature_count), (1, 0, 2)
    )
    pair_output = finish(
        returned, mids, normeds, trimul_matrices[:, 4 * CTRI :], trimul_final_matrix
    )
    return (alignment_updated_embedding, pair_output)


def solution(mesh):
    rows, cols = mesh.devices.shape
    inner = Mesh(mesh.devices.reshape(rows, 2, cols // 2), AXES)
    tile = P("row", ("half", "pos"), None)
    in_specs = (tile, tile) + (P(),) * 8
    return jax.shard_map(
        on_device, mesh=inner, in_specs=in_specs, out_specs=(tile, tile), check_vma=False
    )
```

```python
import functools

import jax
import jax.numpy as jnp
from jax import lax
from jax.experimental import pallas as pl
from jax.experimental.pallas import tpu as pltpu
from jax.sharding import Mesh, PartitionSpec as P

TENSOR_FEATURES = 32
MEAN_GROUPS = 8
GROUP_FEATURES = 32
CTRI = 128

EPS = 1e-05
MASK_PENALTY = 10000.0
QUAD = 4
LANES = 128
MIB = 1024 * 1024
AXES = ("row", "half", "pos")
GROUP = ("row", "pos")
F32 = jnp.float32
BF16 = jnp.bfloat16
NT = (((1,), (1,)), ((), ()))
TN = (((0,), (0,)), ((), ()))


def standardize_features(values_in, axis):
    centre = values_in - jnp.mean(values_in, axis=axis, keepdims=True)
    spread = jnp.mean(centre * centre, axis=axis, keepdims=True)
    return centre * lax.rsqrt(spread + EPS)


def sigmoid(x):
    return 0.5 * jnp.tanh(0.5 * x) + 0.5


def params():
    return pltpu.CompilerParams(
        vmem_limit_bytes=60 * MIB, dimension_semantics=("arbitrary",)
    )


LIGHT = pl.CostEstimate(flops=1000, bytes_accessed=1000, transcendentals=0)


def whole(shape):
    zeros = (0,) * len(shape)
    return pl.BlockSpec(shape, lambda *_: zeros, pipeline_mode=pl.Buffered(1))


def anywhere(after):
    return [pl.BlockSpec(memory_space=pl.ANY)] * len(after)


def fence(values, after):
    return pl.pallas_call(
        lambda *refs: None,
        in_specs=anywhere(values) + anywhere(after),
        out_specs=anywhere(values),
        out_shape=[jax.ShapeDtypeStruct(v.shape, v.dtype) for v in values],
        input_output_aliases={i: i for i in range(len(values))},
        compiler_params=pltpu.CompilerParams(vmem_limit_bytes=60 * MIB),
        cost_estimate=LIGHT,
        name="fence",
    )(*values, *after)


def pack_rows(rows):
    unit = rows[0].shape[0] // 3
    return jnp.concatenate([r[: 2 * unit] for r in rows] + [r[2 * unit :] for r in rows], axis=0)


def unpack_rows(packed):
    unit = packed.shape[0] // 12
    return [
        jnp.concatenate(
            [
                packed[2 * unit * a : 2 * unit * (a + 1)],
                packed[8 * unit + unit * a : 8 * unit + unit * (a + 1)],
            ],
            axis=0,
        )
        for a in range(QUAD)
    ]


def swap_blocks(first, second, width, lane):
    low = (lane // width) % 2 == 0
    size = first.shape[1]
    return (
        jnp.where(low, first, pltpu.roll(second, width, 1)),
        jnp.where(low, pltpu.roll(first, size - width, 1), second),
    )


def exchange_blocks(packed):
    part = packed
    unit = LANES // 4
    lane = lax.broadcasted_iota(jnp.int32, part[0][0].shape, 1)
    out = [[None] * 3 for _ in range(4)]
    for pair in range(2):
        one, two = part[2 * pair], part[2 * pair + 1]
        for t in range(2):
            out[2 * t][pair], out[2 * t + 1][pair] = swap_blocks(one[t], two[t], 2 * unit, lane)
    u0, u2 = swap_blocks(part[0][2], part[2][2], 2 * unit, lane)
    u1, u3 = swap_blocks(part[1][2], part[3][2], 2 * unit, lane)
    out[0][2], out[1][2] = swap_blocks(u0, u1, unit, lane)
    out[2][2], out[3][2] = swap_blocks(u2, u3, unit, lane)
    return out


def front_kernel(place_ref, *refs, row_count, col_count, first_block):
    lefts, rights = refs[:col_count], refs[col_count : col_count + row_count]
    refs = refs[col_count + row_count :]
    prow_ref, coup_ref, weight_ref, pcol_ref, wleft_ref, pside_ref = refs[:6]
    sides_ref, right_ref, tmp_ref = refs[-3:]
    mid_ref, normed_ref = refs[-5:-3]
    step_at = pl.program_id(0) + first_block
    block, cols, wide = coup_ref.shape
    seq_each, _, width = wleft_ref.shape
    seqs = seq_each * row_count
    per_row = col_count // row_count

    @pl.when(pl.program_id(0) == 0)
    def _():
        for t, part in enumerate(lefts):
            index = lax.rem(t + place_ref[1], col_count)
            span = pl.multiple_of(lax.rem(index, per_row) * cols, cols)
            first = index // per_row * seq_each
            present = pside_ref[pl.ds(span, cols), :]
            seq_lane = lax.broadcasted_iota(jnp.int32, present.shape, 1)
            for k in range(seq_each):
                mask = jnp.sum(
                    jnp.where(seq_lane == first + k, present, 0.0), axis=1, keepdims=True
                )
                left = jnp.dot(part[...], wleft_ref[k], preferred_element_type=F32) * mask
                sides_ref[pl.ds(span * seqs + first + k, cols, stride=seqs), 0:width] = left
        right = jnp.zeros(right_ref.shape, F32)
        feature = lax.broadcasted_iota(jnp.int32, (width, width * seqs), 0)
        target = lax.broadcasted_iota(jnp.int32, (width, width * seqs), 1)
        for t, part in enumerate(rights):
            first = lax.rem(t + place_ref[0], row_count) * seq_each
            for k in range(seq_each):
                spread = (target == feature * seqs + (first + k)).astype(F32).astype(BF16)
                right += jnp.dot(part[k], spread, preferred_element_type=F32)
        right_ref[...] = right.astype(BF16)

    span = block * seqs
    start = pl.multiple_of(step_at * span, span)
    left = sides_ref[pl.ds(start, span), 0:width].astype(BF16)
    features = weight_ref.shape[1] // wide
    step = 4
    for low in range(0, features, step):
        part = jnp.dot(
            left, weight_ref[:, low * wide : (low + step) * wide], preferred_element_type=F32
        ).astype(BF16)
        for i in range(block):
            for d in range(step):
                tmp_ref[
                    i // 2,
                    (low + d) * seqs : (low + d + 1) * seqs,
                    (i % 2) * wide : (i % 2 + 1) * wide,
                ] = part[i * seqs : (i + 1) * seqs, d * wide : (d + 1) * wide]
    row_lane = lax.broadcasted_iota(jnp.int32, prow_ref.shape, 1)
    for pair in range(block // 2):
        update = jnp.dot(right_ref[...], tmp_ref[pair], preferred_element_type=F32)
        here = step_at * block + 2 * pair
        wanted = [jnp.where(row_lane == here + e, prow_ref[...], 0.0) for e in range(2)]
        wanted = [
            jnp.broadcast_to(jnp.sum(w, axis=1, keepdims=True), (seqs, wide)) for w in wanted
        ]
        count = jnp.dot(
            pcol_ref[...], jnp.concatenate(wanted, axis=1).astype(BF16), preferred_element_type=F32
        )
        update = update / jnp.maximum(count, 1.0)
        for e in range(2):
            i = 2 * pair + e
            mid = (coup_ref[i].astype(F32) + update[:, e * wide : (e + 1) * wide]).astype(BF16)
            mid_ref[i] = mid
            normed_ref[i] = standardize_features(mid.astype(F32), 1).astype(BF16)


def front(
    first_row, count, place, lefts, rights, present_rows, coupling, w_tensor, present_cols, w_left, after
):
    rows, cols, wide = coupling.shape
    seqs, width = present_rows.shape[0], w_left.shape[2]
    present_sides = present_rows.T
    block = 8
    steps, offset = count // block, first_row // block
    tile = pl.BlockSpec((block, cols, wide), lambda i: (i, 0, 0))
    return pl.pallas_call(
        functools.partial(
            front_kernel,
            row_count=len(rights),
            col_count=len(lefts),
            first_block=offset,
        ),
        grid=(steps,),
        in_specs=[pl.BlockSpec(memory_space=pltpu.SMEM)]
        + [whole(part.shape) for part in lefts + rights]
        + [
            whole(present_rows.shape),
            pl.BlockSpec((block, cols, wide), lambda i: (i + offset, 0, 0)),
            whole(w_tensor.shape),
            whole(present_cols.shape),
            whole(w_left.shape),
            whole(present_sides.shape),
        ]
        + anywhere(after),
        out_specs=[tile, tile],
        out_shape=[jax.ShapeDtypeStruct((count, cols, wide), BF16)] * 2,
        scratch_shapes=[
            pltpu.VMEM((rows * seqs + seqs, LANES), F32),
            pltpu.VMEM((cols, width * seqs), BF16),
            pltpu.VMEM((block // 2, width * seqs, 2 * wide), BF16),
        ],
        compiler_params=params(),
        cost_estimate=LIGHT,
        name="front",
    )(
        place,
        *lefts,
        *rights,
        present_rows,
        coupling,
        w_tensor,
        present_cols,
        w_left,
        present_sides,
        *after,
    )


def exchange_rows(values):
    values = list(values)
    count = len(values)
    step = count // 2
    row = lax.broadcasted_iota(jnp.int32, values[0].shape, 0)
    size = values[0].shape[0]
    while step:
        width = 8 // count * step
        low = (row // width) % 2 == 0
        for m in range(count):
            if m & step == 0:
                one, two = values[m], values[m + step]
                values[m] = jnp.where(low, one, pltpu.roll(two, width, 0))
                values[m + step] = jnp.where(low, pltpu.roll(one, size - width, 0), two)
        step //= 2
    return values


def project_kernel(live_ref, normed_ref, cols_ref, weight_ref, *refs, first_row):
    out_ref, tmp_ref = refs[-2:]
    quads = normed_ref.shape[0] // QUAD
    dests, height, lanes = out_ref.shape
    each = height // quads
    count = dests * each
    unit = lanes // 12
    lane = lax.broadcasted_iota(jnp.int32, (1, lanes), 1)
    place = jnp.where(lane < 8 * unit, lane // (2 * unit), (lane - 8 * unit) // unit)
    group = max(1, 8 // each)
    for first in range(0, quads, group):
        values = []
        for m in range(first, first + group):
            packed = pack_rows([normed_ref[QUAD * m + a] for a in range(QUAD)])
            both = lax.dot_general(weight_ref[...], packed, NT, preferred_element_type=F32)
            row = first_row + (pl.program_id(0) * quads + m) * QUAD
            live = cols_ref[...]
            for a in range(QUAD):
                live = jnp.where(place == a, live * live_ref[row + a], live)
            values.append(sigmoid(both[:count]) * both[count:] * live)
        for b, value in enumerate(exchange_rows(values)):
            size = each * group
            for v in range(count // size):
                tmp_ref[v * group + b, first * each : first * each + size] = value[
                    v * size : (v + 1) * size
                ]
    out_ref[...] = tmp_ref[...].astype(BF16)


def project(first_row, live_rows, normed, live_cols, weight, dests):
    rows, cols, wide = normed.shape
    each = weight.shape[0] // (2 * dests)
    quads = max(8, 16 // each)
    lanes = QUAD * cols
    total = rows // QUAD
    return pl.pallas_call(
        functools.partial(project_kernel, first_row=first_row),
        grid=(total // quads,),
        in_specs=[
            pl.BlockSpec(memory_space=pltpu.SMEM),
            pl.BlockSpec((quads * QUAD, cols, wide), lambda i: (i, 0, 0)),
            whole(live_cols.shape),
            whole(weight.shape),
        ],
        out_specs=pl.BlockSpec((dests, quads * each, lanes), lambda i: (0, i, 0)),
        out_shape=jax.ShapeDtypeStruct((dests, total * each, lanes), BF16),
        scratch_shapes=[pltpu.VMEM((dests, quads * each, lanes), F32)],
        compiler_params=params(),
        cost_estimate=LIGHT,
        name="project",
    )(live_rows, normed, live_cols, weight)


def at_chunk(steps, body, *groups):
    start = 0
    for chunk, count in enumerate(steps):
        here = (pl.program_id(0) >= start) & (pl.program_id(0) < start + count)
        pl.when(here)(functools.partial(body, *[group[chunk] for group in groups]))
        start += count


def chunk_tiles(shape, steps):
    def tile(start, count):
        return pl.BlockSpec(shape, lambda i: (jnp.clip(i - start, 0, count - 1), 0, 0))

    return [tile(sum(steps[:chunk]), count) for chunk, count in enumerate(steps)]


def logit_kernel(live_ref, *refs, steps):
    normeds, weight_ref, out_ref = refs[: len(steps)], refs[len(steps)], refs[-1]
    block = out_ref.shape[0]

    def rows(normed_ref):
        for i in range(block):
            live = live_ref[pl.program_id(0) * block + i]
            out_ref[i] = lax.dot_general(
                weight_ref[...], normed_ref[i], NT, preferred_element_type=F32
            ) + MASK_PENALTY * (live - 1.0)

    at_chunk(steps, rows, normeds)


def logit(live_rows, normeds, weight, after):
    _, cols, wide = normeds[0].shape
    block = 16
    steps = [normed.shape[0] // block for normed in normeds]
    heads = weight.shape[0]
    return pl.pallas_call(
        functools.partial(logit_kernel, steps=steps),
        grid=(sum(steps),),
        in_specs=[pl.BlockSpec(memory_space=pltpu.SMEM)]
        + chunk_tiles((block, cols, wide), steps)
        + [whole(weight.shape)]
        + anywhere(after),
        out_specs=pl.BlockSpec((block, heads, cols), lambda i: (i, 0, 0)),
        out_shape=jax.ShapeDtypeStruct((sum(steps) * block, heads, cols), F32),
        compiler_params=params(),
        cost_estimate=LIGHT,
        name="logit",
    )(live_rows, *normeds, weight, *after)


def assemble_kernel(recv_ref, *refs, row_count, pos_count, spans):
    left_ref, right_ref, flat_ref, rows_ref = refs[-4:]
    channel = pl.program_id(0)
    lanes = recv_ref.shape[2]
    each = left_ref.shape[2]
    height = recv_ref.shape[1] // spans
    stride = height // each
    groups = pos_count // 4
    tiles = lanes // LANES

    @pl.when(channel == 0)
    def _():
        for src in range(row_count * pos_count):
            value = recv_ref[src].astype(F32)
            for t in range(tiles):
                flat_ref[src, t, : recv_ref.shape[1]] = value[:, t * LANES : (t + 1) * LANES]

    def block(row, group, index):
        packed = []
        index = index + group // groups * height
        for p in range(4):
            src = row * pos_count + group % groups * 4 + p
            packed.append(
                [flat_ref[src, t, pl.ds(index, each, stride=stride), :] for t in range(tiles)]
            )
        return exchange_blocks(packed)

    for row in range(row_count):
        for group in range(groups * spans):
            span = slice(group * lanes, (group + 1) * lanes)
            left = block(row, group, channel)
            right = block(row, group, channel + stride // 2)
            for a in range(QUAD):
                left_ref[0, row * QUAD + a, :, span] = jnp.concatenate(left[a], axis=1).astype(BF16)
                for t in range(tiles):
                    rows_ref[t, pl.ds(a, each, stride=QUAD), :] = right[a][t]
            for t in range(tiles):
                at = slice(group * lanes + t * LANES, group * lanes + (t + 1) * LANES)
                right_ref[0, row, 0, :, at] = rows_ref[t, : QUAD * each].astype(BF16)


def assemble(chunk, chunks, spans, received, sides, after, row_count, pos_count, cols):
    sources, height, lanes = received.shape
    depth = spans * pos_count * cols
    each = depth // (row_count * QUAD * chunks)
    channels = height // spans // each // 2
    blocks = row_count * QUAD
    shapes = [
        (channels, blocks, each * chunks, depth),
        (channels, row_count, chunks, QUAD * each, depth),
    ]
    return pl.pallas_call(
        functools.partial(
            assemble_kernel, row_count=row_count, pos_count=pos_count, spans=spans
        ),
        grid=(channels,),
        in_specs=[whole(received.shape)] + anywhere(sides) + anywhere(after),
        out_specs=[
            pl.BlockSpec((1, blocks, each, depth), lambda c: (c, 0, chunk, 0)),
            pl.BlockSpec((1, row_count, 1, QUAD * each, depth), lambda c: (c, 0, chunk, 0, 0)),
        ],
        out_shape=[jax.ShapeDtypeStruct(shape, BF16) for shape in shapes],
        input_output_aliases={1: 0, 2: 1} if sides else {},
        scratch_shapes=[
            pltpu.VMEM((sources, lanes // LANES, height + 16, LANES), F32),
            pltpu.VMEM((lanes // LANES, QUAD * each + 8, LANES), F32),
        ],
        compiler_params=params(),
        cost_estimate=LIGHT,
        name="assemble",
    )(received, *sides, *after)


def multiply_kernel(left_ref, right_ref, *refs, pos_count):
    out_ref, tmp_ref = refs[-2:]
    channel = pl.program_id(0)
    channels = pl.num_programs(0)
    lanes = out_ref.shape[2]
    _, blocks, each, depth = left_ref.shape
    row_count = blocks // QUAD
    unit = lanes // 12
    stride = out_ref.shape[1] // each
    tiles = lanes // LANES
    for group in range(pos_count // 4):
        starts = [(group * 4 + p) * 3 * unit for p in range(4)]
        wanted = jnp.concatenate(
            [right_ref[0, start : start + 2 * unit] for start in starts]
            + [right_ref[0, start + 2 * unit : start + 3 * unit] for start in starts],
            axis=0,
        )
        for row in range(row_count):
            left = left_ref[0, row * QUAD : (row + 1) * QUAD].reshape(QUAD * each, depth)
            value = lax.dot_general(left, wanted, NT, preferred_element_type=F32)
            packed = [
                [
                    value[a * each : (a + 1) * each, t * LANES : (t + 1) * LANES]
                    for t in range(tiles)
                ]
                for a in range(QUAD)
            ]
            for p, part in enumerate(exchange_blocks(packed)):
                dest = row * pos_count + group * 4 + p
                for t in range(tiles):
                    tmp_ref[dest, t, pl.ds(channel, each, stride=stride), :] = part[t]

    @pl.when(channel == channels - 1)
    def _():
        for dest in range(row_count * pos_count):
            for t in range(tiles):
                out_ref[dest, :, t * LANES : (t + 1) * LANES] = tmp_ref[dest, t, : out_ref.shape[1]].astype(BF16)


def multiply(left, right, after, pos_count, cols):
    count, blocks, each, depth = left.shape
    lanes = QUAD * cols
    shape = (blocks // QUAD * pos_count, each * count, lanes)
    return pl.pallas_call(
        functools.partial(multiply_kernel, pos_count=pos_count),
        grid=(count,),
        in_specs=[
            pl.BlockSpec((1, blocks, each, depth), lambda c: (c, 0, 0, 0)),
            pl.BlockSpec((1, depth, depth), lambda c: (c, 0, 0)),
        ]
        + anywhere(after),
        out_specs=whole(shape),
        out_shape=jax.ShapeDtypeStruct(shape, BF16),
        scratch_shapes=[pltpu.VMEM((shape[0], lanes // LANES, shape[1] + 8, LANES), F32)],
        compiler_params=params(),
        cost_estimate=LIGHT,
        name="multiply",
    )(left, right, *after)


def assemble_half_kernel(half_ref, *refs, row_count, pos_count, parts):
    recvs = refs[:parts]
    left_ref, own_ref, send_ref, flat_ref, right_ref = refs[-5:]
    channel = pl.program_id(0)
    lanes = recvs[0].shape[2]
    unit = lanes // 12
    cols = 3 * unit
    each = send_ref.shape[1] // (row_count * QUAD)
    stride = sum(recv.shape[1] for recv in recvs) // each
    groups = pos_count // 4
    tiles = lanes // LANES
    per_row = each * QUAD // cols

    sorted_rows = stride == 8

    def sort(src, carry):
        start = 0
        for recv in recvs:
            for low in range(0, recv.shape[1], 64):
                value = recv[src, low : low + 64].astype(F32)
                values = exchange_rows([value[8 * i : 8 * i + 8] for i in range(8)])
                for index, part in enumerate(values):
                    at = index * each + start
                    for t in range(tiles):
                        flat_ref[src, t, at : at + 8] = part[:, t * LANES : (t + 1) * LANES]
                start += 8
        return carry

    @pl.when(channel == 0)
    def _():
        if sorted_rows:
            lax.fori_loop(0, row_count * pos_count, sort, 0)
            return
        for src in range(row_count * pos_count):
            start = 0
            for recv in recvs:
                value = recv[src].astype(F32)
                end = start + recv.shape[1]
                for t in range(tiles):
                    flat_ref[src, t, start:end] = value[:, t * LANES : (t + 1) * LANES]
                start = end

    def block(row, group, index):
        if sorted_rows:
            place = pl.ds(pl.multiple_of(index * each, each), each)
        else:
            place = pl.ds(index, each, stride=stride)
        packed = []
        for p in range(4):
            src = row * pos_count + group * 4 + p
            packed.append([flat_ref[src, t, place, :] for t in range(tiles)])
        return exchange_blocks(packed)

    for row in range(row_count):
        for group in range(groups):
            span = slice(group * lanes, (group + 1) * lanes)
            left = block(row, group, channel)
            for a in range(QUAD):
                start = (row * QUAD + a) * each
                left_ref[0, start : start + each, span] = jnp.concatenate(left[a], axis=1).astype(
                    BF16
                )
            right = block(row, group, channel + stride // 2)
            for a in range(QUAD):
                for piece in range(per_row):
                    place = row * per_row + piece
                    base = (place // 4) * lanes
                    low = piece * (cols // QUAD)
                    mid = low + 2 * unit // QUAD
                    high = low + cols // QUAD
                    first = base + (place % 4) * 2 * unit + a
                    second = base + 8 * unit + (place % 4) * unit + a
                    for t in range(tiles):
                        value = right[a][t]
                        at = group * tiles + t
                        right_ref[at, pl.ds(first, mid - low, stride=QUAD), :] = value[low:mid]
                        right_ref[at, pl.ds(second, high - mid, stride=QUAD), :] = value[mid:high]
    width = pos_count * cols
    own = pl.multiple_of(half_ref[0] * width, width)
    other = pl.multiple_of((1 - half_ref[0]) * width, width)
    theirs = []
    for at in range(groups * tiles):
        span = slice(at * LANES, (at + 1) * LANES)
        own_ref[0, :, span] = right_ref[at, pl.ds(own, width), :].astype(BF16)
        theirs.append(right_ref[at, pl.ds(other, width), :].astype(BF16))
    theirs = jnp.concatenate(theirs, axis=1)
    send_ref[0] = lax.dot_general(
        left_ref[0], theirs, NT, preferred_element_type=F32
    ).astype(BF16)


def assemble_half(half, received, after, row_count, pos_count, cols):
    sources, _, lanes = received[0].shape
    height = sum(part.shape[1] for part in received)
    each = (2 * pos_count * cols) // (row_count * QUAD)
    channels = height // each // 2
    depth = pos_count * cols
    rows = 2 * depth
    return pl.pallas_call(
        functools.partial(
            assemble_half_kernel, row_count=row_count, pos_count=pos_count, parts=len(received)
        ),
        grid=(channels,),
        in_specs=[pl.BlockSpec(memory_space=pltpu.SMEM)]
        + [whole(part.shape) for part in received]
        + anywhere(after),
        out_specs=[
            pl.BlockSpec((1, rows, depth), lambda c: (c, 0, 0)),
            pl.BlockSpec((1, depth, depth), lambda c: (c, 0, 0)),
            pl.BlockSpec((1, rows, depth), lambda c: (c, 0, 0)),
        ],
        out_shape=[
            jax.ShapeDtypeStruct((channels, rows, depth), BF16),
            jax.ShapeDtypeStruct((channels, depth, depth), BF16),
            jax.ShapeDtypeStruct((channels, rows, depth), BF16),
        ],
        scratch_shapes=[
            pltpu.VMEM((sources, lanes // LANES, height + 16, LANES), F32),
            pltpu.VMEM((depth // LANES, rows + 8, LANES), F32),
        ],
        compiler_params=params(),
        cost_estimate=LIGHT,
        name="assemble_half",
    )(half, *received, *after)


def combine_kernel(left_ref, own_ref, recv_ref, *refs, row_count, pos_count):
    out_ref, tmp_ref = refs[-2:]
    channel = pl.program_id(0)
    channels = pl.num_programs(0)
    lanes = out_ref.shape[2]
    each = left_ref.shape[1] // (row_count * QUAD)
    stride = out_ref.shape[1] // each
    tiles = lanes // LANES
    for group in range(pos_count // 4):
        cols = slice(group * lanes, (group + 1) * lanes)
        whole_value = lax.dot_general(
            left_ref[0], own_ref[0, cols], NT, preferred_element_type=F32
        )
        for row in range(row_count):
            span = slice(row * QUAD * each, (row + 1) * QUAD * each)
            value = whole_value[span] + recv_ref[0, span, cols].astype(F32)
            blocks = [
                [
                    value[a * each : (a + 1) * each, t * LANES : (t + 1) * LANES]
                    for t in range(tiles)
                ]
                for a in range(QUAD)
            ]
            for p, value in enumerate(exchange_blocks(blocks)):
                dest = row * pos_count + group * 4 + p
                for t in range(tiles):
                    tmp_ref[dest, t, pl.ds(channel, each, stride=stride), :] = value[t]

    @pl.when(channel == channels - 1)
    def _():
        for dest in range(row_count * pos_count):
            for t in range(tiles):
                out_ref[dest, :, t * LANES : (t + 1) * LANES] = tmp_ref[dest, t, : out_ref.shape[1]].astype(BF16)


def combine(left, own, received, after, row_count, pos_count, cols):
    channels, rows, depth = left.shape
    each = rows // (row_count * QUAD)
    shape = (row_count * pos_count, each * channels, QUAD * cols)
    return pl.pallas_call(
        functools.partial(combine_kernel, row_count=row_count, pos_count=pos_count),
        grid=(channels,),
        in_specs=[
            pl.BlockSpec((1, rows, depth), lambda c: (c, 0, 0)),
            pl.BlockSpec((1, depth, depth), lambda c: (c, 0, 0)),
            pl.BlockSpec((1, rows, depth), lambda c: (c, 0, 0)),
        ]
        + anywhere(after),
        out_specs=whole(shape),
        out_shape=jax.ShapeDtypeStruct(shape, BF16),
        scratch_shapes=[pltpu.VMEM((shape[0], shape[2] // LANES, shape[1] + 8, LANES), F32)],
        compiler_params=params(),
        cost_estimate=LIGHT,
        name="combine",
    )(left, own, received, *after)


def merge_kernel(*refs, steps):
    def put(piece):
        refs[-1][...] = piece[...]

    at_chunk(steps, put, refs[: len(steps)])


def merge(pieces, first, height, unit, into, after):
    sources, _, lanes = pieces[0].shape
    steps = [piece.shape[1] // unit for piece in pieces]

    def block(start, count):
        return pl.BlockSpec(
            (sources, unit, lanes), lambda i: (0, jnp.clip(i - start, 0, count - 1), 0)
        )

    return pl.pallas_call(
        functools.partial(merge_kernel, steps=steps),
        grid=(sum(steps),),
        in_specs=[block(sum(steps[:at]), count) for at, count in enumerate(steps)]
        + anywhere(into)
        + anywhere(after),
        out_specs=pl.BlockSpec((sources, unit, lanes), lambda i: (0, i + first // unit, 0)),
        out_shape=jax.ShapeDtypeStruct((sources, height, lanes), BF16),
        input_output_aliases={len(pieces): 0} if into else {},
        compiler_params=params(),
        cost_estimate=LIGHT,
        name="merge",
    )(*pieces, *into, *after)


def partial_kernel(place_ref, logit_ref, *refs, row_count, col_count):
    sides, refs = refs[:col_count], refs[col_count:]
    project_ref, outs, exp_ref, value_ref = refs[0], refs[1 : 1 + row_count], *refs[-2:]
    rows, heads, cols = logit_ref.shape
    wide = value_ref.shape[2] // heads
    per_row = col_count // row_count
    for u, side in enumerate(sides):
        index = lax.rem(place_ref[1] + u, col_count)
        part = lax.rem(place_ref[0] + row_count - index // per_row, row_count)
        span = pl.multiple_of(lax.rem(index, per_row) * cols, cols)
        value_ref[part, pl.ds(span, cols), :] = jnp.dot(
            side[...], project_ref[...], preferred_element_type=F32
        ).astype(BF16)
    top = jnp.max(logit_ref[...], axis=0)
    powers = jnp.exp(logit_ref[...] - top[None])
    total = jnp.sum(powers, axis=0)
    exp_ref[: rows * heads, 0:cols] = powers.reshape(rows * heads, cols)
    for h in range(heads):
        weights = exp_ref[pl.ds(h, rows, stride=heads), :][:, :cols].astype(BF16)
        for t, out in enumerate(outs):
            out[h, :cols] = lax.dot_general(
                weights,
                value_ref[t, :, h * wide : (h + 1) * wide],
                TN,
                preferred_element_type=F32,
            )
            out[h, cols:] = jnp.zeros((out.shape[1] - cols, wide), F32)
            out[h, cols : cols + 1, 0:cols] = top[h : h + 1]
            out[h, cols + 1 : cols + 2, 0:cols] = total[h : h + 1]


def partial_average(place, logits, sides, w_value):
    rows, heads, cols = logits.shape
    wide = w_value.shape[1] // heads
    row_count = len(sides) * cols // rows
    shape = (heads, cols + 8, wide)
    return pl.pallas_call(
        functools.partial(partial_kernel, row_count=row_count, col_count=len(sides)),
        grid=(1,),
        in_specs=[pl.BlockSpec(memory_space=pltpu.SMEM)]
        + [whole(v.shape) for v in (logits, *sides, w_value)],
        out_specs=[whole(shape)] * row_count,
        out_shape=[jax.ShapeDtypeStruct(shape, F32)] * row_count,
        scratch_shapes=[
            pltpu.VMEM((rows * heads + heads, LANES), F32),
            pltpu.VMEM((row_count, rows, w_value.shape[1]), BF16),
        ],
        compiler_params=params(),
        cost_estimate=LIGHT,
        name="partial",
    )(place, logits, *sides, w_value)


def average_kernel(*refs):
    parts, (gate_ref, align_ref, weight_ref, out_ref) = refs[:-4], refs[-4:]
    heads, cols, _ = gate_ref.shape
    here = lax.broadcasted_iota(jnp.int32, (cols, cols), 0)
    there = lax.broadcasted_iota(jnp.int32, (cols, cols), 1)
    out = align_ref[...].astype(F32)
    for h in range(heads):
        tops = [part[h, cols : cols + 1, 0:cols] for part in parts]
        sums = [part[h, cols + 1 : cols + 2, 0:cols] for part in parts]
        top = functools.reduce(jnp.maximum, tops)
        scales = [jnp.exp(t - top) for t in tops]
        total = sum(scale * each for scale, each in zip(scales, sums))
        summed = jnp.zeros(gate_ref.shape[1:], F32)
        for part, scale in zip(parts, scales):
            factor = jnp.where(here == there, scale / total, 0.0)
            summed += jnp.dot(
                factor,
                part[h, :cols],
                precision=lax.Precision.HIGHEST,
                preferred_element_type=F32,
            )
        gated = (gate_ref[h] * summed).astype(BF16)
        out += jnp.dot(gated, weight_ref[h], preferred_element_type=F32)
    out_ref[...] = out.astype(BF16)


def average(parts, gate, align, weight):
    operands = [*parts, gate, align, weight]
    return pl.pallas_call(
        average_kernel,
        grid=(1,),
        in_specs=[whole(v.shape) for v in operands],
        out_specs=whole(align.shape),
        out_shape=jax.ShapeDtypeStruct(align.shape, BF16),
        compiler_params=params(),
        cost_estimate=LIGHT,
        name="average",
    )(*operands)


def finish_kernel(*refs, parts, steps):
    chunks = len(steps)
    products = refs[:parts]
    mids = refs[parts : parts + chunks]
    normeds = refs[parts + chunks : parts + 2 * chunks]
    gate_ref, weight_ref, out_ref, tmp_ref = refs[parts + 2 * chunks :]
    quads = out_ref.shape[0] // QUAD
    total = tmp_ref.shape[0] // quads
    first = 0
    for product in products:
        sources, height, _ = product.shape
        group = 8 // (height // quads)
        for low in range(0, sources, group):
            values = [product[src].astype(F32) for src in range(low, low + group)]
            for b, value in enumerate(exchange_rows(values)):
                for v in range(height // 8):
                    start = (v * group + b) * total + first
                    tmp_ref[start : start + 8] = value[8 * v : 8 * v + 8]
            first += 8

    def rows(mid_ref, normed_ref):
        count, cols, wide = normed_ref.shape
        gates = sigmoid(
            jnp.dot(
                normed_ref[...].reshape(count * cols, wide),
                gate_ref[...],
                preferred_element_type=F32,
            )
        )
        for m in range(quads):
            product = tmp_ref[m * total : (m + 1) * total]
            normed = standardize_features(product, 0).astype(BF16)
            out = lax.dot_general(normed, weight_ref[...], TN, preferred_element_type=F32)
            for a, value in enumerate(unpack_rows(out)):
                i = QUAD * m + a
                gate = gates[i * cols : (i + 1) * cols]
                out_ref[i] = (mid_ref[i].astype(F32) + gate * value).astype(BF16)

    at_chunk(steps, rows, mids, normeds)


def finish(products, mids, normeds, w_gate, w_final):
    _, cols, wide = mids[0].shape
    lanes = products[0].shape[2]
    total = sum(mid.shape[0] for mid in mids) // QUAD
    heights = [part.shape[1] // total for part in products]
    quads = max(8, 16 // min(heights))
    steps = [mid.shape[0] // QUAD // quads for mid in mids]
    tiles = chunk_tiles((quads * QUAD, cols, wide), steps)
    return pl.pallas_call(
        functools.partial(finish_kernel, parts=len(products), steps=steps),
        grid=(total // quads,),
        in_specs=[
            pl.BlockSpec((part.shape[0], quads * each, lanes), lambda i: (0, i, 0))
            for part, each in zip(products, heights)
        ]
        + tiles * 2
        + [whole(w_gate.shape), whole(w_final.shape)],
        out_specs=pl.BlockSpec((quads * QUAD, cols, wide), lambda i: (i, 0, 0)),
        out_shape=jax.ShapeDtypeStruct((total * QUAD, cols, wide), BF16),
        scratch_shapes=[pltpu.VMEM((quads * w_final.shape[0], lanes), F32)],
        compiler_params=params(),
        cost_estimate=LIGHT,
        name="finish",
    )(*products, *mids, *normeds, w_gate, w_final)


def on_device(
    alignment_embedding,
    coupling_embedding,
    amino_validity,
    alignment_validity,
    alignment_matrix,
    tensor_final_matrix,
    coupling_logit_matrix,
    mean_final_matrix,
    trimul_matrices,
    trimul_final_matrix,
):
    seq_each, module_number, feature_count = alignment_embedding.shape
    rows, _, wide = coupling_embedding.shape
    row_count = lax.axis_size("row")
    pos_count = lax.axis_size("pos")
    col_count = 2 * pos_count
    row_index = lax.axis_index("row")
    half = lax.axis_index("half")
    col_index = half * pos_count + lax.axis_index("pos")
    seqs = seq_each * row_count
    active_entries = amino_validity.astype(F32)
    sequence_index = lax.broadcasted_iota(jnp.int32, alignment_validity.shape, 0)
    present_entries = (
        jnp.where(sequence_index == 0, F32(1.0), alignment_validity.astype(F32))
        * active_entries[None, :]
    )
    row_start = row_index * rows
    col_start = col_index * module_number
    present_rows = lax.dynamic_slice_in_dim(present_entries, row_start, rows, 1)
    present_cols = lax.dynamic_slice_in_dim(present_entries, col_start, module_number, 1)
    live_rows = lax.dynamic_slice_in_dim(active_entries, row_start, rows, 0)
    live_cols = lax.dynamic_slice_in_dim(active_entries, col_start, module_number, 0)

    own_start = (row_index * seq_each, col_start)
    present_own = lax.dynamic_slice(present_entries, own_start, (seq_each, module_number))
    own_normed = standardize_features(alignment_embedding.astype(F32), 2).astype(BF16)
    own_normed = own_normed.reshape(seq_each * module_number, feature_count)

    def project_msa(matrix):
        return jnp.dot(own_normed, matrix, preferred_element_type=F32).reshape(
            seq_each, module_number, -1
        )

    own_right = project_msa(alignment_matrix[:, TENSOR_FEATURES : 2 * TENSOR_FEATURES])
    own_right = (own_right * present_own[:, :, None]).astype(BF16)
    own_rows = jnp.transpose(
        own_normed.reshape(seq_each, module_number, feature_count), (1, 0, 2)
    ).reshape(module_number, -1)
    apart = jnp.eye(seq_each, dtype=BF16)
    w_left = apart[:, :, None, None] * alignment_matrix[:, :TENSOR_FEATURES]
    w_left = w_left.reshape(seq_each, seq_each * feature_count, TENSOR_FEATURES)
    per_row = rows // module_number
    lefts = []
    for t in range(col_count):
        pairs = []
        for r in range(row_count):
            for q in range(col_count):
                to = (r * per_row + q % per_row - t) % col_count
                pairs.append((r * col_count + q, q // per_row * col_count + to))
        lefts.append(lax.ppermute(own_rows, AXES, pairs))
    rights = [own_right]
    for t in range(1, row_count):
        pairs = [(r, (r - t) % row_count) for r in range(row_count)]
        rights.append(lax.ppermute(own_right, "row", pairs))

    w_tensor = tensor_final_matrix.reshape(TENSOR_FEATURES, TENSOR_FEATURES * wide)
    unit = module_number // 3
    live_packed = jnp.concatenate(
        [live_cols[: 2 * unit]] * QUAD + [live_cols[2 * unit :]] * QUAD
    )[None]
    devices = row_count * col_count
    w_kinds = trimul_matrices[:, : 4 * CTRI].T.reshape(2, 2, CTRI, wide)
    w_logit = coupling_logit_matrix.T

    def side_weights(part):
        return jnp.transpose(part, (1, 2, 0, 3, 4)).reshape(-1, wide)

    def exchange(block, axes):
        return lax.all_to_all(block, axes, split_axis=0, concat_axis=0, tiled=True)

    def front_rows(first_row, count, after):
        return front(
            first_row,
            count,
            place,
            lefts,
            rights,
            present_rows,
            coupling_embedding,
            w_tensor,
            present_cols.T.astype(BF16),
            w_left,
            after,
        )

    def project_rows(first_row, normed, weight, dests):
        return project(first_row, live_rows, normed, live_packed, weight, dests)

    place = jnp.stack([row_index, col_index]).astype(jnp.int32)

    def by_head(part):
        part = part.reshape(seq_each, module_number, MEAN_GROUPS, GROUP_FEATURES)
        return jnp.transpose(part, (2, 1, 0, 3)).reshape(MEAN_GROUPS, module_number, -1)

    first = 2 * TENSOR_FEATURES
    middle = first + MEAN_GROUPS * GROUP_FEATURES
    w_value = alignment_matrix[:, first:middle].reshape(
        1, feature_count, MEAN_GROUPS, 1, GROUP_FEATURES
    )
    w_value = (w_value * apart.reshape(seq_each, 1, 1, seq_each, 1)).reshape(
        seq_each * feature_count, -1
    )
    sequence_gate = by_head(jax.nn.sigmoid(project_msa(alignment_matrix[:, middle:])))
    w_mean = mean_final_matrix.reshape(MEAN_GROUPS, 1, GROUP_FEATURES, 1, feature_count)
    w_mean = (w_mean * apart.reshape(1, seq_each, 1, seq_each, 1)).reshape(
        MEAN_GROUPS, seq_each * GROUP_FEATURES, seq_each * feature_count
    )
    align = jnp.transpose(alignment_embedding, (1, 0, 2)).reshape(module_number, -1)

    def gather_parts(parts):
        gathered = list(parts[:1])
        for t in range(1, row_count):
            pairs = [(r, (r - t) % row_count) for r in range(row_count)]
            gathered.append(lax.ppermute(parts[t], "row", pairs))
        return gathered

    group = devices // 2
    shape_of = (row_count, col_count, module_number)
    half_shape = (row_count, pos_count, module_number)
    mids, normeds, returned = [], [], []
    if CTRI // 2 % devices:
        row_chunks = rows // QUAD // 16
        sent, sides = (), ()
        weight = side_weights(w_kinds.reshape(2, 2, devices, -1, wide))
        for chunk in range(row_chunks):
            first_row = chunk * (rows // row_chunks)
            mid, normed = front_rows(first_row, rows // row_chunks, sent)
            block = project_rows(first_row, normed, weight, devices)
            sent = (block,)
            sides = assemble(chunk, row_chunks, 1, exchange(block, AXES), sides, (), *shape_of)
            mids.append(mid)
            normeds.append(normed)
        left, right = sides
        right = right.reshape(right.shape[0], -1, right.shape[-1])
        last = multiply(left, right, (), *shape_of[1:])
        returned.append(exchange(last, AXES))
        logits = logit(live_rows, normeds, w_logit, ())
        parts = partial_average(place, logits, lefts, w_value)
        parts = gather_parts(fence(parts, (last,)))
    else:
        cut = CTRI // 2
        row_chunks = [rows // 3, rows - rows // 3]
        w_half = side_weights(w_kinds[:, :, :cut].reshape(2, 2, group, -1, wide))
        w_both = w_kinds[:, :, cut:].reshape(2, 2, row_count, 2, pos_count, -1, wide)

        def half_weights(which):
            part = lax.dynamic_index_in_dim(w_both, which, 3, keepdims=False)
            return side_weights(part.reshape(2, 2, group, -1, wide))

        w_own, w_other = half_weights(half), half_weights(1 - half)
        swap = [(0, 1), (1, 0)]
        received, crossed, kept, ahead = [], [], [], ()
        for chunk, count in enumerate(row_chunks):
            first_row = sum(row_chunks[:chunk])
            mid, normed = front_rows(first_row, count, ahead)
            mids.append(mid)
            normeds.append(normed)
            to_half = project_rows(first_row, normed, w_half, group)
            to_other = project_rows(first_row, normed, w_other, group)
            to_other, to_half, w_own = fence([to_other, to_half, w_own], received + crossed)
            crossed.append(lax.ppermute(to_other, "half", swap))
            received.append(exchange(to_half, GROUP))
            ahead = (w_own,)
            kept.append(project_rows(first_row, normed, w_own, group))
        half_scalar = half.astype(jnp.int32).reshape(1)
        logits = logit(live_rows, normeds, w_logit, tuple(kept))
        parts = partial_average(place, logits, lefts, w_value)
        height = 2 * sum(part.shape[1] for part in kept)
        unit, last = kept[0].shape[1], height - kept[-1].shape[1]
        merged = merge(kept + crossed[:-1], 0, height, unit, (), ())
        left, own, theirs = assemble_half(
            half_scalar, received, (parts[0], merged), *half_shape
        )
        merged = merge(crossed[-1:], last, height, unit, (merged,), (left,))
        theirs, *parts = fence([theirs, *parts], ())
        partial = lax.ppermute(theirs, "half", swap)
        both = exchange(merged, GROUP)
        parts = gather_parts(parts)
        product = combine(left, own, partial, (both, *parts[1:]), *half_shape)
        returned.append(exchange(product, GROUP))
        left, right = assemble(0, 1, 2, both, (), (product,), *half_shape)
        right = right.reshape(right.shape[0], -1, right.shape[-1])
        last = multiply(left, right, (), *shape_of[1:])
        returned.append(exchange(last, AXES))
    parts = fence(parts, (last,))
    aligned = average(parts, sequence_gate, align, w_mean)
    alignment_updated_embedding = jnp.transpose(
        aligned.reshape(module_number, seq_each, feature_count), (1, 0, 2)
    )
    pair_output = finish(
        returned, mids, normeds, trimul_matrices[:, 4 * CTRI :], trimul_final_matrix
    )
    return (alignment_updated_embedding, pair_output)


def solution(mesh):
    rows, cols = mesh.devices.shape
    inner = Mesh(mesh.devices.reshape(rows, 2, cols // 2), AXES)
    tile = P("row", ("half", "pos"), None)
    in_specs = (tile, tile) + (P(),) * 8
    return jax.shard_map(
        on_device, mesh=inner, in_specs=in_specs, out_specs=(tile, tile), check_vma=False
    )
```
